32 devices in a mesh: dp: 4 (over y, x), seq: 8 (over z, core).
Axes of the slice: x: 2, y: 2, z: 4, core: 2. Of those that a mesh axis runs over, the one named last changes fastest.
Arguments:
- tokens: bfloat16 [8, 1024, 1024], P('dp', 'seq'), may hold values from -6 to 6
- memory: bfloat16 [8, 128, 1024], P('dp', 'seq'), may hold values from -6 to 6
- lengths: int32 [8, 8], P('dp'), may hold values from 1 to 1017, as said below
- memory_segments: int32 [8, 128], P('dp'), may hold values from 0 to 7, never falling along the last dimension, each value on 1 to 64 neighbouring positions
- out_grad: bfloat16 [8, 1024, 1024], P('dp', 'seq'), may hold values from -6 to 6
- self_query: bfloat16 [1024, 1024], P(('dp', 'seq')), may hold values from -0.1875 to 0.1875
- self_key: bfloat16 [1024, 1024], P(('dp', 'seq')), may hold values from -0.1875 to 0.1875
- self_value: bfloat16 [1024, 1024], P(('dp', 'seq')), may hold values from -0.1875 to 0.1875
- self_out: bfloat16 [1024, 1024], P(('dp', 'seq')), may hold values from -6 to 6
- cross_query: bfloat16 [1024, 1024], P(('dp', 'seq')), may hold values from -0.1875 to 0.1875
- cross_key: bfloat16 [1024, 1024], P(('dp', 'seq')), may hold values from -0.1875 to 0.1875
- cross_value: bfloat16 [1024, 1024], P(('dp', 'seq')), may hold values from -0.1875 to 0.1875
- cross_out: bfloat16 [1024, 1024], P(('dp', 'seq')), may hold values from -6 to 6
- expand_weight: bfloat16 [1024, 4096], P(('dp', 'seq')), may hold values from -0.1875 to 0.1875
- shrink_weight: bfloat16 [4096, 1024], P(('dp', 'seq')), may hold values from -0.5 to 0.5
- norm_gains: bfloat16 [3, 1024], P(None, ('dp', 'seq')), may hold values from 0.5 to 1.5
- norm_biases: bfloat16 [3, 1024], P(None, ('dp', 'seq')), may hold values from -1.75 to 1.75
Outputs:
- output: bfloat16 [8, 1024, 1024], P('dp', 'seq')
- input_grad: float32 [8, 1024, 1024], P('dp', 'seq')
- memory_grad: float32 [8, 128, 1024], P('dp', 'seq')
- self_query_grad: float32 [1024, 1024], P(('dp', 'seq'))
- self_key_grad: float32 [1024, 1024], P(('dp', 'seq'))
- self_value_grad: float32 [1024, 1024], P(('dp', 'seq'))
- self_out_grad: float32 [1024, 1024], P(('dp', 'seq'))
- cross_query_grad: float32 [1024, 1024], P(('dp', 'seq'))
- cross_key_grad: float32 [1024, 1024], P(('dp', 'seq'))
- cross_value_grad: float32 [1024, 1024], P(('dp', 'seq'))
- cross_out_grad: float32 [1024, 1024], P(('dp', 'seq'))
- expand_grad: float32 [1024, 4096], P(('dp', 'seq'))
- shrink_grad: float32 [4096, 1024], P(('dp', 'seq'))
- gains_grad: float32 [3, 1024], P(None, ('dp', 'seq'))
- biases_grad: float32 [3, 1024], P(None, ('dp', 'seq'))
The draws below stay inside these ranges and needn't reach their ends.
Inputs may be any that keep to these rules, and one draw needn't show every extreme that they name: `lengths`: each row gives the token counts of the 8 sentences of a stream, which fill its 1024 tokens in order. In all streams but one, every sentence has 32 to 256 tokens; in one stream a single sentence takes all tokens but one at each side of it and at the end. `memory_segments`: each row gives, in order, the sentence of each memory position of a stream; every sentence has some positions.
All inputs are finite; a program needn't handle non-finite values.
Results may differ from the reference program's by a relative error of at most 0.022.
Values may be sent and summed in bfloat16 or wider, within the bound.
A program may use at most 256 MiB of HBM per device.

```python
import math
import jax
import jax.numpy as jnp
import numpy as np
from jax import lax

D = 1024
H = 16
HD = 64
FF = 4096
NSEG = 8
MEM = 128
STREAMS = 8
SEQ_LEN = 1024


def draw_lengths(key, part):
    key = jax.random.fold_in(key, 11)
    pair_key, pick_key = jax.random.split(key, 2)
    base_len = SEQ_LEN // NSEG
    least = SEQ_LEN // 32
    reach = base_len - least
    deltas = jax.random.randint(pair_key, (STREAMS, NSEG // 2), -reach, reach + 1, dtype=jnp.int32)
    paired = jnp.stack([deltas, -deltas], axis=2).reshape(STREAMS, NSEG)
    regular = base_len + paired
    chosen = jax.random.randint(pick_key, (), 0, STREAMS, dtype=jnp.int32)
    picked = (jnp.arange(STREAMS, dtype=jnp.int32) == chosen)[:, None]
    extreme = jnp.ones((STREAMS, NSEG), jnp.int32).at[:, 1].set(SEQ_LEN - NSEG + 1)
    return jnp.where(picked, extreme, regular)


def steps_of(own_key, shape, pieces, low, top_value):
    loudness, own = 1.0, jax.random.fold_in(own_key, 6)
    for dim, blocks in pieces:
        steps = jnp.exp(jax.random.uniform(jax.random.fold_in(own, dim), (blocks,), jnp.float32, low / len(pieces), top_value / len(pieces)))
        loudness = loudness * jnp.repeat(steps, shape[dim] // blocks).reshape([-1 if axis == dim else 1 for axis in range(len(shape))])
    return loudness


def length_profile(count, total, bound, slope):
    loads = [(1 << 20) // math.isqrt(grade ** slope) + 1 for grade in range(2, count + 1)]
    rest, counts = total - bound - (count - 1), [1] * (count - 1)
    while rest > 0:
        movable = [i for i in range(count - 1) if counts[i] < bound]
        pool, left = sum([loads[i] for i in movable]), rest
        for i in movable:
            extra = min(bound - counts[i], max(1, left * loads[i] // pool), rest)
            counts[i] = counts[i] + extra
            rest = rest - extra
    return np.array([bound] + counts)


def ragged(own_key, number_of, total, limit, lean):
    if number_of == 2:
        one = jax.random.randint(own_key, (), max(1, total - limit), min(limit, total - 1) + 1)
        return jnp.stack([one, total - one])
    tallies = jnp.asarray(length_profile(number_of, total, limit, lean), jnp.int32)
    pairs = (number_of - 1) // 2
    donor, taker = tallies[1:1 + 2 * pairs:2], tallies[2:2 + 2 * pairs:2]
    room = jnp.minimum(donor - 1, limit - taker)
    moved = jax.random.randint(jax.random.fold_in(own_key, 1), (pairs,), 0, 1 << 20) % (room + 1)
    tallies = tallies.at[1:1 + 2 * pairs:2].set(donor - moved).at[2:2 + 2 * pairs:2].set(taker + moved)
    return tallies[jax.random.permutation(jax.random.fold_in(own_key, 2), number_of)]


def gaussian(stream_key, dims, deviation, limit, cuts=(), kind=jnp.bfloat16):
    level = steps_of(stream_key, dims, cuts, -0.22, 0.18) if cuts else 1.0
    array = jax.random.normal(stream_key, dims, jnp.float32) * deviation * level
    return jnp.minimum(jnp.maximum(array, -limit), limit).astype(kind)


def setup_inputs(seed: int = 0) -> dict:
    key_of = jax.random.split(jax.random.key(seed), 18)
    return {
        "tokens": gaussian(key_of[0], (STREAMS, SEQ_LEN, D), 1.0, 6.0, ((0, 4), (1, 8))),
        "memory": gaussian(key_of[1], (STREAMS, MEM, D), 1.0, 6.0, ((0, 4), (1, 8))),
        "lengths": draw_lengths(jax.random.fold_in(key_of[17], 71), 0),
        "memory_segments": jax.vmap(lambda own: jnp.searchsorted(jnp.cumsum(ragged(own, NSEG, MEM, MEM // 2, 0)), jnp.arange(MEM), side="right"))(jax.random.split(key_of[3], STREAMS)).reshape((STREAMS, MEM)).astype(jnp.int32),
        "out_grad": gaussian(key_of[4], (STREAMS, SEQ_LEN, D), 1.0, 6.0, ((0, 4), (1, 8))),
        "self_query": gaussian(key_of[5], (D, D), D ** -0.5, 0.1875, ((0, 32),)),
        "self_key": gaussian(key_of[6], (D, D), D ** -0.5, 0.1875, ((0, 32),)),
        "self_value": gaussian(key_of[7], (D, D), D ** -0.5, 0.1875, ((0, 32),)),
        "self_out": gaussian(key_of[8], (D, D), 1 ** -0.5, 6.0, ((0, 32),)),
        "cross_query": gaussian(key_of[9], (D, D), D ** -0.5, 0.1875, ((0, 32),)),
        "cross_key": gaussian(key_of[10], (D, D), D ** -0.5, 0.1875, ((0, 32),)),
        "cross_value": gaussian(key_of[11], (D, D), D ** -0.5, 0.1875, ((0, 32),)),
        "cross_out": gaussian(key_of[12], (D, D), 1 ** -0.5, 6.0, ((0, 32),)),
        "expand_weight": gaussian(key_of[13], (D, FF), D ** -0.5, 0.1875, ((0, 32),)),
        "shrink_weight": gaussian(key_of[14], (FF, D), (FF // 32) ** -0.5, 0.5, ((0, 32),)),
        "norm_gains": jnp.clip(1.0 + 0.1 * jax.random.normal(key_of[15], (3, D), jnp.float32), 0.5, 1.5).astype(jnp.bfloat16),
        "norm_biases": gaussian(key_of[16], (3, D), 0.3, 1.75, ((1, 32),)),
    }


alpha_scale = 300.0 ** 0.25
norm_eps = 1e-05
masked_score = -1e+30

@jax.custom_vjp
def low(v):
    return lax.optimization_barrier(v.astype(jnp.bfloat16)).astype(jnp.float32)

@jax.custom_vjp
def low_back(v):
    return v

def low_keep(v):
    return (low(v), None)

def low_pass(kept, grad):
    return (grad,)

def back_keep(v):
    return (v, None)

def back_low(kept, grad):
    return (low(grad),)
low.defvjp(low_keep, low_pass)
low_back.defvjp(back_keep, back_low)

def precise(left, right):
    return jnp.dot(left, right, precision=lax.Precision.HIGHEST)

def rounded_both(value):
    return low_back(low(value))

def layer_norm(value, gain, bias):
    average = lax.optimization_barrier(jnp.mean(value, axis=-1, keepdims=True))
    centred = value - average
    spread = lax.optimization_barrier(jnp.mean(centred * centred, axis=-1, keepdims=True))
    return centred * lax.rsqrt(spread + norm_eps) * gain + bias

def sentence_ids(sentence_lengths, places):
    sent_ends = jnp.cumsum(sentence_lengths)[:-1]
    return lax.optimization_barrier(jnp.sum((places[:, None] >= sent_ends[None, :]).astype(jnp.int32), axis=1))

def attend(queries, key_rows, value_rows, query_ids, key_ids, causal):
    count = queries.shape[0]
    span = min(512, count)
    query_blocks = queries.reshape(count // span, span, H, HD)
    id_blocks = query_ids.reshape(count // span, span)
    place_blocks = jnp.arange(count, dtype=jnp.int32).reshape(count // span, span)
    key_heads = key_rows.reshape(key_rows.shape[0], H, HD)
    value_heads = value_rows.reshape(value_rows.shape[0], H, HD)
    key_places = jnp.arange(key_rows.shape[0], dtype=jnp.int32)
    scaling = HD ** (-0.5)

    def one_block(block_item):
        query_block, id_block, place_block = block_item
        scores = low_back(jnp.einsum('qhd,khd->hqk', query_block, key_heads, precision=lax.Precision.HIGHEST) * scaling)
        allowed = id_block[:, None] == key_ids[None, :]
        if causal:
            allowed = allowed & (key_places[None, :] <= place_block[:, None])
        scores = jnp.where(allowed[None], scores, masked_score)
        row_max = lax.optimization_barrier(jnp.max(scores, axis=-1, keepdims=True))
        powers = jnp.exp(scores - row_max)
        probability = powers / lax.optimization_barrier(jnp.sum(powers, axis=-1, keepdims=True))
        return jnp.einsum('hqk,khd->qhd', low(probability), value_heads, precision=lax.Precision.HIGHEST)
    attended = lax.map(jax.checkpoint(one_block), (query_blocks, id_blocks, place_blocks))
    return attended.reshape(count, H * HD)

def layer_forward(token_in, memory_in, token_ids, memory_ids, self_query, self_key, self_value, self_out, cross_query, cross_key, cross_value, cross_out, expand_weight, shrink_weight, norm_gains, norm_biases):
    queries = rounded_both(precise(token_in, self_query))
    key_rows = rounded_both(precise(token_in, self_key))
    value_rows = rounded_both(precise(token_in, self_value))
    attended = rounded_both(attend(queries, key_rows, value_rows, token_ids, token_ids, True))
    first = layer_norm(alpha_scale * token_in + low_back(precise(attended, self_out)), norm_gains[0], norm_biases[0])
    first_low = low(first)
    cross_queries = rounded_both(precise(first_low, cross_query))
    cross_keys = rounded_both(precise(memory_in, cross_key))
    cross_values = rounded_both(precise(memory_in, cross_value))
    cross_attended = rounded_both(attend(cross_queries, cross_keys, cross_values, token_ids, memory_ids, False))
    second = layer_norm(alpha_scale * first + low_back(precise(cross_attended, cross_out)), norm_gains[1], norm_biases[1])
    second_low = low(second)
    active_low = low(jax.nn.gelu(low_back(precise(second_low, expand_weight))))
    return layer_norm(alpha_scale * second + low_back(precise(active_low, shrink_weight)), norm_gains[2], norm_biases[2])

def reference(tokens, memory, lengths, memory_segments, out_grad, self_query, self_key, self_value, self_out, cross_query, cross_key, cross_value, cross_out, expand_weight, shrink_weight, norm_gains, norm_biases):
    params = (self_query.astype(jnp.float32), self_key.astype(jnp.float32), self_value.astype(jnp.float32), self_out.astype(jnp.float32), cross_query.astype(jnp.float32), cross_key.astype(jnp.float32), cross_value.astype(jnp.float32), cross_out.astype(jnp.float32), expand_weight.astype(jnp.float32), shrink_weight.astype(jnp.float32), norm_gains.astype(jnp.float32), norm_biases.astype(jnp.float32))
    places = jnp.arange(SEQ_LEN, dtype=jnp.int32)

    def one_stream(totals, stream_item):
        token_in, memory_in, sentence_lengths, memory_ids, cotangent = stream_item
        token_ids = sentence_ids(sentence_lengths, places)

        def bound_forward(token_arg, memory_arg, *weights):
            return layer_forward(token_arg, memory_arg, token_ids, memory_ids, *weights)
        result, pullback = jax.vjp(bound_forward, token_in.astype(jnp.float32), memory_in.astype(jnp.float32), *params)
        gradients = pullback(cotangent.astype(jnp.float32))
        totals = tuple((running + gradient for running, gradient in zip(totals, gradients[2:])))
        return (totals, (result.astype(jnp.bfloat16), gradients[0], gradients[1]))
    zero_grads = tuple((jnp.zeros_like(param) for param in params))
    totals, (outputs, input_grads, memory_grads) = lax.scan(one_stream, zero_grads, (tokens, memory, lengths, memory_segments, out_grad))
    return (outputs, input_grads, memory_grads, totals[0], totals[1], totals[2], totals[3], totals[4], totals[5], totals[6], totals[7], totals[8], totals[9], totals[10], totals[11])
```

```python
import functools

import jax
import jax.numpy as jnp
from jax import lax
from jax.experimental import pallas as pl
from jax.experimental.pallas import tpu as pltpu
from jax.sharding import PartitionSpec as P

H = 16
HD = 64
MB = 2

MESH = pl.DeviceIdType.MESH
BF = jnp.bfloat16
F32 = jnp.float32
ALL = slice(None)
D = 1024
UNITS = 16
SQUARE = 12
GRID = (2, 2, 4, 2)
VMEM_BYTES = 60 << 20


alpha_scale = 300.0**0.25
norm_eps = 1e-05
masked_score = -1e30


def layer_norm(value, gain, bias):
    average = jnp.mean(value, axis=-1, keepdims=True)
    centred = value - average
    spread = jnp.mean(centred * centred, axis=-1, keepdims=True)
    return centred * lax.rsqrt(spread + norm_eps) * gain + bias


def project(left, right):
    return jnp.dot(left, right, preferred_element_type=jnp.float32)


def project_back(left, right):
    return lax.dot_general(
        left, right, (((1,), (1,)), ((), ())), preferred_element_type=jnp.float32
    )


def weight_term(left, right):
    return lax.dot_general(
        left, right, (((0,), (0,)), ((), ())), preferred_element_type=jnp.float32
    )


def split_heads(value):
    return value.reshape(value.shape[0], value.shape[1], H, HD)


def sentence_ids(sent_ends, places):
    return jnp.sum((places[None, :, None] >= sent_ends[:, None, :]).astype(jnp.int32), axis=2)


def masked_scores(queries, key_heads, allowed, scaling):
    raw_scores = (
        jnp.einsum("gqhd,gkhd->ghqk", queries, key_heads, preferred_element_type=jnp.float32)
        * scaling
    )
    return jnp.where(allowed[:, None], raw_scores, masked_score)


def attend_forward(queries, key_heads, value_heads, allowed, scaling):
    scores = masked_scores(queries, key_heads, allowed, scaling)
    row_max = jnp.max(scores, axis=3, keepdims=True)
    powers = jnp.exp(scores - row_max)
    row_total = jnp.sum(powers, axis=3, keepdims=True)
    prob_low = (powers / row_total).astype(jnp.bfloat16)
    attended = jnp.einsum(
        "ghqk,gkhd->gqhd", prob_low, value_heads, preferred_element_type=jnp.float32
    )
    return (attended, row_max + jnp.log(row_total))


def attend_backward(queries, key_heads, value_heads, allowed, scaling, log_total, attended_grad):
    scores = masked_scores(queries, key_heads, allowed, scaling)
    probability = jnp.exp(scores - log_total)
    prob_grad = jnp.einsum(
        "gqhd,gkhd->ghqk", attended_grad, value_heads, preferred_element_type=jnp.float32
    )
    score_grad = probability * (prob_grad - jnp.sum(prob_grad * probability, axis=3, keepdims=True))
    score_low = score_grad.astype(jnp.bfloat16)
    query_grad = (
        jnp.einsum("ghqk,gkhd->gqhd", score_low, key_heads, preferred_element_type=jnp.float32)
        * scaling
    )
    return (query_grad, score_low, probability.astype(jnp.bfloat16))


def micro_batch(gathered, tokens, memory, lengths, memory_segments, out_grad):
    (
        self_query,
        self_key,
        self_value,
        self_out,
        cross_query,
        cross_key,
        cross_value,
        cross_out,
        expand_weight,
        shrink_weight,
        norm_gains,
        norm_biases,
    ) = gathered
    gains = norm_gains.astype(jnp.float32)
    biases = norm_biases.astype(jnp.float32)
    group_size, local_len, features = tokens.shape
    seq_count = lax.axis_size("seq")
    seq_index = lax.axis_index("seq")
    full_len = local_len * seq_count
    row_count = group_size * local_len
    scaling = HD ** (-0.5)
    sent_ends = jnp.cumsum(lengths, axis=1)[:, :-1]
    query_places = seq_index * local_len + jnp.arange(local_len, dtype=jnp.int32)
    key_places = jnp.arange(full_len, dtype=jnp.int32)
    query_ids = sentence_ids(sent_ends, query_places)
    key_ids = sentence_ids(sent_ends, key_places)
    self_allowed = (query_ids[:, :, None] == key_ids[:, None, :]) & (
        key_places[None, None, :] <= query_places[None, :, None]
    )
    cross_allowed = query_ids[:, :, None] == memory_segments[:, None, :]
    token_rows = tokens.reshape(row_count, features)
    queries = split_heads(
        project(token_rows, self_query)
        .astype(jnp.bfloat16)
        .reshape(group_size, local_len, features)
    )
    own_keys = (
        project(token_rows, self_key).astype(jnp.bfloat16).reshape(group_size, local_len, features)
    )
    own_values = (
        project(token_rows, self_value)
        .astype(jnp.bfloat16)
        .reshape(group_size, local_len, features)
    )
    all_keys, all_values = (
        lax.all_gather(own_keys, "seq", axis=1, tiled=True),
        lax.all_gather(own_values, "seq", axis=1, tiled=True),
    )
    key_heads = split_heads(all_keys)
    value_heads = split_heads(all_values)
    attended, self_log = attend_forward(queries, key_heads, value_heads, self_allowed, scaling)
    attended = attended.reshape(row_count, features).astype(jnp.bfloat16)
    first_pre = alpha_scale * token_rows.astype(jnp.float32) + project(attended, self_out)
    first, first_pull = jax.vjp(layer_norm, first_pre, gains[0], biases[0])
    first_low = first.astype(jnp.bfloat16)
    cross_queries = split_heads(
        project(first_low, cross_query)
        .astype(jnp.bfloat16)
        .reshape(group_size, local_len, features)
    )
    own_memory = memory.reshape(-1, features)
    memory_all = lax.all_gather(memory, "seq", axis=1, tiled=True)
    memory_rows = memory_all.reshape(-1, features)
    cross_keys = (
        project(memory_rows, cross_key).astype(jnp.bfloat16).reshape(group_size, -1, features)
    )
    cross_values = (
        project(memory_rows, cross_value).astype(jnp.bfloat16).reshape(group_size, -1, features)
    )
    cross_key_heads = split_heads(cross_keys)
    cross_value_heads = split_heads(cross_values)
    cross_attended, cross_log = attend_forward(
        cross_queries, cross_key_heads, cross_value_heads, cross_allowed, scaling
    )
    cross_attended = cross_attended.reshape(row_count, features).astype(jnp.bfloat16)
    second_pre = alpha_scale * first + project(cross_attended, cross_out)
    second, second_pull = jax.vjp(layer_norm, second_pre, gains[1], biases[1])
    second_low = second.astype(jnp.bfloat16)
    upward = project(second_low, expand_weight)
    active, gelu_pull = jax.vjp(jax.nn.gelu, upward)
    active_low = active.astype(jnp.bfloat16)
    third_pre = alpha_scale * second + project(active_low, shrink_weight)
    final, third_pull = jax.vjp(layer_norm, third_pre, gains[2], biases[2])
    third_grad, gain_third, bias_third = third_pull(
        out_grad.reshape(row_count, features).astype(jnp.float32)
    )
    branch_grad = third_grad.astype(jnp.bfloat16)
    shrink_grad = weight_term(active_low, branch_grad)
    (up_grad,) = gelu_pull(project_back(branch_grad, shrink_weight))
    up_low = up_grad.astype(jnp.bfloat16)
    expand_grad = weight_term(second_low, up_low)
    second_grad = alpha_scale * third_grad + project_back(up_low, expand_weight)
    second_pre_grad, gain_second, bias_second = second_pull(second_grad)
    cross_branch = second_pre_grad.astype(jnp.bfloat16)
    cross_out_grad = weight_term(cross_attended, cross_branch)
    cross_attended_grad = split_heads(
        project_back(cross_branch, cross_out)
        .astype(jnp.bfloat16)
        .reshape(group_size, local_len, features)
    )
    cross_q_grad, cross_scores, cross_probs = attend_backward(
        cross_queries,
        cross_key_heads,
        cross_value_heads,
        cross_allowed,
        scaling,
        cross_log,
        cross_attended_grad,
    )
    cross_q_low = cross_q_grad.reshape(row_count, features).astype(jnp.bfloat16)
    cross_query_grad = weight_term(first_low, cross_q_low)
    key_term = (
        jnp.einsum(
            "ghqk,gqhd->gkhd", cross_scores, cross_queries, preferred_element_type=jnp.float32
        )
        * scaling
    ).reshape(group_size, -1, features)
    value_term = jnp.einsum(
        "ghqk,gqhd->gkhd", cross_probs, cross_attended_grad, preferred_element_type=jnp.float32
    ).reshape(group_size, -1, features)
    key_summed, value_summed = (
        lax.psum_scatter(
            key_term.astype(jnp.bfloat16), "seq", scatter_dimension=1, tiled=True
        ).astype(jnp.float32),
        lax.psum_scatter(
            value_term.astype(jnp.bfloat16), "seq", scatter_dimension=1, tiled=True
        ).astype(jnp.float32),
    )
    key_low = key_summed.reshape(-1, features).astype(jnp.bfloat16)
    value_low = value_summed.reshape(-1, features).astype(jnp.bfloat16)
    cross_key_grad = weight_term(own_memory, key_low)
    cross_value_grad = weight_term(own_memory, value_low)
    memory_grad = (project_back(key_low, cross_key) + project_back(value_low, cross_value)).reshape(
        memory.shape
    )
    first_grad = alpha_scale * second_pre_grad + project_back(cross_q_low, cross_query)
    first_pre_grad, gain_first, bias_first = first_pull(first_grad)
    self_branch = first_pre_grad.astype(jnp.bfloat16)
    self_out_grad = weight_term(attended, self_branch)
    attended_grad = split_heads(
        project_back(self_branch, self_out)
        .astype(jnp.bfloat16)
        .reshape(group_size, local_len, features)
    )
    self_q_grad, self_scores, self_probs = attend_backward(
        queries, key_heads, value_heads, self_allowed, scaling, self_log, attended_grad
    )
    count = local_len * lax.axis_size("seq")
    key_part = (
        jnp.einsum("ghqk,gqhd->kghd", self_scores, queries, preferred_element_type=jnp.float32)
        * scaling
    )
    value_part = jnp.einsum(
        "ghqk,gqhd->kghd", self_probs, attended_grad, preferred_element_type=jnp.float32
    )
    pair_summed = lax.psum_scatter(
        jnp.concatenate(
            [
                key_part.reshape(count, group_size, features),
                value_part.reshape(count, group_size, features),
            ],
            axis=2,
        ).astype(jnp.bfloat16),
        "seq",
        scatter_dimension=0,
        tiled=True,
    ).astype(jnp.float32)
    key_grad = (
        pair_summed[:, :, :features]
        .astype(jnp.bfloat16)
        .transpose(1, 0, 2)
        .reshape(row_count, features)
    )
    value_grad = (
        pair_summed[:, :, features:]
        .astype(jnp.bfloat16)
        .transpose(1, 0, 2)
        .reshape(row_count, features)
    )
    query_low = self_q_grad.reshape(row_count, features).astype(jnp.bfloat16)
    self_query_grad = weight_term(token_rows, query_low)
    self_key_grad = weight_term(token_rows, key_grad)
    self_value_grad = weight_term(token_rows, value_grad)
    input_grad = (
        alpha_scale * first_pre_grad
        + project_back(query_low, self_query)
        + project_back(key_grad, self_key)
        + project_back(value_grad, self_value)
    )
    gains_grad = jnp.stack([gain_first, gain_second, gain_third])
    biases_grad = jnp.stack([bias_first, bias_second, bias_third])
    gradients = (
        self_query_grad,
        self_key_grad,
        self_value_grad,
        self_out_grad,
        cross_query_grad,
        cross_key_grad,
        cross_value_grad,
        cross_out_grad,
        expand_grad,
        shrink_grad,
        gains_grad,
        biases_grad,
    )
    result = final.astype(jnp.bfloat16).reshape(group_size, local_len, features)
    return (result, input_grad.reshape(group_size, local_len, features), memory_grad, gradients)


def shards(
    tokens,
    memory,
    lengths,
    memory_segments,
    out_grad,
    self_query,
    self_key,
    self_value,
    self_out,
    cross_query,
    cross_key,
    cross_value,
    cross_out,
    expand_weight,
    shrink_weight,
    norm_gains,
    norm_biases,
):
    group_size = tokens.shape[0] // MB
    outputs = []
    input_grads = []
    memory_grads = []
    totals = None
    for batch_index in range(MB):
        gathered = (
            lax.all_gather(self_query, ("dp", "seq"), axis=0, tiled=True),
            lax.all_gather(self_key, ("dp", "seq"), axis=0, tiled=True),
            lax.all_gather(self_value, ("dp", "seq"), axis=0, tiled=True),
            lax.all_gather(self_out, ("dp", "seq"), axis=0, tiled=True),
            lax.all_gather(cross_query, ("dp", "seq"), axis=0, tiled=True),
            lax.all_gather(cross_key, ("dp", "seq"), axis=0, tiled=True),
            lax.all_gather(cross_value, ("dp", "seq"), axis=0, tiled=True),
            lax.all_gather(cross_out, ("dp", "seq"), axis=0, tiled=True),
            lax.all_gather(expand_weight, ("dp", "seq"), axis=0, tiled=True),
            lax.all_gather(shrink_weight, ("dp", "seq"), axis=0, tiled=True),
            lax.all_gather(norm_gains, ("dp", "seq"), axis=1, tiled=True),
            lax.all_gather(norm_biases, ("dp", "seq"), axis=1, tiled=True),
        )
        start = batch_index * group_size
        stop = start + group_size
        result, input_grad, memory_grad, gradients = micro_batch(
            gathered,
            tokens[start:stop],
            memory[start:stop],
            lengths[start:stop],
            memory_segments[start:stop],
            out_grad[start:stop],
        )
        outputs.append(result)
        input_grads.append(input_grad)
        memory_grads.append(memory_grad)
        if totals is None:
            totals = gradients
        else:
            totals = tuple((running + gradient for running, gradient in zip(totals, gradients)))
    summed = (
        lax.psum_scatter(totals[0], ("dp", "seq"), scatter_dimension=0, tiled=True),
        lax.psum_scatter(totals[1], ("dp", "seq"), scatter_dimension=0, tiled=True),
        lax.psum_scatter(totals[2], ("dp", "seq"), scatter_dimension=0, tiled=True),
        lax.psum_scatter(totals[3], ("dp", "seq"), scatter_dimension=0, tiled=True),
        lax.psum_scatter(totals[4], ("dp", "seq"), scatter_dimension=0, tiled=True),
        lax.psum_scatter(totals[5], ("dp", "seq"), scatter_dimension=0, tiled=True),
        lax.psum_scatter(totals[6], ("dp", "seq"), scatter_dimension=0, tiled=True),
        lax.psum_scatter(totals[7], ("dp", "seq"), scatter_dimension=0, tiled=True),
        lax.psum_scatter(totals[8], ("dp", "seq"), scatter_dimension=0, tiled=True),
        lax.psum_scatter(totals[9], ("dp", "seq"), scatter_dimension=0, tiled=True),
        lax.psum_scatter(totals[10], ("dp", "seq"), scatter_dimension=1, tiled=True),
        lax.psum_scatter(totals[11], ("dp", "seq"), scatter_dimension=1, tiled=True),
    )
    return (
        jnp.concatenate(outputs, 0),
        jnp.concatenate(input_grads, 0),
        jnp.concatenate(memory_grads, 0),
        summed[0],
        summed[1],
        summed[2],
        summed[3],
        summed[4],
        summed[5],
        summed[6],
        summed[7],
        summed[8],
        summed[9],
        summed[10],
        summed[11],
    )


class Place:
    def __init__(self):
        dp, seq = lax.axis_index("dp"), lax.axis_index("seq")
        self.x, self.y, self.core, self.z = dp % 2, dp // 2, seq % 2, seq // 2

    def at(self, y=None, x=None, z=None, core=None):
        y = self.y if y is None else y
        x = self.x if x is None else x
        z = self.z if z is None else z
        core = self.core if core is None else core
        return (y * 2 + x, z * 2 + core)

    def across(self, axis):
        if axis == "x":
            return self.at(x=1 - self.x)
        if axis == "y":
            return self.at(y=1 - self.y)
        return self.at(core=1 - self.core)

    def along_z(self, step):
        return self.at(z=(self.z + step) % 4)

    def greet(self):
        barrier = pltpu.get_barrier_semaphore()
        peers = [self.across(axis) for axis in ("x", "y", "core")]
        peers += [self.along_z(step) for step in (1, 2, 3)]
        for peer in peers:
            pl.semaphore_signal(barrier, inc=1, device_id=peer, device_id_type=MESH)
        pl.semaphore_wait(barrier, len(peers))


def all_sum(place, part, total, work, send_sem, recv_sem):
    def copy(number, send_slot, recv_slot, device):
        return pltpu.make_async_remote_copy(
            src_ref=work.at[0],
            dst_ref=work.at[recv_slot],
            send_sem=send_sem.at[send_slot],
            recv_sem=recv_sem.at[recv_slot],
            device_id=device,
            device_id_type=MESH,
        )

    work[0] = part
    for number, axis in enumerate(("core", "y", "x")):
        step = copy(number, number, 1 + number, place.across(axis))
        step.start()
        step.wait()
        work[0] = work[0] + work[1 + number]
    steps = [copy(3, 2 + k, 4 + place.z, place.along_z(k)) for k in (1, 2, 3)]
    for step in steps:
        step.start()
    result = work[0]
    for k in (1, 2, 3):
        source = (place.z + k) % 4
        copy(3, 0, 4 + source, place.along_z(k)).wait_recv()
        result = result + work[4 + source]
    for step in steps:
        step.wait_send()
    total[...] = result


def gather_kernel(own, norms, square, shrink, norms_all, work, send_sem, recv_sem, own_sem, sum_send, sum_recv):
    place = Place()
    y, x, z, core = place.y, place.x, place.z, place.core
    place.greet()
    sent = []

    def block(unit, *index):
        if unit < SQUARE:
            return square.at[(unit,) + index]
        return shrink.at[index + (unit - SQUARE,)]

    def copy(unit, send_slot, recv_slot, source, target, device):
        return pltpu.make_async_remote_copy(
            src_ref=source,
            dst_ref=target,
            send_sem=send_sem.at[unit, send_slot],
            recv_sem=recv_sem.at[unit, recv_slot],
            device_id=device,
            device_id_type=MESH,
        )

    def send(unit, send_slot, recv_slot, source, target, device):
        step = copy(unit, send_slot, recv_slot, source, target, device)
        step.start()
        sent.append(step)

    def share(unit, slot, part, device):
        send(unit, slot, slot, part, part, device)

    def arrived(unit, slot, target):
        copy(unit, 0, slot, target, target, place.across("core")).wait_recv()

    def phase(unit, number):
        by_x = unit % 2 == 0
        first, second = ("x", "y") if by_x else ("y", "x")
        line = (y, x, ALL)
        line_in = (y, 1 - x, ALL) if by_x else (1 - y, x, ALL)
        sheet = (y, ALL, ALL) if by_x else (ALL, x, ALL)
        sheet_in = (1 - y, ALL, ALL) if by_x else (ALL, 1 - x, ALL)
        if number == 0:
            for k in (1, 2, 3):
                send(unit, k, z, own.at[unit], block(unit, y, x, z, core), place.along_z(k))
        if number == 1:
            pltpu.make_async_copy(own.at[unit], block(unit, y, x, z, core), own_sem.at[unit]).wait()
            for k in (1, 2, 3):
                source = (z + k) % 4
                arrived(unit, source, block(unit, y, x, source, core))
            share(unit, 4, block(unit, *line, core), place.across(first))
            share(unit, 6, block(unit, *line, core), place.across("core"))
        if number == 2:
            arrived(unit, 4, block(unit, *line_in, core))
            share(unit, 5, block(unit, *sheet, core), place.across(second))
            share(unit, 7, block(unit, *line_in, core), place.across("core"))
        if number == 3:
            arrived(unit, 5, block(unit, *sheet_in, core))
            share(unit, 8, block(unit, *sheet_in, core), place.across("core"))
        if number == 4:
            arrived(unit, 6, block(unit, *line, 1 - core))
            arrived(unit, 7, block(unit, *line_in, 1 - core))
            arrived(unit, 8, block(unit, *sheet_in, 1 - core))

    for unit in range(UNITS):
        pltpu.make_async_copy(own.at[unit], block(unit, y, x, z, core), own_sem.at[unit]).start()
    for unit in range(4):
        phase(unit, 0)
    all_sum(place, norms[...], norms_all, work, sum_send, sum_recv)
    pairs = UNITS // 2
    for tick in range(1, pairs + 4):
        for number in (0, 4, 3, 2, 1):
            pair = tick + 1 if number == 0 else tick - number
            if (2 if number == 0 else 0) <= pair < pairs:
                for unit in (2 * pair, 2 * pair + 1):
                    phase(unit, number)
    for step in sent:
        step.wait_send()


def scatter_kernel(
    square, shrink, norms, out, norms_all, held, from_core, from_first, from_second, from_z, work,
    load_sem, send_sem, recv_sem, sum_send, sum_recv,
):
    place = Place()
    y, x, z, core = place.y, place.x, place.z, place.core
    place.greet()
    slots = held.shape[0]
    sent = {}

    def load(unit):
        source = square.at[unit] if unit < SQUARE else shrink.at[:, :, :, :, unit - SQUARE]
        return pltpu.make_async_copy(source, held.at[unit % slots], load_sem.at[unit % slots])

    def copy(unit, half, send_slot, recv_slot, source, target, device):
        return pltpu.make_async_remote_copy(
            src_ref=source,
            dst_ref=target,
            send_sem=send_sem.at[unit, half, send_slot],
            recv_sem=recv_sem.at[unit, half, recv_slot],
            device_id=device,
            device_id_type=MESH,
        )

    def send(unit, half, send_slot, recv_slot, source, target, device):
        step = copy(unit, half, send_slot, recv_slot, source, target, device)
        step.start()
        sent.setdefault(unit, []).append(step)

    def arrived(unit, half, slot, target):
        copy(unit, half, 0, slot, target, target, place.across("core")).wait_recv()

    def add(total, part, count):
        def one(index, _):
            mine = total.at[index // 4] if count > 1 else total
            theirs = part.at[index // 4] if count > 1 else part
            row = index % 4
            mine[row] = (mine[row].astype(F32) + theirs[row].astype(F32)).astype(BF)
            return 0

        lax.fori_loop(0, 4 * count, one, 0)

    def phase(unit, half, number):
        here = held.at[unit % slots]
        rows = pl.ds(16 * half, 16)
        by_y = half == 0
        first, second = ("y", "x") if by_y else ("x", "y")
        away = (1 - y, ALL) if by_y else (ALL, 1 - x)
        keep = (y, ALL) if by_y else (ALL, x)
        corner = (y, 1 - x) if by_y else (1 - y, x)
        if number == 0:
            send(unit, half, 0, 0, here.at[:, :, :, 1 - core, rows], from_core.at[unit, :, :, :, rows], place.across("core"))
        if number == 1:
            arrived(unit, half, 0, from_core.at[unit, :, :, :, rows])
            add(here.at[(*away, ALL, core, rows)], from_core.at[(unit, *away, ALL, rows)], 2)
            send(unit, half, 1, 1, here.at[(*away, ALL, core, rows)], from_first.at[unit, :, :, rows], place.across(first))
            add(here.at[(*keep, ALL, core, rows)], from_core.at[(unit, *keep, ALL, rows)], 2)
        if number == 2:
            arrived(unit, half, 1, from_first.at[unit, :, :, rows])
            other, mine = (1 - x, x) if by_y else (1 - y, y)
            add(here.at[(*corner, ALL, core, rows)], from_first.at[unit, other, :, rows], 1)
            send(unit, half, 2, 2, here.at[(*corner, ALL, core, rows)], from_second.at[unit, :, rows], place.across(second))
            add(here.at[y, x, :, core, rows], from_first.at[unit, mine, :, rows], 1)
        if number == 3:
            arrived(unit, half, 2, from_second.at[unit, :, rows])
            add(here.at[y, x, :, core, rows], from_second.at[unit, :, rows], 1)
            for k in (1, 2, 3):
                target = (z + k) % 4
                send(unit, half, 3 + k, 4 + z, here.at[y, x, target, core, rows], from_z.at[unit, z, rows], place.along_z(k))
        if number == 4:
            total = here[y, x, z, core, rows].astype(F32)
            for k in (1, 2, 3):
                source = (z + k) % 4
                arrived(unit, half, 4 + source, from_z.at[unit, source, rows])
                total = total + from_z[unit, source, rows].astype(F32)
            out[unit, rows] = total

    for tick in range(UNITS + 4):
        if tick < UNITS:
            for unit in (0, 1, 2) if tick == 0 else (tick + 2,):
                if unit < UNITS:
                    for step in sent.pop(unit - slots, ()):
                        step.wait_send()
                    load(unit).start()
            load(tick).wait()
        for number in range(5):
            unit = tick - number
            if 0 <= unit < UNITS:
                for half in (0, 1):
                    phase(unit, half, number)
        if tick == 3:
            all_sum(place, norms[...], norms_all, work, sum_send, sum_recv)
    for steps in sent.values():
        for step in steps:
            step.wait_send()


IN_VMEM = pl.BlockSpec(memory_space=pltpu.VMEM)
IN_PLACE = pl.BlockSpec(memory_space=pl.ANY)
SQUARE_SHAPE = (SQUARE, *GRID, 32, D)
SHRINK_SHAPE = (*GRID, UNITS - SQUARE, 32, D)


def gather_weights(own, norms):
    return pl.pallas_call(
        gather_kernel,
        in_specs=[IN_PLACE, IN_VMEM],
        out_specs=(IN_PLACE, IN_PLACE, IN_VMEM),
        out_shape=(
            jax.ShapeDtypeStruct(SQUARE_SHAPE, BF),
            jax.ShapeDtypeStruct(SHRINK_SHAPE, BF),
            jax.ShapeDtypeStruct((8, D), F32),
        ),
        scratch_shapes=[
            pltpu.VMEM((8, 8, D), F32),
            pltpu.SemaphoreType.DMA((UNITS, 9)),
            pltpu.SemaphoreType.DMA((UNITS, 9)),
            pltpu.SemaphoreType.DMA((UNITS,)),
            pltpu.SemaphoreType.DMA((8,)),
            pltpu.SemaphoreType.DMA((8,)),
        ],
        compiler_params=pltpu.CompilerParams(
            collective_id=0, has_side_effects=True, vmem_limit_bytes=VMEM_BYTES
        ),
    )(own, norms)


def scatter_gradients(square, shrink, norms):
    return pl.pallas_call(
        scatter_kernel,
        in_specs=[IN_PLACE, IN_PLACE, IN_VMEM],
        out_specs=(IN_VMEM, IN_VMEM),
        out_shape=(
            jax.ShapeDtypeStruct((UNITS, 32, D), F32),
            jax.ShapeDtypeStruct((8, D), F32),
        ),
        scratch_shapes=[
            pltpu.VMEM((7, *GRID, 32, D), BF),
            pltpu.VMEM((UNITS, 2, 2, 4, 32, D), BF),
            pltpu.VMEM((UNITS, 2, 4, 32, D), BF),
            pltpu.VMEM((UNITS, 4, 32, D), BF),
            pltpu.VMEM((UNITS, 4, 32, D), BF),
            pltpu.VMEM((8, 8, D), F32),
            pltpu.SemaphoreType.DMA((7,)),
            pltpu.SemaphoreType.DMA((UNITS, 2, 8)),
            pltpu.SemaphoreType.DMA((UNITS, 2, 8)),
            pltpu.SemaphoreType.DMA((8,)),
            pltpu.SemaphoreType.DMA((8,)),
        ],
        compiler_params=pltpu.CompilerParams(
            collective_id=1, has_side_effects=True, vmem_limit_bytes=VMEM_BYTES
        ),
    )(square, shrink, norms)


def fast_shards(
    tokens, memory, lengths, memory_segments, out_grad,
    self_query, self_key, self_value, self_out,
    cross_query, cross_key, cross_value, cross_out,
    expand_weight, shrink_weight, norm_gains, norm_biases,
):
    me = lax.axis_index("dp") * lax.axis_size("seq") + lax.axis_index("seq")
    squares = [self_query, self_key, self_value, self_out, cross_query, cross_key, cross_value, cross_out]
    squares += [expand_weight[:, D * part : D * (part + 1)] for part in range(4)]
    own = jnp.concatenate([jnp.stack(squares), shrink_weight.reshape(4, 32, D)])
    norms = jnp.concatenate([norm_gains, norm_biases, jnp.zeros((2, 32), BF)]).astype(F32)
    norms = lax.dynamic_update_slice(jnp.zeros((8, D), F32), norms, (0, 32 * me))
    square, shrink, norms = gather_weights(own, norms)
    square = square.reshape(SQUARE, D, D)
    gathered = (
        *(square[unit] for unit in range(8)),
        square[8:].transpose(1, 0, 2).reshape(D, 4 * D),
        shrink.reshape(4 * D, D),
        norms[:3],
        norms[3:6],
    )
    result, input_grad, memory_grad, gradients = micro_batch(
        gathered, tokens, memory, lengths, memory_segments, out_grad
    )
    gradients = list(gradients)
    expand_parts = [gradients[8][:, D * part : D * (part + 1)] for part in range(4)]
    square_grads = jnp.stack([value.astype(BF) for value in gradients[:8] + expand_parts])
    shrink_grads = gradients[9].astype(BF)
    norm_grads = jnp.concatenate([gradients[10], gradients[11], jnp.zeros((2, D), F32)])
    out, norm_grads = scatter_gradients(
        square_grads.reshape(SQUARE_SHAPE), shrink_grads.reshape(SHRINK_SHAPE), norm_grads
    )
    norm_grads = lax.dynamic_slice(norm_grads, (0, 32 * me), (8, 32))
    return (
        result,
        input_grad,
        memory_grad,
        *(out[unit] for unit in range(8)),
        out[8:12].transpose(1, 0, 2).reshape(32, 4 * D),
        out[12:].reshape(128, D),
        norm_grads[:3],
        norm_grads[3:6],
    )


def solution(mesh):
    quick = dict(mesh.shape) == {"dp": 4, "seq": 8}
    return jax.shard_map(
        fast_shards if quick else shards,
        mesh=mesh,
        in_specs=(
            P("dp", "seq", None),
            P("dp", "seq", None),
            P("dp", None),
            P("dp", None),
            P("dp", "seq", None),
            P(("dp", "seq"), None),
            P(("dp", "seq"), None),
            P(("dp", "seq"), None),
            P(("dp", "seq"), None),
            P(("dp", "seq"), None),
            P(("dp", "seq"), None),
            P(("dp", "seq"), None),
            P(("dp", "seq"), None),
            P(("dp", "seq"), None),
            P(("dp", "seq"), None),
            P(None, ("dp", "seq")),
            P(None, ("dp", "seq")),
        ),
        out_specs=(
            P("dp", "seq", None),
            P("dp", "seq", None),
            P("dp", "seq", None),
            P(("dp", "seq"), None),
            P(("dp", "seq"), None),
            P(("dp", "seq"), None),
            P(("dp", "seq"), None),
            P(("dp", "seq"), None),
            P(("dp", "seq"), None),
            P(("dp", "seq"), None),
            P(("dp", "seq"), None),
            P(("dp", "seq"), None),
            P(("dp", "seq"), None),
            P(None, ("dp", "seq")),
            P(None, ("dp", "seq")),
        ),
        check_vma=False,
    )
```

```python
import jax
import jax.numpy as jnp
from jax import lax
from jax.experimental import pallas as pl
from jax.experimental.pallas import tpu as pltpu
from jax.sharding import PartitionSpec as P

H = 16
HD = 64
MB = 2


alpha_scale = 300.0**0.25
norm_eps = 1e-05
masked_score = -1e30


def layer_norm(value, gain, bias):
    average = jnp.mean(value, axis=-1, keepdims=True)
    centred = value - average
    spread = jnp.mean(centred * centred, axis=-1, keepdims=True)
    return centred * lax.rsqrt(spread + norm_eps) * gain + bias


def project(left, right):
    return jnp.dot(left, right, preferred_element_type=jnp.float32)


def project_back(left, right):
    return lax.dot_general(
        left, right, (((1,), (1,)), ((), ())), preferred_element_type=jnp.float32
    )


def weight_term(left, right):
    return lax.dot_general(
        left, right, (((0,), (0,)), ((), ())), preferred_element_type=jnp.float32
    )


def split_heads(value):
    return value.reshape(value.shape[0], value.shape[1], H, HD)


def sentence_ids(sent_ends, places):
    return jnp.sum((places[None, :, None] >= sent_ends[:, None, :]).astype(jnp.int32), axis=2)


def masked_scores(queries, key_heads, allowed, scaling):
    raw_scores = (
        jnp.einsum("gqhd,gkhd->ghqk", queries, key_heads, preferred_element_type=jnp.float32)
        * scaling
    )
    return jnp.where(allowed[:, None], raw_scores, masked_score)


def attend_forward(queries, key_heads, value_heads, allowed, scaling):
    scores = masked_scores(queries, key_heads, allowed, scaling)
    row_max = jnp.max(scores, axis=3, keepdims=True)
    powers = jnp.exp(scores - row_max)
    row_total = jnp.sum(powers, axis=3, keepdims=True)
    prob_low = (powers / row_total).astype(jnp.bfloat16)
    attended = jnp.einsum(
        "ghqk,gkhd->gqhd", prob_low, value_heads, preferred_element_type=jnp.float32
    )
    return (attended, row_max + jnp.log(row_total))


def attend_backward(queries, key_heads, value_heads, allowed, scaling, log_total, attended_grad):
    scores = masked_scores(queries, key_heads, allowed, scaling)
    probability = jnp.exp(scores - log_total)
    prob_grad = jnp.einsum(
        "gqhd,gkhd->ghqk", attended_grad, value_heads, preferred_element_type=jnp.float32
    )
    score_grad = probability * (prob_grad - jnp.sum(prob_grad * probability, axis=3, keepdims=True))
    score_low = score_grad.astype(jnp.bfloat16)
    query_grad = (
        jnp.einsum("ghqk,gkhd->gqhd", score_low, key_heads, preferred_element_type=jnp.float32)
        * scaling
    )
    return (query_grad, score_low, probability.astype(jnp.bfloat16))


def micro_batch(gathered, tokens, memory, lengths, memory_segments, out_grad):
    (
        self_query,
        self_key,
        self_value,
        self_out,
        cross_query,
        cross_key,
        cross_value,
        cross_out,
        expand_weight,
        shrink_weight,
        norm_gains,
        norm_biases,
    ) = gathered
    gains = norm_gains.astype(jnp.float32)
    biases = norm_biases.astype(jnp.float32)
    group_size, local_len, features = tokens.shape
    seq_count = lax.axis_size("seq")
    seq_index = lax.axis_index("seq")
    full_len = local_len * seq_count
    row_count = group_size * local_len
    scaling = HD ** (-0.5)
    sent_ends = jnp.cumsum(lengths, axis=1)[:, :-1]
    query_places = seq_index * local_len + jnp.arange(local_len, dtype=jnp.int32)
    key_places = jnp.arange(full_len, dtype=jnp.int32)
    query_ids = sentence_ids(sent_ends, query_places)
    key_ids = sentence_ids(sent_ends, key_places)
    self_allowed = (query_ids[:, :, None] == key_ids[:, None, :]) & (
        key_places[None, None, :] <= query_places[None, :, None]
    )
    cross_allowed = query_ids[:, :, None] == memory_segments[:, None, :]
    token_rows = tokens.reshape(row_count, features)
    queries = split_heads(
        project(token_rows, self_query)
        .astype(jnp.bfloat16)
        .reshape(group_size, local_len, features)
    )
    own_keys = (
        project(token_rows, self_key).astype(jnp.bfloat16).reshape(group_size, local_len, features)
    )
    own_values = (
        project(token_rows, self_value)
        .astype(jnp.bfloat16)
        .reshape(group_size, local_len, features)
    )
    all_keys, all_values = (
        lax.all_gather(own_keys, "seq", axis=1, tiled=True),
        lax.all_gather(own_values, "seq", axis=1, tiled=True),
    )
    key_heads = split_heads(all_keys)
    value_heads = split_heads(all_values)
    attended, self_log = attend_forward(queries, key_heads, value_heads, self_allowed, scaling)
    attended = attended.reshape(row_count, features).astype(jnp.bfloat16)
    first_pre = alpha_scale * token_rows.astype(jnp.float32) + project(attended, self_out)
    first, first_pull = jax.vjp(layer_norm, first_pre, gains[0], biases[0])
    first_low = first.astype(jnp.bfloat16)
    cross_queries = split_heads(
        project(first_low, cross_query)
        .astype(jnp.bfloat16)
        .reshape(group_size, local_len, features)
    )
    own_memory = memory.reshape(-1, features)
    memory_all = lax.all_gather(memory, "seq", axis=1, tiled=True)
    memory_rows = memory_all.reshape(-1, features)
    cross_keys = (
        project(memory_rows, cross_key).astype(jnp.bfloat16).reshape(group_size, -1, features)
    )
    cross_values = (
        project(memory_rows, cross_value).astype(jnp.bfloat16).reshape(group_size, -1, features)
    )
    cross_key_heads = split_heads(cross_keys)
    cross_value_heads = split_heads(cross_values)
    cross_attended, cross_log = attend_forward(
        cross_queries, cross_key_heads, cross_value_heads, cross_allowed, scaling
    )
    cross_attended = cross_attended.reshape(row_count, features).astype(jnp.bfloat16)
    second_pre = alpha_scale * first + project(cross_attended, cross_out)
    second, second_pull = jax.vjp(layer_norm, second_pre, gains[1], biases[1])
    second_low = second.astype(jnp.bfloat16)
    upward = project(second_low, expand_weight)
    active, gelu_pull = jax.vjp(jax.nn.gelu, upward)
    active_low = active.astype(jnp.bfloat16)
    third_pre = alpha_scale * second + project(active_low, shrink_weight)
    final, third_pull = jax.vjp(layer_norm, third_pre, gains[2], biases[2])
    third_grad, gain_third, bias_third = third_pull(
        out_grad.reshape(row_count, features).astype(jnp.float32)
    )
    branch_grad = third_grad.astype(jnp.bfloat16)
    shrink_grad = weight_term(active_low, branch_grad)
    (up_grad,) = gelu_pull(project_back(branch_grad, shrink_weight))
    up_low = up_grad.astype(jnp.bfloat16)
    expand_grad = weight_term(second_low, up_low)
    second_grad = alpha_scale * third_grad + project_back(up_low, expand_weight)
    second_pre_grad, gain_second, bias_second = second_pull(second_grad)
    cross_branch = second_pre_grad.astype(jnp.bfloat16)
    cross_out_grad = weight_term(cross_attended, cross_branch)
    cross_attended_grad = split_heads(
        project_back(cross_branch, cross_out)
        .astype(jnp.bfloat16)
        .reshape(group_size, local_len, features)
    )
    cross_q_grad, cross_scores, cross_probs = attend_backward(
        cross_queries,
        cross_key_heads,
        cross_value_heads,
        cross_allowed,
        scaling,
        cross_log,
        cross_attended_grad,
    )
    cross_q_low = cross_q_grad.reshape(row_count, features).astype(jnp.bfloat16)
    cross_query_grad = weight_term(first_low, cross_q_low)
    key_term = (
        jnp.einsum(
            "ghqk,gqhd->gkhd", cross_scores, cross_queries, preferred_element_type=jnp.float32
        )
        * scaling
    ).reshape(group_size, -1, features)
    value_term = jnp.einsum(
        "ghqk,gqhd->gkhd", cross_probs, cross_attended_grad, preferred_element_type=jnp.float32
    ).reshape(group_size, -1, features)
    key_summed, value_summed = (
        lax.psum_scatter(
            key_term.astype(jnp.bfloat16), "seq", scatter_dimension=1, tiled=True
        ).astype(jnp.float32),
        lax.psum_scatter(
            value_term.astype(jnp.bfloat16), "seq", scatter_dimension=1, tiled=True
        ).astype(jnp.float32),
    )
    key_low = key_summed.reshape(-1, features).astype(jnp.bfloat16)
    value_low = value_summed.reshape(-1, features).astype(jnp.bfloat16)
    cross_key_grad = weight_term(own_memory, key_low)
    cross_value_grad = weight_term(own_memory, value_low)
    memory_grad = (project_back(key_low, cross_key) + project_back(value_low, cross_value)).reshape(
        memory.shape
    )
    first_grad = alpha_scale * second_pre_grad + project_back(cross_q_low, cross_query)
    first_pre_grad, gain_first, bias_first = first_pull(first_grad)
    self_branch = first_pre_grad.astype(jnp.bfloat16)
    self_out_grad = weight_term(attended, self_branch)
    attended_grad = split_heads(
        project_back(self_branch, self_out)
        .astype(jnp.bfloat16)
        .reshape(group_size, local_len, features)
    )
    self_q_grad, self_scores, self_probs = attend_backward(
        queries, key_heads, value_heads, self_allowed, scaling, self_log, attended_grad
    )
    count = local_len * lax.axis_size("seq")
    key_part = (
        jnp.einsum("ghqk,gqhd->kghd", self_scores, queries, preferred_element_type=jnp.float32)
        * scaling
    )
    value_part = jnp.einsum(
        "ghqk,gqhd->kghd", self_probs, attended_grad, preferred_element_type=jnp.float32
    )
    pair_summed = lax.psum_scatter(
        jnp.concatenate(
            [
                key_part.reshape(count, group_size, features),
                value_part.reshape(count, group_size, features),
            ],
            axis=2,
        ).astype(jnp.bfloat16),
        "seq",
        scatter_dimension=0,
        tiled=True,
    ).astype(jnp.float32)
    key_grad = (
        pair_summed[:, :, :features]
        .astype(jnp.bfloat16)
        .transpose(1, 0, 2)
        .reshape(row_count, features)
    )
    value_grad = (
        pair_summed[:, :, features:]
        .astype(jnp.bfloat16)
        .transpose(1, 0, 2)
        .reshape(row_count, features)
    )
    query_low = self_q_grad.reshape(row_count, features).astype(jnp.bfloat16)
    self_query_grad = weight_term(token_rows, query_low)
    self_key_grad = weight_term(token_rows, key_grad)
    self_value_grad = weight_term(token_rows, value_grad)
    input_grad = (
        alpha_scale * first_pre_grad
        + project_back(query_low, self_query)
        + project_back(key_grad, self_key)
        + project_back(value_grad, self_value)
    )
    gains_grad = jnp.stack([gain_first, gain_second, gain_third])
    biases_grad = jnp.stack([bias_first, bias_second, bias_third])
    gradients = (
        self_query_grad,
        self_key_grad,
        self_value_grad,
        self_out_grad,
        cross_query_grad,
        cross_key_grad,
        cross_value_grad,
        cross_out_grad,
        expand_grad,
        shrink_grad,
        gains_grad,
        biases_grad,
    )
    result = final.astype(jnp.bfloat16).reshape(group_size, local_len, features)
    return (result, input_grad.reshape(group_size, local_len, features), memory_grad, gradients)


def shards(
    tokens,
    memory,
    lengths,
    memory_segments,
    out_grad,
    self_query,
    self_key,
    self_value,
    self_out,
    cross_query,
    cross_key,
    cross_value,
    cross_out,
    expand_weight,
    shrink_weight,
    norm_gains,
    norm_biases,
):
    group_size = tokens.shape[0] // MB
    outputs = []
    input_grads = []
    memory_grads = []
    totals = None
    for batch_index in range(MB):
        gathered = (
            lax.all_gather(self_query, ("dp", "seq"), axis=0, tiled=True),
            lax.all_gather(self_key, ("dp", "seq"), axis=0, tiled=True),
            lax.all_gather(self_value, ("dp", "seq"), axis=0, tiled=True),
            lax.all_gather(self_out, ("dp", "seq"), axis=0, tiled=True),
            lax.all_gather(cross_query, ("dp", "seq"), axis=0, tiled=True),
            lax.all_gather(cross_key, ("dp", "seq"), axis=0, tiled=True),
            lax.all_gather(cross_value, ("dp", "seq"), axis=0, tiled=True),
            lax.all_gather(cross_out, ("dp", "seq"), axis=0, tiled=True),
            lax.all_gather(expand_weight, ("dp", "seq"), axis=0, tiled=True),
            lax.all_gather(shrink_weight, ("dp", "seq"), axis=0, tiled=True),
            lax.all_gather(norm_gains, ("dp", "seq"), axis=1, tiled=True),
            lax.all_gather(norm_biases, ("dp", "seq"), axis=1, tiled=True),
        )
        start = batch_index * group_size
        stop = start + group_size
        result, input_grad, memory_grad, gradients = micro_batch(
            gathered,
            tokens[start:stop],
            memory[start:stop],
            lengths[start:stop],
            memory_segments[start:stop],
            out_grad[start:stop],
        )
        outputs.append(result)
        input_grads.append(input_grad)
        memory_grads.append(memory_grad)
        if totals is None:
            totals = gradients
        else:
            totals = tuple((running + gradient for running, gradient in zip(totals, gradients)))
    summed = (
        lax.psum_scatter(totals[0], ("dp", "seq"), scatter_dimension=0, tiled=True),
        lax.psum_scatter(totals[1], ("dp", "seq"), scatter_dimension=0, tiled=True),
        lax.psum_scatter(totals[2], ("dp", "seq"), scatter_dimension=0, tiled=True),
        lax.psum_scatter(totals[3], ("dp", "seq"), scatter_dimension=0, tiled=True),
        lax.psum_scatter(totals[4], ("dp", "seq"), scatter_dimension=0, tiled=True),
        lax.psum_scatter(totals[5], ("dp", "seq"), scatter_dimension=0, tiled=True),
        lax.psum_scatter(totals[6], ("dp", "seq"), scatter_dimension=0, tiled=True),
        lax.psum_scatter(totals[7], ("dp", "seq"), scatter_dimension=0, tiled=True),
        lax.psum_scatter(totals[8], ("dp", "seq"), scatter_dimension=0, tiled=True),
        lax.psum_scatter(totals[9], ("dp", "seq"), scatter_dimension=0, tiled=True),
        lax.psum_scatter(totals[10], ("dp", "seq"), scatter_dimension=1, tiled=True),
        lax.psum_scatter(totals[11], ("dp", "seq"), scatter_dimension=1, tiled=True),
    )
    return (
        jnp.concatenate(outputs, 0),
        jnp.concatenate(input_grads, 0),
        jnp.concatenate(memory_grads, 0),
        summed[0],
        summed[1],
        summed[2],
        summed[3],
        summed[4],
        summed[5],
        summed[6],
        summed[7],
        summed[8],
        summed[9],
        summed[10],
        summed[11],
    )


MESH = pl.DeviceIdType.MESH
BF = jnp.bfloat16
F32 = jnp.float32
ALL = slice(None)
D = 1024
LEN = 128
OWN = 2 * LEN
SPAN = 8 * LEN
MEM = 128
KEY, VALUE, QUERY, OUT, CROSS_QUERY, CROSS_KEY, CROSS_VALUE, CROSS_OUT = range(8)
EXPAND = 8
SQUARE = 12
UNITS = 16
GRID = (2, 2, 4, 2)
SQUARE_SHAPE = (SQUARE, *GRID, 32, D)
SHRINK_SHAPE = (*GRID, UNITS - SQUARE, 32, D)
VMEM_BYTES = 60 << 20
GELU_SLOPE = (2.0 / 3.141592653589793) ** 0.5
GELU_CUBE = 0.044715


class Place:
    def __init__(self):
        dp, seq = lax.axis_index("dp"), lax.axis_index("seq")
        self.x, self.y, self.core, self.z, self.seq = dp % 2, dp // 2, seq % 2, seq // 2, seq
        self.group = self.z // 2
        self.low = seq % 4

    def at(self, y=None, x=None, z=None, core=None):
        y = self.y if y is None else y
        x = self.x if x is None else x
        z = self.z if z is None else z
        core = self.core if core is None else core
        return (y * 2 + x, z * 2 + core)

    def across(self, axis):
        if axis == "x":
            return self.at(x=1 - self.x)
        if axis == "y":
            return self.at(y=1 - self.y)
        return self.at(core=1 - self.core)

    def along_z(self, step):
        return self.at(z=(self.z + step) % 4)

    def mate(self):
        return self.at(z=self.z + 1 - 2 * (self.z % 2))

    def greet(self):
        barrier = pltpu.get_barrier_semaphore()
        peers = [self.across(axis) for axis in ("x", "y", "core")]
        peers += [self.along_z(step) for step in (1, 2, 3)]
        for peer in peers:
            pl.semaphore_signal(barrier, inc=1, device_id=peer, device_id_type=MESH)
        pl.semaphore_wait(barrier, len(peers))


class Links:
    def __init__(self, place, send_sem, recv_sem):
        self.place, self.send_sem, self.recv_sem = place, send_sem, recv_sem
        self.sends, self.slots = 0, 0
        self.open = {}

    def slot(self, count=1):
        first = self.slots
        self.slots += count
        assert self.slots <= self.recv_sem.shape[0]
        return first

    def send(self, slot, source, target, device):
        assert self.sends < self.send_sem.shape[0]
        step = pltpu.make_async_remote_copy(
            src_ref=source,
            dst_ref=target,
            send_sem=self.send_sem.at[self.sends],
            recv_sem=self.recv_sem.at[slot],
            device_id=device,
            device_id_type=MESH,
        )
        step.start()
        self.sends += 1
        self.open[id(step)] = step
        return step

    def arrived(self, slot, target):
        pltpu.make_async_remote_copy(
            src_ref=target,
            dst_ref=target,
            send_sem=self.send_sem.at[0],
            recv_sem=self.recv_sem.at[slot],
            device_id=self.place.across("core"),
            device_id_type=MESH,
        ).wait_recv()

    def sent(self, step):
        self.open.pop(id(step)).wait_send()

    def finish(self):
        for step in self.open.values():
            step.wait_send()
        self.open = {}


class Moves:
    def __init__(self, sem):
        self.sem, self.count, self.open = sem, 0, {}

    def start(self, source, target):
        assert self.count < self.sem.shape[0]
        step = pltpu.make_async_copy(source, target, self.sem.at[self.count])
        step.start()
        self.count += 1
        self.open[id(step)] = step
        return step

    def wait(self, step):
        self.open.pop(id(step)).wait()

    def finish(self):
        for step in self.open.values():
            step.wait()
        self.open = {}


def all_sum(links, part, total, work):
    place = links.place
    work[0] = part[...]
    for number, axis in enumerate(("core", "y", "x")):
        slot = links.slot()
        step = links.send(slot, work.at[0], work.at[1 + number], place.across(axis))
        yield
        links.arrived(slot, work.at[1 + number])
        links.sent(step)
        work[0] = work[0] + work[1 + number]
    slot = links.slot(4)
    for k in (1, 2, 3):
        links.send(slot + place.z, work.at[0], work.at[4 + place.z], place.along_z(k))
    yield
    result = work[0]
    for k in (1, 2, 3):
        source = (place.z + k) % 4
        links.arrived(slot + source, work.at[4 + source])
        result = result + work[4 + source]
    total[...] = result
    yield


def loop(count):
    return pl.loop(0, count)


def tile(index, size):
    return pl.ds(pl.multiple_of(index * size, size), size)


def rows_times(left, right, store, rows=OWN, width=256):
    for first in range(0, left.shape[0], rows):

        @loop(D // width)
        def _(index):
            columns = tile(index, width)
            store(pl.ds(first, rows), columns, jnp.dot(left[pl.ds(first, rows), :], right[:, columns], preferred_element_type=F32))


def rows_back(left, right, store, width=256):
    @loop(D // width)
    def _(index):
        columns = tile(index, width)
        store(columns, project_back(left[...], right[columns, :]))


def put(target, dtype=BF):
    def store(rows, columns, value):
        target[rows, columns] = value.astype(dtype)

    return store


def half_masks():
    lane = lax.broadcasted_iota(jnp.int32, (1, LEN), 1)
    return [(lane < HD).astype(F32), (lane >= HD).astype(F32)]


def attend_rows(queries, keys, values, bias, logs, out, segments):
    masks = half_masks()
    logs[...] = jnp.zeros_like(logs)

    @loop(H // 2)
    def _(pair):
        columns = tile(pair, LEN)
        for first, rows, count in segments:
            own = pl.ds(first, rows)
            key, value = keys[pl.ds(0, count), columns], values[pl.ds(0, count), columns]
            query = queries[own, columns]
            lane = lax.broadcasted_iota(jnp.int32, (rows, LEN), 1)
            parts = []
            for half in (0, 1):
                scores = project_back(query * (masks[half] * HD**-0.5).astype(BF), key) + bias[own, pl.ds(0, count)]
                top = jnp.max(scores, axis=1, keepdims=True)
                powers = jnp.exp(scores - top)
                total = jnp.sum(powers, axis=1, keepdims=True)
                parts.append(project((powers * (1.0 / total)).astype(BF), value))
                logs[own, :] = jnp.where(lane == 2 * pair + half, top + jnp.log(total), logs[own, :])
            out[own, columns] = jnp.where(lane < HD, parts[0], parts[1]).astype(BF)


def attend_rows_back(queries, keys, values, bias, logs, grads, query_grads, key_grads, value_grads, segments, pairs, first_pair=0):
    masks = half_masks()

    @loop(pairs)
    def _(step):
        pair = step + first_pair
        columns = tile(pair, LEN)
        for number, (first, rows, count) in enumerate(segments):
            own, met = pl.ds(first, rows), pl.ds(0, count)
            key, value = keys[met, columns], values[met, columns]
            lane = lax.broadcasted_iota(jnp.int32, (rows, LEN), 1)
            halves, score_lows, prob_lows, query_parts, grad_parts = [], [], [], [], []
            for half in (0, 1):
                query = queries[own, columns] * (masks[half] * HD**-0.5).astype(BF)
                grad = grads[own, columns] * masks[half].astype(BF)
                log_total = jnp.sum(jnp.where(lane == 2 * pair + half, logs[own, :], 0.0), axis=1, keepdims=True)
                probs = jnp.exp(project_back(query, key) + bias[own, met] - log_total)
                prob_grad = project_back(grad, value)
                score_grad = probs * (prob_grad - jnp.sum(prob_grad * probs, axis=1, keepdims=True))
                score_low = score_grad.astype(BF)
                halves.append(project(score_low, key) * HD**-0.5)
                score_lows.append(score_low)
                prob_lows.append(probs.astype(BF))
                query_parts.append(query)
                grad_parts.append(grad)
            query_grads[own, columns] = jnp.where(lane < HD, halves[0], halves[1]).astype(BF)
            key_term = weight_term(jnp.concatenate(score_lows), jnp.concatenate(query_parts))
            value_term = weight_term(jnp.concatenate(prob_lows), jnp.concatenate(grad_parts))
            if number == 0:
                key_grads[met, columns] = key_term.astype(BF)
                value_grads[met, columns] = value_term.astype(BF)
            else:
                key_grads[met, columns] = (key_grads[met, columns].astype(F32) + key_term).astype(BF)
                value_grads[met, columns] = (value_grads[met, columns].astype(F32) + value_term).astype(BF)


SELF_SEGMENTS = ((LEN, LEN, SPAN), (0, LEN, SPAN // 2))
CROSS_SEGMENTS = ((0, OWN, MEM),)
STEP = 32


def norm_rows(read, normal, inverse, emit):
    @loop(OWN // STEP)
    def _(index):
        rows = tile(index, STEP)
        value = read(rows)
        centred = value - jnp.mean(value, axis=1, keepdims=True)
        scale = lax.rsqrt(jnp.mean(centred * centred, axis=1, keepdims=True) + norm_eps)
        result = centred * scale
        if normal is not None:
            normal[rows, :] = result
            inverse[rows, :] = jnp.broadcast_to(scale, (STEP, LEN))
        emit(rows, result, scale)


def norm_rows_back(grad, normal, scale, gain, sums, number):
    sums[pl.ds(number, 1), :] += jnp.sum(grad * normal, axis=0, keepdims=True)
    sums[pl.ds(3 + number, 1), :] += jnp.sum(grad, axis=0, keepdims=True)
    scaled = grad * gain
    return scale * (
        scaled
        - jnp.mean(scaled, axis=1, keepdims=True)
        - normal * jnp.mean(scaled * normal, axis=1, keepdims=True)
    )


class Gather:
    ORDER = ((0, 1), (2, 3), (4, 5), (6, 7), (12, 13), (14, 15), (8, 9), (10, 11))

    def __init__(self, links, moves, own, square, shrink):
        self.links, self.moves, self.own, self.square, self.shrink = links, moves, own, square, shrink
        self.slots = {unit: links.slot(9) for unit in range(UNITS)}
        self.local = {unit: moves.start(own(unit), self.block(unit, *self.home())) for unit in range(UNITS)}
        self.now = 0
        self.sent_pairs = 0

    def home(self):
        place = self.links.place
        return (place.y, place.x, place.z, place.core)

    def block(self, unit, *index):
        if unit < SQUARE:
            return self.square.at[(unit,) + index]
        return self.shrink.at[index + (unit - SQUARE,)]

    def phase(self, unit, number):
        links, place, slot = self.links, self.links.place, self.slots[unit]
        y, x, z, core = self.home()
        by_x = unit % 2 == 0
        first, second = ("x", "y") if by_x else ("y", "x")
        line = (y, x, ALL)
        line_in = (y, 1 - x, ALL) if by_x else (1 - y, x, ALL)
        sheet = (y, ALL, ALL) if by_x else (ALL, x, ALL)
        sheet_in = (1 - y, ALL, ALL) if by_x else (ALL, 1 - x, ALL)

        def share(number, index, device):
            part = self.block(unit, *index, core)
            links.send(slot + number, part, part, device)

        def arrived(number, index, plane):
            links.arrived(slot + number, self.block(unit, *index, plane))

        if number == 0:
            for k in (1, 2, 3):
                links.send(slot + z, self.own(unit), self.block(unit, y, x, z, core), place.along_z(k))
        if number == 1:
            self.moves.wait(self.local[unit])
            for k in (1, 2, 3):
                arrived((z + k) % 4, (y, x, (z + k) % 4), core)
            share(4, line, place.across(first))
            share(6, line, place.across("core"))
        if number == 2:
            arrived(4, line_in, core)
            share(5, sheet, place.across(second))
            share(7, line_in, place.across("core"))
        if number == 3:
            arrived(5, sheet_in, core)
            share(8, sheet_in, place.across("core"))
        if number == 4:
            arrived(6, line, 1 - core)
            arrived(7, line_in, 1 - core)
            arrived(8, sheet_in, 1 - core)

    def tick(self):
        if self.now == 0:
            steps = [(0, 0), (1, 0)]
        else:
            steps = [(self.now + 1, 0)] + [(self.now - number, number) for number in (4, 3, 2, 1)]
        for pair, number in steps:
            if 0 <= pair < len(self.ORDER):
                for unit in self.ORDER[pair]:
                    self.phase(unit, number)
        self.now += 1


def core_rows(core, count=OWN):
    return pl.ds(pl.multiple_of(core * count, count), count)


def block_rows(block):
    return pl.ds(pl.multiple_of(block * LEN, LEN), LEN)


FORWARD_SAVES = {
    "queries": ((OWN, D), BF),
    "keys": ((SPAN, D), BF),
    "values": ((SPAN, D), BF),
    "self_bias": ((OWN, SPAN), F32),
    "self_logs": ((OWN, LEN), F32),
    "normal_one": ((OWN, D), F32),
    "inverse_one": ((OWN, LEN), F32),
    "cross_queries": ((OWN, D), BF),
    "cross_keys": ((MEM, D), BF),
    "cross_values": ((MEM, D), BF),
    "cross_bias": ((OWN, MEM), F32),
    "cross_logs": ((OWN, LEN), F32),
    "normal_two": ((OWN, D), F32),
    "inverse_two": ((OWN, LEN), F32),
    "slopes": ((4, OWN, D), BF),
    "third_grad": ((OWN, D), F32),
    "norm_sums": ((8, D), F32),
    "gains": ((8, D), F32),
}
TURNED_SAVES = {
    "tokens_t": ((16, 32, 2 * OWN), BF),
    "attended_t": ((16, 32, 2 * OWN), BF),
    "first_t": ((16, 32, 2 * OWN), BF),
    "cross_t": ((16, 32, 2 * OWN), BF),
    "second_t": ((16, 32, 2 * OWN), BF),
    "active_t": ((4, 4, 4, 32, 2 * OWN), BF),
    "memory_t": ((16, 32, MEM), BF),
    "branch": ((2 * OWN, D), BF),
}
FORWARD_SCRATCH = {
    "stream": ((SPAN, D), BF),
    "mine": ((OWN, D), BF),
    "context": ((4, 2, 16, D), BF),
    "attended": ((OWN, D), BF),
    "first_low": ((OWN, D), BF),
    "cross_attended": ((OWN, D), BF),
    "second_low": ((OWN, D), BF),
    "active": ((OWN, D), BF),
    "sums": ((OWN, D), F32),
    "final_low": ((OWN, D), BF),
    "cotangent": ((OWN, D), BF),
    "branch_own": ((OWN, D), BF),
    "weights": ((4, D, D), BF),
    "turned": ((3, 16, 2, 32, OWN), BF),
    "turned_active": ((2, 4, 2, 4, 32, OWN), BF),
    "turned_memory": ((16, 2, 32, MEM), BF),
    "work": ((8, 8, D), F32),
}
FORWARD_SENDS, FORWARD_SLOTS, FORWARD_MOVES = 192, 224, 96


class Refs:
    def __init__(self, names, refs):
        for name, ref in zip(names, refs):
            setattr(self, name, ref)


def forward_kernel(lengths, segments, norms, tokens, memory, out_grad, *refs):
    squares, expand_own, shrink_own = refs[:8], refs[8], refs[9]
    square, shrink, output = refs[10:13]
    rest = refs[13:]
    kept = Refs(FORWARD_SAVES, rest[: len(FORWARD_SAVES)])
    rest = rest[len(FORWARD_SAVES) :]
    turned = Refs(TURNED_SAVES, rest[: len(TURNED_SAVES)])
    rest = rest[len(TURNED_SAVES) :]
    held = Refs(FORWARD_SAVES, rest[: len(FORWARD_SAVES)])
    rest = rest[len(FORWARD_SAVES) :]
    held.__dict__.update(Refs(FORWARD_SCRATCH, rest[: len(FORWARD_SCRATCH)]).__dict__)
    send_sem, recv_sem, move_sem = rest[len(FORWARD_SCRATCH) :]

    place = Place()
    links, moves = Links(place, send_sem, recv_sem), Moves(move_sem)
    y, x, z, core, group, low, seq = place.y, place.x, place.z, place.core, place.group, place.low, place.seq
    partner = place.across("core")
    opposite = place.along_z(2)
    mate = place.mate()
    place.greet()

    def own(unit):
        if unit < EXPAND:
            return squares[unit]
        if unit < SQUARE:
            return expand_own.at[:, pl.ds(D * (unit - EXPAND), D)]
        return shrink_own.at[pl.ds(32 * (unit - SQUARE), 32)]

    stream = held.stream
    far, mate_seq = (seq + 4) % 8, (seq + 2) % 4 + 4 * group
    other_seq = 2 * z + 1 - core
    other_mate = (other_seq + 2) % 4 + 4 * group
    slot_far, slot_mate, slot_mate_far, slot_core = links.slot(), links.slot(), links.slot(), links.slot(4)
    home = moves.start(tokens.at[group], stream.at[block_rows(seq)])
    links.send(slot_far, tokens.at[1 - group], stream.at[block_rows(seq)], opposite)
    links.send(slot_mate, tokens.at[group], stream.at[block_rows(seq)], mate)
    links.send(slot_core, tokens.at[group], stream.at[block_rows(seq)], partner)
    gather = Gather(links, moves, own, square, shrink)
    gather.tick()
    slot_memory, slot_context = links.slot(4), links.slot()
    context_home = moves.start(memory.at[group], held.context.at[z, core])
    for k in (1, 2, 3):
        links.send(slot_memory + z, memory.at[((z + k) % 4) // 2], held.context.at[z, core], place.along_z(k))
    norm_steps = all_sum(links, norms, held.gains, held.work)
    next(norm_steps)

    def sentence(places):
        result, end = jnp.zeros_like(places), 0
        for index in range(lengths.shape[1] - 1):
            end = end + lengths[group, index]
            result = result + (places >= end).astype(jnp.int32)
        return result

    held.norm_sums[...] = jnp.zeros_like(held.norm_sums)

    @loop(OWN // STEP)
    def _(index):
        row = index * STEP + lax.broadcasted_iota(jnp.int32, (STEP, 1), 0)
        row_place = LEN * low + row + jnp.where(row >= LEN, 3 * LEN, 0)
        row_sentence = sentence(row_place)
        key_place = lax.broadcasted_iota(jnp.int32, (1, SPAN), 1)
        allowed = (row_sentence == sentence(key_place)) & (key_place <= row_place)
        held.self_bias[tile(index, STEP), :] = jnp.where(allowed, 0.0, masked_score)
        met = row_sentence == segments[pl.ds(group, 1), :]
        held.cross_bias[tile(index, STEP), :] = jnp.where(met, 0.0, masked_score)

    def pass_on(number, block):
        links.send(slot_core + number, stream.at[block_rows(block)], stream.at[block_rows(block)], partner)

    links.arrived(slot_far, stream.at[block_rows(far)])
    links.send(slot_mate_far, stream.at[block_rows(far)], stream.at[block_rows(far)], mate)
    pass_on(1, far)
    gather.tick()
    next(norm_steps)
    moves.wait(context_home)
    for k in (1, 2, 3):
        links.arrived(slot_memory + (z + k) % 4, held.context.at[(z + k) % 4, core])
    links.send(slot_context, held.context.at[:, core], held.context.at[:, core], partner)
    links.arrived(slot_mate, stream.at[block_rows(mate_seq)])
    pass_on(2, mate_seq)
    gather.tick()
    next(norm_steps)
    cotangent_rows, cotangent_far = block_rows(group), block_rows(1 - group)
    slot_cotangent = links.slot()
    cotangent_home = moves.start(out_grad.at[group], held.cotangent.at[cotangent_rows])
    links.send(slot_cotangent, out_grad.at[1 - group], held.cotangent.at[cotangent_rows], opposite)
    links.arrived(slot_mate_far, stream.at[block_rows((mate_seq + 4) % 8)])
    pass_on(3, (mate_seq + 4) % 8)
    moves.wait(home)
    for number, block in enumerate((other_seq, (other_seq + 4) % 8, other_mate, (other_mate + 4) % 8)):
        links.arrived(slot_core + number, stream.at[block_rows(block)])
    links.arrived(slot_context, held.context.at[:, 1 - core])
    gather.tick()
    next(norm_steps)
    held.mine[pl.ds(0, LEN), :] = stream[block_rows(low), :]
    held.mine[pl.ds(LEN, LEN), :] = stream[block_rows(low + 4), :]

    loads = {}

    def fetch(unit, slot):
        source = square.at[unit].reshape(D, D) if unit < SQUARE else shrink.at[(unit - SQUARE) // 2, unit % 2].reshape(D, D)
        loads[unit] = (moves.start(source, held.weights.at[slot]), slot)

    def weight(unit):
        step, slot = loads.pop(unit)
        moves.wait(step)
        return held.weights.at[slot]

    turning = {"count": 0, "open": {}}
    landing = []
    mine, theirs = core_rows(core), core_rows(1 - core)

    def turn(source, name):
        number = turning["count"] % 3
        for move, sent in turning["open"].pop(number, ()):
            moves.wait(move)
            links.sent(sent)
        turning["count"] += 1
        buffer, target = held.turned.at[number], getattr(turned, name)

        @loop(4)
        def _(index):
            buffer[pl.ds(4 * index, 4)] = source[:, tile(index, OWN)].T.reshape(4, 2, 32, OWN)

        slot = links.slot()
        move = moves.start(buffer.at[:, core], target.at[:, :, mine])
        sent = links.send(slot, buffer.at[:, 1 - core], target.at[:, :, mine], partner)
        landing.append((slot, target.at[:, :, theirs]))
        turning["open"][number] = [(move, sent)]

    def keep(*names):
        for name in names:
            moves.start(getattr(held, name), getattr(kept, name))

    def gain(number):
        return held.gains[pl.ds(number, 1), :]

    def bias(number):
        return held.gains[pl.ds(3 + number, 1), :]

    gather.tick()
    fetch(KEY, 0)
    fetch(VALUE, 1)
    turn(held.mine, "tokens_t")
    next(norm_steps)
    rows_times(stream, weight(KEY), put(held.keys))
    gather.tick()
    fetch(QUERY, 2)
    fetch(OUT, 3)
    rows_times(stream, weight(VALUE), put(held.values))
    rows_times(held.mine, weight(QUERY), put(held.queries))
    attend_rows(held.queries, held.keys, held.values, held.self_bias, held.self_logs, held.attended, SELF_SEGMENTS)
    gather.tick()
    fetch(CROSS_QUERY, 0)
    fetch(CROSS_KEY, 1)
    keep("queries", "keys", "values", "self_bias", "self_logs", "cross_bias", "gains")
    rows_times(held.attended, weight(OUT), put(held.sums, F32))

    def first_rows(rows, result, _):
        held.first_low[rows, :] = (result * gain(0) + bias(0)).astype(BF)

    def after(rows, previous):
        return held.sums[rows, :] + alpha_scale * previous

    norm_rows(lambda rows: after(rows, held.mine[rows, :].astype(F32)), held.normal_one, held.inverse_one, first_rows)
    turn(held.attended, "attended_t")
    rows_times(held.first_low, weight(CROSS_QUERY), put(held.cross_queries))
    context = held.context.reshape(MEM, D)
    rows_times(context, weight(CROSS_KEY), put(held.cross_keys), MEM)
    gather.tick()
    fetch(CROSS_VALUE, 2)
    fetch(CROSS_OUT, 3)
    turn(held.first_low, "first_t")

    @loop(4)
    def _(index):
        held.turned_memory[pl.ds(4 * index, 4)] = context[:, tile(index, OWN)].T.reshape(4, 2, 32, MEM)

    moves.start(held.turned_memory.at[:, core], turned.memory_t)
    rows_times(context, weight(CROSS_VALUE), put(held.cross_values), MEM)
    attend_rows(
        held.cross_queries, held.cross_keys, held.cross_values, held.cross_bias, held.cross_logs,
        held.cross_attended, CROSS_SEGMENTS,
    )
    keep("cross_queries", "cross_keys", "cross_values", "cross_logs", "normal_one", "inverse_one")
    rows_times(held.cross_attended, weight(CROSS_OUT), put(held.sums, F32))

    def second_rows(rows, result, _):
        held.second_low[rows, :] = (result * gain(1) + bias(1)).astype(BF)

    norm_rows(
        lambda rows: after(rows, held.normal_one[rows, :] * gain(0) + bias(0)),
        held.normal_two, held.inverse_two, second_rows,
    )
    keep("normal_two", "inverse_two")
    gather.tick()
    turn(held.cross_attended, "cross_t")
    turn(held.second_low, "second_t")
    gather.tick()
    held.sums[...] = jnp.zeros_like(held.sums)
    turned_open = {}
    for part in range(4):
        if part % 2 == 0:
            gather.tick()
            for number in (0, 1):
                fetch(EXPAND + part + number, 2 * number)
                fetch(SQUARE + part + number, 2 * number + 1)
        expand = weight(EXPAND + part)
        slopes = held.slopes.at[part]

        def activate(rows, columns, value):
            inner = GELU_SLOPE * (value + GELU_CUBE * value * value * value)
            bend = jnp.tanh(inner)
            held.active[rows, columns] = (0.5 * value * (1.0 + bend)).astype(BF)
            slope = 0.5 * (1.0 + bend) + 0.5 * value * (1.0 - bend * bend) * (
                GELU_SLOPE * (1.0 + 3.0 * GELU_CUBE * value * value)
            )
            slopes[rows, columns] = slope.astype(BF)

        def add(rows, columns, value):
            held.sums[rows, columns] += value

        rows_times(held.second_low, expand, activate)
        rows_times(held.active, weight(SQUARE + part), add)
        number = part % 2
        for move, sent in turned_open.pop(number, ()):
            moves.wait(move)
            links.sent(sent)
        buffer = held.turned_active.at[number]

        @loop(4)
        def _(index):
            buffer[index] = held.active[:, tile(index, OWN)].T.reshape(2, 4, 32, OWN)

        slot = links.slot()
        move = moves.start(buffer.at[:, core], turned.active_t.at[part, :, :, :, mine])
        sent = links.send(slot, buffer.at[:, 1 - core], turned.active_t.at[part, :, :, :, mine], partner)
        landing.append((slot, turned.active_t.at[part, :, :, :, theirs]))
        turned_open[number] = [(move, sent)]
    keep("slopes")
    links.arrived(slot_cotangent, held.cotangent.at[cotangent_far])
    moves.wait(cotangent_home)

    def third_rows(rows, result, scale):
        held.final_low[rows, :] = (result * gain(2) + bias(2)).astype(BF)
        grad = norm_rows_back(held.cotangent[rows, :].astype(F32), result, scale, gain(2), held.norm_sums, 2)
        held.third_grad[rows, :] = grad
        held.branch_own[rows, :] = grad.astype(BF)

    norm_rows(lambda rows: after(rows, held.normal_two[rows, :] * gain(1) + bias(1)), None, None, third_rows)
    slot = links.slot()
    links.send(slot, held.branch_own, turned.branch.at[mine], partner)
    landing.append((slot, turned.branch.at[theirs]))
    moves.start(held.branch_own, turned.branch.at[mine])
    keep("third_grad", "norm_sums")
    slot = links.slot()
    moves.start(held.final_low.at[block_rows(group)], output.at[group])
    links.send(slot, held.final_low.at[block_rows(1 - group)], output.at[group], opposite)
    for arrival in landing:
        links.arrived(*arrival)
    links.arrived(slot, output.at[1 - group])
    moves.finish()
    links.finish()


IN_VMEM = pl.BlockSpec(memory_space=pltpu.VMEM)
IN_SMEM = pl.BlockSpec(memory_space=pltpu.SMEM)
IN_PLACE = pl.BlockSpec(memory_space=pl.ANY)


def shapes_of(table):
    return [jax.ShapeDtypeStruct(shape, dtype) for shape, dtype in table.values()]


def vmem_of(table):
    return [pltpu.VMEM(shape, dtype) for shape, dtype in table.values()]


def forward_call(lengths, segments, norms, tokens, memory, out_grad, weights):
    results = [
        jax.ShapeDtypeStruct(SQUARE_SHAPE, BF),
        jax.ShapeDtypeStruct(SHRINK_SHAPE, BF),
        jax.ShapeDtypeStruct(tokens.shape, BF),
        *shapes_of(FORWARD_SAVES),
        *shapes_of(TURNED_SAVES),
    ]
    values = pl.pallas_call(
        forward_kernel,
        in_specs=[IN_SMEM, IN_VMEM, IN_VMEM] + [IN_PLACE] * 13,
        out_specs=[IN_PLACE] * len(results),
        out_shape=results,
        scratch_shapes=[
            *vmem_of(FORWARD_SAVES),
            *vmem_of(FORWARD_SCRATCH),
            pltpu.SemaphoreType.DMA((FORWARD_SENDS,)),
            pltpu.SemaphoreType.DMA((FORWARD_SLOTS,)),
            pltpu.SemaphoreType.DMA((FORWARD_MOVES,)),
        ],
        compiler_params=pltpu.CompilerParams(collective_id=0, has_side_effects=True, vmem_limit_bytes=VMEM_BYTES),
    )(lengths, segments, norms, tokens, memory, out_grad, *weights)
    saves = dict(zip([*FORWARD_SAVES, *TURNED_SAVES], values[3:]))
    return values[0], values[1], values[2], saves


class Scatter:
    def __init__(self, links, grads, from_first, from_second, from_z, result):
        self.links, self.grads, self.result = links, grads, result
        self.from_first, self.from_second, self.from_z = from_first, from_second, from_z
        self.slots, self.pending, self.now = {}, {}, 0

    def home(self, unit):
        for step in self.pending.pop(unit - self.grads.shape[0], ()):
            self.links.sent(step)
        self.slots[unit] = self.links.slot(12)
        return self.grads.at[unit % self.grads.shape[0]]

    def add(self, total, part):
        for row in range(4):
            total[row] = (total[row].astype(F32) + part[row].astype(F32)).astype(BF)

    def phase(self, unit, half, number):
        links, place = self.links, self.links.place
        y, x, z = place.y, place.x, place.z
        here = self.grads.at[unit % self.grads.shape[0]]
        depth = unit % self.from_first.shape[0]
        rows = pl.ds(16 * half, 16)
        slot = self.slots[unit] + 6 * half
        by_y = half == 0
        first, second = ("y", "x") if by_y else ("x", "y")
        away = (1 - y, ALL) if by_y else (ALL, 1 - x)
        corner, other, mine = ((y, 1 - x), 1 - x, x) if by_y else ((1 - y, x), 1 - y, y)
        home = here.at[y, x, :, rows]
        first_in = self.from_first.at[depth, :, :, rows]
        second_in = self.from_second.at[depth, :, rows]

        def send(number, source, target, device):
            self.pending.setdefault(unit, []).append(links.send(slot + number, source, target, device))

        if number == 0:
            send(0, here.at[(*away, ALL, rows)], first_in, place.across(first))
        if number == 1:
            links.arrived(slot, first_in)
            corner_part = here.at[(*corner, ALL, rows)]
            self.add(corner_part, first_in.at[other])
            send(1, corner_part, second_in, place.across(second))
            self.add(home, first_in.at[mine])
        if number == 2:
            links.arrived(slot + 1, second_in)
            self.add(home, second_in)
            for k in (1, 2, 3):
                send(2 + z, home.at[(z + k) % 4], self.from_z.at[depth, z, rows], place.along_z(k))
        if number == 3:
            total = home[z].astype(F32)
            for k in (1, 2, 3):
                source = (z + k) % 4
                links.arrived(slot + 2 + source, self.from_z.at[depth, source, rows])
                total = total + self.from_z[depth, source, rows].astype(F32)
            self.result(unit, rows, total)

    def tick(self):
        for number in (3, 2, 1, 0):
            unit = self.now - number
            if 0 <= unit < UNITS:
                for half in (0, 1):
                    self.phase(unit, half, number)
        self.now += 1


DEPTH = 4
BACKWARD_SCRATCH = {
    "weights": ((3, D, D), BF),
    "grads": ((6, 2, 2, 4, 32, D), BF),
    "from_first": ((DEPTH, 2, 4, 32, D), BF),
    "from_second": ((DEPTH, 4, 32, D), BF),
    "from_z": ((DEPTH, 4, 32, D), BF),
    "up": ((4, 2 * OWN, D), BF),
    "second_sum": ((OWN, D), F32),
    "cross_branch": ((2 * OWN, D), BF),
    "attended_grad": ((OWN, D), BF),
    "cross_query_grad": ((2 * OWN, D), BF),
    "cross_terms": ((2, 2, MEM, D), BF),
    "cross_sums": ((2, MEM, D), BF),
    "self_branch": ((2 * OWN, D), BF),
    "query_grad": ((2 * OWN, D), BF),
    "terms": ((2, 2, 2, 2, LEN, D), BF),
    "terms_core": ((2, 2, 2, LEN, D), BF),
    "terms_mate": ((2, 2, LEN, D), BF),
    "key_grad": ((2 * OWN, D), BF),
    "value_grad": ((2 * OWN, D), BF),
    "memory_own": ((4, 16, D), BF),
    "memory_in": ((4, 16, D), BF),
    "far_own": ((LEN, D), BF),
    "far_in": ((LEN, D), BF),
    "work": ((8, 8, D), F32),
}
BACKWARD_SENDS, BACKWARD_SLOTS, BACKWARD_MOVES = 240, 256, 64


def backward_kernel(square, shrink, *refs):
    names = [*FORWARD_SAVES, *TURNED_SAVES]
    kept = Refs(names, refs[: len(names)])
    rest = refs[len(names) :]
    input_grad, memory_grad, unit_grads, expand_grad, shrink_grad, norm_grads = rest[0], rest[1], rest[2:10], *rest[10:13]
    rest = rest[13:]
    held = Refs(names, rest[: len(names)])
    rest = rest[len(names) :]
    held.__dict__.update(Refs(BACKWARD_SCRATCH, rest[: len(BACKWARD_SCRATCH)]).__dict__)
    send_sem, recv_sem, move_sem = rest[len(BACKWARD_SCRATCH) :]

    place = Place()
    links, moves = Links(place, send_sem, recv_sem), Moves(move_sem)
    z, core, group = place.z, place.core, place.group
    partner = place.across("core")
    mine, theirs = core_rows(core), core_rows(1 - core)
    loads = {}

    def bring(*wanted):
        for name in wanted:
            loads[name] = moves.start(getattr(kept, name), getattr(held, name))

    def have(*wanted):
        for name in wanted:
            moves.wait(loads.pop(name))

    def fetch(unit, slot):
        source = square.at[unit].reshape(D, D) if unit < SQUARE else shrink.at[(unit - SQUARE) // 2, unit % 2].reshape(D, D)
        loads[unit] = moves.start(source, held.weights.at[slot])

    def weight(unit, slot):
        moves.wait(loads.pop(unit))
        return held.weights.at[slot]

    bring("branch", "active_t")
    fetch(SQUARE, 0)
    fetch(EXPAND, 1)
    fetch(SQUARE + 1, 2)
    bring("slopes", "third_grad", "second_t", "norm_sums", "gains", "normal_two", "inverse_two")
    bring("cross_queries", "cross_keys", "cross_values", "cross_bias", "cross_logs", "cross_t")
    bring("normal_one", "inverse_one", "first_t", "memory_t", "attended_t", "tokens_t")
    bring("queries", "keys", "values", "self_bias", "self_logs")
    place.greet()

    order = [12, 13, 14, 15, 8, 9, 10, 11, CROSS_OUT, CROSS_QUERY, CROSS_KEY, CROSS_VALUE, OUT, QUERY, KEY, VALUE]

    def result(number, rows, total):
        unit = order[number]
        if unit < EXPAND:
            unit_grads[unit][rows, :] = total
        elif unit < SQUARE:
            expand_grad[rows, pl.ds(D * (unit - EXPAND), D)] = total
        else:
            shrink_grad[pl.ds(32 * (unit - SQUARE) + rows.start, rows.size), :] = total

    scatter = Scatter(links, held.grads, held.from_first, held.from_second, held.from_z, result)
    made = {"count": 0}

    def produce(left, right, depth=2 * OWN):
        target = scatter.home(made["count"])
        made["count"] += 1

        @loop(4)
        def _(index):
            columns = tile(index, OWN)
            term = project(left().reshape(512, depth), right[:, columns])
            target[:, :, :, :, columns] = term.astype(BF).reshape(2, 2, 4, 32, OWN)

    def share(ref):
        slot = links.slot()
        links.send(slot, ref.at[mine], ref.at[mine], partner)
        return slot

    def shared(ref, slot):
        links.arrived(slot, ref.at[theirs])

    def gain(number):
        return held.gains[pl.ds(number, 1), :]

    have("branch", "active_t")

    def produce_shrink(part):
        produce(lambda: held.active_t[:, :, part], held.branch)

    def produce_expand(part):
        shared(held.up.at[part], up_slots[part])
        produce(lambda: held.second_t[...], held.up.at[part])

    produce_shrink(0)
    scatter.tick()
    for part in (1, 2, 3):
        produce_shrink(part)
    scatter.tick()
    have("slopes")
    own_branch = held.branch.at[mine]
    up_slots = []
    for part in range(4):
        if part == 2:
            scatter.tick()
        up = held.up.at[part, mine]
        slopes = held.slopes.at[part]

        def bend(columns, value):
            up[:, columns] = (value * slopes[:, columns].astype(F32)).astype(BF)

        rows_back(own_branch, weight(SQUARE + part, 2 * part % 3), bend)
        up_slots.append(share(held.up.at[part]))
        if part < 3:
            fetch(EXPAND + part + 1, 2 * part % 3)

        def add(columns, value):
            if part == 0:
                held.second_sum[:, columns] = value
            else:
                held.second_sum[:, columns] += value

        rows_back(up, weight(EXPAND + part, (2 * part + 1) % 3), add)
        fetch((SQUARE + 2, SQUARE + 3, CROSS_OUT, CROSS_QUERY)[part], (2 * part + 1) % 3)
    fetch(CROSS_KEY, 0)
    scatter.tick()
    have("third_grad", "norm_sums", "gains", "normal_two", "inverse_two", "second_t")

    def spread(inverse, rows):
        return inverse[rows, pl.ds(0, 1)]

    @loop(OWN // STEP)
    def _(index):
        rows = tile(index, STEP)
        grad = held.second_sum[rows, :] + alpha_scale * held.third_grad[rows, :]
        pre = norm_rows_back(grad, held.normal_two[rows, :], spread(held.inverse_two, rows), gain(1), held.norm_sums, 1)
        held.second_sum[rows, :] = pre
        held.cross_branch[pl.ds(pl.multiple_of(OWN * core + STEP * index, STEP), STEP), :] = pre.astype(BF)

    slot_cross_branch = share(held.cross_branch)
    produce_expand(0)
    scatter.tick()

    def low(target):
        def store(columns, value):
            target[:, columns] = value.astype(BF)

        return store

    rows_back(held.cross_branch.at[mine], weight(CROSS_OUT, 2), low(held.attended_grad))
    fetch(CROSS_VALUE, 2)
    have("cross_queries", "cross_keys", "cross_values", "cross_bias", "cross_logs", "cross_t")
    attend_rows_back(
        held.cross_queries, held.cross_keys, held.cross_values, held.cross_bias, held.cross_logs, held.attended_grad,
        held.cross_query_grad.at[mine], held.cross_terms.at[0, core], held.cross_terms.at[1, core], CROSS_SEGMENTS, H // 2,
    )
    slot_cross_query = share(held.cross_query_grad)
    slot_cross_terms = links.slot()
    links.send(slot_cross_terms, held.cross_terms.at[:, core], held.cross_terms.at[:, core], partner)
    produce_expand(1)
    scatter.tick()

    def add_first(columns, value):
        held.third_grad[:, columns] = value

    rows_back(held.cross_query_grad.at[mine], weight(CROSS_QUERY, 1), add_first)
    fetch(OUT, 1)
    have("normal_one", "inverse_one", "first_t", "memory_t", "attended_t", "tokens_t")

    @loop(OWN // STEP)
    def _(index):
        rows = tile(index, STEP)
        grad = held.third_grad[rows, :] + alpha_scale * held.second_sum[rows, :]
        pre = norm_rows_back(grad, held.normal_one[rows, :], spread(held.inverse_one, rows), gain(0), held.norm_sums, 0)
        held.second_sum[rows, :] = pre
        held.self_branch[pl.ds(pl.multiple_of(OWN * core + STEP * index, STEP), STEP), :] = pre.astype(BF)

    slot_self_branch = share(held.self_branch)
    norm_steps = all_sum(links, held.norm_sums, norm_grads, held.work)
    next(norm_steps)
    produce_expand(2)
    scatter.tick()
    rows_back(held.self_branch.at[mine], weight(OUT, 1), low(held.attended_grad))
    fetch(QUERY, 1)
    have("queries", "keys", "values", "self_bias", "self_logs")
    terms = held.terms

    def attend_part(first, pairs):
        attend_rows_back(
            held.queries, held.keys, held.values, held.self_bias, held.self_logs, held.attended_grad,
            held.query_grad.at[mine], terms.at[0].reshape(SPAN, D), terms.at[1].reshape(SPAN, D), SELF_SEGMENTS, pairs, first,
        )

    attend_part(0, 2)
    produce_expand(3)
    scatter.tick()
    next(norm_steps)
    attend_part(2, 2)
    shared(held.cross_branch, slot_cross_branch)
    produce(lambda: held.cross_t[...], held.cross_branch)
    scatter.tick()
    next(norm_steps)
    attend_part(4, 2)
    shared(held.cross_query_grad, slot_cross_query)
    produce(lambda: held.first_t[...], held.cross_query_grad)
    scatter.tick()
    next(norm_steps)
    attend_part(6, 2)
    slot_query = share(held.query_grad)
    slot_terms = links.slot()
    links.send(slot_terms, terms.at[:, :, :, 1 - core], held.terms_core, partner)

    links.arrived(slot_cross_terms, held.cross_terms.at[:, 1 - core])
    for which in (0, 1):
        held.cross_sums[which] = (held.cross_terms[which, 0].astype(F32) + held.cross_terms[which, 1].astype(F32)).astype(BF)
    produce(lambda: held.memory_t[...], held.cross_sums.at[0], MEM)
    scatter.tick()
    next(norm_steps)

    links.arrived(slot_terms, held.terms_core)
    near = z % 2

    def join(place_index):
        for which in (0, 1):
            for high in (0, 1):
                value = terms[which, high, place_index, core].astype(F32) + held.terms_core[which, high, place_index].astype(F32)
                terms[which, high, place_index, core] = value.astype(BF)

    join(1 - near)
    slot_mate = links.slot()
    links.send(slot_mate, terms.at[:, :, 1 - near, core], held.terms_mate, place.mate())
    join(near)

    produce(lambda: held.memory_t[...], held.cross_sums.at[1], MEM)
    scatter.tick()
    key_rows = held.cross_sums[0].reshape(4, 2, 16, D)

    cross_key, cross_value = weight(CROSS_KEY, 0), weight(CROSS_VALUE, 2)
    sums = held.cross_sums.reshape(2, 4, 2, 16, D)

    @loop(4)
    def _(index):
        columns = tile(index, OWN)
        term = project_back(sums[0, :, core].reshape(64, D), cross_key[columns, :])
        term = term + project_back(sums[1, :, core].reshape(64, D), cross_value[columns, :])
        held.memory_own[:, :, columns] = term.astype(BF).reshape(4, 16, OWN)

    fetch(KEY, 0)
    fetch(VALUE, 2)
    slot_memory = links.slot(4)
    for k in (1, 2, 3):
        links.send(slot_memory + z, held.memory_own.at[(z + k) % 4], held.memory_in.at[z], place.along_z(k))
    held.memory_in[z] = held.memory_own[z]

    shared(held.self_branch, slot_self_branch)
    produce(lambda: held.attended_t[...], held.self_branch)
    scatter.tick()
    shared(held.query_grad, slot_query)
    produce(lambda: held.tokens_t[...], held.query_grad)
    scatter.tick()

    def add_input(columns, value):
        held.third_grad[:, columns] = alpha_scale * held.second_sum[:, columns] + value

    rows_back(held.query_grad.at[mine], weight(QUERY, 1), add_input)
    links.arrived(slot_mate, held.terms_mate)
    for which, target in enumerate((held.key_grad, held.value_grad)):
        for high in (0, 1):
            value = terms[which, high, near, core].astype(F32) + held.terms_mate[which, high].astype(F32)
            target[pl.ds(pl.multiple_of(OWN * core + LEN * high, LEN), LEN), :] = value.astype(BF)
    slot_key, slot_value = share(held.key_grad), share(held.value_grad)
    shared(held.key_grad, slot_key)
    produce(lambda: held.tokens_t[...], held.key_grad)
    scatter.tick()
    shared(held.value_grad, slot_value)
    produce(lambda: held.tokens_t[...], held.value_grad)
    scatter.tick()

    def add_more(columns, value):
        held.third_grad[:, columns] += value

    rows_back(held.key_grad.at[mine], weight(KEY, 0), add_more)
    rows_back(held.value_grad.at[mine], weight(VALUE, 2), add_more)
    held.far_own[...] = held.third_grad[block_rows(1 - group), :].astype(BF)
    slot_far = links.slot()
    links.send(slot_far, held.far_own, held.far_in, place.along_z(2))
    input_grad[group] = held.third_grad[block_rows(group), :]
    scatter.tick()
    for k in (1, 2, 3):
        links.arrived(slot_memory + (z + k) % 4, held.memory_in.at[(z + k) % 4])
    for which in (0, 1):
        memory_grad[which] = held.memory_in[2 * which].astype(F32) + held.memory_in[2 * which + 1].astype(F32)
    links.arrived(slot_far, held.far_in)
    input_grad[1 - group] = held.far_in[...].astype(F32)
    scatter.tick()
    scatter.tick()
    moves.finish()
    links.finish()


def backward_call(square, shrink, saves, block_shape, memory_shape):
    results = [jax.ShapeDtypeStruct(block_shape, F32), jax.ShapeDtypeStruct(memory_shape, F32)]
    results += [jax.ShapeDtypeStruct((32, D), F32)] * 8
    results += [jax.ShapeDtypeStruct(shape, F32) for shape in ((32, 4 * D), (LEN, D), (8, D))]
    saved = {**FORWARD_SAVES, **TURNED_SAVES}
    return pl.pallas_call(
        backward_kernel,
        in_specs=[IN_PLACE] * (2 + len(saved)),
        out_specs=[IN_VMEM] * len(results),
        out_shape=results,
        scratch_shapes=[
            *vmem_of(saved),
            *vmem_of(BACKWARD_SCRATCH),
            pltpu.SemaphoreType.DMA((BACKWARD_SENDS,)),
            pltpu.SemaphoreType.DMA((BACKWARD_SLOTS,)),
            pltpu.SemaphoreType.DMA((BACKWARD_MOVES,)),
        ],
        compiler_params=pltpu.CompilerParams(collective_id=1, has_side_effects=True, vmem_limit_bytes=63 << 20),
    )(square, shrink, *(saves[name] for name in saved))


def fast_shards(
    tokens, memory, lengths, memory_segments, out_grad,
    self_query, self_key, self_value, self_out,
    cross_query, cross_key, cross_value, cross_out,
    expand_weight, shrink_weight, norm_gains, norm_biases,
):
    me = lax.axis_index("dp") * lax.axis_size("seq") + lax.axis_index("seq")
    norms = jnp.concatenate([norm_gains, norm_biases, jnp.zeros((2, 32), BF)]).astype(F32)
    norms = lax.dynamic_update_slice(jnp.zeros((8, D), F32), norms, (0, 32 * me))
    weights = (self_key, self_value, self_query, self_out, cross_query, cross_key, cross_value, cross_out)
    square, shrink, output, saves = forward_call(
        lengths, memory_segments, norms, tokens, memory, out_grad, (*weights, expand_weight, shrink_weight)
    )
    values = backward_call(square, shrink, saves, tokens.shape, memory.shape)
    input_grad, memory_grad, units, expand_grad, shrink_grad, norm_grads = values[0], values[1], values[2:10], *values[10:]
    norm_grads = lax.dynamic_slice(norm_grads, (0, 32 * me), (8, 32))
    return (
        output,
        input_grad,
        memory_grad,
        *(units[unit] for unit in (QUERY, KEY, VALUE, OUT, CROSS_QUERY, CROSS_KEY, CROSS_VALUE, CROSS_OUT)),
        expand_grad,
        shrink_grad,
        norm_grads[:3],
        norm_grads[3:6],
    )


def solution(mesh):
    quick = dict(mesh.shape) == {"dp": 4, "seq": 8}
    return jax.shard_map(
        fast_shards if quick else shards,
        mesh=mesh,
        in_specs=(
            P("dp", "seq", None),
            P("dp", "seq", None),
            P("dp", None),
            P("dp", None),
            P("dp", "seq", None),
            P(("dp", "seq"), None),
            P(("dp", "seq"), None),
            P(("dp", "seq"), None),
            P(("dp", "seq"), None),
            P(("dp", "seq"), None),
            P(("dp", "seq"), None),
            P(("dp", "seq"), None),
            P(("dp", "seq"), None),
            P(("dp", "seq"), None),
            P(("dp", "seq"), None),
            P(None, ("dp", "seq")),
            P(None, ("dp", "seq")),
        ),
        out_specs=(
            P("dp", "seq", None),
            P("dp", "seq", None),
            P("dp", "seq", None),
            P(("dp", "seq"), None),
            P(("dp", "seq"), None),
            P(("dp", "seq"), None),
            P(("dp", "seq"), None),
            P(("dp", "seq"), None),
            P(("dp", "seq"), None),
            P(("dp", "seq"), None),
            P(("dp", "seq"), None),
            P(("dp", "seq"), None),
            P(("dp", "seq"), None),
            P(None, ("dp", "seq")),
            P(None, ("dp", "seq")),
        ),
        check_vma=False,
    )
```

```python
import jax
import jax.numpy as jnp
from jax import lax
from jax.experimental import pallas as pl
from jax.experimental.pallas import tpu as pltpu
from jax.sharding import PartitionSpec as P

H = 16
HD = 64
MB = 2


alpha_scale = 300.0**0.25
norm_eps = 1e-05
masked_score = -1e30


def layer_norm(value, gain, bias):
    average = jnp.mean(value, axis=-1, keepdims=True)
    centred = value - average
    spread = jnp.mean(centred * centred, axis=-1, keepdims=True)
    return centred * lax.rsqrt(spread + norm_eps) * gain + bias


def project(left, right):
    return jnp.dot(left, right, preferred_element_type=jnp.float32)


def project_back(left, right):
    return lax.dot_general(
        left, right, (((1,), (1,)), ((), ())), preferred_element_type=jnp.float32
    )


def weight_term(left, right):
    return lax.dot_general(
        left, right, (((0,), (0,)), ((), ())), preferred_element_type=jnp.float32
    )


def split_heads(value):
    return value.reshape(value.shape[0], value.shape[1], H, HD)


def sentence_ids(sent_ends, places):
    return jnp.sum((places[None, :, None] >= sent_ends[:, None, :]).astype(jnp.int32), axis=2)


def masked_scores(queries, key_heads, allowed, scaling):
    raw_scores = (
        jnp.einsum("gqhd,gkhd->ghqk", queries, key_heads, preferred_element_type=jnp.float32)
        * scaling
    )
    return jnp.where(allowed[:, None], raw_scores, masked_score)


def attend_forward(queries, key_heads, value_heads, allowed, scaling):
    scores = masked_scores(queries, key_heads, allowed, scaling)
    row_max = jnp.max(scores, axis=3, keepdims=True)
    powers = jnp.exp(scores - row_max)
    row_total = jnp.sum(powers, axis=3, keepdims=True)
    prob_low = (powers / row_total).astype(jnp.bfloat16)
    attended = jnp.einsum(
        "ghqk,gkhd->gqhd", prob_low, value_heads, preferred_element_type=jnp.float32
    )
    return (attended, row_max + jnp.log(row_total))


def attend_backward(queries, key_heads, value_heads, allowed, scaling, log_total, attended_grad):
    scores = masked_scores(queries, key_heads, allowed, scaling)
    probability = jnp.exp(scores - log_total)
    prob_grad = jnp.einsum(
        "gqhd,gkhd->ghqk", attended_grad, value_heads, preferred_element_type=jnp.float32
    )
    score_grad = probability * (prob_grad - jnp.sum(prob_grad * probability, axis=3, keepdims=True))
    score_low = score_grad.astype(jnp.bfloat16)
    query_grad = (
        jnp.einsum("ghqk,gkhd->gqhd", score_low, key_heads, preferred_element_type=jnp.float32)
        * scaling
    )
    return (query_grad, score_low, probability.astype(jnp.bfloat16))


def micro_batch(gathered, tokens, memory, lengths, memory_segments, out_grad):
    (
        self_query,
        self_key,
        self_value,
        self_out,
        cross_query,
        cross_key,
        cross_value,
        cross_out,
        expand_weight,
        shrink_weight,
        norm_gains,
        norm_biases,
    ) = gathered
    gains = norm_gains.astype(jnp.float32)
    biases = norm_biases.astype(jnp.float32)
    group_size, local_len, features = tokens.shape
    seq_count = lax.axis_size("seq")
    seq_index = lax.axis_index("seq")
    full_len = local_len * seq_count
    row_count = group_size * local_len
    scaling = HD ** (-0.5)
    sent_ends = jnp.cumsum(lengths, axis=1)[:, :-1]
    query_places = seq_index * local_len + jnp.arange(local_len, dtype=jnp.int32)
    key_places = jnp.arange(full_len, dtype=jnp.int32)
    query_ids = sentence_ids(sent_ends, query_places)
    key_ids = sentence_ids(sent_ends, key_places)
    self_allowed = (query_ids[:, :, None] == key_ids[:, None, :]) & (
        key_places[None, None, :] <= query_places[None, :, None]
    )
    cross_allowed = query_ids[:, :, None] == memory_segments[:, None, :]
    token_rows = tokens.reshape(row_count, features)
    queries = split_heads(
        project(token_rows, self_query)
        .astype(jnp.bfloat16)
        .reshape(group_size, local_len, features)
    )
    own_keys = (
        project(token_rows, self_key).astype(jnp.bfloat16).reshape(group_size, local_len, features)
    )
    own_values = (
        project(token_rows, self_value)
        .astype(jnp.bfloat16)
        .reshape(group_size, local_len, features)
    )
    all_keys, all_values = (
        lax.all_gather(own_keys, "seq", axis=1, tiled=True),
        lax.all_gather(own_values, "seq", axis=1, tiled=True),
    )
    key_heads = split_heads(all_keys)
    value_heads = split_heads(all_values)
    attended, self_log = attend_forward(queries, key_heads, value_heads, self_allowed, scaling)
    attended = attended.reshape(row_count, features).astype(jnp.bfloat16)
    first_pre = alpha_scale * token_rows.astype(jnp.float32) + project(attended, self_out)
    first, first_pull = jax.vjp(layer_norm, first_pre, gains[0], biases[0])
    first_low = first.astype(jnp.bfloat16)
    cross_queries = split_heads(
        project(first_low, cross_query)
        .astype(jnp.bfloat16)
        .reshape(group_size, local_len, features)
    )
    own_memory = memory.reshape(-1, features)
    memory_all = lax.all_gather(memory, "seq", axis=1, tiled=True)
    memory_rows = memory_all.reshape(-1, features)
    cross_keys = (
        project(memory_rows, cross_key).astype(jnp.bfloat16).reshape(group_size, -1, features)
    )
    cross_values = (
        project(memory_rows, cross_value).astype(jnp.bfloat16).reshape(group_size, -1, features)
    )
    cross_key_heads = split_heads(cross_keys)
    cross_value_heads = split_heads(cross_values)
    cross_attended, cross_log = attend_forward(
        cross_queries, cross_key_heads, cross_value_heads, cross_allowed, scaling
    )
    cross_attended = cross_attended.reshape(row_count, features).astype(jnp.bfloat16)
    second_pre = alpha_scale * first + project(cross_attended, cross_out)
    second, second_pull = jax.vjp(layer_norm, second_pre, gains[1], biases[1])
    second_low = second.astype(jnp.bfloat16)
    upward = project(second_low, expand_weight)
    active, gelu_pull = jax.vjp(jax.nn.gelu, upward)
    active_low = active.astype(jnp.bfloat16)
    third_pre = alpha_scale * second + project(active_low, shrink_weight)
    final, third_pull = jax.vjp(layer_norm, third_pre, gains[2], biases[2])
    third_grad, gain_third, bias_third = third_pull(
        out_grad.reshape(row_count, features).astype(jnp.float32)
    )
    branch_grad = third_grad.astype(jnp.bfloat16)
    shrink_grad = weight_term(active_low, branch_grad)
    (up_grad,) = gelu_pull(project_back(branch_grad, shrink_weight))
    up_low = up_grad.astype(jnp.bfloat16)
    expand_grad = weight_term(second_low, up_low)
    second_grad = alpha_scale * third_grad + project_back(up_low, expand_weight)
    second_pre_grad, gain_second, bias_second = second_pull(second_grad)
    cross_branch = second_pre_grad.astype(jnp.bfloat16)
    cross_out_grad = weight_term(cross_attended, cross_branch)
    cross_attended_grad = split_heads(
        project_back(cross_branch, cross_out)
        .astype(jnp.bfloat16)
        .reshape(group_size, local_len, features)
    )
    cross_q_grad, cross_scores, cross_probs = attend_backward(
        cross_queries,
        cross_key_heads,
        cross_value_heads,
        cross_allowed,
        scaling,
        cross_log,
        cross_attended_grad,
    )
    cross_q_low = cross_q_grad.reshape(row_count, features).astype(jnp.bfloat16)
    cross_query_grad = weight_term(first_low, cross_q_low)
    key_term = (
        jnp.einsum(
            "ghqk,gqhd->gkhd", cross_scores, cross_queries, preferred_element_type=jnp.float32
        )
        * scaling
    ).reshape(group_size, -1, features)
    value_term = jnp.einsum(
        "ghqk,gqhd->gkhd", cross_probs, cross_attended_grad, preferred_element_type=jnp.float32
    ).reshape(group_size, -1, features)
    key_summed, value_summed = (
        lax.psum_scatter(
            key_term.astype(jnp.bfloat16), "seq", scatter_dimension=1, tiled=True
        ).astype(jnp.float32),
        lax.psum_scatter(
            value_term.astype(jnp.bfloat16), "seq", scatter_dimension=1, tiled=True
        ).astype(jnp.float32),
    )
    key_low = key_summed.reshape(-1, features).astype(jnp.bfloat16)
    value_low = value_summed.reshape(-1, features).astype(jnp.bfloat16)
    cross_key_grad = weight_term(own_memory, key_low)
    cross_value_grad = weight_term(own_memory, value_low)
    memory_grad = (project_back(key_low, cross_key) + project_back(value_low, cross_value)).reshape(
        memory.shape
    )
    first_grad = alpha_scale * second_pre_grad + project_back(cross_q_low, cross_query)
    first_pre_grad, gain_first, bias_first = first_pull(first_grad)
    self_branch = first_pre_grad.astype(jnp.bfloat16)
    self_out_grad = weight_term(attended, self_branch)
    attended_grad = split_heads(
        project_back(self_branch, self_out)
        .astype(jnp.bfloat16)
        .reshape(group_size, local_len, features)
    )
    self_q_grad, self_scores, self_probs = attend_backward(
        queries, key_heads, value_heads, self_allowed, scaling, self_log, attended_grad
    )
    count = local_len * lax.axis_size("seq")
    key_part = (
        jnp.einsum("ghqk,gqhd->kghd", self_scores, queries, preferred_element_type=jnp.float32)
        * scaling
    )
    value_part = jnp.einsum(
        "ghqk,gqhd->kghd", self_probs, attended_grad, preferred_element_type=jnp.float32
    )
    pair_summed = lax.psum_scatter(
        jnp.concatenate(
            [
                key_part.reshape(count, group_size, features),
                value_part.reshape(count, group_size, features),
            ],
            axis=2,
        ).astype(jnp.bfloat16),
        "seq",
        scatter_dimension=0,
        tiled=True,
    ).astype(jnp.float32)
    key_grad = (
        pair_summed[:, :, :features]
        .astype(jnp.bfloat16)
        .transpose(1, 0, 2)
        .reshape(row_count, features)
    )
    value_grad = (
        pair_summed[:, :, features:]
        .astype(jnp.bfloat16)
        .transpose(1, 0, 2)
        .reshape(row_count, features)
    )
    query_low = self_q_grad.reshape(row_count, features).astype(jnp.bfloat16)
    self_query_grad = weight_term(token_rows, query_low)
    self_key_grad = weight_term(token_rows, key_grad)
    self_value_grad = weight_term(token_rows, value_grad)
    input_grad = (
        alpha_scale * first_pre_grad
        + project_back(query_low, self_query)
        + project_back(key_grad, self_key)
        + project_back(value_grad, self_value)
    )
    gains_grad = jnp.stack([gain_first, gain_second, gain_third])
    biases_grad = jnp.stack([bias_first, bias_second, bias_third])
    gradients = (
        self_query_grad,
        self_key_grad,
        self_value_grad,
        self_out_grad,
        cross_query_grad,
        cross_key_grad,
        cross_value_grad,
        cross_out_grad,
        expand_grad,
        shrink_grad,
        gains_grad,
        biases_grad,
    )
    result = final.astype(jnp.bfloat16).reshape(group_size, local_len, features)
    return (result, input_grad.reshape(group_size, local_len, features), memory_grad, gradients)


def shards(
    tokens,
    memory,
    lengths,
    memory_segments,
    out_grad,
    self_query,
    self_key,
    self_value,
    self_out,
    cross_query,
    cross_key,
    cross_value,
    cross_out,
    expand_weight,
    shrink_weight,
    norm_gains,
    norm_biases,
):
    group_size = tokens.shape[0] // MB
    outputs = []
    input_grads = []
    memory_grads = []
    totals = None
    for batch_index in range(MB):
        gathered = (
            lax.all_gather(self_query, ("dp", "seq"), axis=0, tiled=True),
            lax.all_gather(self_key, ("dp", "seq"), axis=0, tiled=True),
            lax.all_gather(self_value, ("dp", "seq"), axis=0, tiled=True),
            lax.all_gather(self_out, ("dp", "seq"), axis=0, tiled=True),
            lax.all_gather(cross_query, ("dp", "seq"), axis=0, tiled=True),
            lax.all_gather(cross_key, ("dp", "seq"), axis=0, tiled=True),
            lax.all_gather(cross_value, ("dp", "seq"), axis=0, tiled=True),
            lax.all_gather(cross_out, ("dp", "seq"), axis=0, tiled=True),
            lax.all_gather(expand_weight, ("dp", "seq"), axis=0, tiled=True),
            lax.all_gather(shrink_weight, ("dp", "seq"), axis=0, tiled=True),
            lax.all_gather(norm_gains, ("dp", "seq"), axis=1, tiled=True),
            lax.all_gather(norm_biases, ("dp", "seq"), axis=1, tiled=True),
        )
        start = batch_index * group_size
        stop = start + group_size
        result, input_grad, memory_grad, gradients = micro_batch(
            gathered,
            tokens[start:stop],
            memory[start:stop],
            lengths[start:stop],
            memory_segments[start:stop],
            out_grad[start:stop],
        )
        outputs.append(result)
        input_grads.append(input_grad)
        memory_grads.append(memory_grad)
        if totals is None:
            totals = gradients
        else:
            totals = tuple((running + gradient for running, gradient in zip(totals, gradients)))
    summed = (
        lax.psum_scatter(totals[0], ("dp", "seq"), scatter_dimension=0, tiled=True),
        lax.psum_scatter(totals[1], ("dp", "seq"), scatter_dimension=0, tiled=True),
        lax.psum_scatter(totals[2], ("dp", "seq"), scatter_dimension=0, tiled=True),
        lax.psum_scatter(totals[3], ("dp", "seq"), scatter_dimension=0, tiled=True),
        lax.psum_scatter(totals[4], ("dp", "seq"), scatter_dimension=0, tiled=True),
        lax.psum_scatter(totals[5], ("dp", "seq"), scatter_dimension=0, tiled=True),
        lax.psum_scatter(totals[6], ("dp", "seq"), scatter_dimension=0, tiled=True),
        lax.psum_scatter(totals[7], ("dp", "seq"), scatter_dimension=0, tiled=True),
        lax.psum_scatter(totals[8], ("dp", "seq"), scatter_dimension=0, tiled=True),
        lax.psum_scatter(totals[9], ("dp", "seq"), scatter_dimension=0, tiled=True),
        lax.psum_scatter(totals[10], ("dp", "seq"), scatter_dimension=1, tiled=True),
        lax.psum_scatter(totals[11], ("dp", "seq"), scatter_dimension=1, tiled=True),
    )
    return (
        jnp.concatenate(outputs, 0),
        jnp.concatenate(input_grads, 0),
        jnp.concatenate(memory_grads, 0),
        summed[0],
        summed[1],
        summed[2],
        summed[3],
        summed[4],
        summed[5],
        summed[6],
        summed[7],
        summed[8],
        summed[9],
        summed[10],
        summed[11],
    )


MESH = pl.DeviceIdType.MESH
BF = jnp.bfloat16
F32 = jnp.float32
ALL = slice(None)
D = 1024
LEN = 128
OWN = 2 * LEN
SPAN = 8 * LEN
MEM = 128
KEY, VALUE, QUERY, OUT, CROSS_QUERY, CROSS_KEY, CROSS_VALUE, CROSS_OUT = range(8)
EXPAND = 8
SQUARE = 12
UNITS = 16
GRID = (2, 2, 4, 2)
SQUARE_SHAPE = (SQUARE, *GRID, 32, D)
SHRINK_SHAPE = (*GRID, UNITS - SQUARE, 32, D)
VMEM_BYTES = 60 << 20
GELU_SLOPE = (2.0 / 3.141592653589793) ** 0.5
GELU_CUBE = 0.044715


class Place:
    def __init__(self):
        dp, seq = lax.axis_index("dp"), lax.axis_index("seq")
        self.x, self.y, self.core, self.z, self.seq = dp % 2, dp // 2, seq % 2, seq // 2, seq
        self.group = self.z // 2
        self.low = seq % 4

    def at(self, y=None, x=None, z=None, core=None):
        y = self.y if y is None else y
        x = self.x if x is None else x
        z = self.z if z is None else z
        core = self.core if core is None else core
        return (y * 2 + x, z * 2 + core)

    def across(self, axis):
        if axis == "x":
            return self.at(x=1 - self.x)
        if axis == "y":
            return self.at(y=1 - self.y)
        return self.at(core=1 - self.core)

    def along_z(self, step):
        return self.at(z=(self.z + step) % 4)

    def mate(self):
        return self.at(z=self.z + 1 - 2 * (self.z % 2))

    def greet(self):
        barrier = pltpu.get_barrier_semaphore()
        peers = [self.across(axis) for axis in ("x", "y", "core")]
        peers += [self.along_z(step) for step in (1, 2, 3)]
        for peer in peers:
            pl.semaphore_signal(barrier, inc=1, device_id=peer, device_id_type=MESH)
        pl.semaphore_wait(barrier, len(peers))


class Links:
    def __init__(self, place, send_sem, recv_sem):
        self.place, self.send_sem, self.recv_sem = place, send_sem, recv_sem
        self.sends, self.slots = 0, 0
        self.open = {}

    def slot(self, count=1):
        first = self.slots
        self.slots += count
        assert self.slots <= self.recv_sem.shape[0]
        return first

    def send(self, slot, source, target, device):
        assert self.sends < self.send_sem.shape[0]
        step = pltpu.make_async_remote_copy(
            src_ref=source,
            dst_ref=target,
            send_sem=self.send_sem.at[self.sends],
            recv_sem=self.recv_sem.at[slot],
            device_id=device,
            device_id_type=MESH,
        )
        step.start()
        self.sends += 1
        self.open[id(step)] = step
        return step

    def arrived(self, slot, target):
        pltpu.make_async_remote_copy(
            src_ref=target,
            dst_ref=target,
            send_sem=self.send_sem.at[0],
            recv_sem=self.recv_sem.at[slot],
            device_id=self.place.across("core"),
            device_id_type=MESH,
        ).wait_recv()

    def sent(self, step):
        self.open.pop(id(step)).wait_send()

    def finish(self):
        for step in self.open.values():
            step.wait_send()
        self.open = {}


class Moves:
    def __init__(self, sem):
        self.sem, self.count, self.open = sem, 0, {}

    def start(self, source, target):
        assert self.count < self.sem.shape[0]
        step = pltpu.make_async_copy(source, target, self.sem.at[self.count])
        step.start()
        self.count += 1
        self.open[id(step)] = step
        return step

    def wait(self, step):
        self.open.pop(id(step)).wait()

    def finish(self):
        for step in self.open.values():
            step.wait()
        self.open = {}


def all_sum(links, part, total, work):
    place = links.place
    work[0] = part[...]
    for number, axis in enumerate(("core", "y", "x")):
        slot = links.slot()
        step = links.send(slot, work.at[0], work.at[1 + number], place.across(axis))
        yield
        links.arrived(slot, work.at[1 + number])
        links.sent(step)
        work[0] = work[0] + work[1 + number]
    slot = links.slot(4)
    for k in (1, 2, 3):
        links.send(slot + place.z, work.at[0], work.at[4 + place.z], place.along_z(k))
    yield
    result = work[0]
    for k in (1, 2, 3):
        source = (place.z + k) % 4
        links.arrived(slot + source, work.at[4 + source])
        result = result + work[4 + source]
    total[...] = result
    yield


def loop(count):
    return pl.loop(0, count)


def tile(index, size):
    return pl.ds(pl.multiple_of(index * size, size), size)


def rows_times(left, right, store, rows=OWN, width=256):
    for first in range(0, left.shape[0], rows):

        @loop(D // width)
        def _(index):
            columns = tile(index, width)
            store(pl.ds(first, rows), columns, jnp.dot(left[pl.ds(first, rows), :], right[:, columns], preferred_element_type=F32))


def rows_back(left, right, store, width=256):
    @loop(D // width)
    def _(index):
        columns = tile(index, width)
        store(columns, project_back(left[...], right[columns, :]))


def put(target, dtype=BF):
    def store(rows, columns, value):
        target[rows, columns] = value.astype(dtype)

    return store


def half_masks():
    lane = lax.broadcasted_iota(jnp.int32, (1, LEN), 1)
    return [(lane < HD).astype(F32), (lane >= HD).astype(F32)]


def attend_rows(queries, keys, values, bias, logs, out, segments, pairs=H // 2, first_pair=0):
    masks = half_masks()

    @loop(pairs)
    def _(step):
        pair = step + first_pair
        columns = tile(pair, LEN)
        for first, rows, count in segments:
            own = pl.ds(first, rows)
            key, value = keys[pl.ds(0, count), columns], values[pl.ds(0, count), columns]
            query = queries[own, columns]
            lane = lax.broadcasted_iota(jnp.int32, (rows, LEN), 1)
            parts = []
            for half in (0, 1):
                scores = project_back(query * (masks[half] * HD**-0.5).astype(BF), key) + bias[own, pl.ds(0, count)]
                top = jnp.max(scores, axis=1, keepdims=True)
                powers = jnp.exp(scores - top)
                total = jnp.sum(powers, axis=1, keepdims=True)
                parts.append(project((powers * (1.0 / total)).astype(BF), value))
                logs[own, :] = jnp.where(lane == 2 * pair + half, top + jnp.log(total), logs[own, :])
            out[own, columns] = jnp.where(lane < HD, parts[0], parts[1]).astype(BF)


def attend_rows_back(queries, keys, values, bias, logs, grads, query_grads, key_grads, value_grads, segments, pairs, first_pair=0):
    masks = half_masks()

    @loop(pairs)
    def _(step):
        pair = step + first_pair
        columns = tile(pair, LEN)
        for number, (first, rows, count) in enumerate(segments):
            own, met = pl.ds(first, rows), pl.ds(0, count)
            key, value = keys[met, columns], values[met, columns]
            lane = lax.broadcasted_iota(jnp.int32, (rows, LEN), 1)
            halves, score_lows, prob_lows, query_parts, grad_parts = [], [], [], [], []
            for half in (0, 1):
                query = queries[own, columns] * (masks[half] * HD**-0.5).astype(BF)
                grad = grads[own, columns] * masks[half].astype(BF)
                log_total = jnp.sum(jnp.where(lane == 2 * pair + half, logs[own, :], 0.0), axis=1, keepdims=True)
                probs = jnp.exp(project_back(query, key) + bias[own, met] - log_total)
                prob_grad = project_back(grad, value)
                score_grad = probs * (prob_grad - jnp.sum(prob_grad * probs, axis=1, keepdims=True))
                score_low = score_grad.astype(BF)
                halves.append(project(score_low, key) * HD**-0.5)
                score_lows.append(score_low)
                prob_lows.append(probs.astype(BF))
                query_parts.append(query)
                grad_parts.append(grad)
            query_grads[own, columns] = jnp.where(lane < HD, halves[0], halves[1]).astype(BF)
            key_term = weight_term(jnp.concatenate(score_lows), jnp.concatenate(query_parts))
            value_term = weight_term(jnp.concatenate(prob_lows), jnp.concatenate(grad_parts))
            if number == 0:
                key_grads[met, columns] = key_term.astype(BF)
                value_grads[met, columns] = value_term.astype(BF)
            else:
                key_grads[met, columns] = (key_grads[met, columns].astype(F32) + key_term).astype(BF)
                value_grads[met, columns] = (value_grads[met, columns].astype(F32) + value_term).astype(BF)


SELF_SEGMENTS = ((LEN, LEN, SPAN), (0, LEN, SPAN // 2))
CROSS_SEGMENTS = ((0, OWN, MEM),)
STEP = 32


def norm_rows(read, normal, inverse, emit):
    @loop(OWN // STEP)
    def _(index):
        rows = tile(index, STEP)
        value = read(rows)
        centred = value - jnp.mean(value, axis=1, keepdims=True)
        scale = lax.rsqrt(jnp.mean(centred * centred, axis=1, keepdims=True) + norm_eps)
        result = centred * scale
        if normal is not None:
            normal[rows, :] = result
            inverse[rows, :] = jnp.broadcast_to(scale, (STEP, LEN))
        emit(rows, result, scale)


def norm_rows_back(grad, normal, scale, gain, sums, number):
    sums[pl.ds(number, 1), :] += jnp.sum(grad * normal, axis=0, keepdims=True)
    sums[pl.ds(3 + number, 1), :] += jnp.sum(grad, axis=0, keepdims=True)
    scaled = grad * gain
    return scale * (
        scaled
        - jnp.mean(scaled, axis=1, keepdims=True)
        - normal * jnp.mean(scaled * normal, axis=1, keepdims=True)
    )


class Gather:
    ORDER = (0, 1, 2, 3, 4, 5, 6, 7, 12, 13, 14, 15, 8, 9, 10, 11)
    WIDE = ()
    EARLY = 3
    ROUTES = {False: ("zxy", "zyx"), True: ("xzy", "yzx")}
    TIMES = {False: (-3, 0, 1, 2, 3), True: (-20, -3, 1, 2, 3)}
    SLOTS = 10

    def __init__(self, links, moves, own, square, shrink):
        self.links, self.moves, self.own, self.square, self.shrink = links, moves, own, square, shrink
        self.first_slot = links.slot(UNITS * 2 * self.SLOTS)
        self.local = {}
        for unit in self.ORDER:
            target = self.block(unit, links.place.y, links.place.x, links.place.z, links.place.core)
            self.local[unit] = moves.start(own(unit), target)
        self.now = -self.EARLY
        self.steps = {}
        for number, unit in enumerate(self.ORDER):
            wide = number in self.WIDE
            for half in (0, 1):
                for phase, time in enumerate(self.TIMES[wide]):
                    step = (phase, number, unit, half, self.ROUTES[wide][half])
                    self.steps.setdefault(max(number + time, self.now), []).append(step)

    def block(self, unit, *index):
        if unit < SQUARE:
            return self.square.at[(unit,) + index]
        return self.shrink.at[index[:4] + (unit - SQUARE,) + index[4:]]

    def tick(self):
        for phase, _, unit, half, route in sorted(self.steps.pop(self.now, ())):
            self.move(phase, unit, half, route)
        self.now += 1

    def move(self, phase, unit, half, route):
        links, place = self.links, self.links.place
        here = {"y": place.y, "x": place.x, "z": place.z}
        slot = self.first_slot + (2 * unit + half) * self.SLOTS
        rows = pl.ds(16 * half, 16)
        turn = route.index("z")

        def part(where, core):
            return self.block(unit, where["y"], where["x"], where["z"], core, rows)

        def reached(count):
            return {**here, **{axis: ALL for axis in route[:count]}}

        def incoming(count):
            axis = route[count]
            if axis == "z":
                return reached(count + 1)
            return {**reached(count), axis: 1 - here[axis]}

        if phase == 1 and unit in self.local:
            self.moves.wait(self.local.pop(unit))
        if 1 <= phase <= 3:
            if phase - 1 == turn:
                for k in (1, 2, 3):
                    source = (place.z + k) % 4
                    links.arrived(slot + source, part({**reached(phase - 1), "z": source}, place.core))
            else:
                links.arrived(slot + 3 + phase, part(incoming(phase - 1), place.core))
        if phase < 3:
            source = self.own(unit).at[rows] if phase == 0 else part(reached(phase), place.core)
            target = part(reached(phase), place.core)
            if phase == turn:
                for k in (1, 2, 3):
                    links.send(slot + place.z, source, target, place.along_z(k))
            else:
                links.send(slot + 4 + phase, source, target, place.across(route[phase]))
        if 1 <= phase <= 3 and phase > turn:
            fresh = part(incoming(phase - 1), place.core)
            links.send(slot + 6 + phase, fresh, fresh, place.across("core"))
        if phase == 4:
            for number in range(turn, 3):
                links.arrived(slot + 7 + number, part(incoming(number), 1 - place.core))


def core_rows(core, count=OWN):
    return pl.ds(pl.multiple_of(core * count, count), count)


def block_rows(block):
    return pl.ds(pl.multiple_of(block * LEN, LEN), LEN)


FORWARD_SAVES = {
    "queries": ((OWN, D), BF),
    "keys": ((SPAN, D), BF),
    "values": ((SPAN, D), BF),
    "self_bias": ((OWN, SPAN), F32),
    "self_logs": ((OWN, LEN), F32),
    "normal_one": ((OWN, D), F32),
    "inverse_one": ((OWN, LEN), F32),
    "cross_queries": ((OWN, D), BF),
    "cross_keys": ((MEM, D), BF),
    "cross_values": ((MEM, D), BF),
    "cross_bias": ((OWN, MEM), F32),
    "cross_logs": ((OWN, LEN), F32),
    "normal_two": ((OWN, D), F32),
    "inverse_two": ((OWN, LEN), F32),
    "slopes": ((4, OWN, D), BF),
    "third_grad": ((OWN, D), F32),
    "norm_sums": ((8, D), F32),
    "gains": ((8, D), F32),
    "final_low": ((OWN, D), BF),
}
TURNED_SAVES = {
    "tokens_t": ((16, 32, 2 * OWN), BF),
    "attended_t": ((16, 32, 2 * OWN), BF),
    "first_t": ((16, 32, 2 * OWN), BF),
    "cross_t": ((16, 32, 2 * OWN), BF),
    "second_t": ((16, 32, 2 * OWN), BF),
    "active_t": ((4, 4, 4, 32, 2 * OWN), BF),
    "memory_t": ((16, 32, MEM), BF),
    "branch": ((2 * OWN, D), BF),
}
FORWARD_SCRATCH = {
    "stream": ((SPAN, D), BF),
    "mine": ((OWN, D), BF),
    "context": ((4, 2, 16, D), BF),
    "attended": ((OWN, D), BF),
    "first_low": ((OWN, D), BF),
    "cross_attended": ((OWN, D), BF),
    "second_low": ((OWN, D), BF),
    "active": ((OWN, D), BF),
    "sums": ((OWN, D), F32),
    "cotangent": ((OWN, D), BF),
    "branch_own": ((OWN, D), BF),
    "weights": ((4, D, D), BF),
    "turned": ((3, 16, 2, 32, OWN), BF),
    "turned_active": ((2, 4, 2, 4, 32, OWN), BF),
    "turned_memory": ((16, 2, 32, MEM), BF),
    "work": ((8, 8, D), F32),
}
FORWARD_SENDS, FORWARD_SLOTS, FORWARD_MOVES = 320, 384, 96


class Refs:
    def __init__(self, names, refs):
        for name, ref in zip(names, refs):
            setattr(self, name, ref)


def forward_kernel(lengths, segments, norms, tokens, memory, out_grad, *refs):
    squares, expand_own, shrink_own = refs[:8], refs[8], refs[9]
    square, shrink = refs[10:12]
    rest = refs[12:]
    kept = Refs(FORWARD_SAVES, rest[: len(FORWARD_SAVES)])
    rest = rest[len(FORWARD_SAVES) :]
    turned = Refs(TURNED_SAVES, rest[: len(TURNED_SAVES)])
    rest = rest[len(TURNED_SAVES) :]
    held = Refs(FORWARD_SAVES, rest[: len(FORWARD_SAVES)])
    rest = rest[len(FORWARD_SAVES) :]
    held.__dict__.update(Refs(FORWARD_SCRATCH, rest[: len(FORWARD_SCRATCH)]).__dict__)
    send_sem, recv_sem, move_sem = rest[len(FORWARD_SCRATCH) :]

    place = Place()
    links, moves = Links(place, send_sem, recv_sem), Moves(move_sem)
    y, x, z, core, group, low, seq = place.y, place.x, place.z, place.core, place.group, place.low, place.seq
    partner = place.across("core")
    opposite = place.along_z(2)
    mate = place.mate()
    place.greet()

    def own(unit):
        if unit < EXPAND:
            return squares[unit]
        if unit < SQUARE:
            return expand_own.at[:, pl.ds(D * (unit - EXPAND), D)]
        return shrink_own.at[pl.ds(32 * (unit - SQUARE), 32)]

    stream = held.stream
    far, mate_seq = (seq + 4) % 8, (seq + 2) % 4 + 4 * group
    other_seq = 2 * z + 1 - core
    other_mate = (other_seq + 2) % 4 + 4 * group
    slot_far, slot_mate, slot_mate_far, slot_core = links.slot(), links.slot(), links.slot(), links.slot(4)
    home = moves.start(tokens.at[group], stream.at[block_rows(seq)])
    gather = Gather(links, moves, own, square, shrink)
    for _ in range(Gather.EARLY):
        gather.tick()
    links.send(slot_far, tokens.at[1 - group], stream.at[block_rows(seq)], opposite)
    links.send(slot_mate, tokens.at[group], stream.at[block_rows(seq)], mate)
    links.send(slot_core, tokens.at[group], stream.at[block_rows(seq)], partner)
    slot_memory, slot_context = links.slot(4), links.slot()
    context_home = moves.start(memory.at[group], held.context.at[z, core])
    for k in (1, 2, 3):
        links.send(slot_memory + z, memory.at[((z + k) % 4) // 2], held.context.at[z, core], place.along_z(k))
    norm_steps = all_sum(links, norms, held.gains, held.work)
    next(norm_steps)

    def sentence(places):
        result, end = jnp.zeros_like(places), 0
        for index in range(lengths.shape[1] - 1):
            end = end + lengths[group, index]
            result = result + (places >= end).astype(jnp.int32)
        return result

    held.norm_sums[...] = jnp.zeros_like(held.norm_sums)
    held.self_logs[...] = jnp.zeros_like(held.self_logs)
    held.cross_logs[...] = jnp.zeros_like(held.cross_logs)

    @loop(OWN // STEP)
    def _(index):
        row = index * STEP + lax.broadcasted_iota(jnp.int32, (STEP, 1), 0)
        row_place = LEN * low + row + jnp.where(row >= LEN, 3 * LEN, 0)
        row_sentence = sentence(row_place)
        key_place = lax.broadcasted_iota(jnp.int32, (1, SPAN), 1)
        allowed = (row_sentence == sentence(key_place)) & (key_place <= row_place)
        held.self_bias[tile(index, STEP), :] = jnp.where(allowed, 0.0, masked_score)
        met = row_sentence == segments[pl.ds(group, 1), :]
        held.cross_bias[tile(index, STEP), :] = jnp.where(met, 0.0, masked_score)

    def pass_on(number, block):
        links.send(slot_core + number, stream.at[block_rows(block)], stream.at[block_rows(block)], partner)

    gather.tick()
    next(norm_steps)
    gather.tick()
    next(norm_steps)
    gather.tick()
    links.arrived(slot_far, stream.at[block_rows(far)])
    links.send(slot_mate_far, stream.at[block_rows(far)], stream.at[block_rows(far)], mate)
    pass_on(1, far)
    gather.tick()
    links.arrived(slot_mate, stream.at[block_rows(mate_seq)])
    pass_on(2, mate_seq)
    moves.wait(context_home)
    for k in (1, 2, 3):
        links.arrived(slot_memory + (z + k) % 4, held.context.at[(z + k) % 4, core])
    links.send(slot_context, held.context.at[:, core], held.context.at[:, core], partner)
    next(norm_steps)
    gather.tick()
    links.arrived(slot_mate_far, stream.at[block_rows((mate_seq + 4) % 8)])
    pass_on(3, (mate_seq + 4) % 8)
    gather.tick()
    cotangent_rows, cotangent_far = block_rows(group), block_rows(1 - group)
    slot_cotangent = links.slot()
    cotangent_home = moves.start(out_grad.at[group], held.cotangent.at[cotangent_rows])
    links.send(slot_cotangent, out_grad.at[1 - group], held.cotangent.at[cotangent_rows], opposite)
    moves.wait(home)
    for number, block in enumerate((other_seq, (other_seq + 4) % 8, other_mate, (other_mate + 4) % 8)):
        links.arrived(slot_core + number, stream.at[block_rows(block)])
    links.arrived(slot_context, held.context.at[:, 1 - core])
    held.mine[pl.ds(0, LEN), :] = stream[block_rows(low), :]
    held.mine[pl.ds(LEN, LEN), :] = stream[block_rows(low + 4), :]

    loads = {}

    def fetch(unit, slot):
        source = square.at[unit].reshape(D, D) if unit < SQUARE else shrink.at[(unit - SQUARE) // 2, unit % 2].reshape(D, D)
        loads[unit] = (moves.start(source, held.weights.at[slot]), slot)

    def weight(unit):
        step, slot = loads.pop(unit)
        moves.wait(step)
        return held.weights.at[slot]

    turning = {"count": 0, "open": {}}
    landing = []
    mine, theirs = core_rows(core), core_rows(1 - core)

    def turn(source, name):
        number = turning["count"] % 3
        for move, sent in turning["open"].pop(number, ()):
            moves.wait(move)
            links.sent(sent)
        turning["count"] += 1
        buffer, target = held.turned.at[number], getattr(turned, name)

        @loop(4)
        def _(index):
            buffer[pl.ds(4 * index, 4)] = source[:, tile(index, OWN)].T.reshape(4, 2, 32, OWN)

        slot = links.slot()
        move = moves.start(buffer.at[:, core], target.at[:, :, mine])
        sent = links.send(slot, buffer.at[:, 1 - core], target.at[:, :, mine], partner)
        landing.append((slot, target.at[:, :, theirs]))
        turning["open"][number] = [(move, sent)]

    def keep(*names):
        for name in names:
            moves.start(getattr(held, name), getattr(kept, name))

    def gain(number):
        return held.gains[pl.ds(number, 1), :]

    def bias(number):
        return held.gains[pl.ds(3 + number, 1), :]

    fetch(KEY, 0)
    turn(held.mine, "tokens_t")
    next(norm_steps)
    fetch(VALUE, 1)
    rows_times(stream, weight(KEY), put(held.keys))
    gather.tick()
    fetch(QUERY, 2)
    rows_times(stream, weight(VALUE), put(held.values))
    rows_times(held.mine, weight(QUERY), put(held.queries))

    def attend_part(first, pairs):
        attend_rows(
            held.queries, held.keys, held.values, held.self_bias, held.self_logs, held.attended, SELF_SEGMENTS, pairs, first
        )

    fetch(OUT, 3)
    attend_part(0, 3)
    gather.tick()
    fetch(CROSS_QUERY, 0)
    attend_part(3, 3)
    gather.tick()
    fetch(CROSS_KEY, 1)
    attend_part(6, 2)
    rows_times(held.attended, weight(OUT), put(held.sums, F32))
    keep("queries", "keys", "values", "self_bias", "self_logs", "cross_bias", "gains")

    def first_rows(rows, result, _):
        held.first_low[rows, :] = (result * gain(0) + bias(0)).astype(BF)

    def after(rows, previous):
        return held.sums[rows, :] + alpha_scale * previous

    norm_rows(lambda rows: after(rows, held.mine[rows, :].astype(F32)), held.normal_one, held.inverse_one, first_rows)
    turn(held.attended, "attended_t")
    rows_times(held.first_low, weight(CROSS_QUERY), put(held.cross_queries))
    context = held.context.reshape(MEM, D)
    rows_times(context, weight(CROSS_KEY), put(held.cross_keys), MEM)
    gather.tick()
    fetch(CROSS_VALUE, 2)
    turn(held.first_low, "first_t")

    @loop(4)
    def _(index):
        held.turned_memory[pl.ds(4 * index, 4)] = context[:, tile(index, OWN)].T.reshape(4, 2, 32, MEM)

    moves.start(held.turned_memory.at[:, core], turned.memory_t)
    rows_times(context, weight(CROSS_VALUE), put(held.cross_values), MEM)
    attend_rows(
        held.cross_queries, held.cross_keys, held.cross_values, held.cross_bias, held.cross_logs,
        held.cross_attended, CROSS_SEGMENTS,
    )
    gather.tick()
    fetch(CROSS_OUT, 3)
    keep("cross_queries", "cross_keys", "cross_values", "cross_logs", "normal_one", "inverse_one")
    rows_times(held.cross_attended, weight(CROSS_OUT), put(held.sums, F32))

    def second_rows(rows, result, _):
        held.second_low[rows, :] = (result * gain(1) + bias(1)).astype(BF)

    norm_rows(
        lambda rows: after(rows, held.normal_one[rows, :] * gain(0) + bias(0)),
        held.normal_two, held.inverse_two, second_rows,
    )
    keep("normal_two", "inverse_two")
    gather.tick()
    turn(held.cross_attended, "cross_t")
    turn(held.second_low, "second_t")
    for _ in range(3):
        gather.tick()
    held.sums[...] = jnp.zeros_like(held.sums)
    turned_open = {}
    for part in range(4):
        fetch(SQUARE + part, 2 * (part % 2) + 1)
        gather.tick()
        fetch(EXPAND + part, 2 * (part % 2))
        expand = weight(EXPAND + part)
        slopes = held.slopes.at[part]

        def activate(rows, columns, value):
            inner = GELU_SLOPE * (value + GELU_CUBE * value * value * value)
            bend = jnp.tanh(inner)
            held.active[rows, columns] = (0.5 * value * (1.0 + bend)).astype(BF)
            slope = 0.5 * (1.0 + bend) + 0.5 * value * (1.0 - bend * bend) * (
                GELU_SLOPE * (1.0 + 3.0 * GELU_CUBE * value * value)
            )
            slopes[rows, columns] = slope.astype(BF)

        def add(rows, columns, value):
            held.sums[rows, columns] += value

        rows_times(held.second_low, expand, activate)
        rows_times(held.active, weight(SQUARE + part), add)
        number = part % 2
        for move, sent in turned_open.pop(number, ()):
            moves.wait(move)
            links.sent(sent)
        buffer = held.turned_active.at[number]

        @loop(4)
        def _(index):
            buffer[index] = held.active[:, tile(index, OWN)].T.reshape(2, 4, 32, OWN)

        slot = links.slot()
        move = moves.start(buffer.at[:, core], turned.active_t.at[part, :, :, :, mine])
        sent = links.send(slot, buffer.at[:, 1 - core], turned.active_t.at[part, :, :, :, mine], partner)
        landing.append((slot, turned.active_t.at[part, :, :, :, theirs]))
        turned_open[number] = [(move, sent)]
    keep("slopes")
    links.arrived(slot_cotangent, held.cotangent.at[cotangent_far])
    moves.wait(cotangent_home)

    def third_rows(rows, result, scale):
        held.final_low[rows, :] = (result * gain(2) + bias(2)).astype(BF)
        grad = norm_rows_back(held.cotangent[rows, :].astype(F32), result, scale, gain(2), held.norm_sums, 2)
        held.third_grad[rows, :] = grad
        held.branch_own[rows, :] = grad.astype(BF)

    norm_rows(lambda rows: after(rows, held.normal_two[rows, :] * gain(1) + bias(1)), None, None, third_rows)
    slot = links.slot()
    links.send(slot, held.branch_own, turned.branch.at[mine], partner)
    landing.append((slot, turned.branch.at[theirs]))
    moves.start(held.branch_own, turned.branch.at[mine])
    keep("third_grad", "norm_sums", "final_low")
    for arrival in landing:
        links.arrived(*arrival)
    moves.finish()
    links.finish()


IN_VMEM = pl.BlockSpec(memory_space=pltpu.VMEM)
IN_SMEM = pl.BlockSpec(memory_space=pltpu.SMEM)
IN_PLACE = pl.BlockSpec(memory_space=pl.ANY)


def shapes_of(table):
    return [jax.ShapeDtypeStruct(shape, dtype) for shape, dtype in table.values()]


def vmem_of(table):
    return [pltpu.VMEM(shape, dtype) for shape, dtype in table.values()]


def forward_call(lengths, segments, norms, tokens, memory, out_grad, weights):
    results = [
        jax.ShapeDtypeStruct(SQUARE_SHAPE, BF),
        jax.ShapeDtypeStruct(SHRINK_SHAPE, BF),
        *shapes_of(FORWARD_SAVES),
        *shapes_of(TURNED_SAVES),
    ]
    values = pl.pallas_call(
        forward_kernel,
        in_specs=[IN_SMEM, IN_VMEM, IN_VMEM] + [IN_PLACE] * 13,
        out_specs=[IN_PLACE] * len(results),
        out_shape=results,
        scratch_shapes=[
            *vmem_of(FORWARD_SAVES),
            *vmem_of(FORWARD_SCRATCH),
            pltpu.SemaphoreType.DMA((FORWARD_SENDS,)),
            pltpu.SemaphoreType.DMA((FORWARD_SLOTS,)),
            pltpu.SemaphoreType.DMA((FORWARD_MOVES,)),
        ],
        compiler_params=pltpu.CompilerParams(collective_id=0, has_side_effects=True, vmem_limit_bytes=VMEM_BYTES),
    )(lengths, segments, norms, tokens, memory, out_grad, *weights)
    saves = dict(zip([*FORWARD_SAVES, *TURNED_SAVES], values[2:]))
    return values[0], values[1], saves


class Scatter:
    def __init__(self, links, grads, from_first, from_second, from_z, result):
        self.links, self.grads, self.result = links, grads, result
        self.from_first, self.from_second, self.from_z = from_first, from_second, from_z
        self.slots, self.pending, self.now = {}, {}, 0

    def home(self, unit):
        for step in self.pending.pop(unit - self.grads.shape[0], ()):
            self.links.sent(step)
        self.slots[unit] = self.links.slot(12)
        return self.grads.at[unit % self.grads.shape[0]]

    def add(self, total, part):
        for row in range(4):
            total[row] = (total[row].astype(F32) + part[row].astype(F32)).astype(BF)

    def phase(self, unit, half, number):
        links, place = self.links, self.links.place
        y, x, z = place.y, place.x, place.z
        here = self.grads.at[unit % self.grads.shape[0]]
        depth = unit % self.from_first.shape[0]
        rows = pl.ds(16 * half, 16)
        slot = self.slots[unit] + 6 * half
        by_y = half == 0
        first, second = ("y", "x") if by_y else ("x", "y")
        away = (1 - y, ALL) if by_y else (ALL, 1 - x)
        corner, other, mine = ((y, 1 - x), 1 - x, x) if by_y else ((1 - y, x), 1 - y, y)
        home = here.at[y, x, :, rows]
        first_in = self.from_first.at[depth, :, :, rows]
        second_in = self.from_second.at[depth, :, rows]

        def send(number, source, target, device):
            self.pending.setdefault(unit, []).append(links.send(slot + number, source, target, device))

        if number == 0:
            send(0, here.at[(*away, ALL, rows)], first_in, place.across(first))
        if number == 1:
            links.arrived(slot, first_in)
            corner_part = here.at[(*corner, ALL, rows)]
            self.add(corner_part, first_in.at[other])
            send(1, corner_part, second_in, place.across(second))
            self.add(home, first_in.at[mine])
        if number == 2:
            links.arrived(slot + 1, second_in)
            self.add(home, second_in)
            for k in (1, 2, 3):
                send(2 + z, home.at[(z + k) % 4], self.from_z.at[depth, z, rows], place.along_z(k))
        if number == 3:
            total = home[z].astype(F32)
            for k in (1, 2, 3):
                source = (z + k) % 4
                links.arrived(slot + 2 + source, self.from_z.at[depth, source, rows])
                total = total + self.from_z[depth, source, rows].astype(F32)
            self.result(unit, rows, total)

    def tick(self):
        for number in (0, 1, 2, 3):
            unit = self.now - number
            if 0 <= unit < UNITS:
                for half in (0, 1):
                    self.phase(unit, half, number)
        self.now += 1


DEPTH = 4
BACKWARD_SCRATCH = {
    "weights": ((3, D, D), BF),
    "grads": ((6, 2, 2, 4, 32, D), BF),
    "from_first": ((DEPTH, 2, 4, 32, D), BF),
    "from_second": ((DEPTH, 4, 32, D), BF),
    "from_z": ((DEPTH, 4, 32, D), BF),
    "up": ((4, 2 * OWN, D), BF),
    "second_sum": ((OWN, D), F32),
    "cross_branch": ((2 * OWN, D), BF),
    "attended_grad": ((OWN, D), BF),
    "cross_query_grad": ((2 * OWN, D), BF),
    "cross_terms": ((2, 2, MEM, D), BF),
    "cross_sums": ((2, MEM, D), BF),
    "self_branch": ((2 * OWN, D), BF),
    "query_grad": ((2 * OWN, D), BF),
    "terms": ((2, 2, 2, 2, LEN, D), BF),
    "terms_core": ((2, 2, 2, LEN, D), BF),
    "terms_mate": ((2, 2, LEN, D), BF),
    "key_grad": ((2 * OWN, D), BF),
    "value_grad": ((2 * OWN, D), BF),
    "memory_own": ((4, 16, D), BF),
    "memory_in": ((4, 16, D), BF),
    "far_own": ((LEN, D), BF),
    "far_in": ((LEN, D), BF),
    "work": ((8, 8, D), F32),
}
BACKWARD_SENDS, BACKWARD_SLOTS, BACKWARD_MOVES = 240, 256, 64


def backward_kernel(square, shrink, *refs):
    saved = [*FORWARD_SAVES, *TURNED_SAVES]
    names = [name for name in saved if name != "final_low"]
    kept = Refs(saved, refs[: len(saved)])
    rest = refs[len(saved) :]
    output, input_grad, memory_grad, *unit_grads = rest[:11]
    expand_grad, shrink_grad, norm_grads = rest[11:14]
    rest = rest[14:]
    held = Refs(names, rest[: len(names)])
    rest = rest[len(names) :]
    held.__dict__.update(Refs(BACKWARD_SCRATCH, rest[: len(BACKWARD_SCRATCH)]).__dict__)
    send_sem, recv_sem, move_sem = rest[len(BACKWARD_SCRATCH) :]

    place = Place()
    links, moves = Links(place, send_sem, recv_sem), Moves(move_sem)
    z, core, group = place.z, place.core, place.group
    partner = place.across("core")
    mine, theirs = core_rows(core), core_rows(1 - core)
    loads = {}

    def bring(*wanted):
        for name in wanted:
            loads[name] = moves.start(getattr(kept, name), getattr(held, name))

    def have(*wanted):
        for name in wanted:
            moves.wait(loads.pop(name))

    def fetch(unit, slot):
        source = square.at[unit].reshape(D, D) if unit < SQUARE else shrink.at[(unit - SQUARE) // 2, unit % 2].reshape(D, D)
        loads[unit] = moves.start(source, held.weights.at[slot])

    def weight(unit, slot):
        moves.wait(loads.pop(unit))
        return held.weights.at[slot]

    bring("branch", "active_t")
    fetch(SQUARE, 0)
    fetch(EXPAND, 1)
    fetch(SQUARE + 1, 2)
    bring("slopes", "third_grad", "second_t", "norm_sums", "gains", "normal_two", "inverse_two")
    bring("cross_queries", "cross_keys", "cross_values", "cross_bias", "cross_logs", "cross_t")
    bring("normal_one", "inverse_one", "first_t", "memory_t", "attended_t", "tokens_t")
    bring("queries", "keys", "values", "self_bias", "self_logs")
    place.greet()

    order = [12, 13, 14, 15, 8, 9, 10, 11, CROSS_OUT, CROSS_QUERY, CROSS_KEY, CROSS_VALUE, OUT, QUERY, KEY, VALUE]

    def result(number, rows, total):
        unit = order[number]
        if unit < EXPAND:
            unit_grads[unit][rows, :] = total
        elif unit < SQUARE:
            expand_grad[rows, pl.ds(D * (unit - EXPAND), D)] = total
        else:
            shrink_grad[pl.ds(32 * (unit - SQUARE) + rows.start, rows.size), :] = total

    scatter = Scatter(links, held.grads, held.from_first, held.from_second, held.from_z, result)
    made = {"count": 0}

    def produce(left, right, depth=2 * OWN):
        target = scatter.home(made["count"])
        made["count"] += 1

        @loop(4)
        def _(index):
            columns = tile(index, OWN)
            term = project(left().reshape(512, depth), right[:, columns])
            target[:, :, :, :, columns] = term.astype(BF).reshape(2, 2, 4, 32, OWN)

    def share(ref):
        slot = links.slot()
        links.send(slot, ref.at[mine], ref.at[mine], partner)
        return slot

    def shared(ref, slot):
        links.arrived(slot, ref.at[theirs])

    def gain(number):
        return held.gains[pl.ds(number, 1), :]

    have("branch", "active_t")

    def produce_shrink(part):
        produce(lambda: held.active_t[:, :, part], held.branch)

    def produce_expand(part):
        shared(held.up.at[part], up_slots[part])
        produce(lambda: held.second_t[...], held.up.at[part])

    produce_shrink(0)
    scatter.tick()
    slot_output = links.slot()
    moves.start(kept.final_low.at[block_rows(group)], output.at[group])
    links.send(slot_output, kept.final_low.at[block_rows(1 - group)], output.at[group], place.along_z(2))
    for part in (1, 2, 3):
        produce_shrink(part)
    scatter.tick()
    have("slopes")
    own_branch = held.branch.at[mine]
    up_slots = []
    for part in range(4):
        if part == 2:
            scatter.tick()
        up = held.up.at[part, mine]
        slopes = held.slopes.at[part]

        def bend(columns, value):
            up[:, columns] = (value * slopes[:, columns].astype(F32)).astype(BF)

        rows_back(own_branch, weight(SQUARE + part, 2 * part % 3), bend)
        up_slots.append(share(held.up.at[part]))
        if part < 3:
            fetch(EXPAND + part + 1, 2 * part % 3)

        def add(columns, value):
            if part == 0:
                held.second_sum[:, columns] = value
            else:
                held.second_sum[:, columns] += value

        rows_back(up, weight(EXPAND + part, (2 * part + 1) % 3), add)
        fetch((SQUARE + 2, SQUARE + 3, CROSS_OUT, CROSS_QUERY)[part], (2 * part + 1) % 3)
    fetch(CROSS_KEY, 0)
    scatter.tick()
    have("third_grad", "norm_sums", "gains", "normal_two", "inverse_two", "second_t")

    def spread(inverse, rows):
        return inverse[rows, pl.ds(0, 1)]

    @loop(OWN // STEP)
    def _(index):
        rows = tile(index, STEP)
        grad = held.second_sum[rows, :] + alpha_scale * held.third_grad[rows, :]
        pre = norm_rows_back(grad, held.normal_two[rows, :], spread(held.inverse_two, rows), gain(1), held.norm_sums, 1)
        held.second_sum[rows, :] = pre
        held.cross_branch[pl.ds(pl.multiple_of(OWN * core + STEP * index, STEP), STEP), :] = pre.astype(BF)

    slot_cross_branch = share(held.cross_branch)
    produce_expand(0)
    scatter.tick()

    def low(target):
        def store(columns, value):
            target[:, columns] = value.astype(BF)

        return store

    rows_back(held.cross_branch.at[mine], weight(CROSS_OUT, 2), low(held.attended_grad))
    fetch(CROSS_VALUE, 2)
    have("cross_queries", "cross_keys", "cross_values", "cross_bias", "cross_logs", "cross_t")
    attend_rows_back(
        held.cross_queries, held.cross_keys, held.cross_values, held.cross_bias, held.cross_logs, held.attended_grad,
        held.cross_query_grad.at[mine], held.cross_terms.at[0, core], held.cross_terms.at[1, core], CROSS_SEGMENTS, H // 2,
    )
    slot_cross_query = share(held.cross_query_grad)
    slot_cross_terms = links.slot()
    links.send(slot_cross_terms, held.cross_terms.at[:, core], held.cross_terms.at[:, core], partner)
    produce_expand(1)
    scatter.tick()

    def add_first(columns, value):
        held.third_grad[:, columns] = value

    rows_back(held.cross_query_grad.at[mine], weight(CROSS_QUERY, 1), add_first)
    fetch(OUT, 1)
    have("normal_one", "inverse_one", "first_t", "memory_t", "attended_t", "tokens_t")

    @loop(OWN // STEP)
    def _(index):
        rows = tile(index, STEP)
        grad = held.third_grad[rows, :] + alpha_scale * held.second_sum[rows, :]
        pre = norm_rows_back(grad, held.normal_one[rows, :], spread(held.inverse_one, rows), gain(0), held.norm_sums, 0)
        held.second_sum[rows, :] = pre
        held.self_branch[pl.ds(pl.multiple_of(OWN * core + STEP * index, STEP), STEP), :] = pre.astype(BF)

    slot_self_branch = share(held.self_branch)
    norm_steps = all_sum(links, held.norm_sums, norm_grads, held.work)
    next(norm_steps)
    produce_expand(2)
    scatter.tick()
    rows_back(held.self_branch.at[mine], weight(OUT, 1), low(held.attended_grad))
    fetch(QUERY, 1)
    have("queries", "keys", "values", "self_bias", "self_logs")
    terms = held.terms

    def attend_part(first, pairs):
        attend_rows_back(
            held.queries, held.keys, held.values, held.self_bias, held.self_logs, held.attended_grad,
            held.query_grad.at[mine], terms.at[0].reshape(SPAN, D), terms.at[1].reshape(SPAN, D), SELF_SEGMENTS, pairs, first,
        )

    attend_part(0, 2)
    produce_expand(3)
    scatter.tick()
    next(norm_steps)
    attend_part(2, 2)
    shared(held.cross_branch, slot_cross_branch)
    produce(lambda: held.cross_t[...], held.cross_branch)
    scatter.tick()
    next(norm_steps)
    attend_part(4, 2)
    shared(held.cross_query_grad, slot_cross_query)
    produce(lambda: held.first_t[...], held.cross_query_grad)
    scatter.tick()
    next(norm_steps)
    attend_part(6, 2)
    slot_query = share(held.query_grad)
    slot_terms = links.slot()
    links.send(slot_terms, terms.at[:, :, :, 1 - core], held.terms_core, partner)

    links.arrived(slot_cross_terms, held.cross_terms.at[:, 1 - core])
    for which in (0, 1):
        held.cross_sums[which] = (held.cross_terms[which, 0].astype(F32) + held.cross_terms[which, 1].astype(F32)).astype(BF)
    produce(lambda: held.memory_t[...], held.cross_sums.at[0], MEM)
    scatter.tick()
    next(norm_steps)

    links.arrived(slot_terms, held.terms_core)
    near = z % 2

    def join(place_index):
        for which in (0, 1):
            for high in (0, 1):
                value = terms[which, high, place_index, core].astype(F32) + held.terms_core[which, high, place_index].astype(F32)
                terms[which, high, place_index, core] = value.astype(BF)

    join(1 - near)
    slot_mate = links.slot()
    links.send(slot_mate, terms.at[:, :, 1 - near, core], held.terms_mate, place.mate())
    join(near)

    produce(lambda: held.memory_t[...], held.cross_sums.at[1], MEM)
    scatter.tick()

    cross_key, cross_value = weight(CROSS_KEY, 0), weight(CROSS_VALUE, 2)
    sums = held.cross_sums.reshape(2, 4, 2, 16, D)

    @loop(4)
    def _(index):
        columns = tile(index, OWN)
        term = project_back(sums[0, :, core].reshape(64, D), cross_key[columns, :])
        term = term + project_back(sums[1, :, core].reshape(64, D), cross_value[columns, :])
        held.memory_own[:, :, columns] = term.astype(BF).reshape(4, 16, OWN)

    fetch(KEY, 0)
    fetch(VALUE, 2)
    slot_memory = links.slot(4)
    for k in (1, 2, 3):
        links.send(slot_memory + z, held.memory_own.at[(z + k) % 4], held.memory_in.at[z], place.along_z(k))
    held.memory_in[z] = held.memory_own[z]

    shared(held.self_branch, slot_self_branch)
    produce(lambda: held.attended_t[...], held.self_branch)
    scatter.tick()
    shared(held.query_grad, slot_query)
    produce(lambda: held.tokens_t[...], held.query_grad)
    scatter.tick()

    def add_input(columns, value):
        held.third_grad[:, columns] = alpha_scale * held.second_sum[:, columns] + value

    rows_back(held.query_grad.at[mine], weight(QUERY, 1), add_input)
    links.arrived(slot_mate, held.terms_mate)
    for which, target in enumerate((held.key_grad, held.value_grad)):
        for high in (0, 1):
            value = terms[which, high, near, core].astype(F32) + held.terms_mate[which, high].astype(F32)
            target[pl.ds(pl.multiple_of(OWN * core + LEN * high, LEN), LEN), :] = value.astype(BF)
    slot_key, slot_value = share(held.key_grad), share(held.value_grad)
    shared(held.key_grad, slot_key)
    produce(lambda: held.tokens_t[...], held.key_grad)
    scatter.tick()
    shared(held.value_grad, slot_value)
    produce(lambda: held.tokens_t[...], held.value_grad)
    scatter.tick()

    def add_more(columns, value):
        held.third_grad[:, columns] += value

    rows_back(held.key_grad.at[mine], weight(KEY, 0), add_more)
    rows_back(held.value_grad.at[mine], weight(VALUE, 2), add_more)
    held.far_own[...] = held.third_grad[block_rows(1 - group), :].astype(BF)
    slot_far = links.slot()
    links.send(slot_far, held.far_own, held.far_in, place.along_z(2))
    input_grad[group] = held.third_grad[block_rows(group), :]
    scatter.tick()
    for k in (1, 2, 3):
        links.arrived(slot_memory + (z + k) % 4, held.memory_in.at[(z + k) % 4])
    for which in (0, 1):
        memory_grad[which] = held.memory_in[2 * which].astype(F32) + held.memory_in[2 * which + 1].astype(F32)
    links.arrived(slot_far, held.far_in)
    input_grad[1 - group] = held.far_in[...].astype(F32)
    scatter.tick()
    scatter.tick()
    links.arrived(slot_output, output.at[1 - group])
    moves.finish()
    links.finish()


def backward_call(square, shrink, saves, block_shape, memory_shape):
    results = [jax.ShapeDtypeStruct(block_shape, BF)]
    results += [jax.ShapeDtypeStruct(shape, F32) for shape in (block_shape, memory_shape)]
    results += [jax.ShapeDtypeStruct((32, D), F32)] * 8
    results += [jax.ShapeDtypeStruct(shape, F32) for shape in ((32, 4 * D), (LEN, D), (8, D))]
    saved = {**FORWARD_SAVES, **TURNED_SAVES}
    held = {name: saved[name] for name in saved if name != "final_low"}
    return pl.pallas_call(
        backward_kernel,
        in_specs=[IN_PLACE] * (2 + len(saved)),
        out_specs=[IN_PLACE] + [IN_VMEM] * (len(results) - 1),
        out_shape=results,
        scratch_shapes=[
            *vmem_of(held),
            *vmem_of(BACKWARD_SCRATCH),
            pltpu.SemaphoreType.DMA((BACKWARD_SENDS,)),
            pltpu.SemaphoreType.DMA((BACKWARD_SLOTS,)),
            pltpu.SemaphoreType.DMA((BACKWARD_MOVES,)),
        ],
        compiler_params=pltpu.CompilerParams(collective_id=1, has_side_effects=True, vmem_limit_bytes=63 << 20),
    )(square, shrink, *(saves[name] for name in saved))


def hand_over_kernel(*refs):
    count = len(refs) // 3
    sem = refs[-1]
    loads = [pltpu.make_async_copy(refs[n], refs[2 * count + n], sem.at[0, n]) for n in range(count)]
    stores = [pltpu.make_async_copy(refs[2 * count + n], refs[count + n], sem.at[1, n]) for n in range(count)]
    for load in loads:
        load.start()
    for load, store in zip(loads, stores):
        load.wait()
        store.start()
    for store in stores:
        store.wait()


def hand_over(values):
    return pl.pallas_call(
        hand_over_kernel,
        in_specs=[IN_PLACE] * len(values),
        out_specs=[IN_PLACE] * len(values),
        out_shape=[jax.ShapeDtypeStruct(value.shape, value.dtype) for value in values],
        scratch_shapes=[
            *(pltpu.VMEM(value.shape, value.dtype) for value in values),
            pltpu.SemaphoreType.DMA((2, len(values))),
        ],
        compiler_params=pltpu.CompilerParams(vmem_limit_bytes=VMEM_BYTES),
    )(*values)


def fast_shards(
    tokens, memory, lengths, memory_segments, out_grad,
    self_query, self_key, self_value, self_out,
    cross_query, cross_key, cross_value, cross_out,
    expand_weight, shrink_weight, norm_gains, norm_biases,
):
    me = lax.axis_index("dp") * lax.axis_size("seq") + lax.axis_index("seq")
    norms = jnp.concatenate([norm_gains, norm_biases, jnp.zeros((2, 32), BF)]).astype(F32)
    norms = lax.dynamic_update_slice(jnp.zeros((8, D), F32), norms, (0, 32 * me))
    weights = (self_key, self_value, self_query, self_out, cross_query, cross_key, cross_value, cross_out)
    square, shrink, saves = forward_call(
        lengths, memory_segments, norms, tokens, memory, out_grad, (*weights, expand_weight, shrink_weight)
    )
    *values, norm_grads = backward_call(square, shrink, saves, tokens.shape, memory.shape)
    output, input_grad, memory_grad, *units, expand_grad, shrink_grad = hand_over(values)
    norm_grads = lax.dynamic_slice(norm_grads, (0, 32 * me), (8, 32))
    return (
        output,
        input_grad,
        memory_grad,
        *(units[unit] for unit in (QUERY, KEY, VALUE, OUT, CROSS_QUERY, CROSS_KEY, CROSS_VALUE, CROSS_OUT)),
        expand_grad,
        shrink_grad,
        norm_grads[:3],
        norm_grads[3:6],
    )


def solution(mesh):
    quick = dict(mesh.shape) == {"dp": 4, "seq": 8}
    return jax.shard_map(
        fast_shards if quick else shards,
        mesh=mesh,
        in_specs=(
            P("dp", "seq", None),
            P("dp", "seq", None),
            P("dp", None),
            P("dp", None),
            P("dp", "seq", None),
            P(("dp", "seq"), None),
            P(("dp", "seq"), None),
            P(("dp", "seq"), None),
            P(("dp", "seq"), None),
            P(("dp", "seq"), None),
            P(("dp", "seq"), None),
            P(("dp", "seq"), None),
            P(("dp", "seq"), None),
            P(("dp", "seq"), None),
            P(("dp", "seq"), None),
            P(None, ("dp", "seq")),
            P(None, ("dp", "seq")),
        ),
        out_specs=(
            P("dp", "seq", None),
            P("dp", "seq", None),
            P("dp", "seq", None),
            P(("dp", "seq"), None),
            P(("dp", "seq"), None),
            P(("dp", "seq"), None),
            P(("dp", "seq"), None),
            P(("dp", "seq"), None),
            P(("dp", "seq"), None),
            P(("dp", "seq"), None),
            P(("dp", "seq"), None),
            P(("dp", "seq"), None),
            P(("dp", "seq"), None),
            P(None, ("dp", "seq")),
            P(None, ("dp", "seq")),
        ),
        check_vma=False,
    )
```

```python
import jax
import jax.numpy as jnp
from jax import lax
from jax.experimental import pallas as pl
from jax.experimental.pallas import tpu as pltpu
from jax.sharding import PartitionSpec as P

H = 16
HD = 64
MB = 2


alpha_scale = 300.0**0.25
norm_eps = 1e-05
masked_score = -1e30


def layer_norm(value, gain, bias):
    average = jnp.mean(value, axis=-1, keepdims=True)
    centred = value - average
    spread = jnp.mean(centred * centred, axis=-1, keepdims=True)
    return centred * lax.rsqrt(spread + norm_eps) * gain + bias


def project(left, right):
    return jnp.dot(left, right, preferred_element_type=jnp.float32)


def project_back(left, right):
    return lax.dot_general(
        left, right, (((1,), (1,)), ((), ())), preferred_element_type=jnp.float32
    )


def weight_term(left, right):
    return lax.dot_general(
        left, right, (((0,), (0,)), ((), ())), preferred_element_type=jnp.float32
    )


def split_heads(value):
    return value.reshape(value.shape[0], value.shape[1], H, HD)


def sentence_ids(sent_ends, places):
    return jnp.sum((places[None, :, None] >= sent_ends[:, None, :]).astype(jnp.int32), axis=2)


def masked_scores(queries, key_heads, allowed, scaling):
    raw_scores = (
        jnp.einsum("gqhd,gkhd->ghqk", queries, key_heads, preferred_element_type=jnp.float32)
        * scaling
    )
    return jnp.where(allowed[:, None], raw_scores, masked_score)


def attend_forward(queries, key_heads, value_heads, allowed, scaling):
    scores = masked_scores(queries, key_heads, allowed, scaling)
    row_max = jnp.max(scores, axis=3, keepdims=True)
    powers = jnp.exp(scores - row_max)
    row_total = jnp.sum(powers, axis=3, keepdims=True)
    prob_low = (powers / row_total).astype(jnp.bfloat16)
    attended = jnp.einsum(
        "ghqk,gkhd->gqhd", prob_low, value_heads, preferred_element_type=jnp.float32
    )
    return (attended, row_max + jnp.log(row_total))


def attend_backward(queries, key_heads, value_heads, allowed, scaling, log_total, attended_grad):
    scores = masked_scores(queries, key_heads, allowed, scaling)
    probability = jnp.exp(scores - log_total)
    prob_grad = jnp.einsum(
        "gqhd,gkhd->ghqk", attended_grad, value_heads, preferred_element_type=jnp.float32
    )
    score_grad = probability * (prob_grad - jnp.sum(prob_grad * probability, axis=3, keepdims=True))
    score_low = score_grad.astype(jnp.bfloat16)
    query_grad = (
        jnp.einsum("ghqk,gkhd->gqhd", score_low, key_heads, preferred_element_type=jnp.float32)
        * scaling
    )
    return (query_grad, score_low, probability.astype(jnp.bfloat16))


def micro_batch(gathered, tokens, memory, lengths, memory_segments, out_grad):
    (
        self_query,
        self_key,
        self_value,
        self_out,
        cross_query,
        cross_key,
        cross_value,
        cross_out,
        expand_weight,
        shrink_weight,
        norm_gains,
        norm_biases,
    ) = gathered
    gains = norm_gains.astype(jnp.float32)
    biases = norm_biases.astype(jnp.float32)
    group_size, local_len, features = tokens.shape
    seq_count = lax.axis_size("seq")
    seq_index = lax.axis_index("seq")
    full_len = local_len * seq_count
    row_count = group_size * local_len
    scaling = HD ** (-0.5)
    sent_ends = jnp.cumsum(lengths, axis=1)[:, :-1]
    query_places = seq_index * local_len + jnp.arange(local_len, dtype=jnp.int32)
    key_places = jnp.arange(full_len, dtype=jnp.int32)
    query_ids = sentence_ids(sent_ends, query_places)
    key_ids = sentence_ids(sent_ends, key_places)
    self_allowed = (query_ids[:, :, None] == key_ids[:, None, :]) & (
        key_places[None, None, :] <= query_places[None, :, None]
    )
    cross_allowed = query_ids[:, :, None] == memory_segments[:, None, :]
    token_rows = tokens.reshape(row_count, features)
    queries = split_heads(
        project(token_rows, self_query)
        .astype(jnp.bfloat16)
        .reshape(group_size, local_len, features)
    )
    own_keys = (
        project(token_rows, self_key).astype(jnp.bfloat16).reshape(group_size, local_len, features)
    )
    own_values = (
        project(token_rows, self_value)
        .astype(jnp.bfloat16)
        .reshape(group_size, local_len, features)
    )
    all_keys, all_values = (
        lax.all_gather(own_keys, "seq", axis=1, tiled=True),
        lax.all_gather(own_values, "seq", axis=1, tiled=True),
    )
    key_heads = split_heads(all_keys)
    value_heads = split_heads(all_values)
    attended, self_log = attend_forward(queries, key_heads, value_heads, self_allowed, scaling)
    attended = attended.reshape(row_count, features).astype(jnp.bfloat16)
    first_pre = alpha_scale * token_rows.astype(jnp.float32) + project(attended, self_out)
    first, first_pull = jax.vjp(layer_norm, first_pre, gains[0], biases[0])
    first_low = first.astype(jnp.bfloat16)
    cross_queries = split_heads(
        project(first_low, cross_query)
        .astype(jnp.bfloat16)
        .reshape(group_size, local_len, features)
    )
    own_memory = memory.reshape(-1, features)
    memory_all = lax.all_gather(memory, "seq", axis=1, tiled=True)
    memory_rows = memory_all.reshape(-1, features)
    cross_keys = (
        project(memory_rows, cross_key).astype(jnp.bfloat16).reshape(group_size, -1, features)
    )
    cross_values = (
        project(memory_rows, cross_value).astype(jnp.bfloat16).reshape(group_size, -1, features)
    )
    cross_key_heads = split_heads(cross_keys)
    cross_value_heads = split_heads(cross_values)
    cross_attended, cross_log = attend_forward(
        cross_queries, cross_key_heads, cross_value_heads, cross_allowed, scaling
    )
    cross_attended = cross_attended.reshape(row_count, features).astype(jnp.bfloat16)
    second_pre = alpha_scale * first + project(cross_attended, cross_out)
    second, second_pull = jax.vjp(layer_norm, second_pre, gains[1], biases[1])
    second_low = second.astype(jnp.bfloat16)
    upward = project(second_low, expand_weight)
    active, gelu_pull = jax.vjp(jax.nn.gelu, upward)
    active_low = active.astype(jnp.bfloat16)
    third_pre = alpha_scale * second + project(active_low, shrink_weight)
    final, third_pull = jax.vjp(layer_norm, third_pre, gains[2], biases[2])
    third_grad, gain_third, bias_third = third_pull(
        out_grad.reshape(row_count, features).astype(jnp.float32)
    )
    branch_grad = third_grad.astype(jnp.bfloat16)
    shrink_grad = weight_term(active_low, branch_grad)
    (up_grad,) = gelu_pull(project_back(branch_grad, shrink_weight))
    up_low = up_grad.astype(jnp.bfloat16)
    expand_grad = weight_term(second_low, up_low)
    second_grad = alpha_scale * third_grad + project_back(up_low, expand_weight)
    second_pre_grad, gain_second, bias_second = second_pull(second_grad)
    cross_branch = second_pre_grad.astype(jnp.bfloat16)
    cross_out_grad = weight_term(cross_attended, cross_branch)
    cross_attended_grad = split_heads(
        project_back(cross_branch, cross_out)
        .astype(jnp.bfloat16)
        .reshape(group_size, local_len, features)
    )
    cross_q_grad, cross_scores, cross_probs = attend_backward(
        cross_queries,
        cross_key_heads,
        cross_value_heads,
        cross_allowed,
        scaling,
        cross_log,
        cross_attended_grad,
    )
    cross_q_low = cross_q_grad.reshape(row_count, features).astype(jnp.bfloat16)
    cross_query_grad = weight_term(first_low, cross_q_low)
    key_term = (
        jnp.einsum(
            "ghqk,gqhd->gkhd", cross_scores, cross_queries, preferred_element_type=jnp.float32
        )
        * scaling
    ).reshape(group_size, -1, features)
    value_term = jnp.einsum(
        "ghqk,gqhd->gkhd", cross_probs, cross_attended_grad, preferred_element_type=jnp.float32
    ).reshape(group_size, -1, features)
    key_summed, value_summed = (
        lax.psum_scatter(
            key_term.astype(jnp.bfloat16), "seq", scatter_dimension=1, tiled=True
        ).astype(jnp.float32),
        lax.psum_scatter(
            value_term.astype(jnp.bfloat16), "seq", scatter_dimension=1, tiled=True
        ).astype(jnp.float32),
    )
    key_low = key_summed.reshape(-1, features).astype(jnp.bfloat16)
    value_low = value_summed.reshape(-1, features).astype(jnp.bfloat16)
    cross_key_grad = weight_term(own_memory, key_low)
    cross_value_grad = weight_term(own_memory, value_low)
    memory_grad = (project_back(key_low, cross_key) + project_back(value_low, cross_value)).reshape(
        memory.shape
    )
    first_grad = alpha_scale * second_pre_grad + project_back(cross_q_low, cross_query)
    first_pre_grad, gain_first, bias_first = first_pull(first_grad)
    self_branch = first_pre_grad.astype(jnp.bfloat16)
    self_out_grad = weight_term(attended, self_branch)
    attended_grad = split_heads(
        project_back(self_branch, self_out)
        .astype(jnp.bfloat16)
        .reshape(group_size, local_len, features)
    )
    self_q_grad, self_scores, self_probs = attend_backward(
        queries, key_heads, value_heads, self_allowed, scaling, self_log, attended_grad
    )
    count = local_len * lax.axis_size("seq")
    key_part = (
        jnp.einsum("ghqk,gqhd->kghd", self_scores, queries, preferred_element_type=jnp.float32)
        * scaling
    )
    value_part = jnp.einsum(
        "ghqk,gqhd->kghd", self_probs, attended_grad, preferred_element_type=jnp.float32
    )
    pair_summed = lax.psum_scatter(
        jnp.concatenate(
            [
                key_part.reshape(count, group_size, features),
                value_part.reshape(count, group_size, features),
            ],
            axis=2,
        ).astype(jnp.bfloat16),
        "seq",
        scatter_dimension=0,
        tiled=True,
    ).astype(jnp.float32)
    key_grad = (
        pair_summed[:, :, :features]
        .astype(jnp.bfloat16)
        .transpose(1, 0, 2)
        .reshape(row_count, features)
    )
    value_grad = (
        pair_summed[:, :, features:]
        .astype(jnp.bfloat16)
        .transpose(1, 0, 2)
        .reshape(row_count, features)
    )
    query_low = self_q_grad.reshape(row_count, features).astype(jnp.bfloat16)
    self_query_grad = weight_term(token_rows, query_low)
    self_key_grad = weight_term(token_rows, key_grad)
    self_value_grad = weight_term(token_rows, value_grad)
    input_grad = (
        alpha_scale * first_pre_grad
        + project_back(query_low, self_query)
        + project_back(key_grad, self_key)
        + project_back(value_grad, self_value)
    )
    gains_grad = jnp.stack([gain_first, gain_second, gain_third])
    biases_grad = jnp.stack([bias_first, bias_second, bias_third])
    gradients = (
        self_query_grad,
        self_key_grad,
        self_value_grad,
        self_out_grad,
        cross_query_grad,
        cross_key_grad,
        cross_value_grad,
        cross_out_grad,
        expand_grad,
        shrink_grad,
        gains_grad,
        biases_grad,
    )
    result = final.astype(jnp.bfloat16).reshape(group_size, local_len, features)
    return (result, input_grad.reshape(group_size, local_len, features), memory_grad, gradients)


def shards(
    tokens,
    memory,
    lengths,
    memory_segments,
    out_grad,
    self_query,
    self_key,
    self_value,
    self_out,
    cross_query,
    cross_key,
    cross_value,
    cross_out,
    expand_weight,
    shrink_weight,
    norm_gains,
    norm_biases,
):
    group_size = tokens.shape[0] // MB
    outputs = []
    input_grads = []
    memory_grads = []
    totals = None
    for batch_index in range(MB):
        gathered = (
            lax.all_gather(self_query, ("dp", "seq"), axis=0, tiled=True),
            lax.all_gather(self_key, ("dp", "seq"), axis=0, tiled=True),
            lax.all_gather(self_value, ("dp", "seq"), axis=0, tiled=True),
            lax.all_gather(self_out, ("dp", "seq"), axis=0, tiled=True),
            lax.all_gather(cross_query, ("dp", "seq"), axis=0, tiled=True),
            lax.all_gather(cross_key, ("dp", "seq"), axis=0, tiled=True),
            lax.all_gather(cross_value, ("dp", "seq"), axis=0, tiled=True),
            lax.all_gather(cross_out, ("dp", "seq"), axis=0, tiled=True),
            lax.all_gather(expand_weight, ("dp", "seq"), axis=0, tiled=True),
            lax.all_gather(shrink_weight, ("dp", "seq"), axis=0, tiled=True),
            lax.all_gather(norm_gains, ("dp", "seq"), axis=1, tiled=True),
            lax.all_gather(norm_biases, ("dp", "seq"), axis=1, tiled=True),
        )
        start = batch_index * group_size
        stop = start + group_size
        result, input_grad, memory_grad, gradients = micro_batch(
            gathered,
            tokens[start:stop],
            memory[start:stop],
            lengths[start:stop],
            memory_segments[start:stop],
            out_grad[start:stop],
        )
        outputs.append(result)
        input_grads.append(input_grad)
        memory_grads.append(memory_grad)
        if totals is None:
            totals = gradients
        else:
            totals = tuple((running + gradient for running, gradient in zip(totals, gradients)))
    summed = (
        lax.psum_scatter(totals[0], ("dp", "seq"), scatter_dimension=0, tiled=True),
        lax.psum_scatter(totals[1], ("dp", "seq"), scatter_dimension=0, tiled=True),
        lax.psum_scatter(totals[2], ("dp", "seq"), scatter_dimension=0, tiled=True),
        lax.psum_scatter(totals[3], ("dp", "seq"), scatter_dimension=0, tiled=True),
        lax.psum_scatter(totals[4], ("dp", "seq"), scatter_dimension=0, tiled=True),
        lax.psum_scatter(totals[5], ("dp", "seq"), scatter_dimension=0, tiled=True),
        lax.psum_scatter(totals[6], ("dp", "seq"), scatter_dimension=0, tiled=True),
        lax.psum_scatter(totals[7], ("dp", "seq"), scatter_dimension=0, tiled=True),
        lax.psum_scatter(totals[8], ("dp", "seq"), scatter_dimension=0, tiled=True),
        lax.psum_scatter(totals[9], ("dp", "seq"), scatter_dimension=0, tiled=True),
        lax.psum_scatter(totals[10], ("dp", "seq"), scatter_dimension=1, tiled=True),
        lax.psum_scatter(totals[11], ("dp", "seq"), scatter_dimension=1, tiled=True),
    )
    return (
        jnp.concatenate(outputs, 0),
        jnp.concatenate(input_grads, 0),
        jnp.concatenate(memory_grads, 0),
        summed[0],
        summed[1],
        summed[2],
        summed[3],
        summed[4],
        summed[5],
        summed[6],
        summed[7],
        summed[8],
        summed[9],
        summed[10],
        summed[11],
    )


MESH = pl.DeviceIdType.MESH
BF = jnp.bfloat16
F32 = jnp.float32
ALL = slice(None)
D = 1024
LEN = 128
OWN = 2 * LEN
SPAN = 8 * LEN
MEM = 128
KEY, VALUE, QUERY, OUT, CROSS_QUERY, CROSS_KEY, CROSS_VALUE, CROSS_OUT = range(8)
EXPAND = 8
SQUARE = 12
UNITS = 16
GRID = (2, 2, 4, 2)
SQUARE_SHAPE = (SQUARE, *GRID, 32, D)
SHRINK_SHAPE = (UNITS - SQUARE, *GRID, LEN, OWN)
VMEM_BYTES = 60 << 20
GELU_SLOPE = (2.0 / 3.141592653589793) ** 0.5
GELU_CUBE = 0.044715


class Place:
    def __init__(self):
        dp, seq = lax.axis_index("dp"), lax.axis_index("seq")
        self.x, self.y, self.core, self.z, self.seq = dp % 2, dp // 2, seq % 2, seq // 2, seq
        self.group = self.z // 2
        self.low = seq % 4

    def at(self, y=None, x=None, z=None, core=None):
        y = self.y if y is None else y
        x = self.x if x is None else x
        z = self.z if z is None else z
        core = self.core if core is None else core
        return (y * 2 + x, z * 2 + core)

    def across(self, axis):
        if axis == "x":
            return self.at(x=1 - self.x)
        if axis == "y":
            return self.at(y=1 - self.y)
        return self.at(core=1 - self.core)

    def along_z(self, step):
        return self.at(z=(self.z + step) % 4)

    def mate(self):
        return self.at(z=self.z + 1 - 2 * (self.z % 2))

    def greet(self):
        barrier = pltpu.get_barrier_semaphore()
        peers = [self.across(axis) for axis in ("x", "y", "core")]
        peers += [self.along_z(step) for step in (1, 2, 3)]
        for peer in peers:
            pl.semaphore_signal(barrier, inc=1, device_id=peer, device_id_type=MESH)
        pl.semaphore_wait(barrier, len(peers))


class Links:
    def __init__(self, place, send_sem, recv_sem):
        self.place, self.send_sem, self.recv_sem = place, send_sem, recv_sem
        self.sends, self.slots = 0, 0
        self.open = {}

    def slot(self, count=1):
        first = self.slots
        self.slots += count
        assert self.slots <= self.recv_sem.shape[0]
        return first

    def send(self, slot, source, target, device):
        assert self.sends < self.send_sem.shape[0]
        step = pltpu.make_async_remote_copy(
            src_ref=source,
            dst_ref=target,
            send_sem=self.send_sem.at[self.sends],
            recv_sem=self.recv_sem.at[slot],
            device_id=device,
            device_id_type=MESH,
        )
        step.start()
        self.sends += 1
        self.open[id(step)] = step
        return step

    def arrived(self, slot, target):
        pltpu.make_async_remote_copy(
            src_ref=target,
            dst_ref=target,
            send_sem=self.send_sem.at[0],
            recv_sem=self.recv_sem.at[slot],
            device_id=self.place.across("core"),
            device_id_type=MESH,
        ).wait_recv()

    def sent(self, step):
        self.open.pop(id(step)).wait_send()

    def finish(self):
        for step in self.open.values():
            step.wait_send()
        self.open = {}


class Moves:
    def __init__(self, sem):
        self.sem, self.count, self.open = sem, 0, {}

    def start(self, source, target):
        assert self.count < self.sem.shape[0]
        step = pltpu.make_async_copy(source, target, self.sem.at[self.count])
        step.start()
        self.count += 1
        self.open[id(step)] = step
        return step

    def wait(self, step):
        self.open.pop(id(step)).wait()

    def finish(self):
        for step in self.open.values():
            step.wait()
        self.open = {}


def all_sum(links, part, total, work):
    place = links.place
    work[0] = part[...]
    for number, axis in enumerate(("core", "y", "x")):
        slot = links.slot()
        step = links.send(slot, work.at[0], work.at[1 + number], place.across(axis))
        yield
        links.arrived(slot, work.at[1 + number])
        links.sent(step)
        work[0] = work[0] + work[1 + number]
    slot = links.slot(4)
    for k in (1, 2, 3):
        links.send(slot + place.z, work.at[0], work.at[4 + place.z], place.along_z(k))
    yield
    result = work[0]
    for k in (1, 2, 3):
        source = (place.z + k) % 4
        links.arrived(slot + source, work.at[4 + source])
        result = result + work[4 + source]
    total[...] = result
    yield


def loop(count):
    return pl.loop(0, count)


def tile(index, size):
    return pl.ds(pl.multiple_of(index * size, size), size)


def rows_times(left, right, store, rows=OWN, width=256):
    for first in range(0, left.shape[0], rows):

        @loop(D // width)
        def _(index):
            columns = tile(index, width)
            store(pl.ds(first, rows), columns, jnp.dot(left[pl.ds(first, rows), :], right[:, columns], preferred_element_type=F32))


def rows_back(left, right, store, width=256):
    @loop(D // width)
    def _(index):
        columns = tile(index, width)
        store(columns, project_back(left[...], right[columns, :]))


def put(target, dtype=BF):
    def store(rows, columns, value):
        target[rows, columns] = value.astype(dtype)

    return store


def half_masks():
    lane = lax.broadcasted_iota(jnp.int32, (1, LEN), 1)
    return [(lane < HD).astype(F32), (lane >= HD).astype(F32)]


def attend_rows(queries, keys, values, bias, logs, out, segments, pairs=H // 2, first_pair=0):
    masks = half_masks()

    @loop(pairs)
    def _(step):
        pair = step + first_pair
        columns = tile(pair, LEN)
        for first, rows, count in segments:
            own = pl.ds(first, rows)
            key, value = keys[pl.ds(0, count), columns], values[pl.ds(0, count), columns]
            query = queries[own, columns]
            lane = lax.broadcasted_iota(jnp.int32, (rows, LEN), 1)
            parts = []
            for half in (0, 1):
                scores = project_back(query * (masks[half] * HD**-0.5).astype(BF), key) + bias[own, pl.ds(0, count)]
                top = jnp.max(scores, axis=1, keepdims=True)
                powers = jnp.exp(scores - top)
                total = jnp.sum(powers, axis=1, keepdims=True)
                parts.append(project((powers * (1.0 / total)).astype(BF), value))
                logs[own, :] = jnp.where(lane == 2 * pair + half, top + jnp.log(total), logs[own, :])
            out[own, columns] = jnp.where(lane < HD, parts[0], parts[1]).astype(BF)


def attend_rows_back(queries, keys, values, bias, logs, grads, query_grads, key_grads, value_grads, segments, pairs, first_pair=0):
    masks = half_masks()

    @loop(pairs)
    def _(step):
        pair = step + first_pair
        columns = tile(pair, LEN)
        for number, (first, rows, count) in enumerate(segments):
            own, met = pl.ds(first, rows), pl.ds(0, count)
            key, value = keys[met, columns], values[met, columns]
            lane = lax.broadcasted_iota(jnp.int32, (rows, LEN), 1)
            halves, score_lows, prob_lows, query_parts, grad_parts = [], [], [], [], []
            for half in (0, 1):
                query = queries[own, columns] * (masks[half] * HD**-0.5).astype(BF)
                grad = grads[own, columns] * masks[half].astype(BF)
                log_total = jnp.sum(jnp.where(lane == 2 * pair + half, logs[own, :], 0.0), axis=1, keepdims=True)
                probs = jnp.exp(project_back(query, key) + bias[own, met] - log_total)
                prob_grad = project_back(grad, value)
                score_grad = probs * (prob_grad - jnp.sum(prob_grad * probs, axis=1, keepdims=True))
                score_low = score_grad.astype(BF)
                halves.append(project(score_low, key) * HD**-0.5)
                score_lows.append(score_low)
                prob_lows.append(probs.astype(BF))
                query_parts.append(query)
                grad_parts.append(grad)
            query_grads[own, columns] = jnp.where(lane < HD, halves[0], halves[1]).astype(BF)
            key_term = weight_term(jnp.concatenate(score_lows), jnp.concatenate(query_parts))
            value_term = weight_term(jnp.concatenate(prob_lows), jnp.concatenate(grad_parts))
            if number == 0:
                key_grads[met, columns] = key_term.astype(BF)
                value_grads[met, columns] = value_term.astype(BF)
            else:
                key_grads[met, columns] = (key_grads[met, columns].astype(F32) + key_term).astype(BF)
                value_grads[met, columns] = (value_grads[met, columns].astype(F32) + value_term).astype(BF)


SELF_SEGMENTS = ((LEN, LEN, SPAN), (0, LEN, SPAN // 2))
CROSS_SEGMENTS = ((0, OWN, MEM),)
STEP = 32


def norm_rows(read, normal, inverse, emit):
    @loop(OWN // STEP)
    def _(index):
        rows = tile(index, STEP)
        value = read(rows)
        centred = value - jnp.mean(value, axis=1, keepdims=True)
        scale = lax.rsqrt(jnp.mean(centred * centred, axis=1, keepdims=True) + norm_eps)
        result = centred * scale
        if normal is not None:
            normal[rows, :] = result
            inverse[rows, :] = jnp.broadcast_to(scale, (STEP, LEN))
        emit(rows, result, scale)


def norm_rows_back(grad, normal, scale, gain, sums, number):
    sums[pl.ds(number, 1), :] += jnp.sum(grad * normal, axis=0, keepdims=True)
    sums[pl.ds(3 + number, 1), :] += jnp.sum(grad, axis=0, keepdims=True)
    scaled = grad * gain
    return scale * (
        scaled
        - jnp.mean(scaled, axis=1, keepdims=True)
        - normal * jnp.mean(scaled * normal, axis=1, keepdims=True)
    )


class Gather:
    WIDE = ()
    EARLY = 3
    ROUTES = {False: ("zxy", "zyx"), True: ("xzy", "yzx")}
    TIMES = {False: (-3, 0, 1, 2, 3), True: (-20, -3, 1, 2, 3)}
    SLOTS = 10

    def __init__(self, links, moves, own, square, shrink):
        self.links, self.moves, self.own, self.square, self.shrink = links, moves, own, square, shrink
        self.first_slot = links.slot(UNITS * 2 * self.SLOTS)
        self.local = {}
        for unit in range(UNITS):
            target = self.block(unit, links.place.y, links.place.x, links.place.z, links.place.core)
            self.local[unit] = moves.start(own(unit), target)
        self.now = -self.EARLY
        self.steps = {}
        for number, unit in enumerate(range(UNITS)):
            wide = number in self.WIDE
            for half in (0, 1):
                for phase, time in enumerate(self.TIMES[wide]):
                    step = (phase, number, unit, half, self.ROUTES[wide][half])
                    self.steps.setdefault(max(number + time, self.now), []).append(step)

    def block(self, unit, *index):
        if unit < SQUARE:
            return self.square.at[(unit,) + index]
        return self.shrink.at[(unit - SQUARE,) + index]

    def tick(self):
        for phase, _, unit, half, route in sorted(self.steps.pop(self.now, ())):
            self.move(phase, unit, half, route)
        self.now += 1

    def move(self, phase, unit, half, route):
        links, place = self.links, self.links.place
        here = {"y": place.y, "x": place.x, "z": place.z}
        slot = self.first_slot + (2 * unit + half) * self.SLOTS
        depth = 16 if unit < SQUARE else 64
        rows = pl.ds(depth * half, depth)
        turn = route.index("z")

        def part(where, core):
            return self.block(unit, where["y"], where["x"], where["z"], core, rows)

        def reached(count):
            return {**here, **{axis: ALL for axis in route[:count]}}

        def incoming(count):
            axis = route[count]
            if axis == "z":
                return reached(count + 1)
            return {**reached(count), axis: 1 - here[axis]}

        if phase == 1 and unit in self.local:
            self.moves.wait(self.local.pop(unit))
        if 1 <= phase <= 3:
            if phase - 1 == turn:
                for k in (1, 2, 3):
                    source = (place.z + k) % 4
                    links.arrived(slot + source, part({**reached(phase - 1), "z": source}, place.core))
            else:
                links.arrived(slot + 3 + phase, part(incoming(phase - 1), place.core))
        if phase < 3:
            source = self.own(unit).at[rows] if phase == 0 else part(reached(phase), place.core)
            target = part(reached(phase), place.core)
            if phase == turn:
                for k in (1, 2, 3):
                    links.send(slot + place.z, source, target, place.along_z(k))
            else:
                links.send(slot + 4 + phase, source, target, place.across(route[phase]))
        if 1 <= phase <= 3 and phase > turn:
            fresh = part(incoming(phase - 1), place.core)
            links.send(slot + 6 + phase, fresh, fresh, place.across("core"))
        if phase == 4:
            for number in range(turn, 3):
                links.arrived(slot + 7 + number, part(incoming(number), 1 - place.core))


def core_rows(core, count=OWN):
    return pl.ds(pl.multiple_of(core * count, count), count)


def block_rows(block):
    return pl.ds(pl.multiple_of(block * LEN, LEN), LEN)


FORWARD_SAVES = {
    "queries": ((OWN, D), BF),
    "keys": ((SPAN, D), BF),
    "values": ((SPAN, D), BF),
    "self_bias": ((OWN, SPAN), F32),
    "self_logs": ((OWN, LEN), F32),
    "normal_one": ((OWN, D), F32),
    "inverse_one": ((OWN, LEN), F32),
    "cross_queries": ((OWN, D), BF),
    "cross_keys": ((MEM, D), BF),
    "cross_values": ((MEM, D), BF),
    "cross_bias": ((OWN, MEM), F32),
    "cross_logs": ((OWN, LEN), F32),
    "normal_two": ((OWN, D), F32),
    "inverse_two": ((OWN, LEN), F32),
    "slopes": ((4, OWN, D), BF),
    "third_grad": ((OWN, D), F32),
    "norm_sums": ((8, D), F32),
    "gains": ((8, D), F32),
    "final_low": ((OWN, D), BF),
}
TURNED_SAVES = {
    "tokens_t": ((16, 32, 2 * OWN), BF),
    "attended_t": ((16, 32, 2 * OWN), BF),
    "first_t": ((16, 32, 2 * OWN), BF),
    "cross_t": ((16, 32, 2 * OWN), BF),
    "second_t": ((16, 32, 2 * OWN), BF),
    "active_t": ((4, 4, 4, 32, 2 * OWN), BF),
    "memory_t": ((16, 32, MEM), BF),
    "branch": ((2 * OWN, D), BF),
}
FORWARD_SCRATCH = {
    "stream": ((SPAN, D), BF),
    "mine": ((OWN, D), BF),
    "context": ((4, 2, 16, D), BF),
    "attended": ((OWN, D), BF),
    "first_low": ((OWN, D), BF),
    "cross_attended": ((OWN, D), BF),
    "second_low": ((OWN, D), BF),
    "active": ((4, OWN, D), BF),
    "sums": ((OWN, D), F32),
    "cotangent": ((OWN, D), BF),
    "branch_own": ((OWN, D), BF),
    "weights": ((4, D, D), BF),
    "shrink_in": ((2, 4, D, OWN), BF),
    "turned": ((3, 16, 2, 32, OWN), BF),
    "turned_active": ((2, 4, 2, 4, 32, OWN), BF),
    "turned_memory": ((16, 2, 32, MEM), BF),
    "work": ((8, 8, D), F32),
}
FORWARD_SENDS, FORWARD_SLOTS, FORWARD_MOVES = 320, 384, 96


class Refs:
    def __init__(self, names, refs):
        for name, ref in zip(names, refs):
            setattr(self, name, ref)


def forward_kernel(lengths, segments, norms, tokens, memory, out_grad, *refs):
    squares, expand_own, shrink_own = refs[:8], refs[8], refs[9]
    square, shrink = refs[10:12]
    rest = refs[12:]
    kept = Refs(FORWARD_SAVES, rest[: len(FORWARD_SAVES)])
    rest = rest[len(FORWARD_SAVES) :]
    turned = Refs(TURNED_SAVES, rest[: len(TURNED_SAVES)])
    rest = rest[len(TURNED_SAVES) :]
    held = Refs(FORWARD_SAVES, rest[: len(FORWARD_SAVES)])
    rest = rest[len(FORWARD_SAVES) :]
    held.__dict__.update(Refs(FORWARD_SCRATCH, rest[: len(FORWARD_SCRATCH)]).__dict__)
    send_sem, recv_sem, move_sem = rest[len(FORWARD_SCRATCH) :]

    place = Place()
    links, moves = Links(place, send_sem, recv_sem), Moves(move_sem)
    y, x, z, core, group, low, seq = place.y, place.x, place.z, place.core, place.group, place.low, place.seq
    partner = place.across("core")
    opposite = place.along_z(2)
    mate = place.mate()
    place.greet()

    def own(unit):
        if unit < EXPAND:
            return squares[unit]
        if unit < SQUARE:
            return expand_own.at[:, pl.ds(D * (unit - EXPAND), D)]
        return shrink_own.at[:, pl.ds(OWN * (unit - SQUARE), OWN)]

    stream = held.stream
    far, mate_seq = (seq + 4) % 8, (seq + 2) % 4 + 4 * group
    other_seq = 2 * z + 1 - core
    other_mate = (other_seq + 2) % 4 + 4 * group
    slot_far, slot_mate, slot_mate_far, slot_core = links.slot(), links.slot(), links.slot(), links.slot(4)
    home = moves.start(tokens.at[group], stream.at[block_rows(seq)])
    gather = Gather(links, moves, own, square, shrink)
    for _ in range(Gather.EARLY):
        gather.tick()
    links.send(slot_far, tokens.at[1 - group], stream.at[block_rows(seq)], opposite)
    links.send(slot_mate, tokens.at[group], stream.at[block_rows(seq)], mate)
    links.send(slot_core, tokens.at[group], stream.at[block_rows(seq)], partner)
    slot_memory, slot_context = links.slot(4), links.slot()
    context_home = moves.start(memory.at[group], held.context.at[z, core])
    for k in (1, 2, 3):
        links.send(slot_memory + z, memory.at[((z + k) % 4) // 2], held.context.at[z, core], place.along_z(k))
    norm_steps = all_sum(links, norms, held.gains, held.work)
    next(norm_steps)

    def sentence(places):
        result, end = jnp.zeros_like(places), 0
        for index in range(lengths.shape[1] - 1):
            end = end + lengths[group, index]
            result = result + (places >= end).astype(jnp.int32)
        return result

    held.norm_sums[...] = jnp.zeros_like(held.norm_sums)
    held.self_logs[...] = jnp.zeros_like(held.self_logs)
    held.cross_logs[...] = jnp.zeros_like(held.cross_logs)

    @loop(OWN // STEP)
    def _(index):
        row = index * STEP + lax.broadcasted_iota(jnp.int32, (STEP, 1), 0)
        row_place = LEN * low + row + jnp.where(row >= LEN, 3 * LEN, 0)
        row_sentence = sentence(row_place)
        key_place = lax.broadcasted_iota(jnp.int32, (1, SPAN), 1)
        allowed = (row_sentence == sentence(key_place)) & (key_place <= row_place)
        held.self_bias[tile(index, STEP), :] = jnp.where(allowed, 0.0, masked_score)
        met = row_sentence == segments[pl.ds(group, 1), :]
        held.cross_bias[tile(index, STEP), :] = jnp.where(met, 0.0, masked_score)

    def pass_on(number, block):
        links.send(slot_core + number, stream.at[block_rows(block)], stream.at[block_rows(block)], partner)

    gather.tick()
    next(norm_steps)
    gather.tick()
    next(norm_steps)
    gather.tick()
    links.arrived(slot_far, stream.at[block_rows(far)])
    links.send(slot_mate_far, stream.at[block_rows(far)], stream.at[block_rows(far)], mate)
    pass_on(1, far)
    gather.tick()
    links.arrived(slot_mate, stream.at[block_rows(mate_seq)])
    pass_on(2, mate_seq)
    moves.wait(context_home)
    for k in (1, 2, 3):
        links.arrived(slot_memory + (z + k) % 4, held.context.at[(z + k) % 4, core])
    links.send(slot_context, held.context.at[:, core], held.context.at[:, core], partner)
    next(norm_steps)
    gather.tick()
    links.arrived(slot_mate_far, stream.at[block_rows((mate_seq + 4) % 8)])
    pass_on(3, (mate_seq + 4) % 8)
    gather.tick()
    cotangent_rows, cotangent_far = block_rows(group), block_rows(1 - group)
    slot_cotangent = links.slot()
    cotangent_home = moves.start(out_grad.at[group], held.cotangent.at[cotangent_rows])
    links.send(slot_cotangent, out_grad.at[1 - group], held.cotangent.at[cotangent_rows], opposite)
    moves.wait(home)
    for number, block in enumerate((other_seq, (other_seq + 4) % 8, other_mate, (other_mate + 4) % 8)):
        links.arrived(slot_core + number, stream.at[block_rows(block)])
    links.arrived(slot_context, held.context.at[:, 1 - core])
    held.mine[pl.ds(0, LEN), :] = stream[block_rows(low), :]
    held.mine[pl.ds(LEN, LEN), :] = stream[block_rows(low + 4), :]

    loads = {}

    def fetch(unit, slot):
        if unit < SQUARE:
            target = held.weights.at[slot]
            loads[unit] = (moves.start(square.at[unit].reshape(D, D), target), target)
        else:
            target = held.shrink_in.at[slot]
            loads[unit] = (moves.start(shrink.at[unit - SQUARE].reshape(4, D, OWN), target), target)

    def weight(unit):
        step, target = loads.pop(unit)
        moves.wait(step)
        return target

    turning = {"count": 0, "open": {}}
    landing = []
    mine, theirs = core_rows(core), core_rows(1 - core)

    def turn(source, name):
        number = turning["count"] % 3
        for move, sent in turning["open"].pop(number, ()):
            moves.wait(move)
            links.sent(sent)
        turning["count"] += 1
        buffer, target = held.turned.at[number], getattr(turned, name)

        @loop(4)
        def _(index):
            buffer[pl.ds(4 * index, 4)] = source[:, tile(index, OWN)].T.reshape(4, 2, 32, OWN)

        slot = links.slot()
        move = moves.start(buffer.at[:, core], target.at[:, :, mine])
        sent = links.send(slot, buffer.at[:, 1 - core], target.at[:, :, mine], partner)
        landing.append((slot, target.at[:, :, theirs]))
        turning["open"][number] = [(move, sent)]

    def keep(*names):
        for name in names:
            moves.start(getattr(held, name), getattr(kept, name))

    def gain(number):
        return held.gains[pl.ds(number, 1), :]

    def bias(number):
        return held.gains[pl.ds(3 + number, 1), :]

    fetch(KEY, 0)
    turn(held.mine, "tokens_t")
    next(norm_steps)
    fetch(VALUE, 1)
    rows_times(stream, weight(KEY), put(held.keys))
    gather.tick()
    fetch(QUERY, 2)
    rows_times(stream, weight(VALUE), put(held.values))
    rows_times(held.mine, weight(QUERY), put(held.queries))

    def attend_part(first, pairs):
        attend_rows(
            held.queries, held.keys, held.values, held.self_bias, held.self_logs, held.attended, SELF_SEGMENTS, pairs, first
        )

    fetch(OUT, 3)
    attend_part(0, 3)
    gather.tick()
    fetch(CROSS_QUERY, 0)
    attend_part(3, 3)
    gather.tick()
    fetch(CROSS_KEY, 1)
    attend_part(6, 2)
    rows_times(held.attended, weight(OUT), put(held.sums, F32))
    keep("queries", "keys", "values", "self_bias", "self_logs", "cross_bias", "gains")

    def first_rows(rows, result, _):
        held.first_low[rows, :] = (result * gain(0) + bias(0)).astype(BF)

    def after(rows, previous):
        return held.sums[rows, :] + alpha_scale * previous

    norm_rows(lambda rows: after(rows, held.mine[rows, :].astype(F32)), held.normal_one, held.inverse_one, first_rows)
    turn(held.attended, "attended_t")
    rows_times(held.first_low, weight(CROSS_QUERY), put(held.cross_queries))
    context = held.context.reshape(MEM, D)
    rows_times(context, weight(CROSS_KEY), put(held.cross_keys), MEM)
    gather.tick()
    fetch(CROSS_VALUE, 2)
    turn(held.first_low, "first_t")

    @loop(4)
    def _(index):
        held.turned_memory[pl.ds(4 * index, 4)] = context[:, tile(index, OWN)].T.reshape(4, 2, 32, MEM)

    moves.start(held.turned_memory.at[:, core], turned.memory_t)
    rows_times(context, weight(CROSS_VALUE), put(held.cross_values), MEM)
    attend_rows(
        held.cross_queries, held.cross_keys, held.cross_values, held.cross_bias, held.cross_logs,
        held.cross_attended, CROSS_SEGMENTS,
    )
    gather.tick()
    fetch(CROSS_OUT, 3)
    keep("cross_queries", "cross_keys", "cross_values", "cross_logs", "normal_one", "inverse_one")
    rows_times(held.cross_attended, weight(CROSS_OUT), put(held.sums, F32))

    def second_rows(rows, result, _):
        held.second_low[rows, :] = (result * gain(1) + bias(1)).astype(BF)

    norm_rows(
        lambda rows: after(rows, held.normal_one[rows, :] * gain(0) + bias(0)),
        held.normal_two, held.inverse_two, second_rows,
    )
    keep("normal_two", "inverse_two")
    gather.tick()
    turn(held.cross_attended, "cross_t")
    turn(held.second_low, "second_t")
    turned_open = {}
    for part in range(4):
        if part > 0:
            gather.tick()
        fetch(EXPAND + part, part)
        active, slopes = held.active.at[part], held.slopes.at[part]

        def activate(rows, columns, value):
            inner = GELU_SLOPE * (value + GELU_CUBE * value * value * value)
            bend = jnp.tanh(inner)
            active[rows, columns] = (0.5 * value * (1.0 + bend)).astype(BF)
            slope = 0.5 * (1.0 + bend) + 0.5 * value * (1.0 - bend * bend) * (
                GELU_SLOPE * (1.0 + 3.0 * GELU_CUBE * value * value)
            )
            slopes[rows, columns] = slope.astype(BF)

        rows_times(held.second_low, weight(EXPAND + part), activate)
        number = part % 2
        for move, sent in turned_open.pop(number, ()):
            moves.wait(move)
            links.sent(sent)
        buffer = held.turned_active.at[number]

        @loop(4)
        def _(index):
            buffer[index] = active[:, tile(index, OWN)].T.reshape(2, 4, 32, OWN)

        slot = links.slot()
        move = moves.start(buffer.at[:, core], turned.active_t.at[part, :, :, :, mine])
        sent = links.send(slot, buffer.at[:, 1 - core], turned.active_t.at[part, :, :, :, mine], partner)
        landing.append((slot, turned.active_t.at[part, :, :, :, theirs]))
        turned_open[number] = [(move, sent)]
    keep("slopes")
    for part in range(4):
        gather.tick()
        fetch(SQUARE + part, part % 2)
        shrink_part = weight(SQUARE + part)
        for first in (0, LEN):
            rows = pl.ds(first, LEN)
            total = project(held.active[0, rows, :], shrink_part[0])
            for depth in (1, 2, 3):
                total = total + project(held.active[depth, rows, :], shrink_part[depth])
            held.sums[rows, pl.ds(OWN * part, OWN)] = total
    links.arrived(slot_cotangent, held.cotangent.at[cotangent_far])
    moves.wait(cotangent_home)

    def third_rows(rows, result, scale):
        held.final_low[rows, :] = (result * gain(2) + bias(2)).astype(BF)
        grad = norm_rows_back(held.cotangent[rows, :].astype(F32), result, scale, gain(2), held.norm_sums, 2)
        held.third_grad[rows, :] = grad
        held.branch_own[rows, :] = grad.astype(BF)

    norm_rows(lambda rows: after(rows, held.normal_two[rows, :] * gain(1) + bias(1)), None, None, third_rows)
    slot = links.slot()
    links.send(slot, held.branch_own, turned.branch.at[mine], partner)
    landing.append((slot, turned.branch.at[theirs]))
    moves.start(held.branch_own, turned.branch.at[mine])
    keep("third_grad", "norm_sums", "final_low")
    for arrival in landing:
        links.arrived(*arrival)
    moves.finish()
    links.finish()


IN_VMEM = pl.BlockSpec(memory_space=pltpu.VMEM)
IN_SMEM = pl.BlockSpec(memory_space=pltpu.SMEM)
IN_PLACE = pl.BlockSpec(memory_space=pl.ANY)


def shapes_of(table):
    return [jax.ShapeDtypeStruct(shape, dtype) for shape, dtype in table.values()]


def vmem_of(table):
    return [pltpu.VMEM(shape, dtype) for shape, dtype in table.values()]


def forward_call(lengths, segments, norms, tokens, memory, out_grad, weights):
    results = [
        jax.ShapeDtypeStruct(SQUARE_SHAPE, BF),
        jax.ShapeDtypeStruct(SHRINK_SHAPE, BF),
        *shapes_of(FORWARD_SAVES),
        *shapes_of(TURNED_SAVES),
    ]
    values = pl.pallas_call(
        forward_kernel,
        in_specs=[IN_SMEM, IN_VMEM, IN_VMEM] + [IN_PLACE] * 13,
        out_specs=[IN_PLACE] * len(results),
        out_shape=results,
        scratch_shapes=[
            *vmem_of(FORWARD_SAVES),
            *vmem_of(FORWARD_SCRATCH),
            pltpu.SemaphoreType.DMA((FORWARD_SENDS,)),
            pltpu.SemaphoreType.DMA((FORWARD_SLOTS,)),
            pltpu.SemaphoreType.DMA((FORWARD_MOVES,)),
        ],
        compiler_params=pltpu.CompilerParams(collective_id=0, has_side_effects=True, vmem_limit_bytes=VMEM_BYTES),
    )(lengths, segments, norms, tokens, memory, out_grad, *weights)
    saves = dict(zip([*FORWARD_SAVES, *TURNED_SAVES], values[2:]))
    return values[0], values[1], saves


class Scatter:
    def __init__(self, links, grads, from_first, from_second, from_z, result):
        self.links, self.grads, self.result = links, grads, result
        self.from_first, self.from_second, self.from_z = from_first, from_second, from_z
        self.slots, self.pending, self.now = {}, {}, 0

    def home(self, unit):
        for step in self.pending.pop(unit - self.grads.shape[0], ()):
            self.links.sent(step)
        self.slots[unit] = self.links.slot(12)
        return self.grads.at[unit % self.grads.shape[0]]

    def add(self, total, part):
        for row in range(4):
            total[row] = (total[row].astype(F32) + part[row].astype(F32)).astype(BF)

    def phase(self, unit, half, number):
        links, place = self.links, self.links.place
        y, x, z = place.y, place.x, place.z
        here = self.grads.at[unit % self.grads.shape[0]]
        depth = unit % self.from_first.shape[0]
        rows = pl.ds(16 * half, 16)
        slot = self.slots[unit] + 6 * half
        by_y = half == 0
        first, second = ("y", "x") if by_y else ("x", "y")
        away = (1 - y, ALL) if by_y else (ALL, 1 - x)
        corner, other, mine = ((y, 1 - x), 1 - x, x) if by_y else ((1 - y, x), 1 - y, y)
        home = here.at[y, x, :, rows]
        first_in = self.from_first.at[depth, :, :, rows]
        second_in = self.from_second.at[depth, :, rows]

        def send(number, source, target, device):
            self.pending.setdefault(unit, []).append(links.send(slot + number, source, target, device))

        if number == 0:
            send(0, here.at[(*away, ALL, rows)], first_in, place.across(first))
        if number == 1:
            links.arrived(slot, first_in)
            corner_part = here.at[(*corner, ALL, rows)]
            self.add(corner_part, first_in.at[other])
            send(1, corner_part, second_in, place.across(second))
            self.add(home, first_in.at[mine])
        if number == 2:
            links.arrived(slot + 1, second_in)
            self.add(home, second_in)
            for k in (1, 2, 3):
                send(2 + z, home.at[(z + k) % 4], self.from_z.at[depth, z, rows], place.along_z(k))
        if number == 3:
            total = home[z].astype(F32)
            for k in (1, 2, 3):
                source = (z + k) % 4
                links.arrived(slot + 2 + source, self.from_z.at[depth, source, rows])
                total = total + self.from_z[depth, source, rows].astype(F32)
            self.result(unit, rows, total)

    def tick(self):
        for number in (0, 1, 2, 3):
            unit = self.now - number
            if 0 <= unit < UNITS:
                for half in (0, 1):
                    self.phase(unit, half, number)
        self.now += 1


DEPTH = 4
BACKWARD_SCRATCH = {
    "weights": ((3, D, D), BF),
    "shrink_in": ((4, D, OWN), BF),
    "grads": ((6, 2, 2, 4, 32, D), BF),
    "from_first": ((DEPTH, 2, 4, 32, D), BF),
    "from_second": ((DEPTH, 4, 32, D), BF),
    "from_z": ((DEPTH, 4, 32, D), BF),
    "up": ((4, 2 * OWN, D), BF),
    "second_sum": ((OWN, D), F32),
    "cross_branch": ((2 * OWN, D), BF),
    "attended_grad": ((OWN, D), BF),
    "cross_query_grad": ((2 * OWN, D), BF),
    "cross_terms": ((2, 2, MEM, D), BF),
    "cross_sums": ((2, MEM, D), BF),
    "self_branch": ((2 * OWN, D), BF),
    "query_grad": ((2 * OWN, D), BF),
    "terms": ((2, 2, 2, 2, LEN, D), BF),
    "terms_core": ((2, 2, 2, LEN, D), BF),
    "terms_mate": ((2, 2, LEN, D), BF),
    "key_grad": ((2 * OWN, D), BF),
    "value_grad": ((2 * OWN, D), BF),
    "memory_own": ((4, 16, D), BF),
    "memory_in": ((4, 16, D), BF),
    "far_own": ((LEN, D), BF),
    "far_in": ((LEN, D), BF),
    "work": ((8, 8, D), F32),
}
BACKWARD_SENDS, BACKWARD_SLOTS, BACKWARD_MOVES = 240, 256, 64


def backward_kernel(square, shrink, *refs):
    saved = [*FORWARD_SAVES, *TURNED_SAVES]
    names = [name for name in saved if name != "final_low"]
    kept = Refs(saved, refs[: len(saved)])
    rest = refs[len(saved) :]
    output, input_grad, memory_grad, *unit_grads = rest[:11]
    expand_grad, shrink_grad, norm_grads = rest[11:14]
    rest = rest[14:]
    held = Refs(names, rest[: len(names)])
    rest = rest[len(names) :]
    held.__dict__.update(Refs(BACKWARD_SCRATCH, rest[: len(BACKWARD_SCRATCH)]).__dict__)
    send_sem, recv_sem, move_sem = rest[len(BACKWARD_SCRATCH) :]

    place = Place()
    links, moves = Links(place, send_sem, recv_sem), Moves(move_sem)
    z, core, group = place.z, place.core, place.group
    partner = place.across("core")
    mine, theirs = core_rows(core), core_rows(1 - core)
    loads = {}

    def bring(*wanted):
        for name in wanted:
            loads[name] = moves.start(getattr(kept, name), getattr(held, name))

    def have(*wanted):
        for name in wanted:
            moves.wait(loads.pop(name))

    def fetch(unit, slot):
        loads[unit] = moves.start(square.at[unit].reshape(D, D), held.weights.at[slot])

    def weight(unit, slot):
        moves.wait(loads.pop(unit))
        return held.weights.at[slot]

    bring("branch", "active_t")

    def fetch_shrink(part):
        loads[SQUARE] = moves.start(shrink.at[:, part], held.shrink_in)

    fetch_shrink(0)
    for part in range(3):
        fetch(EXPAND + part, part)
    bring("slopes", "third_grad", "second_t", "norm_sums", "gains", "normal_two", "inverse_two")
    bring("cross_queries", "cross_keys", "cross_values", "cross_bias", "cross_logs", "cross_t")
    bring("normal_one", "inverse_one", "first_t", "memory_t", "attended_t", "tokens_t")
    bring("queries", "keys", "values", "self_bias", "self_logs")
    place.greet()

    order = [12, 13, 14, 15, 8, 9, 10, 11, CROSS_OUT, CROSS_QUERY, CROSS_KEY, CROSS_VALUE, OUT, QUERY, KEY, VALUE]

    def result(number, rows, total):
        unit = order[number]
        if unit < EXPAND:
            unit_grads[unit][rows, :] = total
        elif unit < SQUARE:
            expand_grad[rows, pl.ds(D * (unit - EXPAND), D)] = total
        else:
            shrink_grad[pl.ds(32 * (unit - SQUARE) + rows.start, rows.size), :] = total

    scatter = Scatter(links, held.grads, held.from_first, held.from_second, held.from_z, result)
    made = {"count": 0}

    def produce(left, right, depth=2 * OWN):
        target = scatter.home(made["count"])
        made["count"] += 1

        @loop(4)
        def _(index):
            columns = tile(index, OWN)
            term = project(left().reshape(512, depth), right[:, columns])
            target[:, :, :, :, columns] = term.astype(BF).reshape(2, 2, 4, 32, OWN)

    def share(ref):
        slot = links.slot()
        links.send(slot, ref.at[mine], ref.at[mine], partner)
        return slot

    def shared(ref, slot):
        links.arrived(slot, ref.at[theirs])

    def gain(number):
        return held.gains[pl.ds(number, 1), :]

    have("branch", "active_t")

    def produce_shrink(part):
        produce(lambda: held.active_t[:, :, part], held.branch)

    def produce_expand(part):
        shared(held.up.at[part], up_slots[part])
        produce(lambda: held.second_t[...], held.up.at[part])

    produce_shrink(0)
    scatter.tick()
    slot_output = links.slot()
    moves.start(kept.final_low.at[block_rows(group)], output.at[group])
    links.send(slot_output, kept.final_low.at[block_rows(1 - group)], output.at[group], place.along_z(2))
    for part in (1, 2, 3):
        produce_shrink(part)
    scatter.tick()
    have("slopes")
    own_branch = held.branch.at[mine]
    up_slots = []
    for part in range(4):
        if part == 2:
            scatter.tick()
        up = held.up.at[part, mine]
        slopes = held.slopes.at[part]

        moves.wait(loads.pop(SQUARE))

        @loop(4)
        def _(index):
            columns = tile(index, OWN)
            total = project_back(own_branch[:, pl.ds(0, OWN)], held.shrink_in[0, columns, :])
            for depth in (1, 2, 3):
                total = total + project_back(own_branch[:, pl.ds(OWN * depth, OWN)], held.shrink_in[depth, columns, :])
            up[:, columns] = (total * slopes[:, columns].astype(F32)).astype(BF)

        up_slots.append(share(held.up.at[part]))
        if part < 3:
            fetch_shrink(part + 1)

        def add(columns, value):
            if part == 0:
                held.second_sum[:, columns] = value
            else:
                held.second_sum[:, columns] += value

        rows_back(up, weight(EXPAND + part, part % 3), add)
        fetch((EXPAND + 3, CROSS_OUT, CROSS_QUERY, CROSS_KEY)[part], part % 3)
    scatter.tick()
    have("third_grad", "norm_sums", "gains", "normal_two", "inverse_two", "second_t")

    def spread(inverse, rows):
        return inverse[rows, pl.ds(0, 1)]

    @loop(OWN // STEP)
    def _(index):
        rows = tile(index, STEP)
        grad = held.second_sum[rows, :] + alpha_scale * held.third_grad[rows, :]
        pre = norm_rows_back(grad, held.normal_two[rows, :], spread(held.inverse_two, rows), gain(1), held.norm_sums, 1)
        held.second_sum[rows, :] = pre
        held.cross_branch[pl.ds(pl.multiple_of(OWN * core + STEP * index, STEP), STEP), :] = pre.astype(BF)

    slot_cross_branch = share(held.cross_branch)
    produce_expand(0)
    scatter.tick()

    def low(target):
        def store(columns, value):
            target[:, columns] = value.astype(BF)

        return store

    rows_back(held.cross_branch.at[mine], weight(CROSS_OUT, 1), low(held.attended_grad))
    fetch(CROSS_VALUE, 1)
    have("cross_queries", "cross_keys", "cross_values", "cross_bias", "cross_logs", "cross_t")
    attend_rows_back(
        held.cross_queries, held.cross_keys, held.cross_values, held.cross_bias, held.cross_logs, held.attended_grad,
        held.cross_query_grad.at[mine], held.cross_terms.at[0, core], held.cross_terms.at[1, core], CROSS_SEGMENTS, H // 2,
    )
    slot_cross_query = share(held.cross_query_grad)
    slot_cross_terms = links.slot()
    links.send(slot_cross_terms, held.cross_terms.at[:, core], held.cross_terms.at[:, core], partner)
    produce_expand(1)
    scatter.tick()

    def add_first(columns, value):
        held.third_grad[:, columns] = value

    rows_back(held.cross_query_grad.at[mine], weight(CROSS_QUERY, 2), add_first)
    fetch(OUT, 2)
    have("normal_one", "inverse_one", "first_t", "memory_t", "attended_t", "tokens_t")

    @loop(OWN // STEP)
    def _(index):
        rows = tile(index, STEP)
        grad = held.third_grad[rows, :] + alpha_scale * held.second_sum[rows, :]
        pre = norm_rows_back(grad, held.normal_one[rows, :], spread(held.inverse_one, rows), gain(0), held.norm_sums, 0)
        held.second_sum[rows, :] = pre
        held.self_branch[pl.ds(pl.multiple_of(OWN * core + STEP * index, STEP), STEP), :] = pre.astype(BF)

    slot_self_branch = share(held.self_branch)
    norm_steps = all_sum(links, held.norm_sums, norm_grads, held.work)
    next(norm_steps)
    produce_expand(2)
    scatter.tick()
    rows_back(held.self_branch.at[mine], weight(OUT, 2), low(held.attended_grad))
    fetch(QUERY, 2)
    have("queries", "keys", "values", "self_bias", "self_logs")
    terms = held.terms

    def attend_part(first, pairs):
        attend_rows_back(
            held.queries, held.keys, held.values, held.self_bias, held.self_logs, held.attended_grad,
            held.query_grad.at[mine], terms.at[0].reshape(SPAN, D), terms.at[1].reshape(SPAN, D), SELF_SEGMENTS, pairs, first,
        )

    attend_part(0, 2)
    produce_expand(3)
    scatter.tick()
    next(norm_steps)
    attend_part(2, 2)
    shared(held.cross_branch, slot_cross_branch)
    produce(lambda: held.cross_t[...], held.cross_branch)
    scatter.tick()
    next(norm_steps)
    attend_part(4, 2)
    shared(held.cross_query_grad, slot_cross_query)
    produce(lambda: held.first_t[...], held.cross_query_grad)
    scatter.tick()
    next(norm_steps)
    attend_part(6, 2)
    slot_query = share(held.query_grad)
    slot_terms = links.slot()
    links.send(slot_terms, terms.at[:, :, :, 1 - core], held.terms_core, partner)

    links.arrived(slot_cross_terms, held.cross_terms.at[:, 1 - core])
    for which in (0, 1):
        held.cross_sums[which] = (held.cross_terms[which, 0].astype(F32) + held.cross_terms[which, 1].astype(F32)).astype(BF)
    produce(lambda: held.memory_t[...], held.cross_sums.at[0], MEM)
    scatter.tick()
    next(norm_steps)

    links.arrived(slot_terms, held.terms_core)
    near = z % 2

    def join(place_index):
        for which in (0, 1):
            for high in (0, 1):
                value = terms[which, high, place_index, core].astype(F32) + held.terms_core[which, high, place_index].astype(F32)
                terms[which, high, place_index, core] = value.astype(BF)

    join(1 - near)
    slot_mate = links.slot()
    links.send(slot_mate, terms.at[:, :, 1 - near, core], held.terms_mate, place.mate())
    join(near)

    produce(lambda: held.memory_t[...], held.cross_sums.at[1], MEM)
    scatter.tick()

    cross_key, cross_value = weight(CROSS_KEY, 0), weight(CROSS_VALUE, 1)
    sums = held.cross_sums.reshape(2, 4, 2, 16, D)

    @loop(4)
    def _(index):
        columns = tile(index, OWN)
        term = project_back(sums[0, :, core].reshape(64, D), cross_key[columns, :])
        term = term + project_back(sums[1, :, core].reshape(64, D), cross_value[columns, :])
        held.memory_own[:, :, columns] = term.astype(BF).reshape(4, 16, OWN)

    fetch(KEY, 0)
    fetch(VALUE, 1)
    slot_memory = links.slot(4)
    for k in (1, 2, 3):
        links.send(slot_memory + z, held.memory_own.at[(z + k) % 4], held.memory_in.at[z], place.along_z(k))
    held.memory_in[z] = held.memory_own[z]

    shared(held.self_branch, slot_self_branch)
    produce(lambda: held.attended_t[...], held.self_branch)
    scatter.tick()
    shared(held.query_grad, slot_query)
    produce(lambda: held.tokens_t[...], held.query_grad)
    scatter.tick()

    def add_input(columns, value):
        held.third_grad[:, columns] = alpha_scale * held.second_sum[:, columns] + value

    rows_back(held.query_grad.at[mine], weight(QUERY, 2), add_input)
    links.arrived(slot_mate, held.terms_mate)
    for which, target in enumerate((held.key_grad, held.value_grad)):
        for high in (0, 1):
            value = terms[which, high, near, core].astype(F32) + held.terms_mate[which, high].astype(F32)
            target[pl.ds(pl.multiple_of(OWN * core + LEN * high, LEN), LEN), :] = value.astype(BF)
    slot_key, slot_value = share(held.key_grad), share(held.value_grad)

    def add_more(columns, value):
        held.third_grad[:, columns] += value

    rows_back(held.key_grad.at[mine], weight(KEY, 0), add_more)
    rows_back(held.value_grad.at[mine], weight(VALUE, 1), add_more)
    held.far_own[...] = held.third_grad[block_rows(1 - group), :].astype(BF)
    slot_far = links.slot()
    links.send(slot_far, held.far_own, held.far_in, place.along_z(2))
    shared(held.key_grad, slot_key)
    produce(lambda: held.tokens_t[...], held.key_grad)
    scatter.tick()
    shared(held.value_grad, slot_value)
    produce(lambda: held.tokens_t[...], held.value_grad)
    scatter.tick()
    input_grad[group] = held.third_grad[block_rows(group), :]
    scatter.tick()
    for k in (1, 2, 3):
        links.arrived(slot_memory + (z + k) % 4, held.memory_in.at[(z + k) % 4])
    for which in (0, 1):
        memory_grad[which] = held.memory_in[2 * which].astype(F32) + held.memory_in[2 * which + 1].astype(F32)
    scatter.tick()
    scatter.tick()
    links.arrived(slot_far, held.far_in)
    input_grad[1 - group] = held.far_in[...].astype(F32)
    links.arrived(slot_output, output.at[1 - group])
    moves.finish()
    links.finish()


def backward_call(square, shrink, saves, block_shape, memory_shape):
    results = [jax.ShapeDtypeStruct(block_shape, BF)]
    results += [jax.ShapeDtypeStruct(shape, F32) for shape in (block_shape, memory_shape)]
    results += [jax.ShapeDtypeStruct((32, D), F32)] * 8
    results += [jax.ShapeDtypeStruct(shape, F32) for shape in ((32, 4 * D), (LEN, D), (8, D))]
    saved = {**FORWARD_SAVES, **TURNED_SAVES}
    held = {name: saved[name] for name in saved if name != "final_low"}
    return pl.pallas_call(
        backward_kernel,
        in_specs=[IN_PLACE] * (2 + len(saved)),
        out_specs=[IN_PLACE] + [IN_VMEM] * (len(results) - 1),
        out_shape=results,
        scratch_shapes=[
            *vmem_of(held),
            *vmem_of(BACKWARD_SCRATCH),
            pltpu.SemaphoreType.DMA((BACKWARD_SENDS,)),
            pltpu.SemaphoreType.DMA((BACKWARD_SLOTS,)),
            pltpu.SemaphoreType.DMA((BACKWARD_MOVES,)),
        ],
        compiler_params=pltpu.CompilerParams(collective_id=1, has_side_effects=True, vmem_limit_bytes=63 << 20),
    )(square, shrink.reshape(4, 4, D, OWN), *(saves[name] for name in saved))


def hand_over_kernel(*refs):
    count = len(refs) // 3
    sem = refs[-1]
    loads = [pltpu.make_async_copy(refs[n], refs[2 * count + n], sem.at[0, n]) for n in range(count)]
    stores = [pltpu.make_async_copy(refs[2 * count + n], refs[count + n], sem.at[1, n]) for n in range(count)]
    for load in loads:
        load.start()
    for load, store in zip(loads, stores):
        load.wait()
        store.start()
    for store in stores:
        store.wait()


def hand_over(values):
    return pl.pallas_call(
        hand_over_kernel,
        in_specs=[IN_PLACE] * len(values),
        out_specs=[IN_PLACE] * len(values),
        out_shape=[jax.ShapeDtypeStruct(value.shape, value.dtype) for value in values],
        scratch_shapes=[
            *(pltpu.VMEM(value.shape, value.dtype) for value in values),
            pltpu.SemaphoreType.DMA((2, len(values))),
        ],
        compiler_params=pltpu.CompilerParams(vmem_limit_bytes=VMEM_BYTES),
    )(*values)


def fast_shards(
    tokens, memory, lengths, memory_segments, out_grad,
    self_query, self_key, self_value, self_out,
    cross_query, cross_key, cross_value, cross_out,
    expand_weight, shrink_weight, norm_gains, norm_biases,
):
    me = lax.axis_index("dp") * lax.axis_size("seq") + lax.axis_index("seq")
    norms = jnp.concatenate([norm_gains, norm_biases, jnp.zeros((2, 32), BF)]).astype(F32)
    norms = lax.dynamic_update_slice(jnp.zeros((8, D), F32), norms, (0, 32 * me))
    weights = (self_key, self_value, self_query, self_out, cross_query, cross_key, cross_value, cross_out)
    square, shrink, saves = forward_call(
        lengths, memory_segments, norms, tokens, memory, out_grad, (*weights, expand_weight, shrink_weight)
    )
    *values, norm_grads = backward_call(square, shrink, saves, tokens.shape, memory.shape)
    output, input_grad, memory_grad, *units, expand_grad, shrink_grad = hand_over(values)
    norm_grads = lax.dynamic_slice(norm_grads, (0, 32 * me), (8, 32))
    return (
        output,
        input_grad,
        memory_grad,
        *(units[unit] for unit in (QUERY, KEY, VALUE, OUT, CROSS_QUERY, CROSS_KEY, CROSS_VALUE, CROSS_OUT)),
        expand_grad,
        shrink_grad,
        norm_grads[:3],
        norm_grads[3:6],
    )


def solution(mesh):
    quick = dict(mesh.shape) == {"dp": 4, "seq": 8}
    return jax.shard_map(
        fast_shards if quick else shards,
        mesh=mesh,
        in_specs=(
            P("dp", "seq", None),
            P("dp", "seq", None),
            P("dp", None),
            P("dp", None),
            P("dp", "seq", None),
            P(("dp", "seq"), None),
            P(("dp", "seq"), None),
            P(("dp", "seq"), None),
            P(("dp", "seq"), None),
            P(("dp", "seq"), None),
            P(("dp", "seq"), None),
            P(("dp", "seq"), None),
            P(("dp", "seq"), None),
            P(("dp", "seq"), None),
            P(("dp", "seq"), None),
            P(None, ("dp", "seq")),
            P(None, ("dp", "seq")),
        ),
        out_specs=(
            P("dp", "seq", None),
            P("dp", "seq", None),
            P("dp", "seq", None),
            P(("dp", "seq"), None),
            P(("dp", "seq"), None),
            P(("dp", "seq"), None),
            P(("dp", "seq"), None),
            P(("dp", "seq"), None),
            P(("dp", "seq"), None),
            P(("dp", "seq"), None),
            P(("dp", "seq"), None),
            P(("dp", "seq"), None),
            P(("dp", "seq"), None),
            P(None, ("dp", "seq")),
            P(None, ("dp", "seq")),
        ),
        check_vma=False,
    )
```

```python
import functools

import jax
import jax.numpy as jnp
from jax import lax
from jax.experimental import pallas as pl
from jax.experimental.pallas import tpu as pltpu
from jax.sharding import PartitionSpec as P

H = 16
HD = 64
MB = 2


alpha_scale = 300.0**0.25
norm_eps = 1e-05
masked_score = -1e30


def layer_norm(value, gain, bias):
    average = jnp.mean(value, axis=-1, keepdims=True)
    centred = value - average
    spread = jnp.mean(centred * centred, axis=-1, keepdims=True)
    return centred * lax.rsqrt(spread + norm_eps) * gain + bias


def project(left, right):
    return jnp.dot(left, right, preferred_element_type=jnp.float32)


def project_back(left, right):
    return lax.dot_general(
        left, right, (((1,), (1,)), ((), ())), preferred_element_type=jnp.float32
    )


def weight_term(left, right):
    return lax.dot_general(
        left, right, (((0,), (0,)), ((), ())), preferred_element_type=jnp.float32
    )


def split_heads(value):
    return value.reshape(value.shape[0], value.shape[1], H, HD)


def sentence_ids(sent_ends, places):
    return jnp.sum((places[None, :, None] >= sent_ends[:, None, :]).astype(jnp.int32), axis=2)


def masked_scores(queries, key_heads, allowed, scaling):
    raw_scores = (
        jnp.einsum("gqhd,gkhd->ghqk", queries, key_heads, preferred_element_type=jnp.float32)
        * scaling
    )
    return jnp.where(allowed[:, None], raw_scores, masked_score)


def attend_forward(queries, key_heads, value_heads, allowed, scaling):
    scores = masked_scores(queries, key_heads, allowed, scaling)
    row_max = jnp.max(scores, axis=3, keepdims=True)
    powers = jnp.exp(scores - row_max)
    row_total = jnp.sum(powers, axis=3, keepdims=True)
    prob_low = (powers / row_total).astype(jnp.bfloat16)
    attended = jnp.einsum(
        "ghqk,gkhd->gqhd", prob_low, value_heads, preferred_element_type=jnp.float32
    )
    return (attended, row_max + jnp.log(row_total))


def attend_backward(queries, key_heads, value_heads, allowed, scaling, log_total, attended_grad):
    scores = masked_scores(queries, key_heads, allowed, scaling)
    probability = jnp.exp(scores - log_total)
    prob_grad = jnp.einsum(
        "gqhd,gkhd->ghqk", attended_grad, value_heads, preferred_element_type=jnp.float32
    )
    score_grad = probability * (prob_grad - jnp.sum(prob_grad * probability, axis=3, keepdims=True))
    score_low = score_grad.astype(jnp.bfloat16)
    query_grad = (
        jnp.einsum("ghqk,gkhd->gqhd", score_low, key_heads, preferred_element_type=jnp.float32)
        * scaling
    )
    return (query_grad, score_low, probability.astype(jnp.bfloat16))


def micro_batch(gathered, tokens, memory, lengths, memory_segments, out_grad):
    (
        self_query,
        self_key,
        self_value,
        self_out,
        cross_query,
        cross_key,
        cross_value,
        cross_out,
        expand_weight,
        shrink_weight,
        norm_gains,
        norm_biases,
    ) = gathered
    gains = norm_gains.astype(jnp.float32)
    biases = norm_biases.astype(jnp.float32)
    group_size, local_len, features = tokens.shape
    seq_count = lax.axis_size("seq")
    seq_index = lax.axis_index("seq")
    full_len = local_len * seq_count
    row_count = group_size * local_len
    scaling = HD ** (-0.5)
    sent_ends = jnp.cumsum(lengths, axis=1)[:, :-1]
    query_places = seq_index * local_len + jnp.arange(local_len, dtype=jnp.int32)
    key_places = jnp.arange(full_len, dtype=jnp.int32)
    query_ids = sentence_ids(sent_ends, query_places)
    key_ids = sentence_ids(sent_ends, key_places)
    self_allowed = (query_ids[:, :, None] == key_ids[:, None, :]) & (
        key_places[None, None, :] <= query_places[None, :, None]
    )
    cross_allowed = query_ids[:, :, None] == memory_segments[:, None, :]
    token_rows = tokens.reshape(row_count, features)
    queries = split_heads(
        project(token_rows, self_query)
        .astype(jnp.bfloat16)
        .reshape(group_size, local_len, features)
    )
    own_keys = (
        project(token_rows, self_key).astype(jnp.bfloat16).reshape(group_size, local_len, features)
    )
    own_values = (
        project(token_rows, self_value)
        .astype(jnp.bfloat16)
        .reshape(group_size, local_len, features)
    )
    all_keys, all_values = (
        lax.all_gather(own_keys, "seq", axis=1, tiled=True),
        lax.all_gather(own_values, "seq", axis=1, tiled=True),
    )
    key_heads = split_heads(all_keys)
    value_heads = split_heads(all_values)
    attended, self_log = attend_forward(queries, key_heads, value_heads, self_allowed, scaling)
    attended = attended.reshape(row_count, features).astype(jnp.bfloat16)
    first_pre = alpha_scale * token_rows.astype(jnp.float32) + project(attended, self_out)
    first, first_pull = jax.vjp(layer_norm, first_pre, gains[0], biases[0])
    first_low = first.astype(jnp.bfloat16)
    cross_queries = split_heads(
        project(first_low, cross_query)
        .astype(jnp.bfloat16)
        .reshape(group_size, local_len, features)
    )
    own_memory = memory.reshape(-1, features)
    memory_all = lax.all_gather(memory, "seq", axis=1, tiled=True)
    memory_rows = memory_all.reshape(-1, features)
    cross_keys = (
        project(memory_rows, cross_key).astype(jnp.bfloat16).reshape(group_size, -1, features)
    )
    cross_values = (
        project(memory_rows, cross_value).astype(jnp.bfloat16).reshape(group_size, -1, features)
    )
    cross_key_heads = split_heads(cross_keys)
    cross_value_heads = split_heads(cross_values)
    cross_attended, cross_log = attend_forward(
        cross_queries, cross_key_heads, cross_value_heads, cross_allowed, scaling
    )
    cross_attended = cross_attended.reshape(row_count, features).astype(jnp.bfloat16)
    second_pre = alpha_scale * first + project(cross_attended, cross_out)
    second, second_pull = jax.vjp(layer_norm, second_pre, gains[1], biases[1])
    second_low = second.astype(jnp.bfloat16)
    upward = project(second_low, expand_weight)
    active, gelu_pull = jax.vjp(jax.nn.gelu, upward)
    active_low = active.astype(jnp.bfloat16)
    third_pre = alpha_scale * second + project(active_low, shrink_weight)
    final, third_pull = jax.vjp(layer_norm, third_pre, gains[2], biases[2])
    third_grad, gain_third, bias_third = third_pull(
        out_grad.reshape(row_count, features).astype(jnp.float32)
    )
    branch_grad = third_grad.astype(jnp.bfloat16)
    shrink_grad = weight_term(active_low, branch_grad)
    (up_grad,) = gelu_pull(project_back(branch_grad, shrink_weight))
    up_low = up_grad.astype(jnp.bfloat16)
    expand_grad = weight_term(second_low, up_low)
    second_grad = alpha_scale * third_grad + project_back(up_low, expand_weight)
    second_pre_grad, gain_second, bias_second = second_pull(second_grad)
    cross_branch = second_pre_grad.astype(jnp.bfloat16)
    cross_out_grad = weight_term(cross_attended, cross_branch)
    cross_attended_grad = split_heads(
        project_back(cross_branch, cross_out)
        .astype(jnp.bfloat16)
        .reshape(group_size, local_len, features)
    )
    cross_q_grad, cross_scores, cross_probs = attend_backward(
        cross_queries,
        cross_key_heads,
        cross_value_heads,
        cross_allowed,
        scaling,
        cross_log,
        cross_attended_grad,
    )
    cross_q_low = cross_q_grad.reshape(row_count, features).astype(jnp.bfloat16)
    cross_query_grad = weight_term(first_low, cross_q_low)
    key_term = (
        jnp.einsum(
            "ghqk,gqhd->gkhd", cross_scores, cross_queries, preferred_element_type=jnp.float32
        )
        * scaling
    ).reshape(group_size, -1, features)
    value_term = jnp.einsum(
        "ghqk,gqhd->gkhd", cross_probs, cross_attended_grad, preferred_element_type=jnp.float32
    ).reshape(group_size, -1, features)
    key_summed, value_summed = (
        lax.psum_scatter(
            key_term.astype(jnp.bfloat16), "seq", scatter_dimension=1, tiled=True
        ).astype(jnp.float32),
        lax.psum_scatter(
            value_term.astype(jnp.bfloat16), "seq", scatter_dimension=1, tiled=True
        ).astype(jnp.float32),
    )
    key_low = key_summed.reshape(-1, features).astype(jnp.bfloat16)
    value_low = value_summed.reshape(-1, features).astype(jnp.bfloat16)
    cross_key_grad = weight_term(own_memory, key_low)
    cross_value_grad = weight_term(own_memory, value_low)
    memory_grad = (project_back(key_low, cross_key) + project_back(value_low, cross_value)).reshape(
        memory.shape
    )
    first_grad = alpha_scale * second_pre_grad + project_back(cross_q_low, cross_query)
    first_pre_grad, gain_first, bias_first = first_pull(first_grad)
    self_branch = first_pre_grad.astype(jnp.bfloat16)
    self_out_grad = weight_term(attended, self_branch)
    attended_grad = split_heads(
        project_back(self_branch, self_out)
        .astype(jnp.bfloat16)
        .reshape(group_size, local_len, features)
    )
    self_q_grad, self_scores, self_probs = attend_backward(
        queries, key_heads, value_heads, self_allowed, scaling, self_log, attended_grad
    )
    count = local_len * lax.axis_size("seq")
    key_part = (
        jnp.einsum("ghqk,gqhd->kghd", self_scores, queries, preferred_element_type=jnp.float32)
        * scaling
    )
    value_part = jnp.einsum(
        "ghqk,gqhd->kghd", self_probs, attended_grad, preferred_element_type=jnp.float32
    )
    pair_summed = lax.psum_scatter(
        jnp.concatenate(
            [
                key_part.reshape(count, group_size, features),
                value_part.reshape(count, group_size, features),
            ],
            axis=2,
        ).astype(jnp.bfloat16),
        "seq",
        scatter_dimension=0,
        tiled=True,
    ).astype(jnp.float32)
    key_grad = (
        pair_summed[:, :, :features]
        .astype(jnp.bfloat16)
        .transpose(1, 0, 2)
        .reshape(row_count, features)
    )
    value_grad = (
        pair_summed[:, :, features:]
        .astype(jnp.bfloat16)
        .transpose(1, 0, 2)
        .reshape(row_count, features)
    )
    query_low = self_q_grad.reshape(row_count, features).astype(jnp.bfloat16)
    self_query_grad = weight_term(token_rows, query_low)
    self_key_grad = weight_term(token_rows, key_grad)
    self_value_grad = weight_term(token_rows, value_grad)
    input_grad = (
        alpha_scale * first_pre_grad
        + project_back(query_low, self_query)
        + project_back(key_grad, self_key)
        + project_back(value_grad, self_value)
    )
    gains_grad = jnp.stack([gain_first, gain_second, gain_third])
    biases_grad = jnp.stack([bias_first, bias_second, bias_third])
    gradients = (
        self_query_grad,
        self_key_grad,
        self_value_grad,
        self_out_grad,
        cross_query_grad,
        cross_key_grad,
        cross_value_grad,
        cross_out_grad,
        expand_grad,
        shrink_grad,
        gains_grad,
        biases_grad,
    )
    result = final.astype(jnp.bfloat16).reshape(group_size, local_len, features)
    return (result, input_grad.reshape(group_size, local_len, features), memory_grad, gradients)


def shards(
    tokens,
    memory,
    lengths,
    memory_segments,
    out_grad,
    self_query,
    self_key,
    self_value,
    self_out,
    cross_query,
    cross_key,
    cross_value,
    cross_out,
    expand_weight,
    shrink_weight,
    norm_gains,
    norm_biases,
):
    group_size = tokens.shape[0] // MB
    outputs = []
    input_grads = []
    memory_grads = []
    totals = None
    for batch_index in range(MB):
        gathered = (
            lax.all_gather(self_query, ("dp", "seq"), axis=0, tiled=True),
            lax.all_gather(self_key, ("dp", "seq"), axis=0, tiled=True),
            lax.all_gather(self_value, ("dp", "seq"), axis=0, tiled=True),
            lax.all_gather(self_out, ("dp", "seq"), axis=0, tiled=True),
            lax.all_gather(cross_query, ("dp", "seq"), axis=0, tiled=True),
            lax.all_gather(cross_key, ("dp", "seq"), axis=0, tiled=True),
            lax.all_gather(cross_value, ("dp", "seq"), axis=0, tiled=True),
            lax.all_gather(cross_out, ("dp", "seq"), axis=0, tiled=True),
            lax.all_gather(expand_weight, ("dp", "seq"), axis=0, tiled=True),
            lax.all_gather(shrink_weight, ("dp", "seq"), axis=0, tiled=True),
            lax.all_gather(norm_gains, ("dp", "seq"), axis=1, tiled=True),
            lax.all_gather(norm_biases, ("dp", "seq"), axis=1, tiled=True),
        )
        start = batch_index * group_size
        stop = start + group_size
        result, input_grad, memory_grad, gradients = micro_batch(
            gathered,
            tokens[start:stop],
            memory[start:stop],
            lengths[start:stop],
            memory_segments[start:stop],
            out_grad[start:stop],
        )
        outputs.append(result)
        input_grads.append(input_grad)
        memory_grads.append(memory_grad)
        if totals is None:
            totals = gradients
        else:
            totals = tuple((running + gradient for running, gradient in zip(totals, gradients)))
    summed = (
        lax.psum_scatter(totals[0], ("dp", "seq"), scatter_dimension=0, tiled=True),
        lax.psum_scatter(totals[1], ("dp", "seq"), scatter_dimension=0, tiled=True),
        lax.psum_scatter(totals[2], ("dp", "seq"), scatter_dimension=0, tiled=True),
        lax.psum_scatter(totals[3], ("dp", "seq"), scatter_dimension=0, tiled=True),
        lax.psum_scatter(totals[4], ("dp", "seq"), scatter_dimension=0, tiled=True),
        lax.psum_scatter(totals[5], ("dp", "seq"), scatter_dimension=0, tiled=True),
        lax.psum_scatter(totals[6], ("dp", "seq"), scatter_dimension=0, tiled=True),
        lax.psum_scatter(totals[7], ("dp", "seq"), scatter_dimension=0, tiled=True),
        lax.psum_scatter(totals[8], ("dp", "seq"), scatter_dimension=0, tiled=True),
        lax.psum_scatter(totals[9], ("dp", "seq"), scatter_dimension=0, tiled=True),
        lax.psum_scatter(totals[10], ("dp", "seq"), scatter_dimension=1, tiled=True),
        lax.psum_scatter(totals[11], ("dp", "seq"), scatter_dimension=1, tiled=True),
    )
    return (
        jnp.concatenate(outputs, 0),
        jnp.concatenate(input_grads, 0),
        jnp.concatenate(memory_grads, 0),
        summed[0],
        summed[1],
        summed[2],
        summed[3],
        summed[4],
        summed[5],
        summed[6],
        summed[7],
        summed[8],
        summed[9],
        summed[10],
        summed[11],
    )


MESH = pl.DeviceIdType.MESH
BF = jnp.bfloat16
F32 = jnp.float32
ALL = slice(None)
D = 1024
LEN = 128
OWN = 2 * LEN
SPAN = 8 * LEN
MEM = 128
KEY, VALUE, QUERY, OUT, CROSS_QUERY, CROSS_KEY, CROSS_VALUE, CROSS_OUT = range(8)
EXPAND = 8
SQUARE = 12
UNITS = 16
GRID = (2, 2, 4, 2)
SQUARE_SHAPE = (SQUARE, *GRID, 32, D)
SHRINK_SHAPE = (UNITS - SQUARE, *GRID, LEN, OWN)
VMEM_BYTES = 60 << 20
GELU_SLOPE = (2.0 / 3.141592653589793) ** 0.5
GELU_CUBE = 0.044715


class Place:
    def __init__(self):
        dp, seq = lax.axis_index("dp"), lax.axis_index("seq")
        self.x, self.y, self.core, self.z, self.seq = dp % 2, dp // 2, seq % 2, seq // 2, seq
        self.group = self.z // 2
        self.low = seq % 4
        self.mate_z = self.z + 1 - 2 * (self.z % 2)
        self.inner_z = 2 - self.group
        self.next_z = (self.z + 2) % 4
        self.inner = self.z % 3 != 0
        self.outer = self.z % 3 == 0

    def at(self, y=None, x=None, z=None, core=None):
        y = self.y if y is None else y
        x = self.x if x is None else x
        z = self.z if z is None else z
        core = self.core if core is None else core
        return (y * 2 + x, z * 2 + core)

    def across(self, axis):
        if axis == "x":
            return self.at(x=1 - self.x)
        if axis == "y":
            return self.at(y=1 - self.y)
        return self.at(core=1 - self.core)

    def along_z(self, step):
        return self.at(z=(self.z + step) % 4)

    def mate(self):
        return self.at(z=self.mate_z)

    def greet(self):
        barrier = pltpu.get_barrier_semaphore()
        peers = [self.across(axis) for axis in ("x", "y", "core")]
        peers += [self.along_z(step) for step in (1, 2, 3)]
        for peer in peers:
            pl.semaphore_signal(barrier, inc=1, device_id=peer, device_id_type=MESH)
        pl.semaphore_wait(barrier, len(peers))


def under(when, act):
    if when is None:
        act()
    else:
        pl.when(when)(act)


class Links:
    def __init__(self, place, send_sem, recv_sem):
        self.place, self.send_sem, self.recv_sem = place, send_sem, recv_sem
        self.sends, self.slots = 0, 0
        self.open = {}

    def slot(self, count=1):
        first = self.slots
        self.slots += count
        assert self.slots <= self.recv_sem.shape[0]
        return first

    def send(self, slot, source, target, device, when=None):
        assert self.sends < self.send_sem.shape[0]
        step = pltpu.make_async_remote_copy(
            src_ref=source,
            dst_ref=target,
            send_sem=self.send_sem.at[self.sends],
            recv_sem=self.recv_sem.at[slot],
            device_id=device,
            device_id_type=MESH,
        )
        under(when, step.start)
        self.sends += 1
        self.open[id(step)] = step, when
        return step

    def arrived(self, slot, target):
        pltpu.make_async_remote_copy(
            src_ref=target,
            dst_ref=target,
            send_sem=self.send_sem.at[0],
            recv_sem=self.recv_sem.at[slot],
            device_id=self.place.across("core"),
            device_id_type=MESH,
        ).wait_recv()

    def sent(self, step):
        step, when = self.open.pop(id(step))
        under(when, step.wait_send)

    def finish(self):
        for step, when in self.open.values():
            under(when, step.wait_send)
        self.open = {}


class Moves:
    def __init__(self, sem):
        self.sem, self.count, self.open = sem, 0, {}

    def start(self, source, target):
        assert self.count < self.sem.shape[0]
        step = pltpu.make_async_copy(source, target, self.sem.at[self.count])
        step.start()
        self.count += 1
        self.open[id(step)] = step
        return step

    def wait(self, step):
        self.open.pop(id(step)).wait()

    def finish(self):
        for step in self.open.values():
            step.wait()
        self.open = {}


def all_sum(links, part, total, work):
    place = links.place
    work[0] = part[...]
    for number, axis in enumerate(("core", "y", "x")):
        slot = links.slot()
        step = links.send(slot, work.at[0], work.at[1 + number], place.across(axis))
        yield
        links.arrived(slot, work.at[1 + number])
        links.sent(step)
        work[0] = work[0] + work[1 + number]
    slot = links.slot(4)
    for k in (1, 2, 3):
        links.send(slot + place.z, work.at[0], work.at[4 + place.z], place.along_z(k))
    yield
    result = work[0]
    for k in (1, 2, 3):
        source = (place.z + k) % 4
        links.arrived(slot + source, work.at[4 + source])
        result = result + work[4 + source]
    total[...] = result
    yield


def loop(count):
    return pl.loop(0, count)


def tile(index, size):
    return pl.ds(pl.multiple_of(index * size, size), size)


def rows_times(left, right, store, rows=OWN, width=256):
    for first in range(0, left.shape[0], rows):

        @loop(D // width)
        def _(index):
            columns = tile(index, width)
            store(pl.ds(first, rows), columns, jnp.dot(left[pl.ds(first, rows), :], right[:, columns], preferred_element_type=F32))


def rows_back(left, right, store, width=256):
    @loop(D // width)
    def _(index):
        columns = tile(index, width)
        store(columns, project_back(left[...], right[columns, :]))


def put(target, dtype=BF):
    def store(rows, columns, value):
        target[rows, columns] = value.astype(dtype)

    return store


def half_masks():
    lane = lax.broadcasted_iota(jnp.int32, (1, LEN), 1)
    return [(lane < HD).astype(F32), (lane >= HD).astype(F32)]


def attend_rows(queries, keys, values, bias, logs, out, segments, pairs=H // 2, first_pair=0):
    masks = half_masks()

    @loop(pairs)
    def _(step):
        pair = step + first_pair
        columns = tile(pair, LEN)
        for first, rows, count in segments:
            own = pl.ds(first, rows)
            key, value = keys[pl.ds(0, count), columns], values[pl.ds(0, count), columns]
            query = queries[own, columns]
            lane = lax.broadcasted_iota(jnp.int32, (rows, LEN), 1)
            parts = []
            for half in (0, 1):
                scores = project_back(query * (masks[half] * HD**-0.5).astype(BF), key) + bias[own, pl.ds(0, count)]
                top = jnp.max(scores, axis=1, keepdims=True)
                powers = jnp.exp(scores - top)
                total = jnp.sum(powers, axis=1, keepdims=True)
                parts.append(project((powers * (1.0 / total)).astype(BF), value))
                logs[own, :] = jnp.where(lane == 2 * pair + half, top + jnp.log(total), logs[own, :])
            out[own, columns] = jnp.where(lane < HD, parts[0], parts[1]).astype(BF)


def attend_rows_back(queries, keys, values, bias, logs, grads, query_grads, key_grads, value_grads, segments, pairs, first_pair=0):
    masks = half_masks()

    @loop(pairs)
    def _(step):
        pair = step + first_pair
        columns = tile(pair, LEN)
        for number, (first, rows, count) in enumerate(segments):
            own, met = pl.ds(first, rows), pl.ds(0, count)
            key, value = keys[met, columns], values[met, columns]
            lane = lax.broadcasted_iota(jnp.int32, (rows, LEN), 1)
            halves, score_lows, prob_lows, query_parts, grad_parts = [], [], [], [], []
            for half in (0, 1):
                query = queries[own, columns] * (masks[half] * HD**-0.5).astype(BF)
                grad = grads[own, columns] * masks[half].astype(BF)
                log_total = jnp.sum(jnp.where(lane == 2 * pair + half, logs[own, :], 0.0), axis=1, keepdims=True)
                probs = jnp.exp(project_back(query, key) + bias[own, met] - log_total)
                prob_grad = project_back(grad, value)
                score_grad = probs * (prob_grad - jnp.sum(prob_grad * probs, axis=1, keepdims=True))
                score_low = score_grad.astype(BF)
                halves.append(project(score_low, key) * HD**-0.5)
                score_lows.append(score_low)
                prob_lows.append(probs.astype(BF))
                query_parts.append(query)
                grad_parts.append(grad)
            query_grads[own, columns] = jnp.where(lane < HD, halves[0], halves[1]).astype(BF)
            key_term = weight_term(jnp.concatenate(score_lows), jnp.concatenate(query_parts))
            value_term = weight_term(jnp.concatenate(prob_lows), jnp.concatenate(grad_parts))
            if number == 0:
                key_grads[met, columns] = key_term.astype(BF)
                value_grads[met, columns] = value_term.astype(BF)
            else:
                key_grads[met, columns] = (key_grads[met, columns].astype(F32) + key_term).astype(BF)
                value_grads[met, columns] = (value_grads[met, columns].astype(F32) + value_term).astype(BF)


SELF_SEGMENTS = ((LEN, LEN, SPAN), (0, LEN, SPAN // 2))
CROSS_SEGMENTS = ((0, OWN, MEM),)
STEP = 32


def norm_rows(read, normal, inverse, emit):
    @loop(OWN // STEP)
    def _(index):
        rows = tile(index, STEP)
        value = read(rows)
        centred = value - jnp.mean(value, axis=1, keepdims=True)
        scale = lax.rsqrt(jnp.mean(centred * centred, axis=1, keepdims=True) + norm_eps)
        result = centred * scale
        if normal is not None:
            normal[rows, :] = result
            inverse[rows, :] = jnp.broadcast_to(scale, (STEP, LEN))
        emit(rows, result, scale)


def norm_rows_back(grad, normal, scale, gain, sums, number):
    sums[pl.ds(number, 1), :] += jnp.sum(grad * normal, axis=0, keepdims=True)
    sums[pl.ds(3 + number, 1), :] += jnp.sum(grad, axis=0, keepdims=True)
    scaled = grad * gain
    return scale * (
        scaled
        - jnp.mean(scaled, axis=1, keepdims=True)
        - normal * jnp.mean(scaled * normal, axis=1, keepdims=True)
    )


class Gather:
    WIDE = (6, 7, 8, 10, 11, 12, 13, 14, 15)
    EARLY = 3
    RELAY = 1
    ROUTES = {False: ("zxy", "zyx"), True: ("xzy", "yzx")}
    TIMES = {False: (-3, 0, 1, 2, 3), True: (-20, -3, 1, 2, 3)}
    SLOTS = 10

    def __init__(self, links, moves, own, square, shrink):
        self.links, self.moves, self.own, self.square, self.shrink = links, moves, own, square, shrink
        self.first_slot = links.slot(UNITS * 2 * self.SLOTS)
        self.local = {}
        for unit in range(UNITS):
            target = self.block(unit, links.place.y, links.place.x, links.place.z, links.place.core)
            self.local[unit] = moves.start(own(unit), target)
        self.now = -self.EARLY
        self.steps = {}
        for number, unit in enumerate(range(UNITS)):
            wide = number in self.WIDE
            for half in (0, 1):
                for phase, time in enumerate(self.TIMES[wide]):
                    step = (phase, number, unit, half, self.ROUTES[wide][half])
                    self.steps.setdefault(max(number + time, self.now), []).append(step)
                step = (-1, number, unit, half, self.ROUTES[wide][half])
                self.steps.setdefault(max(number - self.RELAY, self.now + 1), []).append(step)

    def block(self, unit, *index):
        if unit < SQUARE:
            return self.square.at[(unit,) + index]
        return self.shrink.at[(unit - SQUARE,) + index]

    def tick(self):
        for phase, _, unit, half, route in sorted(self.steps.pop(self.now, ())):
            self.move(phase, unit, half, route)
        self.now += 1

    def move(self, phase, unit, half, route):
        links, place = self.links, self.links.place
        here = {"y": place.y, "x": place.x, "z": place.z}
        slot = self.first_slot + (2 * unit + half) * self.SLOTS
        depth = 16 if unit < SQUARE else 64
        rows = pl.ds(depth * half, depth)
        turn = route.index("z")

        def part(where, core):
            return self.block(unit, where["y"], where["x"], where["z"], core, rows)

        def reached(count):
            return {**here, **{axis: ALL for axis in route[:count]}}

        def incoming(count):
            axis = route[count]
            if axis == "z":
                return reached(count + 1)
            return {**reached(count), axis: 1 - here[axis]}

        def line(source):
            return part({**reached(turn), "z": source}, place.core)

        if phase == -1:
            def hand_on():
                links.arrived(slot + place.next_z, line(place.next_z))

            under(place.inner, hand_on)
            links.send(slot + place.next_z, line(place.next_z), line(place.next_z), place.mate(), place.inner)
            return
        if phase == 1 and unit in self.local:
            self.moves.wait(self.local.pop(unit))
        if 1 <= phase <= 3:
            if phase - 1 == turn:
                links.arrived(slot + place.mate_z, line(place.mate_z))
                for source, when in ((place.next_z, place.outer), ((6 - place.z - place.mate_z - place.next_z), None)):
                    under(when, functools.partial(links.arrived, slot + source, line(source)))
            else:
                links.arrived(slot + 3 + phase, part(incoming(phase - 1), place.core))
        if phase < 3:
            source = self.own(unit).at[rows] if phase == 0 else part(reached(phase), place.core)
            target = part(reached(phase), place.core)
            if phase == turn:
                links.send(slot + place.z, source, target, place.mate())
                links.send(slot + place.z, source, target, place.at(z=place.inner_z))
                links.send(slot + place.z, source, target, place.at(z=place.next_z), place.inner)
            else:
                links.send(slot + 4 + phase, source, target, place.across(route[phase]))
        if 1 <= phase <= 3 and phase > turn:
            fresh = part(incoming(phase - 1), place.core)
            links.send(slot + 6 + phase, fresh, fresh, place.across("core"))
        if phase == 4:
            for number in range(turn, 3):
                links.arrived(slot + 7 + number, part(incoming(number), 1 - place.core))


def core_rows(core, count=OWN):
    return pl.ds(pl.multiple_of(core * count, count), count)


def block_rows(block):
    return pl.ds(pl.multiple_of(block * LEN, LEN), LEN)


FORWARD_SAVES = {
    "queries": ((OWN, D), BF),
    "keys": ((SPAN, D), BF),
    "values": ((SPAN, D), BF),
    "self_bias": ((OWN, SPAN), F32),
    "self_logs": ((OWN, LEN), F32),
    "normal_one": ((OWN, D), F32),
    "inverse_one": ((OWN, LEN), F32),
    "cross_queries": ((OWN, D), BF),
    "cross_keys": ((MEM, D), BF),
    "cross_values": ((MEM, D), BF),
    "cross_bias": ((OWN, MEM), F32),
    "cross_logs": ((OWN, LEN), F32),
    "normal_two": ((OWN, D), F32),
    "inverse_two": ((OWN, LEN), F32),
    "slopes": ((4, OWN, D), BF),
    "third_grad": ((OWN, D), F32),
    "norm_sums": ((8, D), F32),
    "gains": ((8, D), F32),
    "final_low": ((OWN, D), BF),
}
TURNED_SAVES = {
    "tokens_t": ((16, 32, 2 * OWN), BF),
    "attended_t": ((16, 32, 2 * OWN), BF),
    "first_t": ((16, 32, 2 * OWN), BF),
    "cross_t": ((16, 32, 2 * OWN), BF),
    "second_t": ((16, 32, 2 * OWN), BF),
    "active_t": ((4, 4, 4, 32, 2 * OWN), BF),
    "memory_t": ((16, 32, MEM), BF),
    "branch": ((2 * OWN, D), BF),
}
FORWARD_SCRATCH = {
    "stream": ((SPAN, D), BF),
    "mine": ((OWN, D), BF),
    "context": ((4, 2, 16, D), BF),
    "attended": ((OWN, D), BF),
    "first_low": ((OWN, D), BF),
    "cross_attended": ((OWN, D), BF),
    "second_low": ((OWN, D), BF),
    "active": ((4, OWN, D), BF),
    "sums": ((OWN, D), F32),
    "cotangent": ((OWN, D), BF),
    "branch_own": ((OWN, D), BF),
    "weights": ((4, D, D), BF),
    "shrink_in": ((2, 4, D, OWN), BF),
    "turned": ((3, 16, 2, 32, OWN), BF),
    "turned_active": ((2, 4, 2, 4, 32, OWN), BF),
    "turned_memory": ((16, 2, 32, MEM), BF),
    "work": ((8, 8, D), F32),
}
FORWARD_SENDS, FORWARD_SLOTS, FORWARD_MOVES = 352, 384, 96


class Refs:
    def __init__(self, names, refs):
        for name, ref in zip(names, refs):
            setattr(self, name, ref)


def forward_kernel(lengths, segments, norms, tokens, memory, out_grad, *refs):
    squares, expand_own, shrink_own = refs[:8], refs[8], refs[9]
    square, shrink = refs[10:12]
    rest = refs[12:]
    kept = Refs(FORWARD_SAVES, rest[: len(FORWARD_SAVES)])
    rest = rest[len(FORWARD_SAVES) :]
    turned = Refs(TURNED_SAVES, rest[: len(TURNED_SAVES)])
    rest = rest[len(TURNED_SAVES) :]
    held = Refs(FORWARD_SAVES, rest[: len(FORWARD_SAVES)])
    rest = rest[len(FORWARD_SAVES) :]
    held.__dict__.update(Refs(FORWARD_SCRATCH, rest[: len(FORWARD_SCRATCH)]).__dict__)
    send_sem, recv_sem, move_sem = rest[len(FORWARD_SCRATCH) :]

    place = Place()
    links, moves = Links(place, send_sem, recv_sem), Moves(move_sem)
    y, x, z, core, group, low, seq = place.y, place.x, place.z, place.core, place.group, place.low, place.seq
    partner = place.across("core")
    opposite = place.along_z(2)
    mate = place.mate()
    place.greet()

    def own(unit):
        if unit < EXPAND:
            return squares[unit]
        if unit < SQUARE:
            return expand_own.at[:, pl.ds(D * (unit - EXPAND), D)]
        return shrink_own.at[:, pl.ds(OWN * (unit - SQUARE), OWN)]

    stream = held.stream
    far, mate_seq = (seq + 4) % 8, (seq + 2) % 4 + 4 * group
    other_seq = 2 * z + 1 - core
    other_mate = (other_seq + 2) % 4 + 4 * group
    slot_far, slot_mate, slot_mate_far, slot_core = links.slot(), links.slot(), links.slot(), links.slot(4)
    home = moves.start(tokens.at[group], stream.at[block_rows(seq)])
    gather = Gather(links, moves, own, square, shrink)
    for _ in range(Gather.EARLY):
        gather.tick()
    links.send(slot_far, tokens.at[1 - group], stream.at[block_rows(seq)], opposite)
    links.send(slot_mate, tokens.at[group], stream.at[block_rows(seq)], mate)
    links.send(slot_core, tokens.at[group], stream.at[block_rows(seq)], partner)
    slot_memory, slot_context = links.slot(4), links.slot()
    context_home = moves.start(memory.at[group], held.context.at[z, core])
    for k in (1, 2, 3):
        links.send(slot_memory + z, memory.at[((z + k) % 4) // 2], held.context.at[z, core], place.along_z(k))
    norm_steps = all_sum(links, norms, held.gains, held.work)
    next(norm_steps)

    def sentence(places):
        result, end = jnp.zeros_like(places), 0
        for index in range(lengths.shape[1] - 1):
            end = end + lengths[group, index]
            result = result + (places >= end).astype(jnp.int32)
        return result

    held.norm_sums[...] = jnp.zeros_like(held.norm_sums)
    held.self_logs[...] = jnp.zeros_like(held.self_logs)
    held.cross_logs[...] = jnp.zeros_like(held.cross_logs)

    @loop(OWN // STEP)
    def _(index):
        row = index * STEP + lax.broadcasted_iota(jnp.int32, (STEP, 1), 0)
        row_place = LEN * low + row + jnp.where(row >= LEN, 3 * LEN, 0)
        row_sentence = sentence(row_place)
        key_place = lax.broadcasted_iota(jnp.int32, (1, SPAN), 1)
        allowed = (row_sentence == sentence(key_place)) & (key_place <= row_place)
        held.self_bias[tile(index, STEP), :] = jnp.where(allowed, 0.0, masked_score)
        met = row_sentence == segments[pl.ds(group, 1), :]
        held.cross_bias[tile(index, STEP), :] = jnp.where(met, 0.0, masked_score)

    def pass_on(number, block):
        links.send(slot_core + number, stream.at[block_rows(block)], stream.at[block_rows(block)], partner)

    gather.tick()
    next(norm_steps)
    gather.tick()
    next(norm_steps)
    gather.tick()
    links.arrived(slot_far, stream.at[block_rows(far)])
    links.send(slot_mate_far, stream.at[block_rows(far)], stream.at[block_rows(far)], mate)
    pass_on(1, far)
    gather.tick()
    links.arrived(slot_mate, stream.at[block_rows(mate_seq)])
    pass_on(2, mate_seq)
    moves.wait(context_home)
    for k in (1, 2, 3):
        links.arrived(slot_memory + (z + k) % 4, held.context.at[(z + k) % 4, core])
    links.send(slot_context, held.context.at[:, core], held.context.at[:, core], partner)
    next(norm_steps)
    gather.tick()
    links.arrived(slot_mate_far, stream.at[block_rows((mate_seq + 4) % 8)])
    pass_on(3, (mate_seq + 4) % 8)
    gather.tick()
    cotangent_rows, cotangent_far = block_rows(group), block_rows(1 - group)
    slot_cotangent = links.slot()
    cotangent_home = moves.start(out_grad.at[group], held.cotangent.at[cotangent_rows])
    links.send(slot_cotangent, out_grad.at[1 - group], held.cotangent.at[cotangent_rows], opposite)
    moves.wait(home)
    for number, block in enumerate((other_seq, (other_seq + 4) % 8, other_mate, (other_mate + 4) % 8)):
        links.arrived(slot_core + number, stream.at[block_rows(block)])
    links.arrived(slot_context, held.context.at[:, 1 - core])
    held.mine[pl.ds(0, LEN), :] = stream[block_rows(low), :]
    held.mine[pl.ds(LEN, LEN), :] = stream[block_rows(low + 4), :]

    loads = {}

    def fetch(unit, slot):
        if unit < SQUARE:
            target = held.weights.at[slot]
            loads[unit] = (moves.start(square.at[unit].reshape(D, D), target), target)
        else:
            target = held.shrink_in.at[slot]
            loads[unit] = (moves.start(shrink.at[unit - SQUARE].reshape(4, D, OWN), target), target)

    def weight(unit):
        step, target = loads.pop(unit)
        moves.wait(step)
        return target

    turning = {"count": 0, "open": {}}
    landing = []
    mine, theirs = core_rows(core), core_rows(1 - core)

    def turn(source, name):
        number = turning["count"] % 3
        for move, sent in turning["open"].pop(number, ()):
            moves.wait(move)
            links.sent(sent)
        turning["count"] += 1
        buffer, target = held.turned.at[number], getattr(turned, name)

        @loop(4)
        def _(index):
            buffer[pl.ds(4 * index, 4)] = source[:, tile(index, OWN)].T.reshape(4, 2, 32, OWN)

        slot = links.slot()
        move = moves.start(buffer.at[:, core], target.at[:, :, mine])
        sent = links.send(slot, buffer.at[:, 1 - core], target.at[:, :, mine], partner)
        landing.append((slot, target.at[:, :, theirs]))
        turning["open"][number] = [(move, sent)]

    def keep(*names):
        for name in names:
            moves.start(getattr(held, name), getattr(kept, name))

    def gain(number):
        return held.gains[pl.ds(number, 1), :]

    def bias(number):
        return held.gains[pl.ds(3 + number, 1), :]

    fetch(KEY, 0)
    turn(held.mine, "tokens_t")
    next(norm_steps)
    fetch(VALUE, 1)
    rows_times(stream, weight(KEY), put(held.keys))
    gather.tick()
    fetch(QUERY, 2)
    rows_times(stream, weight(VALUE), put(held.values))
    rows_times(held.mine, weight(QUERY), put(held.queries))

    def attend_part(first, pairs):
        attend_rows(
            held.queries, held.keys, held.values, held.self_bias, held.self_logs, held.attended, SELF_SEGMENTS, pairs, first
        )

    fetch(OUT, 3)
    attend_part(0, 3)
    gather.tick()
    fetch(CROSS_QUERY, 0)
    attend_part(3, 3)
    gather.tick()
    fetch(CROSS_KEY, 1)
    attend_part(6, 2)
    rows_times(held.attended, weight(OUT), put(held.sums, F32))
    keep("queries", "keys", "values", "self_bias", "self_logs", "cross_bias", "gains")

    def first_rows(rows, result, _):
        held.first_low[rows, :] = (result * gain(0) + bias(0)).astype(BF)

    def after(rows, previous):
        return held.sums[rows, :] + alpha_scale * previous

    norm_rows(lambda rows: after(rows, held.mine[rows, :].astype(F32)), held.normal_one, held.inverse_one, first_rows)
    turn(held.attended, "attended_t")
    rows_times(held.first_low, weight(CROSS_QUERY), put(held.cross_queries))
    context = held.context.reshape(MEM, D)
    rows_times(context, weight(CROSS_KEY), put(held.cross_keys), MEM)
    gather.tick()
    fetch(CROSS_VALUE, 2)
    turn(held.first_low, "first_t")

    @loop(4)
    def _(index):
        held.turned_memory[pl.ds(4 * index, 4)] = context[:, tile(index, OWN)].T.reshape(4, 2, 32, MEM)

    moves.start(held.turned_memory.at[:, core], turned.memory_t)
    rows_times(context, weight(CROSS_VALUE), put(held.cross_values), MEM)
    attend_rows(
        held.cross_queries, held.cross_keys, held.cross_values, held.cross_bias, held.cross_logs,
        held.cross_attended, CROSS_SEGMENTS,
    )
    gather.tick()
    fetch(CROSS_OUT, 3)
    keep("cross_queries", "cross_keys", "cross_values", "cross_logs", "normal_one", "inverse_one")
    rows_times(held.cross_attended, weight(CROSS_OUT), put(held.sums, F32))

    def second_rows(rows, result, _):
        held.second_low[rows, :] = (result * gain(1) + bias(1)).astype(BF)

    norm_rows(
        lambda rows: after(rows, held.normal_one[rows, :] * gain(0) + bias(0)),
        held.normal_two, held.inverse_two, second_rows,
    )
    keep("normal_two", "inverse_two")
    gather.tick()
    turn(held.cross_attended, "cross_t")
    turn(held.second_low, "second_t")
    turned_open = {}
    for part in range(4):
        if part > 0:
            gather.tick()
        fetch(EXPAND + part, part)
        active, slopes = held.active.at[part], held.slopes.at[part]

        def activate(rows, columns, value):
            inner = GELU_SLOPE * (value + GELU_CUBE * value * value * value)
            bend = jnp.tanh(inner)
            active[rows, columns] = (0.5 * value * (1.0 + bend)).astype(BF)
            slope = 0.5 * (1.0 + bend) + 0.5 * value * (1.0 - bend * bend) * (
                GELU_SLOPE * (1.0 + 3.0 * GELU_CUBE * value * value)
            )
            slopes[rows, columns] = slope.astype(BF)

        rows_times(held.second_low, weight(EXPAND + part), activate)
        number = part % 2
        for move, sent in turned_open.pop(number, ()):
            moves.wait(move)
            links.sent(sent)
        buffer = held.turned_active.at[number]

        @loop(4)
        def _(index):
            buffer[index] = active[:, tile(index, OWN)].T.reshape(2, 4, 32, OWN)

        slot = links.slot()
        move = moves.start(buffer.at[:, core], turned.active_t.at[part, :, :, :, mine])
        sent = links.send(slot, buffer.at[:, 1 - core], turned.active_t.at[part, :, :, :, mine], partner)
        landing.append((slot, turned.active_t.at[part, :, :, :, theirs]))
        turned_open[number] = [(move, sent)]
    keep("slopes")
    for part in range(4):
        gather.tick()
        fetch(SQUARE + part, part % 2)
        shrink_part = weight(SQUARE + part)
        for first in (0, LEN):
            rows = pl.ds(first, LEN)
            total = project(held.active[0, rows, :], shrink_part[0])
            for depth in (1, 2, 3):
                total = total + project(held.active[depth, rows, :], shrink_part[depth])
            held.sums[rows, pl.ds(OWN * part, OWN)] = total
    links.arrived(slot_cotangent, held.cotangent.at[cotangent_far])
    moves.wait(cotangent_home)

    def third_rows(rows, result, scale):
        held.final_low[rows, :] = (result * gain(2) + bias(2)).astype(BF)
        grad = norm_rows_back(held.cotangent[rows, :].astype(F32), result, scale, gain(2), held.norm_sums, 2)
        held.third_grad[rows, :] = grad
        held.branch_own[rows, :] = grad.astype(BF)

    norm_rows(lambda rows: after(rows, held.normal_two[rows, :] * gain(1) + bias(1)), None, None, third_rows)
    slot = links.slot()
    links.send(slot, held.branch_own, turned.branch.at[mine], partner)
    landing.append((slot, turned.branch.at[theirs]))
    moves.start(held.branch_own, turned.branch.at[mine])
    keep("third_grad", "norm_sums", "final_low")
    for arrival in landing:
        links.arrived(*arrival)
    moves.finish()
    links.finish()


IN_VMEM = pl.BlockSpec(memory_space=pltpu.VMEM)
IN_SMEM = pl.BlockSpec(memory_space=pltpu.SMEM)
IN_PLACE = pl.BlockSpec(memory_space=pl.ANY)


def shapes_of(table):
    return [jax.ShapeDtypeStruct(shape, dtype) for shape, dtype in table.values()]


def vmem_of(table):
    return [pltpu.VMEM(shape, dtype) for shape, dtype in table.values()]


def forward_call(lengths, segments, norms, tokens, memory, out_grad, weights):
    results = [
        jax.ShapeDtypeStruct(SQUARE_SHAPE, BF),
        jax.ShapeDtypeStruct(SHRINK_SHAPE, BF),
        *shapes_of(FORWARD_SAVES),
        *shapes_of(TURNED_SAVES),
    ]
    values = pl.pallas_call(
        forward_kernel,
        in_specs=[IN_SMEM, IN_VMEM, IN_VMEM] + [IN_PLACE] * 13,
        out_specs=[IN_PLACE] * len(results),
        out_shape=results,
        scratch_shapes=[
            *vmem_of(FORWARD_SAVES),
            *vmem_of(FORWARD_SCRATCH),
            pltpu.SemaphoreType.DMA((FORWARD_SENDS,)),
            pltpu.SemaphoreType.DMA((FORWARD_SLOTS,)),
            pltpu.SemaphoreType.DMA((FORWARD_MOVES,)),
        ],
        compiler_params=pltpu.CompilerParams(collective_id=0, has_side_effects=True, vmem_limit_bytes=VMEM_BYTES),
    )(lengths, segments, norms, tokens, memory, out_grad, *weights)
    saves = dict(zip([*FORWARD_SAVES, *TURNED_SAVES], values[2:]))
    return values[0], values[1], saves


class Scatter:
    def __init__(self, links, grads, from_first, from_second, from_z, result):
        self.links, self.grads, self.result = links, grads, result
        self.from_first, self.from_second, self.from_z = from_first, from_second, from_z
        self.slots, self.pending, self.now = {}, {}, 0

    def home(self, unit):
        for step in self.pending.pop(unit - self.grads.shape[0], ()):
            self.links.sent(step)
        self.slots[unit] = self.links.slot(12)
        return self.grads.at[unit % self.grads.shape[0]]

    def add(self, total, part):
        for row in range(4):
            total[row] = (total[row].astype(F32) + part[row].astype(F32)).astype(BF)

    def phase(self, unit, half, number):
        links, place = self.links, self.links.place
        y, x, z = place.y, place.x, place.z
        here = self.grads.at[unit % self.grads.shape[0]]
        depth = unit % self.from_first.shape[0]
        rows = pl.ds(16 * half, 16)
        slot = self.slots[unit] + 6 * half
        by_y = half == 0
        first, second = ("y", "x") if by_y else ("x", "y")
        away = (1 - y, ALL) if by_y else (ALL, 1 - x)
        corner, other, mine = ((y, 1 - x), 1 - x, x) if by_y else ((1 - y, x), 1 - y, y)
        home = here.at[y, x, :, rows]
        first_in = self.from_first.at[depth, :, :, rows]
        second_in = self.from_second.at[depth, :, rows]

        def send(number, source, target, device):
            self.pending.setdefault(unit, []).append(links.send(slot + number, source, target, device))

        if number == 0:
            send(0, here.at[(*away, ALL, rows)], first_in, place.across(first))
        if number == 1:
            links.arrived(slot, first_in)
            corner_part = here.at[(*corner, ALL, rows)]
            self.add(corner_part, first_in.at[other])
            send(1, corner_part, second_in, place.across(second))
            self.add(home, first_in.at[mine])
        if number == 2:
            links.arrived(slot + 1, second_in)
            self.add(home, second_in)
            for k in (1, 2, 3):
                send(2 + z, home.at[(z + k) % 4], self.from_z.at[depth, z, rows], place.along_z(k))
        if number == 3:
            total = home[z].astype(F32)
            for k in (1, 2, 3):
                source = (z + k) % 4
                links.arrived(slot + 2 + source, self.from_z.at[depth, source, rows])
                total = total + self.from_z[depth, source, rows].astype(F32)
            self.result(unit, rows, total)

    def tick(self):
        for number in (0, 1, 2, 3):
            unit = self.now - number
            if 0 <= unit < UNITS:
                for half in (0, 1):
                    self.phase(unit, half, number)
        self.now += 1


DEPTH = 4
BACKWARD_SCRATCH = {
    "weights": ((3, D, D), BF),
    "shrink_in": ((4, D, OWN), BF),
    "grads": ((6, 2, 2, 4, 32, D), BF),
    "from_first": ((DEPTH, 2, 4, 32, D), BF),
    "from_second": ((DEPTH, 4, 32, D), BF),
    "from_z": ((DEPTH, 4, 32, D), BF),
    "up": ((4, 2 * OWN, D), BF),
    "second_sum": ((OWN, D), F32),
    "cross_branch": ((2 * OWN, D), BF),
    "attended_grad": ((OWN, D), BF),
    "cross_query_grad": ((2 * OWN, D), BF),
    "cross_terms": ((2, 2, MEM, D), BF),
    "cross_sums": ((2, MEM, D), BF),
    "self_branch": ((2 * OWN, D), BF),
    "query_grad": ((2 * OWN, D), BF),
    "terms": ((2, 2, 2, 2, LEN, D), BF),
    "terms_core": ((2, 2, 2, LEN, D), BF),
    "terms_mate": ((2, 2, LEN, D), BF),
    "key_grad": ((2 * OWN, D), BF),
    "value_grad": ((2 * OWN, D), BF),
    "memory_own": ((4, 16, D), BF),
    "memory_in": ((4, 16, D), BF),
    "far_own": ((LEN, D), BF),
    "far_in": ((LEN, D), BF),
    "work": ((8, 8, D), F32),
}
BACKWARD_SENDS, BACKWARD_SLOTS, BACKWARD_MOVES = 240, 256, 64


def backward_kernel(square, shrink, *refs):
    saved = [*FORWARD_SAVES, *TURNED_SAVES]
    names = [name for name in saved if name != "final_low"]
    kept = Refs(saved, refs[: len(saved)])
    rest = refs[len(saved) :]
    output, input_grad, memory_grad, *unit_grads = rest[:11]
    expand_grad, shrink_grad, norm_grads = rest[11:14]
    rest = rest[14:]
    held = Refs(names, rest[: len(names)])
    rest = rest[len(names) :]
    held.__dict__.update(Refs(BACKWARD_SCRATCH, rest[: len(BACKWARD_SCRATCH)]).__dict__)
    send_sem, recv_sem, move_sem = rest[len(BACKWARD_SCRATCH) :]

    place = Place()
    links, moves = Links(place, send_sem, recv_sem), Moves(move_sem)
    z, core, group = place.z, place.core, place.group
    partner = place.across("core")
    mine, theirs = core_rows(core), core_rows(1 - core)
    loads = {}

    def bring(*wanted):
        for name in wanted:
            loads[name] = moves.start(getattr(kept, name), getattr(held, name))

    def have(*wanted):
        for name in wanted:
            moves.wait(loads.pop(name))

    def fetch(unit, slot):
        loads[unit] = moves.start(square.at[unit].reshape(D, D), held.weights.at[slot])

    def weight(unit, slot):
        moves.wait(loads.pop(unit))
        return held.weights.at[slot]

    bring("branch", "active_t")

    def fetch_shrink(part):
        loads[SQUARE] = moves.start(shrink.at[:, part], held.shrink_in)

    fetch_shrink(0)
    for part in range(3):
        fetch(EXPAND + part, part)
    bring("slopes", "third_grad", "second_t", "norm_sums", "gains", "normal_two", "inverse_two")
    bring("cross_queries", "cross_keys", "cross_values", "cross_bias", "cross_logs", "cross_t")
    bring("normal_one", "inverse_one", "first_t", "memory_t", "attended_t", "tokens_t")
    bring("queries", "keys", "values", "self_bias", "self_logs")
    place.greet()

    order = [12, 13, 14, 15, 8, 9, 10, 11, CROSS_OUT, CROSS_QUERY, CROSS_KEY, CROSS_VALUE, OUT, QUERY, KEY, VALUE]

    def result(number, rows, total):
        unit = order[number]
        if unit < EXPAND:
            unit_grads[unit][rows, :] = total
        elif unit < SQUARE:
            expand_grad[rows, pl.ds(D * (unit - EXPAND), D)] = total
        else:
            shrink_grad[pl.ds(32 * (unit - SQUARE) + rows.start, rows.size), :] = total

    scatter = Scatter(links, held.grads, held.from_first, held.from_second, held.from_z, result)
    made = {"count": 0}

    def produce(left, right, depth=2 * OWN):
        target = scatter.home(made["count"])
        made["count"] += 1

        @loop(4)
        def _(index):
            columns = tile(index, OWN)
            term = project(left().reshape(512, depth), right[:, columns])
            target[:, :, :, :, columns] = term.astype(BF).reshape(2, 2, 4, 32, OWN)

    def share(ref):
        slot = links.slot()
        links.send(slot, ref.at[mine], ref.at[mine], partner)
        return slot

    def shared(ref, slot):
        links.arrived(slot, ref.at[theirs])

    def gain(number):
        return held.gains[pl.ds(number, 1), :]

    have("branch", "active_t")

    def produce_shrink(part):
        produce(lambda: held.active_t[:, :, part], held.branch)

    def produce_expand(part):
        shared(held.up.at[part], up_slots[part])
        produce(lambda: held.second_t[...], held.up.at[part])

    produce_shrink(0)
    scatter.tick()
    slot_output = links.slot()
    moves.start(kept.final_low.at[block_rows(group)], output.at[group])
    links.send(slot_output, kept.final_low.at[block_rows(1 - group)], output.at[group], place.along_z(2))
    for part in (1, 2, 3):
        produce_shrink(part)
    scatter.tick()
    have("slopes")
    own_branch = held.branch.at[mine]
    up_slots = []
    for part in range(4):
        if part == 2:
            scatter.tick()
        up = held.up.at[part, mine]
        slopes = held.slopes.at[part]

        moves.wait(loads.pop(SQUARE))

        @loop(4)
        def _(index):
            columns = tile(index, OWN)
            total = project_back(own_branch[:, pl.ds(0, OWN)], held.shrink_in[0, columns, :])
            for depth in (1, 2, 3):
                total = total + project_back(own_branch[:, pl.ds(OWN * depth, OWN)], held.shrink_in[depth, columns, :])
            up[:, columns] = (total * slopes[:, columns].astype(F32)).astype(BF)

        up_slots.append(share(held.up.at[part]))
        if part < 3:
            fetch_shrink(part + 1)

        def add(columns, value):
            if part == 0:
                held.second_sum[:, columns] = value
            else:
                held.second_sum[:, columns] += value

        rows_back(up, weight(EXPAND + part, part % 3), add)
        fetch((EXPAND + 3, CROSS_OUT, CROSS_QUERY, CROSS_KEY)[part], part % 3)
    scatter.tick()
    have("third_grad", "norm_sums", "gains", "normal_two", "inverse_two", "second_t")

    def spread(inverse, rows):
        return inverse[rows, pl.ds(0, 1)]

    @loop(OWN // STEP)
    def _(index):
        rows = tile(index, STEP)
        grad = held.second_sum[rows, :] + alpha_scale * held.third_grad[rows, :]
        pre = norm_rows_back(grad, held.normal_two[rows, :], spread(held.inverse_two, rows), gain(1), held.norm_sums, 1)
        held.second_sum[rows, :] = pre
        held.cross_branch[pl.ds(pl.multiple_of(OWN * core + STEP * index, STEP), STEP), :] = pre.astype(BF)

    slot_cross_branch = share(held.cross_branch)
    produce_expand(0)
    scatter.tick()

    def low(target):
        def store(columns, value):
            target[:, columns] = value.astype(BF)

        return store

    rows_back(held.cross_branch.at[mine], weight(CROSS_OUT, 1), low(held.attended_grad))
    fetch(CROSS_VALUE, 1)
    have("cross_queries", "cross_keys", "cross_values", "cross_bias", "cross_logs", "cross_t")
    attend_rows_back(
        held.cross_queries, held.cross_keys, held.cross_values, held.cross_bias, held.cross_logs, held.attended_grad,
        held.cross_query_grad.at[mine], held.cross_terms.at[0, core], held.cross_terms.at[1, core], CROSS_SEGMENTS, H // 2,
    )
    slot_cross_query = share(held.cross_query_grad)
    slot_cross_terms = links.slot()
    links.send(slot_cross_terms, held.cross_terms.at[:, core], held.cross_terms.at[:, core], partner)
    produce_expand(1)
    scatter.tick()

    def add_first(columns, value):
        held.third_grad[:, columns] = value

    rows_back(held.cross_query_grad.at[mine], weight(CROSS_QUERY, 2), add_first)
    fetch(OUT, 2)
    have("normal_one", "inverse_one", "first_t", "memory_t", "attended_t", "tokens_t")

    @loop(OWN // STEP)
    def _(index):
        rows = tile(index, STEP)
        grad = held.third_grad[rows, :] + alpha_scale * held.second_sum[rows, :]
        pre = norm_rows_back(grad, held.normal_one[rows, :], spread(held.inverse_one, rows), gain(0), held.norm_sums, 0)
        held.second_sum[rows, :] = pre
        held.self_branch[pl.ds(pl.multiple_of(OWN * core + STEP * index, STEP), STEP), :] = pre.astype(BF)

    slot_self_branch = share(held.self_branch)
    norm_steps = all_sum(links, held.norm_sums, norm_grads, held.work)
    next(norm_steps)
    produce_expand(2)
    scatter.tick()
    rows_back(held.self_branch.at[mine], weight(OUT, 2), low(held.attended_grad))
    fetch(QUERY, 2)
    have("queries", "keys", "values", "self_bias", "self_logs")
    terms = held.terms

    def attend_part(first, pairs):
        attend_rows_back(
            held.queries, held.keys, held.values, held.self_bias, held.self_logs, held.attended_grad,
            held.query_grad.at[mine], terms.at[0].reshape(SPAN, D), terms.at[1].reshape(SPAN, D), SELF_SEGMENTS, pairs, first,
        )

    attend_part(0, 2)
    produce_expand(3)
    scatter.tick()
    next(norm_steps)
    attend_part(2, 2)
    shared(held.cross_branch, slot_cross_branch)
    produce(lambda: held.cross_t[...], held.cross_branch)
    scatter.tick()
    next(norm_steps)
    attend_part(4, 2)
    shared(held.cross_query_grad, slot_cross_query)
    produce(lambda: held.first_t[...], held.cross_query_grad)
    scatter.tick()
    next(norm_steps)
    attend_part(6, 2)
    slot_query = share(held.query_grad)
    slot_terms = links.slot()
    links.send(slot_terms, terms.at[:, :, :, 1 - core], held.terms_core, partner)

    links.arrived(slot_cross_terms, held.cross_terms.at[:, 1 - core])
    for which in (0, 1):
        held.cross_sums[which] = (held.cross_terms[which, 0].astype(F32) + held.cross_terms[which, 1].astype(F32)).astype(BF)
    produce(lambda: held.memory_t[...], held.cross_sums.at[0], MEM)
    scatter.tick()
    next(norm_steps)

    links.arrived(slot_terms, held.terms_core)
    near = z % 2

    def join(place_index):
        for which in (0, 1):
            for high in (0, 1):
                value = terms[which, high, place_index, core].astype(F32) + held.terms_core[which, high, place_index].astype(F32)
                terms[which, high, place_index, core] = value.astype(BF)

    join(1 - near)
    slot_mate = links.slot()
    links.send(slot_mate, terms.at[:, :, 1 - near, core], held.terms_mate, place.mate())
    join(near)

    produce(lambda: held.memory_t[...], held.cross_sums.at[1], MEM)
    scatter.tick()

    cross_key, cross_value = weight(CROSS_KEY, 0), weight(CROSS_VALUE, 1)
    sums = held.cross_sums.reshape(2, 4, 2, 16, D)

    @loop(4)
    def _(index):
        columns = tile(index, OWN)
        term = project_back(sums[0, :, core].reshape(64, D), cross_key[columns, :])
        term = term + project_back(sums[1, :, core].reshape(64, D), cross_value[columns, :])
        held.memory_own[:, :, columns] = term.astype(BF).reshape(4, 16, OWN)

    fetch(KEY, 0)
    fetch(VALUE, 1)
    slot_memory = links.slot(4)
    for k in (1, 2, 3):
        links.send(slot_memory + z, held.memory_own.at[(z + k) % 4], held.memory_in.at[z], place.along_z(k))
    held.memory_in[z] = held.memory_own[z]

    shared(held.self_branch, slot_self_branch)
    produce(lambda: held.attended_t[...], held.self_branch)
    scatter.tick()
    shared(held.query_grad, slot_query)
    produce(lambda: held.tokens_t[...], held.query_grad)
    scatter.tick()

    def add_input(columns, value):
        held.third_grad[:, columns] = alpha_scale * held.second_sum[:, columns] + value

    rows_back(held.query_grad.at[mine], weight(QUERY, 2), add_input)
    links.arrived(slot_mate, held.terms_mate)
    for which, target in enumerate((held.key_grad, held.value_grad)):
        for high in (0, 1):
            value = terms[which, high, near, core].astype(F32) + held.terms_mate[which, high].astype(F32)
            target[pl.ds(pl.multiple_of(OWN * core + LEN * high, LEN), LEN), :] = value.astype(BF)
    slot_key, slot_value = share(held.key_grad), share(held.value_grad)

    def add_more(columns, value):
        held.third_grad[:, columns] += value

    rows_back(held.key_grad.at[mine], weight(KEY, 0), add_more)
    rows_back(held.value_grad.at[mine], weight(VALUE, 1), add_more)
    held.far_own[...] = held.third_grad[block_rows(1 - group), :].astype(BF)
    slot_far = links.slot()
    links.send(slot_far, held.far_own, held.far_in, place.along_z(2))
    shared(held.key_grad, slot_key)
    produce(lambda: held.tokens_t[...], held.key_grad)
    scatter.tick()
    shared(held.value_grad, slot_value)
    produce(lambda: held.tokens_t[...], held.value_grad)
    scatter.tick()
    input_grad[group] = held.third_grad[block_rows(group), :]
    scatter.tick()
    for k in (1, 2, 3):
        links.arrived(slot_memory + (z + k) % 4, held.memory_in.at[(z + k) % 4])
    for which in (0, 1):
        memory_grad[which] = held.memory_in[2 * which].astype(F32) + held.memory_in[2 * which + 1].astype(F32)
    scatter.tick()
    scatter.tick()
    links.arrived(slot_far, held.far_in)
    input_grad[1 - group] = held.far_in[...].astype(F32)
    links.arrived(slot_output, output.at[1 - group])
    moves.finish()
    links.finish()


def backward_call(square, shrink, saves, block_shape, memory_shape):
    results = [jax.ShapeDtypeStruct(block_shape, BF)]
    results += [jax.ShapeDtypeStruct(shape, F32) for shape in (block_shape, memory_shape)]
    results += [jax.ShapeDtypeStruct((32, D), F32)] * 8
    results += [jax.ShapeDtypeStruct(shape, F32) for shape in ((32, 4 * D), (LEN, D), (8, D))]
    saved = {**FORWARD_SAVES, **TURNED_SAVES}
    held = {name: saved[name] for name in saved if name != "final_low"}
    return pl.pallas_call(
        backward_kernel,
        in_specs=[IN_PLACE] * (2 + len(saved)),
        out_specs=[IN_PLACE] + [IN_VMEM] * (len(results) - 1),
        out_shape=results,
        scratch_shapes=[
            *vmem_of(held),
            *vmem_of(BACKWARD_SCRATCH),
            pltpu.SemaphoreType.DMA((BACKWARD_SENDS,)),
            pltpu.SemaphoreType.DMA((BACKWARD_SLOTS,)),
            pltpu.SemaphoreType.DMA((BACKWARD_MOVES,)),
        ],
        compiler_params=pltpu.CompilerParams(collective_id=1, has_side_effects=True, vmem_limit_bytes=63 << 20),
    )(square, shrink.reshape(4, 4, D, OWN), *(saves[name] for name in saved))


def hand_over_kernel(*refs):
    count = len(refs) // 3
    sem = refs[-1]
    loads = [pltpu.make_async_copy(refs[n], refs[2 * count + n], sem.at[0, n]) for n in range(count)]
    stores = [pltpu.make_async_copy(refs[2 * count + n], refs[count + n], sem.at[1, n]) for n in range(count)]
    for load in loads:
        load.start()
    for load, store in zip(loads, stores):
        load.wait()
        store.start()
    for store in stores:
        store.wait()


def hand_over(values):
    return pl.pallas_call(
        hand_over_kernel,
        in_specs=[IN_PLACE] * len(values),
        out_specs=[IN_PLACE] * len(values),
        out_shape=[jax.ShapeDtypeStruct(value.shape, value.dtype) for value in values],
        scratch_shapes=[
            *(pltpu.VMEM(value.shape, value.dtype) for value in values),
            pltpu.SemaphoreType.DMA((2, len(values))),
        ],
        compiler_params=pltpu.CompilerParams(vmem_limit_bytes=VMEM_BYTES),
    )(*values)


def fast_shards(
    tokens, memory, lengths, memory_segments, out_grad,
    self_query, self_key, self_value, self_out,
    cross_query, cross_key, cross_value, cross_out,
    expand_weight, shrink_weight, norm_gains, norm_biases,
):
    me = lax.axis_index("dp") * lax.axis_size("seq") + lax.axis_index("seq")
    norms = jnp.concatenate([norm_gains, norm_biases, jnp.zeros((2, 32), BF)]).astype(F32)
    norms = lax.dynamic_update_slice(jnp.zeros((8, D), F32), norms, (0, 32 * me))
    weights = (self_key, self_value, self_query, self_out, cross_query, cross_key, cross_value, cross_out)
    square, shrink, saves = forward_call(
        lengths, memory_segments, norms, tokens, memory, out_grad, (*weights, expand_weight, shrink_weight)
    )
    *values, norm_grads = backward_call(square, shrink, saves, tokens.shape, memory.shape)
    output, input_grad, memory_grad, *units, expand_grad, shrink_grad = hand_over(values)
    norm_grads = lax.dynamic_slice(norm_grads, (0, 32 * me), (8, 32))
    return (
        output,
        input_grad,
        memory_grad,
        *(units[unit] for unit in (QUERY, KEY, VALUE, OUT, CROSS_QUERY, CROSS_KEY, CROSS_VALUE, CROSS_OUT)),
        expand_grad,
        shrink_grad,
        norm_grads[:3],
        norm_grads[3:6],
    )


def solution(mesh):
    quick = dict(mesh.shape) == {"dp": 4, "seq": 8}
    return jax.shard_map(
        fast_shards if quick else shards,
        mesh=mesh,
        in_specs=(
            P("dp", "seq", None),
            P("dp", "seq", None),
            P("dp", None),
            P("dp", None),
            P("dp", "seq", None),
            P(("dp", "seq"), None),
            P(("dp", "seq"), None),
            P(("dp", "seq"), None),
            P(("dp", "seq"), None),
            P(("dp", "seq"), None),
            P(("dp", "seq"), None),
            P(("dp", "seq"), None),
            P(("dp", "seq"), None),
            P(("dp", "seq"), None),
            P(("dp", "seq"), None),
            P(None, ("dp", "seq")),
            P(None, ("dp", "seq")),
        ),
        out_specs=(
            P("dp", "seq", None),
            P("dp", "seq", None),
            P("dp", "seq", None),
            P(("dp", "seq"), None),
            P(("dp", "seq"), None),
            P(("dp", "seq"), None),
            P(("dp", "seq"), None),
            P(("dp", "seq"), None),
            P(("dp", "seq"), None),
            P(("dp", "seq"), None),
            P(("dp", "seq"), None),
            P(("dp", "seq"), None),
            P(("dp", "seq"), None),
            P(None, ("dp", "seq")),
            P(None, ("dp", "seq")),
        ),
        check_vma=False,
    )
```

```python
import functools

import jax
import jax.numpy as jnp
from jax import lax
from jax.experimental import pallas as pl
from jax.experimental.pallas import tpu as pltpu
from jax.sharding import PartitionSpec as P

H = 16
HD = 64
MB = 2


alpha_scale = 300.0**0.25
norm_eps = 1e-05
masked_score = -1e30


def layer_norm(value, gain, bias):
    average = jnp.mean(value, axis=-1, keepdims=True)
    centred = value - average
    spread = jnp.mean(centred * centred, axis=-1, keepdims=True)
    return centred * lax.rsqrt(spread + norm_eps) * gain + bias


def project(left, right):
    return jnp.dot(left, right, preferred_element_type=jnp.float32)


def project_back(left, right):
    return lax.dot_general(
        left, right, (((1,), (1,)), ((), ())), preferred_element_type=jnp.float32
    )


def weight_term(left, right):
    return lax.dot_general(
        left, right, (((0,), (0,)), ((), ())), preferred_element_type=jnp.float32
    )


def split_heads(value):
    return value.reshape(value.shape[0], value.shape[1], H, HD)


def sentence_ids(sent_ends, places):
    return jnp.sum((places[None, :, None] >= sent_ends[:, None, :]).astype(jnp.int32), axis=2)


def masked_scores(queries, key_heads, allowed, scaling):
    raw_scores = (
        jnp.einsum("gqhd,gkhd->ghqk", queries, key_heads, preferred_element_type=jnp.float32)
        * scaling
    )
    return jnp.where(allowed[:, None], raw_scores, masked_score)


def attend_forward(queries, key_heads, value_heads, allowed, scaling):
    scores = masked_scores(queries, key_heads, allowed, scaling)
    row_max = jnp.max(scores, axis=3, keepdims=True)
    powers = jnp.exp(scores - row_max)
    row_total = jnp.sum(powers, axis=3, keepdims=True)
    prob_low = (powers / row_total).astype(jnp.bfloat16)
    attended = jnp.einsum(
        "ghqk,gkhd->gqhd", prob_low, value_heads, preferred_element_type=jnp.float32
    )
    return (attended, row_max + jnp.log(row_total))


def attend_backward(queries, key_heads, value_heads, allowed, scaling, log_total, attended_grad):
    scores = masked_scores(queries, key_heads, allowed, scaling)
    probability = jnp.exp(scores - log_total)
    prob_grad = jnp.einsum(
        "gqhd,gkhd->ghqk", attended_grad, value_heads, preferred_element_type=jnp.float32
    )
    score_grad = probability * (prob_grad - jnp.sum(prob_grad * probability, axis=3, keepdims=True))
    score_low = score_grad.astype(jnp.bfloat16)
    query_grad = (
        jnp.einsum("ghqk,gkhd->gqhd", score_low, key_heads, preferred_element_type=jnp.float32)
        * scaling
    )
    return (query_grad, score_low, probability.astype(jnp.bfloat16))


def micro_batch(gathered, tokens, memory, lengths, memory_segments, out_grad):
    (
        self_query,
        self_key,
        self_value,
        self_out,
        cross_query,
        cross_key,
        cross_value,
        cross_out,
        expand_weight,
        shrink_weight,
        norm_gains,
        norm_biases,
    ) = gathered
    gains = norm_gains.astype(jnp.float32)
    biases = norm_biases.astype(jnp.float32)
    group_size, local_len, features = tokens.shape
    seq_count = lax.axis_size("seq")
    seq_index = lax.axis_index("seq")
    full_len = local_len * seq_count
    row_count = group_size * local_len
    scaling = HD ** (-0.5)
    sent_ends = jnp.cumsum(lengths, axis=1)[:, :-1]
    query_places = seq_index * local_len + jnp.arange(local_len, dtype=jnp.int32)
    key_places = jnp.arange(full_len, dtype=jnp.int32)
    query_ids = sentence_ids(sent_ends, query_places)
    key_ids = sentence_ids(sent_ends, key_places)
    self_allowed = (query_ids[:, :, None] == key_ids[:, None, :]) & (
        key_places[None, None, :] <= query_places[None, :, None]
    )
    cross_allowed = query_ids[:, :, None] == memory_segments[:, None, :]
    token_rows = tokens.reshape(row_count, features)
    queries = split_heads(
        project(token_rows, self_query)
        .astype(jnp.bfloat16)
        .reshape(group_size, local_len, features)
    )
    own_keys = (
        project(token_rows, self_key).astype(jnp.bfloat16).reshape(group_size, local_len, features)
    )
    own_values = (
        project(token_rows, self_value)
        .astype(jnp.bfloat16)
        .reshape(group_size, local_len, features)
    )
    all_keys, all_values = (
        lax.all_gather(own_keys, "seq", axis=1, tiled=True),
        lax.all_gather(own_values, "seq", axis=1, tiled=True),
    )
    key_heads = split_heads(all_keys)
    value_heads = split_heads(all_values)
    attended, self_log = attend_forward(queries, key_heads, value_heads, self_allowed, scaling)
    attended = attended.reshape(row_count, features).astype(jnp.bfloat16)
    first_pre = alpha_scale * token_rows.astype(jnp.float32) + project(attended, self_out)
    first, first_pull = jax.vjp(layer_norm, first_pre, gains[0], biases[0])
    first_low = first.astype(jnp.bfloat16)
    cross_queries = split_heads(
        project(first_low, cross_query)
        .astype(jnp.bfloat16)
        .reshape(group_size, local_len, features)
    )
    own_memory = memory.reshape(-1, features)
    memory_all = lax.all_gather(memory, "seq", axis=1, tiled=True)
    memory_rows = memory_all.reshape(-1, features)
    cross_keys = (
        project(memory_rows, cross_key).astype(jnp.bfloat16).reshape(group_size, -1, features)
    )
    cross_values = (
        project(memory_rows, cross_value).astype(jnp.bfloat16).reshape(group_size, -1, features)
    )
    cross_key_heads = split_heads(cross_keys)
    cross_value_heads = split_heads(cross_values)
    cross_attended, cross_log = attend_forward(
        cross_queries, cross_key_heads, cross_value_heads, cross_allowed, scaling
    )
    cross_attended = cross_attended.reshape(row_count, features).astype(jnp.bfloat16)
    second_pre = alpha_scale * first + project(cross_attended, cross_out)
    second, second_pull = jax.vjp(layer_norm, second_pre, gains[1], biases[1])
    second_low = second.astype(jnp.bfloat16)
    upward = project(second_low, expand_weight)
    active, gelu_pull = jax.vjp(jax.nn.gelu, upward)
    active_low = active.astype(jnp.bfloat16)
    third_pre = alpha_scale * second + project(active_low, shrink_weight)
    final, third_pull = jax.vjp(layer_norm, third_pre, gains[2], biases[2])
    third_grad, gain_third, bias_third = third_pull(
        out_grad.reshape(row_count, features).astype(jnp.float32)
    )
    branch_grad = third_grad.astype(jnp.bfloat16)
    shrink_grad = weight_term(active_low, branch_grad)
    (up_grad,) = gelu_pull(project_back(branch_grad, shrink_weight))
    up_low = up_grad.astype(jnp.bfloat16)
    expand_grad = weight_term(second_low, up_low)
    second_grad = alpha_scale * third_grad + project_back(up_low, expand_weight)
    second_pre_grad, gain_second, bias_second = second_pull(second_grad)
    cross_branch = second_pre_grad.astype(jnp.bfloat16)
    cross_out_grad = weight_term(cross_attended, cross_branch)
    cross_attended_grad = split_heads(
        project_back(cross_branch, cross_out)
        .astype(jnp.bfloat16)
        .reshape(group_size, local_len, features)
    )
    cross_q_grad, cross_scores, cross_probs = attend_backward(
        cross_queries,
        cross_key_heads,
        cross_value_heads,
        cross_allowed,
        scaling,
        cross_log,
        cross_attended_grad,
    )
    cross_q_low = cross_q_grad.reshape(row_count, features).astype(jnp.bfloat16)
    cross_query_grad = weight_term(first_low, cross_q_low)
    key_term = (
        jnp.einsum(
            "ghqk,gqhd->gkhd", cross_scores, cross_queries, preferred_element_type=jnp.float32
        )
        * scaling
    ).reshape(group_size, -1, features)
    value_term = jnp.einsum(
        "ghqk,gqhd->gkhd", cross_probs, cross_attended_grad, preferred_element_type=jnp.float32
    ).reshape(group_size, -1, features)
    key_summed, value_summed = (
        lax.psum_scatter(
            key_term.astype(jnp.bfloat16), "seq", scatter_dimension=1, tiled=True
        ).astype(jnp.float32),
        lax.psum_scatter(
            value_term.astype(jnp.bfloat16), "seq", scatter_dimension=1, tiled=True
        ).astype(jnp.float32),
    )
    key_low = key_summed.reshape(-1, features).astype(jnp.bfloat16)
    value_low = value_summed.reshape(-1, features).astype(jnp.bfloat16)
    cross_key_grad = weight_term(own_memory, key_low)
    cross_value_grad = weight_term(own_memory, value_low)
    memory_grad = (project_back(key_low, cross_key) + project_back(value_low, cross_value)).reshape(
        memory.shape
    )
    first_grad = alpha_scale * second_pre_grad + project_back(cross_q_low, cross_query)
    first_pre_grad, gain_first, bias_first = first_pull(first_grad)
    self_branch = first_pre_grad.astype(jnp.bfloat16)
    self_out_grad = weight_term(attended, self_branch)
    attended_grad = split_heads(
        project_back(self_branch, self_out)
        .astype(jnp.bfloat16)
        .reshape(group_size, local_len, features)
    )
    self_q_grad, self_scores, self_probs = attend_backward(
        queries, key_heads, value_heads, self_allowed, scaling, self_log, attended_grad
    )
    count = local_len * lax.axis_size("seq")
    key_part = (
        jnp.einsum("ghqk,gqhd->kghd", self_scores, queries, preferred_element_type=jnp.float32)
        * scaling
    )
    value_part = jnp.einsum(
        "ghqk,gqhd->kghd", self_probs, attended_grad, preferred_element_type=jnp.float32
    )
    pair_summed = lax.psum_scatter(
        jnp.concatenate(
            [
                key_part.reshape(count, group_size, features),
                value_part.reshape(count, group_size, features),
            ],
            axis=2,
        ).astype(jnp.bfloat16),
        "seq",
        scatter_dimension=0,
        tiled=True,
    ).astype(jnp.float32)
    key_grad = (
        pair_summed[:, :, :features]
        .astype(jnp.bfloat16)
        .transpose(1, 0, 2)
        .reshape(row_count, features)
    )
    value_grad = (
        pair_summed[:, :, features:]
        .astype(jnp.bfloat16)
        .transpose(1, 0, 2)
        .reshape(row_count, features)
    )
    query_low = self_q_grad.reshape(row_count, features).astype(jnp.bfloat16)
    self_query_grad = weight_term(token_rows, query_low)
    self_key_grad = weight_term(token_rows, key_grad)
    self_value_grad = weight_term(token_rows, value_grad)
    input_grad = (
        alpha_scale * first_pre_grad
        + project_back(query_low, self_query)
        + project_back(key_grad, self_key)
        + project_back(value_grad, self_value)
    )
    gains_grad = jnp.stack([gain_first, gain_second, gain_third])
    biases_grad = jnp.stack([bias_first, bias_second, bias_third])
    gradients = (
        self_query_grad,
        self_key_grad,
        self_value_grad,
        self_out_grad,
        cross_query_grad,
        cross_key_grad,
        cross_value_grad,
        cross_out_grad,
        expand_grad,
        shrink_grad,
        gains_grad,
        biases_grad,
    )
    result = final.astype(jnp.bfloat16).reshape(group_size, local_len, features)
    return (result, input_grad.reshape(group_size, local_len, features), memory_grad, gradients)


def shards(
    tokens,
    memory,
    lengths,
    memory_segments,
    out_grad,
    self_query,
    self_key,
    self_value,
    self_out,
    cross_query,
    cross_key,
    cross_value,
    cross_out,
    expand_weight,
    shrink_weight,
    norm_gains,
    norm_biases,
):
    group_size = tokens.shape[0] // MB
    outputs = []
    input_grads = []
    memory_grads = []
    totals = None
    for batch_index in range(MB):
        gathered = (
            lax.all_gather(self_query, ("dp", "seq"), axis=0, tiled=True),
            lax.all_gather(self_key, ("dp", "seq"), axis=0, tiled=True),
            lax.all_gather(self_value, ("dp", "seq"), axis=0, tiled=True),
            lax.all_gather(self_out, ("dp", "seq"), axis=0, tiled=True),
            lax.all_gather(cross_query, ("dp", "seq"), axis=0, tiled=True),
            lax.all_gather(cross_key, ("dp", "seq"), axis=0, tiled=True),
            lax.all_gather(cross_value, ("dp", "seq"), axis=0, tiled=True),
            lax.all_gather(cross_out, ("dp", "seq"), axis=0, tiled=True),
            lax.all_gather(expand_weight, ("dp", "seq"), axis=0, tiled=True),
            lax.all_gather(shrink_weight, ("dp", "seq"), axis=0, tiled=True),
            lax.all_gather(norm_gains, ("dp", "seq"), axis=1, tiled=True),
            lax.all_gather(norm_biases, ("dp", "seq"), axis=1, tiled=True),
        )
        start = batch_index * group_size
        stop = start + group_size
        result, input_grad, memory_grad, gradients = micro_batch(
            gathered,
            tokens[start:stop],
            memory[start:stop],
            lengths[start:stop],
            memory_segments[start:stop],
            out_grad[start:stop],
        )
        outputs.append(result)
        input_grads.append(input_grad)
        memory_grads.append(memory_grad)
        if totals is None:
            totals = gradients
        else:
            totals = tuple((running + gradient for running, gradient in zip(totals, gradients)))
    summed = (
        lax.psum_scatter(totals[0], ("dp", "seq"), scatter_dimension=0, tiled=True),
        lax.psum_scatter(totals[1], ("dp", "seq"), scatter_dimension=0, tiled=True),
        lax.psum_scatter(totals[2], ("dp", "seq"), scatter_dimension=0, tiled=True),
        lax.psum_scatter(totals[3], ("dp", "seq"), scatter_dimension=0, tiled=True),
        lax.psum_scatter(totals[4], ("dp", "seq"), scatter_dimension=0, tiled=True),
        lax.psum_scatter(totals[5], ("dp", "seq"), scatter_dimension=0, tiled=True),
        lax.psum_scatter(totals[6], ("dp", "seq"), scatter_dimension=0, tiled=True),
        lax.psum_scatter(totals[7], ("dp", "seq"), scatter_dimension=0, tiled=True),
        lax.psum_scatter(totals[8], ("dp", "seq"), scatter_dimension=0, tiled=True),
        lax.psum_scatter(totals[9], ("dp", "seq"), scatter_dimension=0, tiled=True),
        lax.psum_scatter(totals[10], ("dp", "seq"), scatter_dimension=1, tiled=True),
        lax.psum_scatter(totals[11], ("dp", "seq"), scatter_dimension=1, tiled=True),
    )
    return (
        jnp.concatenate(outputs, 0),
        jnp.concatenate(input_grads, 0),
        jnp.concatenate(memory_grads, 0),
        summed[0],
        summed[1],
        summed[2],
        summed[3],
        summed[4],
        summed[5],
        summed[6],
        summed[7],
        summed[8],
        summed[9],
        summed[10],
        summed[11],
    )


MESH = pl.DeviceIdType.MESH
BF = jnp.bfloat16
F32 = jnp.float32
ALL = slice(None)
D = 1024
LEN = 128
OWN = 2 * LEN
SPAN = 8 * LEN
MEM = 128
KEY, VALUE, QUERY, OUT, CROSS_QUERY, CROSS_KEY, CROSS_VALUE, CROSS_OUT = range(8)
EXPAND = 8
SQUARE = 12
UNITS = 16
GRID = (2, 2, 4, 2)
SQUARE_SHAPE = (SQUARE, *GRID, 32, D)
SHRINK_SHAPE = (UNITS - SQUARE, *GRID, LEN, OWN)
VMEM_BYTES = 60 << 20
GELU_SLOPE = (2.0 / 3.141592653589793) ** 0.5
GELU_CUBE = 0.044715


class Place:
    def __init__(self):
        dp, seq = lax.axis_index("dp"), lax.axis_index("seq")
        self.x, self.y, self.core, self.z, self.seq = dp % 2, dp // 2, seq % 2, seq // 2, seq
        self.group = self.z // 2
        self.low = seq % 4
        self.mate_z = self.z + 1 - 2 * (self.z % 2)
        self.inner_z = 2 - self.group
        self.next_z = (self.z + 2) % 4
        self.inner = self.z % 3 != 0
        self.outer = self.z % 3 == 0

    def at(self, y=None, x=None, z=None, core=None):
        y = self.y if y is None else y
        x = self.x if x is None else x
        z = self.z if z is None else z
        core = self.core if core is None else core
        return (y * 2 + x, z * 2 + core)

    def across(self, axis):
        if axis == "x":
            return self.at(x=1 - self.x)
        if axis == "y":
            return self.at(y=1 - self.y)
        return self.at(core=1 - self.core)

    def along_z(self, step):
        return self.at(z=(self.z + step) % 4)

    def mate(self):
        return self.at(z=self.mate_z)

    def greet(self):
        barrier = pltpu.get_barrier_semaphore()
        peers = [self.across(axis) for axis in ("x", "y", "core")]
        peers += [self.along_z(step) for step in (1, 2, 3)]
        for peer in peers:
            pl.semaphore_signal(barrier, inc=1, device_id=peer, device_id_type=MESH)
        pl.semaphore_wait(barrier, len(peers))


def under(when, act):
    if when is None:
        act()
    else:
        pl.when(when)(act)


class Links:
    def __init__(self, place, send_sem, recv_sem):
        self.place, self.send_sem, self.recv_sem = place, send_sem, recv_sem
        self.sends, self.slots = 0, 0
        self.open = {}

    def slot(self, count=1):
        first = self.slots
        self.slots += count
        assert self.slots <= self.recv_sem.shape[0]
        return first

    def send(self, slot, source, target, device, when=None):
        assert self.sends < self.send_sem.shape[0]
        step = pltpu.make_async_remote_copy(
            src_ref=source,
            dst_ref=target,
            send_sem=self.send_sem.at[self.sends],
            recv_sem=self.recv_sem.at[slot],
            device_id=device,
            device_id_type=MESH,
        )
        under(when, step.start)
        self.sends += 1
        self.open[id(step)] = step, when
        return step

    def arrived(self, slot, target):
        pltpu.make_async_remote_copy(
            src_ref=target,
            dst_ref=target,
            send_sem=self.send_sem.at[0],
            recv_sem=self.recv_sem.at[slot],
            device_id=self.place.across("core"),
            device_id_type=MESH,
        ).wait_recv()

    def sent(self, step):
        step, when = self.open.pop(id(step))
        under(when, step.wait_send)

    def finish(self):
        for step, when in self.open.values():
            under(when, step.wait_send)
        self.open = {}


class Moves:
    def __init__(self, sem):
        self.sem, self.count, self.open = sem, 0, {}

    def start(self, source, target):
        assert self.count < self.sem.shape[0]
        step = pltpu.make_async_copy(source, target, self.sem.at[self.count])
        step.start()
        self.count += 1
        self.open[id(step)] = step
        return step

    def wait(self, step):
        self.open.pop(id(step)).wait()

    def finish(self):
        for step in self.open.values():
            step.wait()
        self.open = {}


def all_sum(links, part, total, work):
    place = links.place
    work[0] = part[...]
    for number, axis in enumerate(("core", "y", "x")):
        slot = links.slot()
        step = links.send(slot, work.at[0], work.at[1 + number], place.across(axis))
        yield
        links.arrived(slot, work.at[1 + number])
        links.sent(step)
        work[0] = work[0] + work[1 + number]
    slot = links.slot(4)
    for k in (1, 2, 3):
        links.send(slot + place.z, work.at[0], work.at[4 + place.z], place.along_z(k))
    yield
    result = work[0]
    for k in (1, 2, 3):
        source = (place.z + k) % 4
        links.arrived(slot + source, work.at[4 + source])
        result = result + work[4 + source]
    total[...] = result
    yield


def loop(count):
    return pl.loop(0, count)


def tile(index, size):
    return pl.ds(pl.multiple_of(index * size, size), size)


def rows_times(left, right, store, rows=OWN, width=256):
    for first in range(0, left.shape[0], rows):

        @loop(D // width)
        def _(index):
            columns = tile(index, width)
            store(pl.ds(first, rows), columns, jnp.dot(left[pl.ds(first, rows), :], right[:, columns], preferred_element_type=F32))


def rows_back(left, right, store, width=256):
    @loop(D // width)
    def _(index):
        columns = tile(index, width)
        store(columns, project_back(left[...], right[columns, :]))


def put(target, dtype=BF):
    def store(rows, columns, value):
        target[rows, columns] = value.astype(dtype)

    return store


def half_masks():
    lane = lax.broadcasted_iota(jnp.int32, (1, LEN), 1)
    return [(lane < HD).astype(F32), (lane >= HD).astype(F32)]


def attend_rows(queries, keys, values, bias, logs, out, segments, pairs=H // 2, first_pair=0):
    masks = half_masks()

    @loop(pairs)
    def _(step):
        pair = step + first_pair
        columns = tile(pair, LEN)
        for first, rows, count in segments:
            own = pl.ds(first, rows)
            key, value = keys[pl.ds(0, count), columns], values[pl.ds(0, count), columns]
            query = queries[own, columns]
            lane = lax.broadcasted_iota(jnp.int32, (rows, LEN), 1)
            parts = []
            for half in (0, 1):
                scores = project_back(query * (masks[half] * HD**-0.5).astype(BF), key) + bias[own, pl.ds(0, count)]
                top = jnp.max(scores, axis=1, keepdims=True)
                powers = jnp.exp(scores - top)
                total = jnp.sum(powers, axis=1, keepdims=True)
                parts.append(project((powers * (1.0 / total)).astype(BF), value))
                logs[own, :] = jnp.where(lane == 2 * pair + half, top + jnp.log(total), logs[own, :])
            out[own, columns] = jnp.where(lane < HD, parts[0], parts[1]).astype(BF)


def attend_rows_back(queries, keys, values, bias, logs, grads, query_grads, key_grads, value_grads, segments, pairs, first_pair=0):
    masks = half_masks()

    @loop(pairs)
    def _(step):
        pair = step + first_pair
        columns = tile(pair, LEN)
        for number, (first, rows, count) in enumerate(segments):
            own, met = pl.ds(first, rows), pl.ds(0, count)
            key, value = keys[met, columns], values[met, columns]
            lane = lax.broadcasted_iota(jnp.int32, (rows, LEN), 1)
            halves, score_lows, prob_lows, query_parts, grad_parts = [], [], [], [], []
            for half in (0, 1):
                query = queries[own, columns] * (masks[half] * HD**-0.5).astype(BF)
                grad = grads[own, columns] * masks[half].astype(BF)
                log_total = jnp.sum(jnp.where(lane == 2 * pair + half, logs[own, :], 0.0), axis=1, keepdims=True)
                probs = jnp.exp(project_back(query, key) + bias[own, met] - log_total)
                prob_grad = project_back(grad, value)
                score_grad = probs * (prob_grad - jnp.sum(prob_grad * probs, axis=1, keepdims=True))
                score_low = score_grad.astype(BF)
                halves.append(project(score_low, key) * HD**-0.5)
                score_lows.append(score_low)
                prob_lows.append(probs.astype(BF))
                query_parts.append(query)
                grad_parts.append(grad)
            query_grads[own, columns] = jnp.where(lane < HD, halves[0], halves[1]).astype(BF)
            key_term = weight_term(jnp.concatenate(score_lows), jnp.concatenate(query_parts))
            value_term = weight_term(jnp.concatenate(prob_lows), jnp.concatenate(grad_parts))
            if number == 0:
                key_grads[met, columns] = key_term.astype(BF)
                value_grads[met, columns] = value_term.astype(BF)
            else:
                key_grads[met, columns] = (key_grads[met, columns].astype(F32) + key_term).astype(BF)
                value_grads[met, columns] = (value_grads[met, columns].astype(F32) + value_term).astype(BF)


SELF_SEGMENTS = ((LEN, LEN, SPAN), (0, LEN, SPAN // 2))
CROSS_SEGMENTS = ((0, OWN, MEM),)
STEP = 32


def norm_rows(read, normal, inverse, emit):
    @loop(OWN // STEP)
    def _(index):
        rows = tile(index, STEP)
        value = read(rows)
        centred = value - jnp.mean(value, axis=1, keepdims=True)
        scale = lax.rsqrt(jnp.mean(centred * centred, axis=1, keepdims=True) + norm_eps)
        result = centred * scale
        if normal is not None:
            normal[rows, :] = result
            inverse[rows, :] = jnp.broadcast_to(scale, (STEP, LEN))
        emit(rows, result, scale)


def norm_rows_back(grad, normal, scale, gain, sums, number):
    sums[pl.ds(number, 1), :] += jnp.sum(grad * normal, axis=0, keepdims=True)
    sums[pl.ds(3 + number, 1), :] += jnp.sum(grad, axis=0, keepdims=True)
    scaled = grad * gain
    return scale * (
        scaled
        - jnp.mean(scaled, axis=1, keepdims=True)
        - normal * jnp.mean(scaled * normal, axis=1, keepdims=True)
    )


class Gather:
    WIDE = (6, 7, 8, 10, 11, 12, 13, 14, 15)
    EARLY = 3
    RELAY = 1
    ROUTES = {False: ("zxy", "zyx"), True: ("xzy", "yzx")}
    TIMES = {False: (-3, 0, 1, 2, 3), True: (-20, -3, 1, 2, 3)}
    SLOTS = 10

    def __init__(self, links, moves, own, square, shrink):
        self.links, self.moves, self.own, self.square, self.shrink = links, moves, own, square, shrink
        self.first_slot = links.slot(UNITS * 2 * self.SLOTS)
        self.local = {}
        for unit in range(UNITS):
            target = self.block(unit, links.place.y, links.place.x, links.place.z, links.place.core)
            self.local[unit] = moves.start(own(unit), target)
        self.now = -self.EARLY
        self.steps = {}
        for number, unit in enumerate(range(UNITS)):
            wide = number in self.WIDE
            for half in (0, 1):
                for phase, time in enumerate(self.TIMES[wide]):
                    step = (phase, number, unit, half, self.ROUTES[wide][half])
                    self.steps.setdefault(max(number + time, self.now), []).append(step)
                step = (-1, number, unit, half, self.ROUTES[wide][half])
                self.steps.setdefault(max(number - self.RELAY, self.now + 1), []).append(step)

    def block(self, unit, *index):
        if unit < SQUARE:
            return self.square.at[(unit,) + index]
        return self.shrink.at[(unit - SQUARE,) + index]

    def tick(self):
        for phase, _, unit, half, route in sorted(self.steps.pop(self.now, ())):
            self.move(phase, unit, half, route)
        self.now += 1

    def move(self, phase, unit, half, route):
        links, place = self.links, self.links.place
        here = {"y": place.y, "x": place.x, "z": place.z}
        slot = self.first_slot + (2 * unit + half) * self.SLOTS
        depth = 16 if unit < SQUARE else 64
        rows = pl.ds(depth * half, depth)
        turn = route.index("z")

        def part(where, core):
            return self.block(unit, where["y"], where["x"], where["z"], core, rows)

        def reached(count):
            return {**here, **{axis: ALL for axis in route[:count]}}

        def incoming(count):
            axis = route[count]
            if axis == "z":
                return reached(count + 1)
            return {**reached(count), axis: 1 - here[axis]}

        def line(source):
            return part({**reached(turn), "z": source}, place.core)

        if phase == -1:
            def hand_on():
                links.arrived(slot + place.next_z, line(place.next_z))

            under(place.inner, hand_on)
            links.send(slot + place.next_z, line(place.next_z), line(place.next_z), place.mate(), place.inner)
            return
        if phase == 1 and unit in self.local:
            self.moves.wait(self.local.pop(unit))
        if 1 <= phase <= 3:
            if phase - 1 == turn:
                links.arrived(slot + place.mate_z, line(place.mate_z))
                for source, when in ((place.next_z, place.outer), ((6 - place.z - place.mate_z - place.next_z), None)):
                    under(when, functools.partial(links.arrived, slot + source, line(source)))
            else:
                links.arrived(slot + 3 + phase, part(incoming(phase - 1), place.core))
        if phase < 3:
            source = self.own(unit).at[rows] if phase == 0 else part(reached(phase), place.core)
            target = part(reached(phase), place.core)
            if phase == turn:
                links.send(slot + place.z, source, target, place.mate())
                links.send(slot + place.z, source, target, place.at(z=place.inner_z))
                links.send(slot + place.z, source, target, place.at(z=place.next_z), place.inner)
            else:
                links.send(slot + 4 + phase, source, target, place.across(route[phase]))
        if 1 <= phase <= 3 and phase > turn:
            fresh = part(incoming(phase - 1), place.core)
            links.send(slot + 6 + phase, fresh, fresh, place.across("core"))
        if phase == 4:
            for number in range(turn, 3):
                links.arrived(slot + 7 + number, part(incoming(number), 1 - place.core))


def core_rows(core, count=OWN):
    return pl.ds(pl.multiple_of(core * count, count), count)


def block_rows(block):
    return pl.ds(pl.multiple_of(block * LEN, LEN), LEN)


FORWARD_SAVES = {
    "queries": ((OWN, D), BF),
    "keys": ((SPAN, D), BF),
    "values": ((SPAN, D), BF),
    "self_bias": ((OWN, SPAN), F32),
    "self_logs": ((OWN, LEN), F32),
    "normal_one": ((OWN, D), F32),
    "inverse_one": ((OWN, LEN), F32),
    "cross_queries": ((OWN, D), BF),
    "cross_keys": ((MEM, D), BF),
    "cross_values": ((MEM, D), BF),
    "cross_bias": ((OWN, MEM), F32),
    "cross_logs": ((OWN, LEN), F32),
    "normal_two": ((OWN, D), F32),
    "inverse_two": ((OWN, LEN), F32),
    "slopes": ((4, OWN, D), BF),
    "third_grad": ((OWN, D), F32),
    "norm_sums": ((8, D), F32),
    "gains": ((8, D), F32),
    "final_low": ((OWN, D), BF),
}
TURNED_SAVES = {
    "tokens_t": ((16, 32, 2 * OWN), BF),
    "attended_t": ((16, 32, 2 * OWN), BF),
    "first_t": ((16, 32, 2 * OWN), BF),
    "cross_t": ((16, 32, 2 * OWN), BF),
    "second_t": ((16, 32, 2 * OWN), BF),
    "active_t": ((4, 4, 4, 32, 2 * OWN), BF),
    "memory_t": ((16, 32, MEM), BF),
    "branch": ((2 * OWN, D), BF),
}
FORWARD_SCRATCH = {
    "stream": ((SPAN, D), BF),
    "mine": ((OWN, D), BF),
    "context": ((4, 2, 16, D), BF),
    "attended": ((OWN, D), BF),
    "first_low": ((OWN, D), BF),
    "cross_attended": ((OWN, D), BF),
    "second_low": ((OWN, D), BF),
    "active": ((4, OWN, D), BF),
    "sums": ((OWN, D), F32),
    "cotangent": ((OWN, D), BF),
    "branch_own": ((OWN, D), BF),
    "weights": ((4, D, D), BF),
    "shrink_in": ((2, 4, D, OWN), BF),
    "turned": ((3, 16, 2, 32, OWN), BF),
    "turned_active": ((2, 4, 2, 4, 32, OWN), BF),
    "turned_memory": ((16, 2, 32, MEM), BF),
    "work": ((8, 8, D), F32),
}
FORWARD_SENDS, FORWARD_SLOTS, FORWARD_MOVES = 352, 384, 96


class Refs:
    def __init__(self, names, refs):
        for name, ref in zip(names, refs):
            setattr(self, name, ref)


def forward_kernel(lengths, segments, norms, tokens, memory, out_grad, *refs):
    squares, expand_own, shrink_own = refs[:8], refs[8], refs[9]
    square, shrink = refs[10:12]
    rest = refs[12:]
    kept = Refs(FORWARD_SAVES, rest[: len(FORWARD_SAVES)])
    rest = rest[len(FORWARD_SAVES) :]
    turned = Refs(TURNED_SAVES, rest[: len(TURNED_SAVES)])
    rest = rest[len(TURNED_SAVES) :]
    held = Refs(FORWARD_SAVES, rest[: len(FORWARD_SAVES)])
    rest = rest[len(FORWARD_SAVES) :]
    held.__dict__.update(Refs(FORWARD_SCRATCH, rest[: len(FORWARD_SCRATCH)]).__dict__)
    send_sem, recv_sem, move_sem = rest[len(FORWARD_SCRATCH) :]

    place = Place()
    links, moves = Links(place, send_sem, recv_sem), Moves(move_sem)
    y, x, z, core, group, low, seq = place.y, place.x, place.z, place.core, place.group, place.low, place.seq
    partner = place.across("core")
    opposite = place.along_z(2)
    mate = place.mate()
    place.greet()

    def own(unit):
        if unit < EXPAND:
            return squares[unit]
        if unit < SQUARE:
            return expand_own.at[:, pl.ds(D * (unit - EXPAND), D)]
        return shrink_own.at[:, pl.ds(OWN * (unit - SQUARE), OWN)]

    stream = held.stream
    far, mate_seq = (seq + 4) % 8, (seq + 2) % 4 + 4 * group
    other_seq = 2 * z + 1 - core
    other_mate = (other_seq + 2) % 4 + 4 * group
    slot_far, slot_mate, slot_mate_far, slot_core = links.slot(), links.slot(), links.slot(), links.slot(4)
    home = moves.start(tokens.at[group], stream.at[block_rows(seq)])
    gather = Gather(links, moves, own, square, shrink)
    for _ in range(Gather.EARLY):
        gather.tick()
    links.send(slot_far, tokens.at[1 - group], stream.at[block_rows(seq)], opposite)
    links.send(slot_mate, tokens.at[group], stream.at[block_rows(seq)], mate)
    links.send(slot_core, tokens.at[group], stream.at[block_rows(seq)], partner)
    slot_memory, slot_context = links.slot(4), links.slot()
    context_home = moves.start(memory.at[group], held.context.at[z, core])
    for k in (1, 2, 3):
        links.send(slot_memory + z, memory.at[((z + k) % 4) // 2], held.context.at[z, core], place.along_z(k))
    norm_steps = all_sum(links, norms, held.gains, held.work)
    next(norm_steps)

    def sentence(places):
        result, end = jnp.zeros_like(places), 0
        for index in range(lengths.shape[1] - 1):
            end = end + lengths[group, index]
            result = result + (places >= end).astype(jnp.int32)
        return result

    held.norm_sums[...] = jnp.zeros_like(held.norm_sums)
    held.self_logs[...] = jnp.zeros_like(held.self_logs)
    held.cross_logs[...] = jnp.zeros_like(held.cross_logs)

    @loop(OWN // STEP)
    def _(index):
        row = index * STEP + lax.broadcasted_iota(jnp.int32, (STEP, 1), 0)
        row_place = LEN * low + row + jnp.where(row >= LEN, 3 * LEN, 0)
        row_sentence = sentence(row_place)
        key_place = lax.broadcasted_iota(jnp.int32, (1, SPAN), 1)
        allowed = (row_sentence == sentence(key_place)) & (key_place <= row_place)
        held.self_bias[tile(index, STEP), :] = jnp.where(allowed, 0.0, masked_score)
        met = row_sentence == segments[pl.ds(group, 1), :]
        held.cross_bias[tile(index, STEP), :] = jnp.where(met, 0.0, masked_score)

    def pass_on(number, block):
        links.send(slot_core + number, stream.at[block_rows(block)], stream.at[block_rows(block)], partner)

    gather.tick()
    next(norm_steps)
    gather.tick()
    next(norm_steps)
    gather.tick()
    links.arrived(slot_far, stream.at[block_rows(far)])
    links.send(slot_mate_far, stream.at[block_rows(far)], stream.at[block_rows(far)], mate)
    pass_on(1, far)
    gather.tick()
    links.arrived(slot_mate, stream.at[block_rows(mate_seq)])
    pass_on(2, mate_seq)
    moves.wait(context_home)
    for k in (1, 2, 3):
        links.arrived(slot_memory + (z + k) % 4, held.context.at[(z + k) % 4, core])
    links.send(slot_context, held.context.at[:, core], held.context.at[:, core], partner)
    next(norm_steps)
    gather.tick()
    links.arrived(slot_mate_far, stream.at[block_rows((mate_seq + 4) % 8)])
    pass_on(3, (mate_seq + 4) % 8)
    gather.tick()
    cotangent_rows, cotangent_far = block_rows(group), block_rows(1 - group)
    slot_cotangent = links.slot()
    cotangent_home = moves.start(out_grad.at[group], held.cotangent.at[cotangent_rows])
    links.send(slot_cotangent, out_grad.at[1 - group], held.cotangent.at[cotangent_rows], opposite)
    moves.wait(home)
    for number, block in enumerate((other_seq, (other_seq + 4) % 8, other_mate, (other_mate + 4) % 8)):
        links.arrived(slot_core + number, stream.at[block_rows(block)])
    links.arrived(slot_context, held.context.at[:, 1 - core])
    held.mine[pl.ds(0, LEN), :] = stream[block_rows(low), :]
    held.mine[pl.ds(LEN, LEN), :] = stream[block_rows(low + 4), :]

    loads = {}

    def fetch(unit, slot):
        if unit < SQUARE:
            target = held.weights.at[slot]
            loads[unit] = (moves.start(square.at[unit].reshape(D, D), target), target)
        else:
            target = held.shrink_in.at[slot]
            loads[unit] = (moves.start(shrink.at[unit - SQUARE].reshape(4, D, OWN), target), target)

    def weight(unit):
        step, target = loads.pop(unit)
        moves.wait(step)
        return target

    turning = {"count": 0, "open": {}}
    landing = []
    mine, theirs = core_rows(core), core_rows(1 - core)

    def turn(source, name):
        number = turning["count"] % 3
        for move, sent in turning["open"].pop(number, ()):
            moves.wait(move)
            links.sent(sent)
        turning["count"] += 1
        buffer, target = held.turned.at[number], getattr(turned, name)

        @loop(4)
        def _(index):
            buffer[pl.ds(4 * index, 4)] = source[:, tile(index, OWN)].T.reshape(4, 2, 32, OWN)

        slot = links.slot()
        move = moves.start(buffer.at[:, core], target.at[:, :, mine])
        sent = links.send(slot, buffer.at[:, 1 - core], target.at[:, :, mine], partner)
        landing.append((slot, target.at[:, :, theirs]))
        turning["open"][number] = [(move, sent)]

    def keep(*names):
        for name in names:
            moves.start(getattr(held, name), getattr(kept, name))

    def gain(number):
        return held.gains[pl.ds(number, 1), :]

    def bias(number):
        return held.gains[pl.ds(3 + number, 1), :]

    fetch(KEY, 0)
    turn(held.mine, "tokens_t")
    next(norm_steps)
    fetch(VALUE, 1)
    rows_times(stream, weight(KEY), put(held.keys))
    gather.tick()
    fetch(QUERY, 2)
    rows_times(stream, weight(VALUE), put(held.values))
    rows_times(held.mine, weight(QUERY), put(held.queries))

    def attend_part(first, pairs):
        attend_rows(
            held.queries, held.keys, held.values, held.self_bias, held.self_logs, held.attended, SELF_SEGMENTS, pairs, first
        )

    fetch(OUT, 3)
    attend_part(0, 3)
    gather.tick()
    fetch(CROSS_QUERY, 0)
    attend_part(3, 3)
    gather.tick()
    fetch(CROSS_KEY, 1)
    attend_part(6, 2)
    rows_times(held.attended, weight(OUT), put(held.sums, F32))
    keep("queries", "keys", "values", "self_bias", "self_logs", "cross_bias", "gains")

    def first_rows(rows, result, _):
        held.first_low[rows, :] = (result * gain(0) + bias(0)).astype(BF)

    def after(rows, previous):
        return held.sums[rows, :] + alpha_scale * previous

    norm_rows(lambda rows: after(rows, held.mine[rows, :].astype(F32)), held.normal_one, held.inverse_one, first_rows)
    turn(held.attended, "attended_t")
    rows_times(held.first_low, weight(CROSS_QUERY), put(held.cross_queries))
    context = held.context.reshape(MEM, D)
    rows_times(context, weight(CROSS_KEY), put(held.cross_keys), MEM)
    gather.tick()
    fetch(CROSS_VALUE, 2)
    turn(held.first_low, "first_t")

    @loop(4)
    def _(index):
        held.turned_memory[pl.ds(4 * index, 4)] = context[:, tile(index, OWN)].T.reshape(4, 2, 32, MEM)

    moves.start(held.turned_memory.at[:, core], turned.memory_t)
    rows_times(context, weight(CROSS_VALUE), put(held.cross_values), MEM)
    attend_rows(
        held.cross_queries, held.cross_keys, held.cross_values, held.cross_bias, held.cross_logs,
        held.cross_attended, CROSS_SEGMENTS,
    )
    gather.tick()
    fetch(CROSS_OUT, 3)
    keep("cross_queries", "cross_keys", "cross_values", "cross_logs", "normal_one", "inverse_one")
    rows_times(held.cross_attended, weight(CROSS_OUT), put(held.sums, F32))

    def second_rows(rows, result, _):
        held.second_low[rows, :] = (result * gain(1) + bias(1)).astype(BF)

    norm_rows(
        lambda rows: after(rows, held.normal_one[rows, :] * gain(0) + bias(0)),
        held.normal_two, held.inverse_two, second_rows,
    )
    keep("normal_two", "inverse_two")
    gather.tick()
    turn(held.cross_attended, "cross_t")
    turn(held.second_low, "second_t")
    turned_open = {}
    for part in range(4):
        if part > 0:
            gather.tick()
        fetch(EXPAND + part, part)
        active, slopes = held.active.at[part], held.slopes.at[part]

        def activate(rows, columns, value):
            inner = GELU_SLOPE * (value + GELU_CUBE * value * value * value)
            bend = jnp.tanh(inner)
            active[rows, columns] = (0.5 * value * (1.0 + bend)).astype(BF)
            slope = 0.5 * (1.0 + bend) + 0.5 * value * (1.0 - bend * bend) * (
                GELU_SLOPE * (1.0 + 3.0 * GELU_CUBE * value * value)
            )
            slopes[rows, columns] = slope.astype(BF)

        rows_times(held.second_low, weight(EXPAND + part), activate)
        number = part % 2
        for move, sent in turned_open.pop(number, ()):
            moves.wait(move)
            links.sent(sent)
        buffer = held.turned_active.at[number]

        @loop(4)
        def _(index):
            buffer[index] = active[:, tile(index, OWN)].T.reshape(2, 4, 32, OWN)

        slot = links.slot()
        move = moves.start(buffer.at[:, core], turned.active_t.at[part, :, :, :, mine])
        sent = links.send(slot, buffer.at[:, 1 - core], turned.active_t.at[part, :, :, :, mine], partner)
        landing.append((slot, turned.active_t.at[part, :, :, :, theirs]))
        turned_open[number] = [(move, sent)]
    keep("slopes")
    for part in range(4):
        gather.tick()
        fetch(SQUARE + part, part % 2)
        shrink_part = weight(SQUARE + part)
        for first in (0, LEN):
            rows = pl.ds(first, LEN)
            total = project(held.active[0, rows, :], shrink_part[0])
            for depth in (1, 2, 3):
                total = total + project(held.active[depth, rows, :], shrink_part[depth])
            held.sums[rows, pl.ds(OWN * part, OWN)] = total
    links.arrived(slot_cotangent, held.cotangent.at[cotangent_far])
    moves.wait(cotangent_home)

    def third_rows(rows, result, scale):
        held.final_low[rows, :] = (result * gain(2) + bias(2)).astype(BF)
        grad = norm_rows_back(held.cotangent[rows, :].astype(F32), result, scale, gain(2), held.norm_sums, 2)
        held.third_grad[rows, :] = grad
        held.branch_own[rows, :] = grad.astype(BF)

    norm_rows(lambda rows: after(rows, held.normal_two[rows, :] * gain(1) + bias(1)), None, None, third_rows)
    slot = links.slot()
    links.send(slot, held.branch_own, turned.branch.at[mine], partner)
    landing.append((slot, turned.branch.at[theirs]))
    moves.start(held.branch_own, turned.branch.at[mine])
    keep("third_grad", "norm_sums", "final_low")
    for arrival in landing:
        links.arrived(*arrival)
    moves.finish()
    links.finish()


IN_VMEM = pl.BlockSpec(memory_space=pltpu.VMEM)
IN_SMEM = pl.BlockSpec(memory_space=pltpu.SMEM)
IN_PLACE = pl.BlockSpec(memory_space=pl.ANY)


def shapes_of(table):
    return [jax.ShapeDtypeStruct(shape, dtype) for shape, dtype in table.values()]


def vmem_of(table):
    return [pltpu.VMEM(shape, dtype) for shape, dtype in table.values()]


def forward_call(lengths, segments, norms, tokens, memory, out_grad, weights):
    results = [
        jax.ShapeDtypeStruct(SQUARE_SHAPE, BF),
        jax.ShapeDtypeStruct(SHRINK_SHAPE, BF),
        *shapes_of(FORWARD_SAVES),
        *shapes_of(TURNED_SAVES),
    ]
    values = pl.pallas_call(
        forward_kernel,
        in_specs=[IN_SMEM, IN_VMEM, IN_VMEM] + [IN_PLACE] * 13,
        out_specs=[IN_PLACE] * len(results),
        out_shape=results,
        scratch_shapes=[
            *vmem_of(FORWARD_SAVES),
            *vmem_of(FORWARD_SCRATCH),
            pltpu.SemaphoreType.DMA((FORWARD_SENDS,)),
            pltpu.SemaphoreType.DMA((FORWARD_SLOTS,)),
            pltpu.SemaphoreType.DMA((FORWARD_MOVES,)),
        ],
        compiler_params=pltpu.CompilerParams(collective_id=0, has_side_effects=True, vmem_limit_bytes=VMEM_BYTES),
    )(lengths, segments, norms, tokens, memory, out_grad, *weights)
    saves = dict(zip([*FORWARD_SAVES, *TURNED_SAVES], values[2:]))
    return values[0], values[1], saves


class Scatter:
    WIDE = (0, 2, 4, 6, 8)

    def __init__(self, links, grads, from_first, from_second, from_z, from_line, from_last, result):
        self.links, self.grads, self.result = links, grads, result
        self.from_first, self.from_second, self.from_z = from_first, from_second, from_z
        self.from_line, self.from_last = from_line, from_last
        self.slots, self.pending, self.now = {}, {}, 0

    def home(self, unit):
        for step in self.pending.pop(unit - self.grads.shape[0], ()):
            self.links.sent(step)
        self.slots[unit] = self.links.slot(12)
        return self.grads.at[unit % self.grads.shape[0]]

    def add(self, total, part):
        for row in range(total.shape[0]):
            if len(total.shape) > 3:
                self.add(total.at[row], part.at[row])
            else:
                total[row] = (total[row].astype(F32) + part[row].astype(F32)).astype(BF)

    def phase(self, unit, half, number):
        links, place, wide = self.links, self.links.place, unit in self.WIDE
        y, x, z = place.y, place.x, place.z
        here = self.grads.at[unit % self.grads.shape[0]]
        depth = unit % self.from_first.shape[0]
        rows = pl.ds(16 * half, 16)
        slot = self.slots[unit] + 6 * half
        by_y = half == 0
        first, second = ("y", "x") if by_y else ("x", "y")
        away = (1 - y, ALL) if by_y else (ALL, 1 - x)
        kept = (y, ALL) if by_y else (ALL, x)
        corner, other, mine = ((y, 1 - x), 1 - x, x) if by_y else ((1 - y, x), 1 - y, y)
        home = here.at[y, x, :, rows]
        first_in = self.from_first.at[depth, :, :, rows]
        second_in = self.from_second.at[depth, :, rows]
        if wide:
            index = self.WIDE.index(unit)
            line_in = self.from_line.at[index, :, :, rows]
            last_in = self.from_last.at[index, rows]
        else:
            before = sum(wider < unit for wider in self.WIDE)
            line_in = self.from_z.at[(unit - before) % self.from_z.shape[0], :, :, rows]

        def owned(owner):
            return here.at[(*kept, owner, rows)] if wide else here.at[y, x, pl.ds(owner, 1), rows]

        def send(number, source, target, device, when=None):
            self.pending.setdefault(unit, []).append(links.send(slot + number, source, target, device, when))

        def along_line():
            send(2 + z, owned(place.mate_z), line_in.at[z], place.mate())
            send(2 + z, owned(place.inner_z), line_in.at[z], place.at(z=place.inner_z))
            send(2 + place.mate_z, owned(3 - z), line_in.at[place.mate_z], place.mate(), place.outer)

        def hand_on():
            def join():
                links.arrived(slot + 2 + z, line_in.at[z])
                self.add(owned(place.next_z), line_in.at[z])

            under(place.inner, join)
            send(2 + z, owned(place.next_z), line_in.at[z], place.at(z=place.next_z), place.inner)

        def line_sum():
            for source in (place.mate_z, place.next_z):
                links.arrived(slot + 2 + source, line_in.at[source])
                self.add(owned(z), line_in.at[source])

            def third():
                links.arrived(slot + 2 + 3 - z, line_in.at[3 - z])
                self.add(owned(z), line_in.at[3 - z])

            under(place.inner, third)

        if number == 0:
            send(0, here.at[(*away, ALL, rows)], first_in, place.across(first))
        if number == 1 and not wide:
            links.arrived(slot, first_in)
            corner_part = here.at[(*corner, ALL, rows)]
            self.add(corner_part, first_in.at[other])
            send(1, corner_part, second_in, place.across(second))
            self.add(home, first_in.at[mine])
        if number == 2 and not wide:
            links.arrived(slot + 1, second_in)
            self.add(home, second_in)
            along_line()
        if number == 3 and not wide:
            hand_on()
        if number == 4 and not wide:
            line_sum()
            self.result(unit, rows, home[z].astype(F32))
        if number == 1 and wide:
            links.arrived(slot, first_in)
            self.add(here.at[(*kept, ALL, rows)], first_in)
            along_line()
        if number == 2 and wide:
            hand_on()
        if number == 3 and wide:
            line_sum()
            send(1, owned(z).at[other], last_in, place.across(second))
        if number == 4 and wide:
            links.arrived(slot + 1, last_in)
            self.result(unit, rows, home[z].astype(F32) + last_in[...].astype(F32))

    def tick(self):
        for number in range(5):
            unit = self.now - number
            if 0 <= unit < UNITS:
                for half in (0, 1):
                    self.phase(unit, half, number)
        self.now += 1


DEPTH = 4
BACKWARD_SCRATCH = {
    "weights": ((3, D, D), BF),
    "shrink_in": ((4, D, OWN), BF),
    "grads": ((5, 2, 2, 4, 32, D), BF),
    "from_first": ((DEPTH, 2, 4, 32, D), BF),
    "from_second": ((DEPTH, 4, 32, D), BF),
    "from_z": ((6, 4, 1, 32, D), BF),
    "from_line": ((len(Scatter.WIDE), 4, 2, 32, D), BF),
    "from_last": ((len(Scatter.WIDE), 32, D), BF),
    "up": ((4, 2 * OWN, D), BF),
    "second_sum": ((OWN, D), F32),
    "cross_branch": ((2 * OWN, D), BF),
    "attended_grad": ((OWN, D), BF),
    "cross_query_grad": ((2 * OWN, D), BF),
    "cross_terms": ((2, 2, MEM, D), BF),
    "cross_sums": ((2, MEM, D), BF),
    "self_branch": ((2 * OWN, D), BF),
    "query_grad": ((2 * OWN, D), BF),
    "terms_core": ((2, 2, 2, LEN, D), BF),
    "terms_mate": ((2, 2, LEN, D), BF),
    "key_grad": ((2 * OWN, D), BF),
    "value_grad": ((2 * OWN, D), BF),
    "memory_own": ((4, 16, D), BF),
    "memory_in": ((4, 16, D), BF),
    "far_own": ((LEN, D), BF),
    "far_in": ((LEN, D), BF),
    "work": ((8, 8, D), F32),
}
BACKWARD_SENDS, BACKWARD_SLOTS, BACKWARD_MOVES = 256, 256, 64


def backward_kernel(square, shrink, *refs):
    saved = [*FORWARD_SAVES, *TURNED_SAVES]
    names = [name for name in saved if name != "final_low"]
    kept = Refs(saved, refs[: len(saved)])
    rest = refs[len(saved) :]
    output, input_grad, memory_grad, *unit_grads = rest[:11]
    expand_grad, shrink_grad, norm_grads = rest[11:14]
    rest = rest[14:]
    held = Refs(names, rest[: len(names)])
    rest = rest[len(names) :]
    held.__dict__.update(Refs(BACKWARD_SCRATCH, rest[: len(BACKWARD_SCRATCH)]).__dict__)
    send_sem, recv_sem, move_sem = rest[len(BACKWARD_SCRATCH) :]

    place = Place()
    links, moves = Links(place, send_sem, recv_sem), Moves(move_sem)
    z, core, group = place.z, place.core, place.group
    partner = place.across("core")
    mine, theirs = core_rows(core), core_rows(1 - core)
    loads = {}

    def bring(*wanted):
        for name in wanted:
            loads[name] = moves.start(getattr(kept, name), getattr(held, name))

    def have(*wanted):
        for name in wanted:
            moves.wait(loads.pop(name))

    def fetch(unit, slot):
        loads[unit] = moves.start(square.at[unit].reshape(D, D), held.weights.at[slot])

    def weight(unit, slot):
        moves.wait(loads.pop(unit))
        return held.weights.at[slot]

    bring("branch", "active_t")

    def fetch_shrink(part):
        loads[SQUARE] = moves.start(shrink.at[:, part], held.shrink_in)

    fetch_shrink(0)
    for part in range(3):
        fetch(EXPAND + part, part)
    bring("slopes", "third_grad", "second_t", "norm_sums", "gains", "normal_two", "inverse_two")
    bring("cross_queries", "cross_keys", "cross_values", "cross_bias", "cross_logs", "cross_t")
    bring("normal_one", "inverse_one", "first_t", "memory_t", "attended_t", "tokens_t")
    bring("queries", "keys", "values", "self_bias", "self_logs")
    place.greet()

    order = [12, 13, 14, 15, 8, 9, 10, 11, CROSS_OUT, CROSS_QUERY, CROSS_KEY, CROSS_VALUE, OUT, QUERY, KEY, VALUE]

    def result(number, rows, total):
        unit = order[number]
        if unit < EXPAND:
            unit_grads[unit][rows, :] = total
        elif unit < SQUARE:
            expand_grad[rows, pl.ds(D * (unit - EXPAND), D)] = total
        else:
            shrink_grad[pl.ds(32 * (unit - SQUARE) + rows.start, rows.size), :] = total

    buffers = (held.from_first, held.from_second, held.from_z, held.from_line, held.from_last)
    scatter = Scatter(links, held.grads, *buffers, result)
    made = {"count": 0}

    def produce(left, right, depth=2 * OWN):
        target = scatter.home(made["count"])
        made["count"] += 1

        @loop(4)
        def _(index):
            columns = tile(index, OWN)
            term = project(left().reshape(512, depth), right[:, columns])
            target[:, :, :, :, columns] = term.astype(BF).reshape(2, 2, 4, 32, OWN)

    def share(ref):
        slot = links.slot()
        links.send(slot, ref.at[mine], ref.at[mine], partner)
        return slot

    def shared(ref, slot):
        links.arrived(slot, ref.at[theirs])

    def gain(number):
        return held.gains[pl.ds(number, 1), :]

    have("branch", "active_t")

    def produce_shrink(part):
        produce(lambda: held.active_t[:, :, part], held.branch)

    def produce_expand(part):
        shared(held.up.at[part], up_slots[part])
        produce(lambda: held.second_t[...], held.up.at[part])

    produce_shrink(0)
    scatter.tick()
    slot_output = links.slot()
    moves.start(kept.final_low.at[block_rows(group)], output.at[group])
    links.send(slot_output, kept.final_low.at[block_rows(1 - group)], output.at[group], place.along_z(2))
    for part in (1, 2, 3):
        produce_shrink(part)
    scatter.tick()
    have("slopes")
    own_branch = held.branch.at[mine]
    up_slots, up_sends = [], []
    for part in range(4):
        if part == 2:
            scatter.tick()
        up = held.up.at[part, mine]
        slopes = held.slopes.at[part]

        moves.wait(loads.pop(SQUARE))

        @loop(4)
        def _(index):
            columns = tile(index, OWN)
            total = project_back(own_branch[:, pl.ds(0, OWN)], held.shrink_in[0, columns, :])
            for depth in (1, 2, 3):
                total = total + project_back(own_branch[:, pl.ds(OWN * depth, OWN)], held.shrink_in[depth, columns, :])
            up[:, columns] = (total * slopes[:, columns].astype(F32)).astype(BF)

        up_slots.append(links.slot())
        up_sends.append(links.send(up_slots[part], up, up, partner))
        if part < 3:
            fetch_shrink(part + 1)

        def add(columns, value):
            if part == 0:
                held.second_sum[:, columns] = value
            else:
                held.second_sum[:, columns] += value

        rows_back(up, weight(EXPAND + part, part % 3), add)
        fetch((EXPAND + 3, CROSS_OUT, CROSS_QUERY, CROSS_KEY)[part], part % 3)
    scatter.tick()
    have("third_grad", "norm_sums", "gains", "normal_two", "inverse_two", "second_t")

    def spread(inverse, rows):
        return inverse[rows, pl.ds(0, 1)]

    @loop(OWN // STEP)
    def _(index):
        rows = tile(index, STEP)
        grad = held.second_sum[rows, :] + alpha_scale * held.third_grad[rows, :]
        pre = norm_rows_back(grad, held.normal_two[rows, :], spread(held.inverse_two, rows), gain(1), held.norm_sums, 1)
        held.second_sum[rows, :] = pre
        held.cross_branch[pl.ds(pl.multiple_of(OWN * core + STEP * index, STEP), STEP), :] = pre.astype(BF)

    slot_cross_branch = share(held.cross_branch)
    produce_expand(0)
    scatter.tick()

    def low(target):
        def store(columns, value):
            target[:, columns] = value.astype(BF)

        return store

    rows_back(held.cross_branch.at[mine], weight(CROSS_OUT, 1), low(held.attended_grad))
    fetch(CROSS_VALUE, 1)
    have("cross_queries", "cross_keys", "cross_values", "cross_bias", "cross_logs", "cross_t")
    attend_rows_back(
        held.cross_queries, held.cross_keys, held.cross_values, held.cross_bias, held.cross_logs, held.attended_grad,
        held.cross_query_grad.at[mine], held.cross_terms.at[0, core], held.cross_terms.at[1, core], CROSS_SEGMENTS, H // 2,
    )
    slot_cross_query = share(held.cross_query_grad)
    slot_cross_terms = links.slot()
    links.send(slot_cross_terms, held.cross_terms.at[:, core], held.cross_terms.at[:, core], partner)
    produce_expand(1)
    scatter.tick()

    def add_first(columns, value):
        held.third_grad[:, columns] = value

    rows_back(held.cross_query_grad.at[mine], weight(CROSS_QUERY, 2), add_first)
    fetch(OUT, 2)
    have("normal_one", "inverse_one", "first_t", "memory_t", "attended_t", "tokens_t")

    @loop(OWN // STEP)
    def _(index):
        rows = tile(index, STEP)
        grad = held.third_grad[rows, :] + alpha_scale * held.second_sum[rows, :]
        pre = norm_rows_back(grad, held.normal_one[rows, :], spread(held.inverse_one, rows), gain(0), held.norm_sums, 0)
        held.second_sum[rows, :] = pre
        held.self_branch[pl.ds(pl.multiple_of(OWN * core + STEP * index, STEP), STEP), :] = pre.astype(BF)

    slot_self_branch = share(held.self_branch)
    norm_steps = all_sum(links, held.norm_sums, norm_grads, held.work)
    next(norm_steps)
    produce_expand(2)
    scatter.tick()
    produce_expand(3)
    rows_back(held.self_branch.at[mine], weight(OUT, 2), low(held.attended_grad))
    fetch(QUERY, 2)
    have("queries", "keys", "values", "self_bias", "self_logs")
    for step in up_sends:
        links.sent(step)
    terms = held.up.reshape(2, 2, 2, 2, LEN, D)
    key_terms, value_terms = (held.up.at[pl.ds(2 * which, 2)].reshape(SPAN, D) for which in (0, 1))

    def attend_part(first, pairs):
        attend_rows_back(
            held.queries, held.keys, held.values, held.self_bias, held.self_logs, held.attended_grad,
            held.query_grad.at[mine], key_terms, value_terms, SELF_SEGMENTS, pairs, first,
        )

    attend_part(0, 2)
    scatter.tick()
    next(norm_steps)
    attend_part(2, 2)
    shared(held.cross_branch, slot_cross_branch)
    produce(lambda: held.cross_t[...], held.cross_branch)
    scatter.tick()
    next(norm_steps)
    attend_part(4, 2)
    shared(held.cross_query_grad, slot_cross_query)
    produce(lambda: held.first_t[...], held.cross_query_grad)
    scatter.tick()
    next(norm_steps)
    attend_part(6, 2)
    slot_query = share(held.query_grad)
    slot_terms = links.slot()
    links.send(slot_terms, terms.at[:, :, :, 1 - core], held.terms_core, partner)

    links.arrived(slot_cross_terms, held.cross_terms.at[:, 1 - core])
    for which in (0, 1):
        held.cross_sums[which] = (held.cross_terms[which, 0].astype(F32) + held.cross_terms[which, 1].astype(F32)).astype(BF)
    produce(lambda: held.memory_t[...], held.cross_sums.at[0], MEM)
    scatter.tick()
    next(norm_steps)

    links.arrived(slot_terms, held.terms_core)
    near = z % 2

    def join(place_index):
        for which in (0, 1):
            for high in (0, 1):
                value = terms[which, high, place_index, core].astype(F32) + held.terms_core[which, high, place_index].astype(F32)
                terms[which, high, place_index, core] = value.astype(BF)

    join(1 - near)
    slot_mate = links.slot()
    links.send(slot_mate, terms.at[:, :, 1 - near, core], held.terms_mate, place.mate())
    join(near)

    produce(lambda: held.memory_t[...], held.cross_sums.at[1], MEM)
    scatter.tick()

    cross_key, cross_value = weight(CROSS_KEY, 0), weight(CROSS_VALUE, 1)
    sums = held.cross_sums.reshape(2, 4, 2, 16, D)

    @loop(4)
    def _(index):
        columns = tile(index, OWN)
        term = project_back(sums[0, :, core].reshape(64, D), cross_key[columns, :])
        term = term + project_back(sums[1, :, core].reshape(64, D), cross_value[columns, :])
        held.memory_own[:, :, columns] = term.astype(BF).reshape(4, 16, OWN)

    fetch(KEY, 0)
    fetch(VALUE, 1)
    slot_memory = links.slot(4)
    for k in (1, 2, 3):
        links.send(slot_memory + z, held.memory_own.at[(z + k) % 4], held.memory_in.at[z], place.along_z(k))
    held.memory_in[z] = held.memory_own[z]

    shared(held.self_branch, slot_self_branch)
    produce(lambda: held.attended_t[...], held.self_branch)
    scatter.tick()
    shared(held.query_grad, slot_query)
    produce(lambda: held.tokens_t[...], held.query_grad)
    scatter.tick()

    def add_input(columns, value):
        held.third_grad[:, columns] = alpha_scale * held.second_sum[:, columns] + value

    rows_back(held.query_grad.at[mine], weight(QUERY, 2), add_input)
    links.arrived(slot_mate, held.terms_mate)
    for which, target in enumerate((held.key_grad, held.value_grad)):
        for high in (0, 1):
            value = terms[which, high, near, core].astype(F32) + held.terms_mate[which, high].astype(F32)
            target[pl.ds(pl.multiple_of(OWN * core + LEN * high, LEN), LEN), :] = value.astype(BF)
    slot_key, slot_value = share(held.key_grad), share(held.value_grad)

    def add_more(columns, value):
        held.third_grad[:, columns] += value

    rows_back(held.key_grad.at[mine], weight(KEY, 0), add_more)
    rows_back(held.value_grad.at[mine], weight(VALUE, 1), add_more)
    held.far_own[...] = held.third_grad[block_rows(1 - group), :].astype(BF)
    slot_far = links.slot()
    links.send(slot_far, held.far_own, held.far_in, place.along_z(2))
    shared(held.key_grad, slot_key)
    produce(lambda: held.tokens_t[...], held.key_grad)
    scatter.tick()
    shared(held.value_grad, slot_value)
    produce(lambda: held.tokens_t[...], held.value_grad)
    scatter.tick()
    input_grad[group] = held.third_grad[block_rows(group), :]
    scatter.tick()
    for k in (1, 2, 3):
        links.arrived(slot_memory + (z + k) % 4, held.memory_in.at[(z + k) % 4])
    for which in (0, 1):
        memory_grad[which] = held.memory_in[2 * which].astype(F32) + held.memory_in[2 * which + 1].astype(F32)
    for _ in range(3):
        scatter.tick()
    links.arrived(slot_far, held.far_in)
    input_grad[1 - group] = held.far_in[...].astype(F32)
    links.arrived(slot_output, output.at[1 - group])
    moves.finish()
    links.finish()


def backward_call(square, shrink, saves, block_shape, memory_shape):
    results = [jax.ShapeDtypeStruct(block_shape, BF)]
    results += [jax.ShapeDtypeStruct(shape, F32) for shape in (block_shape, memory_shape)]
    results += [jax.ShapeDtypeStruct((32, D), F32)] * 8
    results += [jax.ShapeDtypeStruct(shape, F32) for shape in ((32, 4 * D), (LEN, D), (8, D))]
    saved = {**FORWARD_SAVES, **TURNED_SAVES}
    held = {name: saved[name] for name in saved if name != "final_low"}
    return pl.pallas_call(
        backward_kernel,
        in_specs=[IN_PLACE] * (2 + len(saved)),
        out_specs=[IN_PLACE] + [IN_VMEM] * (len(results) - 1),
        out_shape=results,
        scratch_shapes=[
            *vmem_of(held),
            *vmem_of(BACKWARD_SCRATCH),
            pltpu.SemaphoreType.DMA((BACKWARD_SENDS,)),
            pltpu.SemaphoreType.DMA((BACKWARD_SLOTS,)),
            pltpu.SemaphoreType.DMA((BACKWARD_MOVES,)),
        ],
        compiler_params=pltpu.CompilerParams(collective_id=1, has_side_effects=True, vmem_limit_bytes=63 << 20),
    )(square, shrink.reshape(4, 4, D, OWN), *(saves[name] for name in saved))


def hand_over_kernel(*refs):
    count = len(refs) // 3
    sem = refs[-1]
    loads = [pltpu.make_async_copy(refs[n], refs[2 * count + n], sem.at[0, n]) for n in range(count)]
    stores = [pltpu.make_async_copy(refs[2 * count + n], refs[count + n], sem.at[1, n]) for n in range(count)]
    for load in loads:
        load.start()
    for load, store in zip(loads, stores):
        load.wait()
        store.start()
    for store in stores:
        store.wait()


def hand_over(values):
    return pl.pallas_call(
        hand_over_kernel,
        in_specs=[IN_PLACE] * len(values),
        out_specs=[IN_PLACE] * len(values),
        out_shape=[jax.ShapeDtypeStruct(value.shape, value.dtype) for value in values],
        scratch_shapes=[
            *(pltpu.VMEM(value.shape, value.dtype) for value in values),
            pltpu.SemaphoreType.DMA((2, len(values))),
        ],
        compiler_params=pltpu.CompilerParams(vmem_limit_bytes=VMEM_BYTES),
    )(*values)


def fast_shards(
    tokens, memory, lengths, memory_segments, out_grad,
    self_query, self_key, self_value, self_out,
    cross_query, cross_key, cross_value, cross_out,
    expand_weight, shrink_weight, norm_gains, norm_biases,
):
    me = lax.axis_index("dp") * lax.axis_size("seq") + lax.axis_index("seq")
    norms = jnp.concatenate([norm_gains, norm_biases, jnp.zeros((2, 32), BF)]).astype(F32)
    norms = lax.dynamic_update_slice(jnp.zeros((8, D), F32), norms, (0, 32 * me))
    weights = (self_key, self_value, self_query, self_out, cross_query, cross_key, cross_value, cross_out)
    square, shrink, saves = forward_call(
        lengths, memory_segments, norms, tokens, memory, out_grad, (*weights, expand_weight, shrink_weight)
    )
    *values, norm_grads = backward_call(square, shrink, saves, tokens.shape, memory.shape)
    output, input_grad, memory_grad, *units, expand_grad, shrink_grad = hand_over(values)
    norm_grads = lax.dynamic_slice(norm_grads, (0, 32 * me), (8, 32))
    return (
        output,
        input_grad,
        memory_grad,
        *(units[unit] for unit in (QUERY, KEY, VALUE, OUT, CROSS_QUERY, CROSS_KEY, CROSS_VALUE, CROSS_OUT)),
        expand_grad,
        shrink_grad,
        norm_grads[:3],
        norm_grads[3:6],
    )


def solution(mesh):
    quick = dict(mesh.shape) == {"dp": 4, "seq": 8}
    return jax.shard_map(
        fast_shards if quick else shards,
        mesh=mesh,
        in_specs=(
            P("dp", "seq", None),
            P("dp", "seq", None),
            P("dp", None),
            P("dp", None),
            P("dp", "seq", None),
            P(("dp", "seq"), None),
            P(("dp", "seq"), None),
            P(("dp", "seq"), None),
            P(("dp", "seq"), None),
            P(("dp", "seq"), None),
            P(("dp", "seq"), None),
            P(("dp", "seq"), None),
            P(("dp", "seq"), None),
            P(("dp", "seq"), None),
            P(("dp", "seq"), None),
            P(None, ("dp", "seq")),
            P(None, ("dp", "seq")),
        ),
        out_specs=(
            P("dp", "seq", None),
            P("dp", "seq", None),
            P("dp", "seq", None),
            P(("dp", "seq"), None),
            P(("dp", "seq"), None),
            P(("dp", "seq"), None),
            P(("dp", "seq"), None),
            P(("dp", "seq"), None),
            P(("dp", "seq"), None),
            P(("dp", "seq"), None),
            P(("dp", "seq"), None),
            P(("dp", "seq"), None),
            P(("dp", "seq"), None),
            P(None, ("dp", "seq")),
            P(None, ("dp", "seq")),
        ),
        check_vma=False,
    )
```

```python
import functools

import jax
import jax.numpy as jnp
from jax import lax
from jax.experimental import pallas as pl
from jax.experimental.pallas import tpu as pltpu
from jax.sharding import PartitionSpec as P

H = 16
HD = 64
MB = 2


alpha_scale = 300.0**0.25
norm_eps = 1e-05
masked_score = -1e30


def layer_norm(value, gain, bias):
    average = jnp.mean(value, axis=-1, keepdims=True)
    centred = value - average
    spread = jnp.mean(centred * centred, axis=-1, keepdims=True)
    return centred * lax.rsqrt(spread + norm_eps) * gain + bias


def project(left, right):
    return jnp.dot(left, right, preferred_element_type=jnp.float32)


def project_back(left, right):
    return lax.dot_general(
        left, right, (((1,), (1,)), ((), ())), preferred_element_type=jnp.float32
    )


def weight_term(left, right):
    return lax.dot_general(
        left, right, (((0,), (0,)), ((), ())), preferred_element_type=jnp.float32
    )


def split_heads(value):
    return value.reshape(value.shape[0], value.shape[1], H, HD)


def sentence_ids(sent_ends, places):
    return jnp.sum((places[None, :, None] >= sent_ends[:, None, :]).astype(jnp.int32), axis=2)


def masked_scores(queries, key_heads, allowed, scaling):
    raw_scores = (
        jnp.einsum("gqhd,gkhd->ghqk", queries, key_heads, preferred_element_type=jnp.float32)
        * scaling
    )
    return jnp.where(allowed[:, None], raw_scores, masked_score)


def attend_forward(queries, key_heads, value_heads, allowed, scaling):
    scores = masked_scores(queries, key_heads, allowed, scaling)
    row_max = jnp.max(scores, axis=3, keepdims=True)
    powers = jnp.exp(scores - row_max)
    row_total = jnp.sum(powers, axis=3, keepdims=True)
    prob_low = (powers / row_total).astype(jnp.bfloat16)
    attended = jnp.einsum(
        "ghqk,gkhd->gqhd", prob_low, value_heads, preferred_element_type=jnp.float32
    )
    return (attended, row_max + jnp.log(row_total))


def attend_backward(queries, key_heads, value_heads, allowed, scaling, log_total, attended_grad):
    scores = masked_scores(queries, key_heads, allowed, scaling)
    probability = jnp.exp(scores - log_total)
    prob_grad = jnp.einsum(
        "gqhd,gkhd->ghqk", attended_grad, value_heads, preferred_element_type=jnp.float32
    )
    score_grad = probability * (prob_grad - jnp.sum(prob_grad * probability, axis=3, keepdims=True))
    score_low = score_grad.astype(jnp.bfloat16)
    query_grad = (
        jnp.einsum("ghqk,gkhd->gqhd", score_low, key_heads, preferred_element_type=jnp.float32)
        * scaling
    )
    return (query_grad, score_low, probability.astype(jnp.bfloat16))


def micro_batch(gathered, tokens, memory, lengths, memory_segments, out_grad):
    (
        self_query,
        self_key,
        self_value,
        self_out,
        cross_query,
        cross_key,
        cross_value,
        cross_out,
        expand_weight,
        shrink_weight,
        norm_gains,
        norm_biases,
    ) = gathered
    gains = norm_gains.astype(jnp.float32)
    biases = norm_biases.astype(jnp.float32)
    group_size, local_len, features = tokens.shape
    seq_count = lax.axis_size("seq")
    seq_index = lax.axis_index("seq")
    full_len = local_len * seq_count
    row_count = group_size * local_len
    scaling = HD ** (-0.5)
    sent_ends = jnp.cumsum(lengths, axis=1)[:, :-1]
    query_places = seq_index * local_len + jnp.arange(local_len, dtype=jnp.int32)
    key_places = jnp.arange(full_len, dtype=jnp.int32)
    query_ids = sentence_ids(sent_ends, query_places)
    key_ids = sentence_ids(sent_ends, key_places)
    self_allowed = (query_ids[:, :, None] == key_ids[:, None, :]) & (
        key_places[None, None, :] <= query_places[None, :, None]
    )
    cross_allowed = query_ids[:, :, None] == memory_segments[:, None, :]
    token_rows = tokens.reshape(row_count, features)
    queries = split_heads(
        project(token_rows, self_query)
        .astype(jnp.bfloat16)
        .reshape(group_size, local_len, features)
    )
    own_keys = (
        project(token_rows, self_key).astype(jnp.bfloat16).reshape(group_size, local_len, features)
    )
    own_values = (
        project(token_rows, self_value)
        .astype(jnp.bfloat16)
        .reshape(group_size, local_len, features)
    )
    all_keys, all_values = (
        lax.all_gather(own_keys, "seq", axis=1, tiled=True),
        lax.all_gather(own_values, "seq", axis=1, tiled=True),
    )
    key_heads = split_heads(all_keys)
    value_heads = split_heads(all_values)
    attended, self_log = attend_forward(queries, key_heads, value_heads, self_allowed, scaling)
    attended = attended.reshape(row_count, features).astype(jnp.bfloat16)
    first_pre = alpha_scale * token_rows.astype(jnp.float32) + project(attended, self_out)
    first, first_pull = jax.vjp(layer_norm, first_pre, gains[0], biases[0])
    first_low = first.astype(jnp.bfloat16)
    cross_queries = split_heads(
        project(first_low, cross_query)
        .astype(jnp.bfloat16)
        .reshape(group_size, local_len, features)
    )
    own_memory = memory.reshape(-1, features)
    memory_all = lax.all_gather(memory, "seq", axis=1, tiled=True)
    memory_rows = memory_all.reshape(-1, features)
    cross_keys = (
        project(memory_rows, cross_key).astype(jnp.bfloat16).reshape(group_size, -1, features)
    )
    cross_values = (
        project(memory_rows, cross_value).astype(jnp.bfloat16).reshape(group_size, -1, features)
    )
    cross_key_heads = split_heads(cross_keys)
    cross_value_heads = split_heads(cross_values)
    cross_attended, cross_log = attend_forward(
        cross_queries, cross_key_heads, cross_value_heads, cross_allowed, scaling
    )
    cross_attended = cross_attended.reshape(row_count, features).astype(jnp.bfloat16)
    second_pre = alpha_scale * first + project(cross_attended, cross_out)
    second, second_pull = jax.vjp(layer_norm, second_pre, gains[1], biases[1])
    second_low = second.astype(jnp.bfloat16)
    upward = project(second_low, expand_weight)
    active, gelu_pull = jax.vjp(jax.nn.gelu, upward)
    active_low = active.astype(jnp.bfloat16)
    third_pre = alpha_scale * second + project(active_low, shrink_weight)
    final, third_pull = jax.vjp(layer_norm, third_pre, gains[2], biases[2])
    third_grad, gain_third, bias_third = third_pull(
        out_grad.reshape(row_count, features).astype(jnp.float32)
    )
    branch_grad = third_grad.astype(jnp.bfloat16)
    shrink_grad = weight_term(active_low, branch_grad)
    (up_grad,) = gelu_pull(project_back(branch_grad, shrink_weight))
    up_low = up_grad.astype(jnp.bfloat16)
    expand_grad = weight_term(second_low, up_low)
    second_grad = alpha_scale * third_grad + project_back(up_low, expand_weight)
    second_pre_grad, gain_second, bias_second = second_pull(second_grad)
    cross_branch = second_pre_grad.astype(jnp.bfloat16)
    cross_out_grad = weight_term(cross_attended, cross_branch)
    cross_attended_grad = split_heads(
        project_back(cross_branch, cross_out)
        .astype(jnp.bfloat16)
        .reshape(group_size, local_len, features)
    )
    cross_q_grad, cross_scores, cross_probs = attend_backward(
        cross_queries,
        cross_key_heads,
        cross_value_heads,
        cross_allowed,
        scaling,
        cross_log,
        cross_attended_grad,
    )
    cross_q_low = cross_q_grad.reshape(row_count, features).astype(jnp.bfloat16)
    cross_query_grad = weight_term(first_low, cross_q_low)
    key_term = (
        jnp.einsum(
            "ghqk,gqhd->gkhd", cross_scores, cross_queries, preferred_element_type=jnp.float32
        )
        * scaling
    ).reshape(group_size, -1, features)
    value_term = jnp.einsum(
        "ghqk,gqhd->gkhd", cross_probs, cross_attended_grad, preferred_element_type=jnp.float32
    ).reshape(group_size, -1, features)
    key_summed, value_summed = (
        lax.psum_scatter(
            key_term.astype(jnp.bfloat16), "seq", scatter_dimension=1, tiled=True
        ).astype(jnp.float32),
        lax.psum_scatter(
            value_term.astype(jnp.bfloat16), "seq", scatter_dimension=1, tiled=True
        ).astype(jnp.float32),
    )
    key_low = key_summed.reshape(-1, features).astype(jnp.bfloat16)
    value_low = value_summed.reshape(-1, features).astype(jnp.bfloat16)
    cross_key_grad = weight_term(own_memory, key_low)
    cross_value_grad = weight_term(own_memory, value_low)
    memory_grad = (project_back(key_low, cross_key) + project_back(value_low, cross_value)).reshape(
        memory.shape
    )
    first_grad = alpha_scale * second_pre_grad + project_back(cross_q_low, cross_query)
    first_pre_grad, gain_first, bias_first = first_pull(first_grad)
    self_branch = first_pre_grad.astype(jnp.bfloat16)
    self_out_grad = weight_term(attended, self_branch)
    attended_grad = split_heads(
        project_back(self_branch, self_out)
        .astype(jnp.bfloat16)
        .reshape(group_size, local_len, features)
    )
    self_q_grad, self_scores, self_probs = attend_backward(
        queries, key_heads, value_heads, self_allowed, scaling, self_log, attended_grad
    )
    count = local_len * lax.axis_size("seq")
    key_part = (
        jnp.einsum("ghqk,gqhd->kghd", self_scores, queries, preferred_element_type=jnp.float32)
        * scaling
    )
    value_part = jnp.einsum(
        "ghqk,gqhd->kghd", self_probs, attended_grad, preferred_element_type=jnp.float32
    )
    pair_summed = lax.psum_scatter(
        jnp.concatenate(
            [
                key_part.reshape(count, group_size, features),
                value_part.reshape(count, group_size, features),
            ],
            axis=2,
        ).astype(jnp.bfloat16),
        "seq",
        scatter_dimension=0,
        tiled=True,
    ).astype(jnp.float32)
    key_grad = (
        pair_summed[:, :, :features]
        .astype(jnp.bfloat16)
        .transpose(1, 0, 2)
        .reshape(row_count, features)
    )
    value_grad = (
        pair_summed[:, :, features:]
        .astype(jnp.bfloat16)
        .transpose(1, 0, 2)
        .reshape(row_count, features)
    )
    query_low = self_q_grad.reshape(row_count, features).astype(jnp.bfloat16)
    self_query_grad = weight_term(token_rows, query_low)
    self_key_grad = weight_term(token_rows, key_grad)
    self_value_grad = weight_term(token_rows, value_grad)
    input_grad = (
        alpha_scale * first_pre_grad
        + project_back(query_low, self_query)
        + project_back(key_grad, self_key)
        + project_back(value_grad, self_value)
    )
    gains_grad = jnp.stack([gain_first, gain_second, gain_third])
    biases_grad = jnp.stack([bias_first, bias_second, bias_third])
    gradients = (
        self_query_grad,
        self_key_grad,
        self_value_grad,
        self_out_grad,
        cross_query_grad,
        cross_key_grad,
        cross_value_grad,
        cross_out_grad,
        expand_grad,
        shrink_grad,
        gains_grad,
        biases_grad,
    )
    result = final.astype(jnp.bfloat16).reshape(group_size, local_len, features)
    return (result, input_grad.reshape(group_size, local_len, features), memory_grad, gradients)


def shards(
    tokens,
    memory,
    lengths,
    memory_segments,
    out_grad,
    self_query,
    self_key,
    self_value,
    self_out,
    cross_query,
    cross_key,
    cross_value,
    cross_out,
    expand_weight,
    shrink_weight,
    norm_gains,
    norm_biases,
):
    group_size = tokens.shape[0] // MB
    outputs = []
    input_grads = []
    memory_grads = []
    totals = None
    for batch_index in range(MB):
        gathered = (
            lax.all_gather(self_query, ("dp", "seq"), axis=0, tiled=True),
            lax.all_gather(self_key, ("dp", "seq"), axis=0, tiled=True),
            lax.all_gather(self_value, ("dp", "seq"), axis=0, tiled=True),
            lax.all_gather(self_out, ("dp", "seq"), axis=0, tiled=True),
            lax.all_gather(cross_query, ("dp", "seq"), axis=0, tiled=True),
            lax.all_gather(cross_key, ("dp", "seq"), axis=0, tiled=True),
            lax.all_gather(cross_value, ("dp", "seq"), axis=0, tiled=True),
            lax.all_gather(cross_out, ("dp", "seq"), axis=0, tiled=True),
            lax.all_gather(expand_weight, ("dp", "seq"), axis=0, tiled=True),
            lax.all_gather(shrink_weight, ("dp", "seq"), axis=0, tiled=True),
            lax.all_gather(norm_gains, ("dp", "seq"), axis=1, tiled=True),
            lax.all_gather(norm_biases, ("dp", "seq"), axis=1, tiled=True),
        )
        start = batch_index * group_size
        stop = start + group_size
        result, input_grad, memory_grad, gradients = micro_batch(
            gathered,
            tokens[start:stop],
            memory[start:stop],
            lengths[start:stop],
            memory_segments[start:stop],
            out_grad[start:stop],
        )
        outputs.append(result)
        input_grads.append(input_grad)
        memory_grads.append(memory_grad)
        if totals is None:
            totals = gradients
        else:
            totals = tuple((running + gradient for running, gradient in zip(totals, gradients)))
    summed = (
        lax.psum_scatter(totals[0], ("dp", "seq"), scatter_dimension=0, tiled=True),
        lax.psum_scatter(totals[1], ("dp", "seq"), scatter_dimension=0, tiled=True),
        lax.psum_scatter(totals[2], ("dp", "seq"), scatter_dimension=0, tiled=True),
        lax.psum_scatter(totals[3], ("dp", "seq"), scatter_dimension=0, tiled=True),
        lax.psum_scatter(totals[4], ("dp", "seq"), scatter_dimension=0, tiled=True),
        lax.psum_scatter(totals[5], ("dp", "seq"), scatter_dimension=0, tiled=True),
        lax.psum_scatter(totals[6], ("dp", "seq"), scatter_dimension=0, tiled=True),
        lax.psum_scatter(totals[7], ("dp", "seq"), scatter_dimension=0, tiled=True),
        lax.psum_scatter(totals[8], ("dp", "seq"), scatter_dimension=0, tiled=True),
        lax.psum_scatter(totals[9], ("dp", "seq"), scatter_dimension=0, tiled=True),
        lax.psum_scatter(totals[10], ("dp", "seq"), scatter_dimension=1, tiled=True),
        lax.psum_scatter(totals[11], ("dp", "seq"), scatter_dimension=1, tiled=True),
    )
    return (
        jnp.concatenate(outputs, 0),
        jnp.concatenate(input_grads, 0),
        jnp.concatenate(memory_grads, 0),
        summed[0],
        summed[1],
        summed[2],
        summed[3],
        summed[4],
        summed[5],
        summed[6],
        summed[7],
        summed[8],
        summed[9],
        summed[10],
        summed[11],
    )


MESH = pl.DeviceIdType.MESH
BF = jnp.bfloat16
F32 = jnp.float32
ALL = slice(None)
D = 1024
LEN = 128
OWN = 2 * LEN
SPAN = 8 * LEN
MEM = 128
KEY, VALUE, QUERY, OUT, CROSS_QUERY, CROSS_KEY, CROSS_VALUE, CROSS_OUT = range(8)
EXPAND = 8
SQUARE = 12
UNITS = 16
GRID = (2, 2, 4, 2)
SQUARE_SHAPE = (SQUARE, *GRID, 32, D)
SHRINK_SHAPE = (UNITS - SQUARE, *GRID, LEN, OWN)
VMEM_BYTES = 60 << 20
GELU_SLOPE = (2.0 / 3.141592653589793) ** 0.5
GELU_CUBE = 0.044715


class Place:
    def __init__(self):
        dp, seq = lax.axis_index("dp"), lax.axis_index("seq")
        self.x, self.y, self.core, self.z, self.seq = dp % 2, dp // 2, seq % 2, seq // 2, seq
        self.number = dp * 8 + seq
        self.group = self.z // 2
        self.low = seq % 4
        self.mate_z = self.z + 1 - 2 * (self.z % 2)
        self.inner_z = 2 - self.group
        self.next_z = (self.z + 2) % 4
        self.inner = self.z % 3 != 0
        self.outer = self.z % 3 == 0

    def at(self, y=None, x=None, z=None, core=None):
        y = self.y if y is None else y
        x = self.x if x is None else x
        z = self.z if z is None else z
        core = self.core if core is None else core
        return (y * 2 + x, z * 2 + core)

    def across(self, axis):
        if axis == "x":
            return self.at(x=1 - self.x)
        if axis == "y":
            return self.at(y=1 - self.y)
        return self.at(core=1 - self.core)

    def along_z(self, step):
        return self.at(z=(self.z + step) % 4)

    def mate(self):
        return self.at(z=self.mate_z)

    def greet(self):
        barrier = pltpu.get_barrier_semaphore()
        peers = [self.across(axis) for axis in ("x", "y", "core")]
        peers += [self.along_z(step) for step in (1, 2, 3)]
        for peer in peers:
            pl.semaphore_signal(barrier, inc=1, device_id=peer, device_id_type=MESH)
        pl.semaphore_wait(barrier, len(peers))


def under(when, act):
    if when is None:
        act()
    else:
        pl.when(when)(act)


class Links:
    def __init__(self, place, send_sem, recv_sem):
        self.place, self.send_sem, self.recv_sem = place, send_sem, recv_sem
        self.sends, self.slots = 0, 0
        self.open = {}

    def slot(self, count=1):
        first = self.slots
        self.slots += count
        assert self.slots <= self.recv_sem.shape[0]
        return first

    def send(self, slot, source, target, device, when=None):
        assert self.sends < self.send_sem.shape[0]
        step = pltpu.make_async_remote_copy(
            src_ref=source,
            dst_ref=target,
            send_sem=self.send_sem.at[self.sends],
            recv_sem=self.recv_sem.at[slot],
            device_id=device,
            device_id_type=MESH,
        )
        under(when, step.start)
        self.sends += 1
        self.open[id(step)] = step, when
        return step

    def arrived(self, slot, target):
        pltpu.make_async_remote_copy(
            src_ref=target,
            dst_ref=target,
            send_sem=self.send_sem.at[0],
            recv_sem=self.recv_sem.at[slot],
            device_id=self.place.across("core"),
            device_id_type=MESH,
        ).wait_recv()

    def sent(self, step):
        step, when = self.open.pop(id(step))
        under(when, step.wait_send)

    def finish(self):
        for step, when in self.open.values():
            under(when, step.wait_send)
        self.open = {}


class Moves:
    def __init__(self, sem):
        self.sem, self.count, self.open = sem, 0, {}

    def start(self, source, target):
        assert self.count < self.sem.shape[0]
        step = pltpu.make_async_copy(source, target, self.sem.at[self.count])
        step.start()
        self.count += 1
        self.open[id(step)] = step
        return step

    def wait(self, step):
        self.open.pop(id(step)).wait()

    def finish(self):
        for step in self.open.values():
            step.wait()
        self.open = {}


def all_sum(links, part, total, work):
    place = links.place
    work[0] = part[...]
    for number, axis in enumerate(("core", "y", "x")):
        slot = links.slot()
        step = links.send(slot, work.at[0], work.at[1 + number], place.across(axis))
        yield
        links.arrived(slot, work.at[1 + number])
        links.sent(step)
        work[0] = work[0] + work[1 + number]
    slot = links.slot(4)
    for k in (1, 2, 3):
        links.send(slot + place.z, work.at[0], work.at[4 + place.z], place.along_z(k))
    yield
    result = work[0]
    for k in (1, 2, 3):
        source = (place.z + k) % 4
        links.arrived(slot + source, work.at[4 + source])
        result = result + work[4 + source]
    total[...] = result
    yield


def loop(count):
    return pl.loop(0, count)


def tile(index, size):
    return pl.ds(pl.multiple_of(index * size, size), size)


def rows_times(left, right, store, rows=OWN, width=256):
    for first in range(0, left.shape[0], rows):

        @loop(D // width)
        def _(index):
            columns = tile(index, width)
            store(pl.ds(first, rows), columns, jnp.dot(left[pl.ds(first, rows), :], right[:, columns], preferred_element_type=F32))


def rows_back(left, right, store, width=256):
    @loop(D // width)
    def _(index):
        columns = tile(index, width)
        store(columns, project_back(left[...], right[columns, :]))


def put(target, dtype=BF):
    def store(rows, columns, value):
        target[rows, columns] = value.astype(dtype)

    return store


def half_masks():
    lane = lax.broadcasted_iota(jnp.int32, (1, LEN), 1)
    return [(lane < HD).astype(F32), (lane >= HD).astype(F32)]


def attend_rows(queries, keys, values, bias, logs, out, segments, pairs=H // 2, first_pair=0):
    masks = half_masks()

    @loop(pairs)
    def _(step):
        pair = step + first_pair
        columns = tile(pair, LEN)
        for first, rows, count in segments:
            own = pl.ds(first, rows)
            key, value = keys[pl.ds(0, count), columns], values[pl.ds(0, count), columns]
            query = queries[own, columns]
            lane = lax.broadcasted_iota(jnp.int32, (rows, LEN), 1)
            parts = []
            for half in (0, 1):
                scores = project_back(query * (masks[half] * HD**-0.5).astype(BF), key) + bias[own, pl.ds(0, count)]
                top = jnp.max(scores, axis=1, keepdims=True)
                powers = jnp.exp(scores - top)
                total = jnp.sum(powers, axis=1, keepdims=True)
                parts.append(project((powers * (1.0 / total)).astype(BF), value))
                logs[own, :] = jnp.where(lane == 2 * pair + half, top + jnp.log(total), logs[own, :])
            out[own, columns] = jnp.where(lane < HD, parts[0], parts[1]).astype(BF)


def attend_rows_back(queries, keys, values, bias, logs, grads, query_grads, key_grads, value_grads, segments, pairs, first_pair=0):
    masks = half_masks()

    @loop(pairs)
    def _(step):
        pair = step + first_pair
        columns = tile(pair, LEN)
        for number, (first, rows, count) in enumerate(segments):
            own, met = pl.ds(first, rows), pl.ds(0, count)
            key, value = keys[met, columns], values[met, columns]
            lane = lax.broadcasted_iota(jnp.int32, (rows, LEN), 1)
            halves, score_lows, prob_lows, query_parts, grad_parts = [], [], [], [], []
            for half in (0, 1):
                query = queries[own, columns] * (masks[half] * HD**-0.5).astype(BF)
                grad = grads[own, columns] * masks[half].astype(BF)
                log_total = jnp.sum(jnp.where(lane == 2 * pair + half, logs[own, :], 0.0), axis=1, keepdims=True)
                probs = jnp.exp(project_back(query, key) + bias[own, met] - log_total)
                prob_grad = project_back(grad, value)
                score_grad = probs * (prob_grad - jnp.sum(prob_grad * probs, axis=1, keepdims=True))
                score_low = score_grad.astype(BF)
                halves.append(project(score_low, key) * HD**-0.5)
                score_lows.append(score_low)
                prob_lows.append(probs.astype(BF))
                query_parts.append(query)
                grad_parts.append(grad)
            query_grads[own, columns] = jnp.where(lane < HD, halves[0], halves[1]).astype(BF)
            key_term = weight_term(jnp.concatenate(score_lows), jnp.concatenate(query_parts))
            value_term = weight_term(jnp.concatenate(prob_lows), jnp.concatenate(grad_parts))
            if number == 0:
                key_grads[met, columns] = key_term.astype(BF)
                value_grads[met, columns] = value_term.astype(BF)
            else:
                key_grads[met, columns] = (key_grads[met, columns].astype(F32) + key_term).astype(BF)
                value_grads[met, columns] = (value_grads[met, columns].astype(F32) + value_term).astype(BF)


SELF_SEGMENTS = ((LEN, LEN, SPAN), (0, LEN, SPAN // 2))
CROSS_SEGMENTS = ((0, OWN, MEM),)
STEP = 32


def norm_rows(read, normal, inverse, emit):
    @loop(OWN // STEP)
    def _(index):
        rows = tile(index, STEP)
        value = read(rows)
        centred = value - jnp.mean(value, axis=1, keepdims=True)
        scale = lax.rsqrt(jnp.mean(centred * centred, axis=1, keepdims=True) + norm_eps)
        result = centred * scale
        if normal is not None:
            normal[rows, :] = result
            inverse[rows, :] = jnp.broadcast_to(scale, (STEP, LEN))
        emit(rows, result, scale)


def norm_rows_back(grad, normal, scale, gain, sums, number):
    sums[pl.ds(number, 1), :] += jnp.sum(grad * normal, axis=0, keepdims=True)
    sums[pl.ds(3 + number, 1), :] += jnp.sum(grad, axis=0, keepdims=True)
    scaled = grad * gain
    return scale * (
        scaled
        - jnp.mean(scaled, axis=1, keepdims=True)
        - normal * jnp.mean(scaled * normal, axis=1, keepdims=True)
    )


class Gather:
    WIDE = (6, 7, 8, 10, 11, 12, 13, 14, 15)
    EARLY = 3
    RELAY = 1
    ROUTES = {False: ("zxy", "zyx"), True: ("xzy", "yzx")}
    TIMES = {False: (-3, 0, 1, 2, 3), True: (-20, -3, 1, 2, 3)}
    SLOTS = 10

    def __init__(self, links, moves, own, square, shrink):
        self.links, self.moves, self.own, self.square, self.shrink = links, moves, own, square, shrink
        self.first_slot = links.slot(UNITS * 2 * self.SLOTS)
        self.local = {}
        for unit in range(UNITS):
            target = self.block(unit, links.place.y, links.place.x, links.place.z, links.place.core)
            self.local[unit] = moves.start(own(unit), target)
        self.now = -self.EARLY
        self.steps = {}
        for number, unit in enumerate(range(UNITS)):
            wide = number in self.WIDE
            for half in (0, 1):
                for phase, time in enumerate(self.TIMES[wide]):
                    step = (phase, number, unit, half, self.ROUTES[wide][half])
                    self.steps.setdefault(max(number + time, self.now), []).append(step)
                step = (-1, number, unit, half, self.ROUTES[wide][half])
                self.steps.setdefault(max(number - self.RELAY, self.now + 1), []).append(step)

    def block(self, unit, *index):
        if unit < SQUARE:
            return self.square.at[(unit,) + index]
        return self.shrink.at[(unit - SQUARE,) + index]

    def tick(self):
        for phase, _, unit, half, route in sorted(self.steps.pop(self.now, ())):
            self.move(phase, unit, half, route)
        self.now += 1

    def move(self, phase, unit, half, route):
        links, place = self.links, self.links.place
        here = {"y": place.y, "x": place.x, "z": place.z}
        slot = self.first_slot + (2 * unit + half) * self.SLOTS
        depth = 16 if unit < SQUARE else 64
        rows = pl.ds(depth * half, depth)
        turn = route.index("z")

        def part(where, core):
            return self.block(unit, where["y"], where["x"], where["z"], core, rows)

        def reached(count):
            return {**here, **{axis: ALL for axis in route[:count]}}

        def incoming(count):
            axis = route[count]
            if axis == "z":
                return reached(count + 1)
            return {**reached(count), axis: 1 - here[axis]}

        def line(source):
            return part({**reached(turn), "z": source}, place.core)

        if phase == -1:
            def hand_on():
                links.arrived(slot + place.next_z, line(place.next_z))

            under(place.inner, hand_on)
            links.send(slot + place.next_z, line(place.next_z), line(place.next_z), place.mate(), place.inner)
            return
        if phase == 1 and unit in self.local:
            self.moves.wait(self.local.pop(unit))
        if 1 <= phase <= 3:
            if phase - 1 == turn:
                links.arrived(slot + place.mate_z, line(place.mate_z))
                for source, when in ((place.next_z, place.outer), ((6 - place.z - place.mate_z - place.next_z), None)):
                    under(when, functools.partial(links.arrived, slot + source, line(source)))
            else:
                links.arrived(slot + 3 + phase, part(incoming(phase - 1), place.core))
        if phase < 3:
            source = self.own(unit).at[rows] if phase == 0 else part(reached(phase), place.core)
            target = part(reached(phase), place.core)
            if phase == turn:
                links.send(slot + place.z, source, target, place.mate())
                links.send(slot + place.z, source, target, place.at(z=place.inner_z))
                links.send(slot + place.z, source, target, place.at(z=place.next_z), place.inner)
            else:
                links.send(slot + 4 + phase, source, target, place.across(route[phase]))
        if 1 <= phase <= 3 and phase > turn:
            fresh = part(incoming(phase - 1), place.core)
            links.send(slot + 6 + phase, fresh, fresh, place.across("core"))
        if phase == 4:
            for number in range(turn, 3):
                links.arrived(slot + 7 + number, part(incoming(number), 1 - place.core))


def core_rows(core, count=OWN):
    return pl.ds(pl.multiple_of(core * count, count), count)


def block_rows(block):
    return pl.ds(pl.multiple_of(block * LEN, LEN), LEN)


FORWARD_SAVES = {
    "queries": ((OWN, D), BF),
    "keys": ((SPAN, D), BF),
    "values": ((SPAN, D), BF),
    "self_bias": ((OWN, SPAN), F32),
    "self_logs": ((OWN, LEN), F32),
    "normal_one": ((OWN, D), F32),
    "inverse_one": ((OWN, LEN), F32),
    "cross_queries": ((OWN, D), BF),
    "cross_keys": ((MEM, D), BF),
    "cross_values": ((MEM, D), BF),
    "cross_bias": ((OWN, MEM), F32),
    "cross_logs": ((OWN, LEN), F32),
    "normal_two": ((OWN, D), F32),
    "inverse_two": ((OWN, LEN), F32),
    "slopes": ((4, OWN, D), BF),
    "third_grad": ((OWN, D), F32),
    "norm_sums": ((8, D), F32),
    "gains": ((8, D), F32),
    "final_low": ((OWN, D), BF),
}
TURNED_SAVES = {
    "tokens_t": ((16, 32, 2 * OWN), BF),
    "attended_t": ((16, 32, 2 * OWN), BF),
    "first_t": ((16, 32, 2 * OWN), BF),
    "cross_t": ((16, 32, 2 * OWN), BF),
    "second_t": ((16, 32, 2 * OWN), BF),
    "active_t": ((4, 4, 4, 32, 2 * OWN), BF),
    "memory_t": ((16, 32, MEM), BF),
    "branch": ((2 * OWN, D), BF),
}
FORWARD_SCRATCH = {
    "stream": ((SPAN, D), BF),
    "mine": ((OWN, D), BF),
    "context": ((4, 2, 16, D), BF),
    "attended": ((OWN, D), BF),
    "first_low": ((OWN, D), BF),
    "cross_attended": ((OWN, D), BF),
    "second_low": ((OWN, D), BF),
    "active": ((4, OWN, D), BF),
    "sums": ((OWN, D), F32),
    "cotangent": ((OWN, D), BF),
    "branch_own": ((OWN, D), BF),
    "weights": ((4, D, D), BF),
    "shrink_in": ((2, 4, D, OWN), BF),
    "turned": ((3, 16, 2, 32, OWN), BF),
    "turned_active": ((2, 4, 2, 4, 32, OWN), BF),
    "turned_memory": ((16, 2, 32, MEM), BF),
    "work": ((8, 8, D), F32),
    "norms": ((8, D), F32),
}
FORWARD_SENDS, FORWARD_SLOTS, FORWARD_MOVES = 352, 384, 96


class Refs:
    def __init__(self, names, refs):
        for name, ref in zip(names, refs):
            setattr(self, name, ref)


def forward_kernel(lengths, segments, norm_gains, norm_biases, tokens, memory, out_grad, *refs):
    squares, expand_own, shrink_own = refs[:8], refs[8], refs[9]
    square, shrink = refs[10:12]
    rest = refs[12:]
    kept = Refs(FORWARD_SAVES, rest[: len(FORWARD_SAVES)])
    rest = rest[len(FORWARD_SAVES) :]
    turned = Refs(TURNED_SAVES, rest[: len(TURNED_SAVES)])
    rest = rest[len(TURNED_SAVES) :]
    held = Refs(FORWARD_SAVES, rest[: len(FORWARD_SAVES)])
    rest = rest[len(FORWARD_SAVES) :]
    held.__dict__.update(Refs(FORWARD_SCRATCH, rest[: len(FORWARD_SCRATCH)]).__dict__)
    send_sem, recv_sem, move_sem = rest[len(FORWARD_SCRATCH) :]

    place = Place()
    links, moves = Links(place, send_sem, recv_sem), Moves(move_sem)
    y, x, z, core, group, low, seq = place.y, place.x, place.z, place.core, place.group, place.low, place.seq
    partner = place.across("core")
    opposite = place.along_z(2)
    mate = place.mate()
    place.greet()

    def own(unit):
        if unit < EXPAND:
            return squares[unit]
        if unit < SQUARE:
            return expand_own.at[:, pl.ds(D * (unit - EXPAND), D)]
        return shrink_own.at[:, pl.ds(OWN * (unit - SQUARE), OWN)]

    stream = held.stream
    far, mate_seq = (seq + 4) % 8, (seq + 2) % 4 + 4 * group
    other_seq = 2 * z + 1 - core
    other_mate = (other_seq + 2) % 4 + 4 * group
    slot_far, slot_mate, slot_mate_far, slot_core = links.slot(), links.slot(), links.slot(), links.slot(4)
    home = moves.start(tokens.at[group], stream.at[block_rows(seq)])
    gather = Gather(links, moves, own, square, shrink)
    for _ in range(Gather.EARLY):
        gather.tick()
    links.send(slot_far, tokens.at[1 - group], stream.at[block_rows(seq)], opposite)
    links.send(slot_mate, tokens.at[group], stream.at[block_rows(seq)], mate)
    links.send(slot_core, tokens.at[group], stream.at[block_rows(seq)], partner)
    slot_memory, slot_context = links.slot(4), links.slot()
    context_home = moves.start(memory.at[group], held.context.at[z, core])
    for k in (1, 2, 3):
        links.send(slot_memory + z, memory.at[((z + k) % 4) // 2], held.context.at[z, core], place.along_z(k))
    held.norms[...] = jnp.zeros_like(held.norms)
    held.norms[pl.ds(0, 3), pl.ds(0, 32)] = norm_gains[...].astype(F32)
    held.norms[pl.ds(3, 3), pl.ds(0, 32)] = norm_biases[...].astype(F32)
    held.norms[...] = pltpu.roll(held.norms[...], 32 * place.number, 1)
    norm_steps = all_sum(links, held.norms, held.gains, held.work)
    next(norm_steps)

    def sentence(places):
        result, end = jnp.zeros_like(places), 0
        for index in range(lengths.shape[1] - 1):
            end = end + lengths[group, index]
            result = result + (places >= end).astype(jnp.int32)
        return result

    held.norm_sums[...] = jnp.zeros_like(held.norm_sums)
    held.self_logs[...] = jnp.zeros_like(held.self_logs)
    held.cross_logs[...] = jnp.zeros_like(held.cross_logs)

    @loop(OWN // STEP)
    def _(index):
        row = index * STEP + lax.broadcasted_iota(jnp.int32, (STEP, 1), 0)
        row_place = LEN * low + row + jnp.where(row >= LEN, 3 * LEN, 0)
        row_sentence = sentence(row_place)
        key_place = lax.broadcasted_iota(jnp.int32, (1, SPAN), 1)
        allowed = (row_sentence == sentence(key_place)) & (key_place <= row_place)
        held.self_bias[tile(index, STEP), :] = jnp.where(allowed, 0.0, masked_score)
        met = row_sentence == segments[pl.ds(group, 1), :]
        held.cross_bias[tile(index, STEP), :] = jnp.where(met, 0.0, masked_score)

    def pass_on(number, block):
        links.send(slot_core + number, stream.at[block_rows(block)], stream.at[block_rows(block)], partner)

    gather.tick()
    next(norm_steps)
    gather.tick()
    next(norm_steps)
    gather.tick()
    links.arrived(slot_far, stream.at[block_rows(far)])
    links.send(slot_mate_far, stream.at[block_rows(far)], stream.at[block_rows(far)], mate)
    pass_on(1, far)
    gather.tick()
    links.arrived(slot_mate, stream.at[block_rows(mate_seq)])
    pass_on(2, mate_seq)
    moves.wait(context_home)
    for k in (1, 2, 3):
        links.arrived(slot_memory + (z + k) % 4, held.context.at[(z + k) % 4, core])
    links.send(slot_context, held.context.at[:, core], held.context.at[:, core], partner)
    next(norm_steps)
    gather.tick()
    links.arrived(slot_mate_far, stream.at[block_rows((mate_seq + 4) % 8)])
    pass_on(3, (mate_seq + 4) % 8)
    gather.tick()
    moves.wait(home)
    for number, block in enumerate((other_seq, (other_seq + 4) % 8, other_mate, (other_mate + 4) % 8)):
        links.arrived(slot_core + number, stream.at[block_rows(block)])
    links.arrived(slot_context, held.context.at[:, 1 - core])
    held.mine[pl.ds(0, LEN), :] = stream[block_rows(low), :]
    held.mine[pl.ds(LEN, LEN), :] = stream[block_rows(low + 4), :]

    loads = {}

    def fetch(unit, slot):
        if unit < SQUARE:
            target = held.weights.at[slot]
            loads[unit] = (moves.start(square.at[unit].reshape(D, D), target), target)
        else:
            target = held.shrink_in.at[slot]
            loads[unit] = (moves.start(shrink.at[unit - SQUARE].reshape(4, D, OWN), target), target)

    def weight(unit):
        step, target = loads.pop(unit)
        moves.wait(step)
        return target

    turning = {"count": 0, "open": {}}
    landing = []
    mine, theirs = core_rows(core), core_rows(1 - core)

    def turn(source, name):
        number = turning["count"] % 3
        for move, sent in turning["open"].pop(number, ()):
            moves.wait(move)
            links.sent(sent)
        turning["count"] += 1
        buffer, target = held.turned.at[number], getattr(turned, name)

        @loop(4)
        def _(index):
            buffer[pl.ds(4 * index, 4)] = source[:, tile(index, OWN)].T.reshape(4, 2, 32, OWN)

        slot = links.slot()
        move = moves.start(buffer.at[:, core], target.at[:, :, mine])
        sent = links.send(slot, buffer.at[:, 1 - core], target.at[:, :, mine], partner)
        landing.append((slot, target.at[:, :, theirs]))
        turning["open"][number] = [(move, sent)]

    def keep(*names):
        for name in names:
            moves.start(getattr(held, name), getattr(kept, name))

    def gain(number):
        return held.gains[pl.ds(number, 1), :]

    def bias(number):
        return held.gains[pl.ds(3 + number, 1), :]

    fetch(KEY, 0)
    turn(held.mine, "tokens_t")
    next(norm_steps)
    fetch(VALUE, 1)
    rows_times(stream, weight(KEY), put(held.keys))
    gather.tick()
    fetch(QUERY, 2)
    rows_times(stream, weight(VALUE), put(held.values))
    rows_times(held.mine, weight(QUERY), put(held.queries))

    def attend_part(first, pairs):
        attend_rows(
            held.queries, held.keys, held.values, held.self_bias, held.self_logs, held.attended, SELF_SEGMENTS, pairs, first
        )

    fetch(OUT, 3)
    attend_part(0, 3)
    gather.tick()
    fetch(CROSS_QUERY, 0)
    attend_part(3, 3)
    gather.tick()
    fetch(CROSS_KEY, 1)
    attend_part(6, 2)
    rows_times(held.attended, weight(OUT), put(held.sums, F32))
    keep("queries", "keys", "values", "self_bias", "self_logs", "cross_bias", "gains")

    def first_rows(rows, result, _):
        held.first_low[rows, :] = (result * gain(0) + bias(0)).astype(BF)

    def after(rows, previous):
        return held.sums[rows, :] + alpha_scale * previous

    norm_rows(lambda rows: after(rows, held.mine[rows, :].astype(F32)), held.normal_one, held.inverse_one, first_rows)
    turn(held.attended, "attended_t")
    rows_times(held.first_low, weight(CROSS_QUERY), put(held.cross_queries))
    context = held.context.reshape(MEM, D)
    rows_times(context, weight(CROSS_KEY), put(held.cross_keys), MEM)
    gather.tick()
    fetch(CROSS_VALUE, 2)
    turn(held.first_low, "first_t")

    @loop(4)
    def _(index):
        held.turned_memory[pl.ds(4 * index, 4)] = context[:, tile(index, OWN)].T.reshape(4, 2, 32, MEM)

    moves.start(held.turned_memory.at[:, core], turned.memory_t)
    rows_times(context, weight(CROSS_VALUE), put(held.cross_values), MEM)
    attend_rows(
        held.cross_queries, held.cross_keys, held.cross_values, held.cross_bias, held.cross_logs,
        held.cross_attended, CROSS_SEGMENTS,
    )
    gather.tick()
    cotangent_rows, cotangent_far = block_rows(group), block_rows(1 - group)
    slot_cotangent = links.slot()
    cotangent_home = moves.start(out_grad.at[group], held.cotangent.at[cotangent_rows])
    links.send(slot_cotangent, out_grad.at[1 - group], held.cotangent.at[cotangent_rows], opposite)
    fetch(CROSS_OUT, 3)
    keep("cross_queries", "cross_keys", "cross_values", "cross_logs", "normal_one", "inverse_one")
    rows_times(held.cross_attended, weight(CROSS_OUT), put(held.sums, F32))

    def second_rows(rows, result, _):
        held.second_low[rows, :] = (result * gain(1) + bias(1)).astype(BF)

    norm_rows(
        lambda rows: after(rows, held.normal_one[rows, :] * gain(0) + bias(0)),
        held.normal_two, held.inverse_two, second_rows,
    )
    keep("normal_two", "inverse_two")
    gather.tick()
    turn(held.cross_attended, "cross_t")
    turn(held.second_low, "second_t")
    turned_open = {}
    for part in range(4):
        if part > 0:
            gather.tick()
        fetch(EXPAND + part, part)
        active, slopes = held.active.at[part], held.slopes.at[part]

        def activate(rows, columns, value):
            inner = GELU_SLOPE * (value + GELU_CUBE * value * value * value)
            bend = jnp.tanh(inner)
            active[rows, columns] = (0.5 * value * (1.0 + bend)).astype(BF)
            slope = 0.5 * (1.0 + bend) + 0.5 * value * (1.0 - bend * bend) * (
                GELU_SLOPE * (1.0 + 3.0 * GELU_CUBE * value * value)
            )
            slopes[rows, columns] = slope.astype(BF)

        rows_times(held.second_low, weight(EXPAND + part), activate)
        number = part % 2
        for move, sent in turned_open.pop(number, ()):
            moves.wait(move)
            links.sent(sent)
        buffer = held.turned_active.at[number]

        @loop(4)
        def _(index):
            buffer[index] = active[:, tile(index, OWN)].T.reshape(2, 4, 32, OWN)

        slot = links.slot()
        move = moves.start(buffer.at[:, core], turned.active_t.at[part, :, :, :, mine])
        sent = links.send(slot, buffer.at[:, 1 - core], turned.active_t.at[part, :, :, :, mine], partner)
        landing.append((slot, turned.active_t.at[part, :, :, :, theirs]))
        turned_open[number] = [(move, sent)]
    keep("slopes")
    for part in range(4):
        gather.tick()
        fetch(SQUARE + part, part % 2)
        shrink_part = weight(SQUARE + part)
        for first in (0, LEN):
            rows = pl.ds(first, LEN)
            total = project(held.active[0, rows, :], shrink_part[0])
            for depth in (1, 2, 3):
                total = total + project(held.active[depth, rows, :], shrink_part[depth])
            held.sums[rows, pl.ds(OWN * part, OWN)] = total
    links.arrived(slot_cotangent, held.cotangent.at[cotangent_far])
    moves.wait(cotangent_home)

    def third_rows(rows, result, scale):
        held.final_low[rows, :] = (result * gain(2) + bias(2)).astype(BF)
        grad = norm_rows_back(held.cotangent[rows, :].astype(F32), result, scale, gain(2), held.norm_sums, 2)
        held.third_grad[rows, :] = grad
        held.branch_own[rows, :] = grad.astype(BF)

    norm_rows(lambda rows: after(rows, held.normal_two[rows, :] * gain(1) + bias(1)), None, None, third_rows)
    slot = links.slot()
    links.send(slot, held.branch_own, turned.branch.at[mine], partner)
    landing.append((slot, turned.branch.at[theirs]))
    moves.start(held.branch_own, turned.branch.at[mine])
    keep("third_grad", "norm_sums", "final_low")
    for arrival in landing:
        links.arrived(*arrival)
    moves.finish()
    links.finish()


IN_VMEM = pl.BlockSpec(memory_space=pltpu.VMEM)
IN_SMEM = pl.BlockSpec(memory_space=pltpu.SMEM)
IN_PLACE = pl.BlockSpec(memory_space=pl.ANY)


def shapes_of(table):
    return [jax.ShapeDtypeStruct(shape, dtype) for shape, dtype in table.values()]


def vmem_of(table):
    return [pltpu.VMEM(shape, dtype) for shape, dtype in table.values()]


def forward_call(lengths, segments, norm_gains, norm_biases, tokens, memory, out_grad, weights):
    results = [
        jax.ShapeDtypeStruct(SQUARE_SHAPE, BF),
        jax.ShapeDtypeStruct(SHRINK_SHAPE, BF),
        *shapes_of(FORWARD_SAVES),
        *shapes_of(TURNED_SAVES),
    ]
    values = pl.pallas_call(
        forward_kernel,
        in_specs=[IN_SMEM] + [IN_VMEM] * 3 + [IN_PLACE] * 13,
        out_specs=[IN_PLACE] * len(results),
        out_shape=results,
        scratch_shapes=[
            *vmem_of(FORWARD_SAVES),
            *vmem_of(FORWARD_SCRATCH),
            pltpu.SemaphoreType.DMA((FORWARD_SENDS,)),
            pltpu.SemaphoreType.DMA((FORWARD_SLOTS,)),
            pltpu.SemaphoreType.DMA((FORWARD_MOVES,)),
        ],
        compiler_params=pltpu.CompilerParams(collective_id=0, has_side_effects=True, vmem_limit_bytes=VMEM_BYTES),
    )(lengths, segments, norm_gains, norm_biases, tokens, memory, out_grad, *weights)
    saves = dict(zip([*FORWARD_SAVES, *TURNED_SAVES], values[2:]))
    return values[0], values[1], saves


class Scatter:
    WIDE = (0, 2, 4, 6, 8)

    def __init__(self, links, grads, from_first, from_second, from_z, from_line, from_last, result):
        self.links, self.grads, self.result = links, grads, result
        self.from_first, self.from_second, self.from_z = from_first, from_second, from_z
        self.from_line, self.from_last = from_line, from_last
        self.slots, self.pending, self.now = {}, {}, 0

    def home(self, unit):
        for step in self.pending.pop(unit - self.grads.shape[0], ()):
            self.links.sent(step)
        self.slots[unit] = self.links.slot(12)
        return self.grads.at[unit % self.grads.shape[0]]

    def add(self, total, part):
        for row in range(total.shape[0]):
            if len(total.shape) > 3:
                self.add(total.at[row], part.at[row])
            else:
                total[row] = (total[row].astype(F32) + part[row].astype(F32)).astype(BF)

    def phase(self, unit, half, number):
        links, place, wide = self.links, self.links.place, unit in self.WIDE
        y, x, z = place.y, place.x, place.z
        here = self.grads.at[unit % self.grads.shape[0]]
        depth = unit % self.from_first.shape[0]
        rows = pl.ds(16 * half, 16)
        slot = self.slots[unit] + 6 * half
        by_y = half == 0
        first, second = ("y", "x") if by_y else ("x", "y")
        away = (1 - y, ALL) if by_y else (ALL, 1 - x)
        kept = (y, ALL) if by_y else (ALL, x)
        corner, other, mine = ((y, 1 - x), 1 - x, x) if by_y else ((1 - y, x), 1 - y, y)
        home = here.at[y, x, :, rows]
        first_in = self.from_first.at[depth, :, :, rows]
        second_in = self.from_second.at[depth, :, rows]
        if wide:
            index = self.WIDE.index(unit)
            line_in = self.from_line.at[index, :, :, rows]
            last_in = self.from_last.at[index, rows]
        else:
            before = sum(wider < unit for wider in self.WIDE)
            line_in = self.from_z.at[(unit - before) % self.from_z.shape[0], :, :, rows]

        def owned(owner):
            return here.at[(*kept, owner, rows)] if wide else here.at[y, x, pl.ds(owner, 1), rows]

        def send(number, source, target, device, when=None):
            self.pending.setdefault(unit, []).append(links.send(slot + number, source, target, device, when))

        def along_line():
            send(2 + z, owned(place.mate_z), line_in.at[z], place.mate())
            send(2 + z, owned(place.inner_z), line_in.at[z], place.at(z=place.inner_z))
            send(2 + place.mate_z, owned(3 - z), line_in.at[place.mate_z], place.mate(), place.outer)

        def hand_on():
            def join():
                links.arrived(slot + 2 + z, line_in.at[z])
                self.add(owned(place.next_z), line_in.at[z])

            under(place.inner, join)
            send(2 + z, owned(place.next_z), line_in.at[z], place.at(z=place.next_z), place.inner)

        def line_sum():
            for source in (place.mate_z, place.next_z):
                links.arrived(slot + 2 + source, line_in.at[source])
                self.add(owned(z), line_in.at[source])

            def third():
                links.arrived(slot + 2 + 3 - z, line_in.at[3 - z])
                self.add(owned(z), line_in.at[3 - z])

            under(place.inner, third)

        if number == 0:
            send(0, here.at[(*away, ALL, rows)], first_in, place.across(first))
        if number == 1 and not wide:
            links.arrived(slot, first_in)
            corner_part = here.at[(*corner, ALL, rows)]
            self.add(corner_part, first_in.at[other])
            send(1, corner_part, second_in, place.across(second))
            self.add(home, first_in.at[mine])
        if number == 2 and not wide:
            links.arrived(slot + 1, second_in)
            self.add(home, second_in)
            along_line()
        if number == 3 and not wide:
            hand_on()
        if number == 4 and not wide:
            line_sum()
            self.result(unit, rows, home[z].astype(F32))
        if number == 1 and wide:
            links.arrived(slot, first_in)
            self.add(here.at[(*kept, ALL, rows)], first_in)
            along_line()
        if number == 2 and wide:
            hand_on()
        if number == 3 and wide:
            line_sum()
            send(1, owned(z).at[other], last_in, place.across(second))
        if number == 4 and wide:
            links.arrived(slot + 1, last_in)
            self.result(unit, rows, home[z].astype(F32) + last_in[...].astype(F32))

    def tick(self):
        for number in range(5):
            unit = self.now - number
            if 0 <= unit < UNITS:
                for half in (0, 1):
                    self.phase(unit, half, number)
        self.now += 1


DEPTH = 4
BACKWARD_SCRATCH = {
    "weights": ((3, D, D), BF),
    "shrink_in": ((4, D, OWN), BF),
    "grads": ((5, 2, 2, 4, 32, D), BF),
    "from_first": ((DEPTH, 2, 4, 32, D), BF),
    "from_second": ((DEPTH, 4, 32, D), BF),
    "from_z": ((6, 4, 1, 32, D), BF),
    "from_line": ((len(Scatter.WIDE), 4, 2, 32, D), BF),
    "from_last": ((len(Scatter.WIDE), 32, D), BF),
    "up": ((4, 2 * OWN, D), BF),
    "second_sum": ((OWN, D), F32),
    "cross_branch": ((2 * OWN, D), BF),
    "attended_grad": ((OWN, D), BF),
    "cross_query_grad": ((2 * OWN, D), BF),
    "cross_terms": ((2, 2, MEM, D), BF),
    "cross_sums": ((2, MEM, D), BF),
    "self_branch": ((2 * OWN, D), BF),
    "query_grad": ((2 * OWN, D), BF),
    "terms_core": ((2, 2, 2, LEN, D), BF),
    "terms_mate": ((2, 2, LEN, D), BF),
    "key_grad": ((2 * OWN, D), BF),
    "value_grad": ((2 * OWN, D), BF),
    "memory_own": ((4, 16, D), BF),
    "memory_in": ((4, 16, D), BF),
    "far_own": ((LEN, D), BF),
    "far_in": ((LEN, D), BF),
    "work": ((8, 8, D), F32),
}
BACKWARD_SENDS, BACKWARD_SLOTS, BACKWARD_MOVES = 256, 256, 64


def backward_kernel(square, shrink, *refs):
    saved = [*FORWARD_SAVES, *TURNED_SAVES]
    names = [name for name in saved if name != "final_low"]
    kept = Refs(saved, refs[: len(saved)])
    rest = refs[len(saved) :]
    output, input_grad, memory_grad, *unit_grads = rest[:11]
    expand_grad, shrink_grad, norm_grads = rest[11:14]
    rest = rest[14:]
    held = Refs(names, rest[: len(names)])
    rest = rest[len(names) :]
    held.__dict__.update(Refs(BACKWARD_SCRATCH, rest[: len(BACKWARD_SCRATCH)]).__dict__)
    send_sem, recv_sem, move_sem = rest[len(BACKWARD_SCRATCH) :]

    place = Place()
    links, moves = Links(place, send_sem, recv_sem), Moves(move_sem)
    z, core, group = place.z, place.core, place.group
    partner = place.across("core")
    mine, theirs = core_rows(core), core_rows(1 - core)
    loads = {}

    def bring(*wanted):
        for name in wanted:
            loads[name] = moves.start(getattr(kept, name), getattr(held, name))

    def have(*wanted):
        for name in wanted:
            moves.wait(loads.pop(name))

    def fetch(unit, slot):
        loads[unit] = moves.start(square.at[unit].reshape(D, D), held.weights.at[slot])

    def weight(unit, slot):
        moves.wait(loads.pop(unit))
        return held.weights.at[slot]

    bring("branch", "active_t")

    def fetch_shrink(part):
        loads[SQUARE] = moves.start(shrink.at[:, part], held.shrink_in)

    fetch_shrink(0)
    for part in range(3):
        fetch(EXPAND + part, part)
    bring("slopes", "third_grad", "second_t", "norm_sums", "gains", "normal_two", "inverse_two")
    bring("cross_queries", "cross_keys", "cross_values", "cross_bias", "cross_logs", "cross_t")
    bring("normal_one", "inverse_one", "first_t", "memory_t", "attended_t", "tokens_t")
    bring("queries", "keys", "values", "self_bias", "self_logs")
    place.greet()

    order = [12, 13, 14, 15, 8, 9, 10, 11, CROSS_OUT, CROSS_QUERY, CROSS_KEY, CROSS_VALUE, OUT, QUERY, KEY, VALUE]

    def result(number, rows, total):
        unit = order[number]
        if unit < EXPAND:
            unit_grads[unit][rows, :] = total
        elif unit < SQUARE:
            expand_grad[rows, pl.ds(D * (unit - EXPAND), D)] = total
        else:
            shrink_grad[pl.ds(32 * (unit - SQUARE) + rows.start, rows.size), :] = total

    buffers = (held.from_first, held.from_second, held.from_z, held.from_line, held.from_last)
    scatter = Scatter(links, held.grads, *buffers, result)
    made = {"count": 0}

    def produce(left, right, depth=2 * OWN):
        target = scatter.home(made["count"])
        made["count"] += 1

        @loop(4)
        def _(index):
            columns = tile(index, OWN)
            term = project(left().reshape(512, depth), right[:, columns])
            target[:, :, :, :, columns] = term.astype(BF).reshape(2, 2, 4, 32, OWN)

    def share(ref):
        slot = links.slot()
        links.send(slot, ref.at[mine], ref.at[mine], partner)
        return slot

    def shared(ref, slot):
        links.arrived(slot, ref.at[theirs])

    def gain(number):
        return held.gains[pl.ds(number, 1), :]

    have("branch", "active_t")

    def produce_shrink(part):
        produce(lambda: held.active_t[:, :, part], held.branch)

    def produce_expand(part):
        shared(held.up.at[part], up_slots[part])
        produce(lambda: held.second_t[...], held.up.at[part])

    produce_shrink(0)
    scatter.tick()
    slot_output = links.slot()
    moves.start(kept.final_low.at[block_rows(group)], output.at[group])
    links.send(slot_output, kept.final_low.at[block_rows(1 - group)], output.at[group], place.along_z(2))
    for part in (1, 2, 3):
        produce_shrink(part)
    scatter.tick()
    have("slopes")
    own_branch = held.branch.at[mine]
    up_slots, up_sends = [], []
    for part in range(4):
        if part == 2:
            scatter.tick()
        up = held.up.at[part, mine]
        slopes = held.slopes.at[part]

        moves.wait(loads.pop(SQUARE))

        @loop(4)
        def _(index):
            columns = tile(index, OWN)
            total = project_back(own_branch[:, pl.ds(0, OWN)], held.shrink_in[0, columns, :])
            for depth in (1, 2, 3):
                total = total + project_back(own_branch[:, pl.ds(OWN * depth, OWN)], held.shrink_in[depth, columns, :])
            up[:, columns] = (total * slopes[:, columns].astype(F32)).astype(BF)

        up_slots.append(links.slot())
        up_sends.append(links.send(up_slots[part], up, up, partner))
        if part < 3:
            fetch_shrink(part + 1)

        def add(columns, value):
            if part == 0:
                held.second_sum[:, columns] = value
            else:
                held.second_sum[:, columns] += value

        rows_back(up, weight(EXPAND + part, part % 3), add)
        fetch((EXPAND + 3, CROSS_OUT, CROSS_QUERY, CROSS_KEY)[part], part % 3)
    scatter.tick()
    have("third_grad", "norm_sums", "gains", "normal_two", "inverse_two", "second_t")

    def spread(inverse, rows):
        return inverse[rows, pl.ds(0, 1)]

    @loop(OWN // STEP)
    def _(index):
        rows = tile(index, STEP)
        grad = held.second_sum[rows, :] + alpha_scale * held.third_grad[rows, :]
        pre = norm_rows_back(grad, held.normal_two[rows, :], spread(held.inverse_two, rows), gain(1), held.norm_sums, 1)
        held.second_sum[rows, :] = pre
        held.cross_branch[pl.ds(pl.multiple_of(OWN * core + STEP * index, STEP), STEP), :] = pre.astype(BF)

    slot_cross_branch = share(held.cross_branch)
    produce_expand(0)
    scatter.tick()

    def low(target):
        def store(columns, value):
            target[:, columns] = value.astype(BF)

        return store

    rows_back(held.cross_branch.at[mine], weight(CROSS_OUT, 1), low(held.attended_grad))
    fetch(CROSS_VALUE, 1)
    have("cross_queries", "cross_keys", "cross_values", "cross_bias", "cross_logs", "cross_t")
    attend_rows_back(
        held.cross_queries, held.cross_keys, held.cross_values, held.cross_bias, held.cross_logs, held.attended_grad,
        held.cross_query_grad.at[mine], held.cross_terms.at[0, core], held.cross_terms.at[1, core], CROSS_SEGMENTS, H // 2,
    )
    slot_cross_query = share(held.cross_query_grad)
    slot_cross_terms = links.slot()
    links.send(slot_cross_terms, held.cross_terms.at[:, core], held.cross_terms.at[:, core], partner)
    produce_expand(1)
    scatter.tick()

    def add_first(columns, value):
        held.third_grad[:, columns] = value

    rows_back(held.cross_query_grad.at[mine], weight(CROSS_QUERY, 2), add_first)
    fetch(OUT, 2)
    have("normal_one", "inverse_one", "first_t", "memory_t", "attended_t", "tokens_t")

    @loop(OWN // STEP)
    def _(index):
        rows = tile(index, STEP)
        grad = held.third_grad[rows, :] + alpha_scale * held.second_sum[rows, :]
        pre = norm_rows_back(grad, held.normal_one[rows, :], spread(held.inverse_one, rows), gain(0), held.norm_sums, 0)
        held.second_sum[rows, :] = pre
        held.self_branch[pl.ds(pl.multiple_of(OWN * core + STEP * index, STEP), STEP), :] = pre.astype(BF)

    slot_self_branch = share(held.self_branch)
    norm_steps = all_sum(links, held.norm_sums, norm_grads, held.work)
    next(norm_steps)
    produce_expand(2)
    scatter.tick()
    produce_expand(3)
    rows_back(held.self_branch.at[mine], weight(OUT, 2), low(held.attended_grad))
    fetch(QUERY, 2)
    have("queries", "keys", "values", "self_bias", "self_logs")
    for step in up_sends:
        links.sent(step)
    terms = held.up.reshape(2, 2, 2, 2, LEN, D)
    key_terms, value_terms = (held.up.at[pl.ds(2 * which, 2)].reshape(SPAN, D) for which in (0, 1))

    def attend_part(first, pairs):
        attend_rows_back(
            held.queries, held.keys, held.values, held.self_bias, held.self_logs, held.attended_grad,
            held.query_grad.at[mine], key_terms, value_terms, SELF_SEGMENTS, pairs, first,
        )

    attend_part(0, 2)
    scatter.tick()
    next(norm_steps)
    attend_part(2, 2)
    shared(held.cross_branch, slot_cross_branch)
    produce(lambda: held.cross_t[...], held.cross_branch)
    scatter.tick()
    next(norm_steps)
    attend_part(4, 2)
    shared(held.cross_query_grad, slot_cross_query)
    produce(lambda: held.first_t[...], held.cross_query_grad)
    scatter.tick()
    next(norm_steps)
    attend_part(6, 2)
    slot_query = share(held.query_grad)
    slot_terms = links.slot()
    links.send(slot_terms, terms.at[:, :, :, 1 - core], held.terms_core, partner)

    links.arrived(slot_cross_terms, held.cross_terms.at[:, 1 - core])
    for which in (0, 1):
        held.cross_sums[which] = (held.cross_terms[which, 0].astype(F32) + held.cross_terms[which, 1].astype(F32)).astype(BF)
    produce(lambda: held.memory_t[...], held.cross_sums.at[0], MEM)
    scatter.tick()
    next(norm_steps)

    links.arrived(slot_terms, held.terms_core)
    near = z % 2

    def join(place_index):
        for which in (0, 1):
            for high in (0, 1):
                value = terms[which, high, place_index, core].astype(F32) + held.terms_core[which, high, place_index].astype(F32)
                terms[which, high, place_index, core] = value.astype(BF)

    join(1 - near)
    slot_mate = links.slot()
    links.send(slot_mate, terms.at[:, :, 1 - near, core], held.terms_mate, place.mate())
    join(near)

    produce(lambda: held.memory_t[...], held.cross_sums.at[1], MEM)
    scatter.tick()

    cross_key, cross_value = weight(CROSS_KEY, 0), weight(CROSS_VALUE, 1)
    sums = held.cross_sums.reshape(2, 4, 2, 16, D)

    @loop(4)
    def _(index):
        columns = tile(index, OWN)
        term = project_back(sums[0, :, core].reshape(64, D), cross_key[columns, :])
        term = term + project_back(sums[1, :, core].reshape(64, D), cross_value[columns, :])
        held.memory_own[:, :, columns] = term.astype(BF).reshape(4, 16, OWN)

    fetch(KEY, 0)
    fetch(VALUE, 1)
    slot_memory = links.slot(4)
    for k in (1, 2, 3):
        links.send(slot_memory + z, held.memory_own.at[(z + k) % 4], held.memory_in.at[z], place.along_z(k))
    held.memory_in[z] = held.memory_own[z]

    shared(held.self_branch, slot_self_branch)
    produce(lambda: held.attended_t[...], held.self_branch)
    scatter.tick()
    shared(held.query_grad, slot_query)
    produce(lambda: held.tokens_t[...], held.query_grad)
    scatter.tick()

    def add_input(columns, value):
        held.third_grad[:, columns] = alpha_scale * held.second_sum[:, columns] + value

    rows_back(held.query_grad.at[mine], weight(QUERY, 2), add_input)
    links.arrived(slot_mate, held.terms_mate)
    for which, target in enumerate((held.key_grad, held.value_grad)):
        for high in (0, 1):
            value = terms[which, high, near, core].astype(F32) + held.terms_mate[which, high].astype(F32)
            target[pl.ds(pl.multiple_of(OWN * core + LEN * high, LEN), LEN), :] = value.astype(BF)
    slot_key, slot_value = share(held.key_grad), share(held.value_grad)

    def add_more(columns, value):
        held.third_grad[:, columns] += value

    rows_back(held.key_grad.at[mine], weight(KEY, 0), add_more)
    rows_back(held.value_grad.at[mine], weight(VALUE, 1), add_more)
    held.far_own[...] = held.third_grad[block_rows(1 - group), :].astype(BF)
    slot_far = links.slot()
    links.send(slot_far, held.far_own, held.far_in, place.along_z(2))
    shared(held.key_grad, slot_key)
    produce(lambda: held.tokens_t[...], held.key_grad)
    scatter.tick()
    shared(held.value_grad, slot_value)
    produce(lambda: held.tokens_t[...], held.value_grad)
    scatter.tick()
    input_grad[group] = held.third_grad[block_rows(group), :]
    scatter.tick()
    for k in (1, 2, 3):
        links.arrived(slot_memory + (z + k) % 4, held.memory_in.at[(z + k) % 4])
    for which in (0, 1):
        memory_grad[which] = held.memory_in[2 * which].astype(F32) + held.memory_in[2 * which + 1].astype(F32)
    for _ in range(3):
        scatter.tick()
    links.arrived(slot_far, held.far_in)
    input_grad[1 - group] = held.far_in[...].astype(F32)
    links.arrived(slot_output, output.at[1 - group])
    moves.finish()
    links.finish()


def backward_call(square, shrink, saves, block_shape, memory_shape):
    results = [jax.ShapeDtypeStruct(block_shape, BF)]
    results += [jax.ShapeDtypeStruct(shape, F32) for shape in (block_shape, memory_shape)]
    results += [jax.ShapeDtypeStruct((32, D), F32)] * 8
    results += [jax.ShapeDtypeStruct(shape, F32) for shape in ((32, 4 * D), (LEN, D), (8, D))]
    saved = {**FORWARD_SAVES, **TURNED_SAVES}
    held = {name: saved[name] for name in saved if name != "final_low"}
    return pl.pallas_call(
        backward_kernel,
        in_specs=[IN_PLACE] * (2 + len(saved)),
        out_specs=[IN_PLACE] + [IN_VMEM] * (len(results) - 1),
        out_shape=results,
        scratch_shapes=[
            *vmem_of(held),
            *vmem_of(BACKWARD_SCRATCH),
            pltpu.SemaphoreType.DMA((BACKWARD_SENDS,)),
            pltpu.SemaphoreType.DMA((BACKWARD_SLOTS,)),
            pltpu.SemaphoreType.DMA((BACKWARD_MOVES,)),
        ],
        compiler_params=pltpu.CompilerParams(collective_id=1, has_side_effects=True, vmem_limit_bytes=63 << 20),
    )(square, shrink.reshape(4, 4, D, OWN), *(saves[name] for name in saved))


def hand_over_kernel(norms, *refs):
    count = (len(refs) - 3) // 3
    gains, biases, sem = refs[2 * count], refs[2 * count + 1], refs[-1]
    held = refs[2 * count + 2 : -1]
    loads = [pltpu.make_async_copy(refs[n], held[n], sem.at[0, n]) for n in range(count)]
    stores = [pltpu.make_async_copy(held[n], refs[count + n], sem.at[1, n]) for n in range(count)]
    for load in loads:
        load.start()
    for load, store in zip(loads, stores):
        load.wait()
        store.start()
    own = pltpu.roll(norms[...], (D - 32 * Place().number) % D, 1)
    gains[...] = own[:3, :32]
    biases[...] = own[3:6, :32]
    for store in stores:
        store.wait()


def hand_over(norms, values):
    shapes = [jax.ShapeDtypeStruct(value.shape, value.dtype) for value in values]
    return pl.pallas_call(
        hand_over_kernel,
        in_specs=[IN_VMEM] + [IN_PLACE] * len(values),
        out_specs=[IN_PLACE] * len(values) + [IN_VMEM] * 2,
        out_shape=shapes + [jax.ShapeDtypeStruct((3, 32), F32)] * 2,
        scratch_shapes=[
            *(pltpu.VMEM(shape.shape, shape.dtype) for shape in shapes),
            pltpu.SemaphoreType.DMA((2, len(values))),
        ],
        compiler_params=pltpu.CompilerParams(vmem_limit_bytes=VMEM_BYTES),
    )(norms, *values)


def fast_shards(
    tokens, memory, lengths, memory_segments, out_grad,
    self_query, self_key, self_value, self_out,
    cross_query, cross_key, cross_value, cross_out,
    expand_weight, shrink_weight, norm_gains, norm_biases,
):
    weights = (self_key, self_value, self_query, self_out, cross_query, cross_key, cross_value, cross_out)
    square, shrink, saves = forward_call(
        lengths, memory_segments, norm_gains, norm_biases, tokens, memory, out_grad, (*weights, expand_weight, shrink_weight)
    )
    *values, norm_grads = backward_call(square, shrink, saves, tokens.shape, memory.shape)
    output, input_grad, memory_grad, *units, expand_grad, shrink_grad, gains_grad, biases_grad = hand_over(norm_grads, values)
    return (
        output,
        input_grad,
        memory_grad,
        *(units[unit] for unit in (QUERY, KEY, VALUE, OUT, CROSS_QUERY, CROSS_KEY, CROSS_VALUE, CROSS_OUT)),
        expand_grad,
        shrink_grad,
        gains_grad,
        biases_grad,
    )


def solution(mesh):
    quick = dict(mesh.shape) == {"dp": 4, "seq": 8}
    return jax.shard_map(
        fast_shards if quick else shards,
        mesh=mesh,
        in_specs=(
            P("dp", "seq", None),
            P("dp", "seq", None),
            P("dp", None),
            P("dp", None),
            P("dp", "seq", None),
            P(("dp", "seq"), None),
            P(("dp", "seq"), None),
            P(("dp", "seq"), None),
            P(("dp", "seq"), None),
            P(("dp", "seq"), None),
            P(("dp", "seq"), None),
            P(("dp", "seq"), None),
            P(("dp", "seq"), None),
            P(("dp", "seq"), None),
            P(("dp", "seq"), None),
            P(None, ("dp", "seq")),
            P(None, ("dp", "seq")),
        ),
        out_specs=(
            P("dp", "seq", None),
            P("dp", "seq", None),
            P("dp", "seq", None),
            P(("dp", "seq"), None),
            P(("dp", "seq"), None),
            P(("dp", "seq"), None),
            P(("dp", "seq"), None),
            P(("dp", "seq"), None),
            P(("dp", "seq"), None),
            P(("dp", "seq"), None),
            P(("dp", "seq"), None),
            P(("dp", "seq"), None),
            P(("dp", "seq"), None),
            P(None, ("dp", "seq")),
            P(None, ("dp", "seq")),
        ),
        check_vma=False,
    )
```

```python
import functools

import jax
import jax.numpy as jnp
from jax import lax
from jax.experimental import pallas as pl
from jax.experimental.pallas import tpu as pltpu
from jax.sharding import PartitionSpec as P

H = 16
HD = 64
MB = 2


alpha_scale = 300.0**0.25
norm_eps = 1e-05
masked_score = -1e30


def layer_norm(value, gain, bias):
    average = jnp.mean(value, axis=-1, keepdims=True)
    centred = value - average
    spread = jnp.mean(centred * centred, axis=-1, keepdims=True)
    return centred * lax.rsqrt(spread + norm_eps) * gain + bias


def project(left, right):
    return jnp.dot(left, right, preferred_element_type=jnp.float32)


def project_back(left, right):
    return lax.dot_general(
        left, right, (((1,), (1,)), ((), ())), preferred_element_type=jnp.float32
    )


def weight_term(left, right):
    return lax.dot_general(
        left, right, (((0,), (0,)), ((), ())), preferred_element_type=jnp.float32
    )


def split_heads(value):
    return value.reshape(value.shape[0], value.shape[1], H, HD)


def sentence_ids(sent_ends, places):
    return jnp.sum((places[None, :, None] >= sent_ends[:, None, :]).astype(jnp.int32), axis=2)


def masked_scores(queries, key_heads, allowed, scaling):
    raw_scores = (
        jnp.einsum("gqhd,gkhd->ghqk", queries, key_heads, preferred_element_type=jnp.float32)
        * scaling
    )
    return jnp.where(allowed[:, None], raw_scores, masked_score)


def attend_forward(queries, key_heads, value_heads, allowed, scaling):
    scores = masked_scores(queries, key_heads, allowed, scaling)
    row_max = jnp.max(scores, axis=3, keepdims=True)
    powers = jnp.exp(scores - row_max)
    row_total = jnp.sum(powers, axis=3, keepdims=True)
    prob_low = (powers / row_total).astype(jnp.bfloat16)
    attended = jnp.einsum(
        "ghqk,gkhd->gqhd", prob_low, value_heads, preferred_element_type=jnp.float32
    )
    return (attended, row_max + jnp.log(row_total))


def attend_backward(queries, key_heads, value_heads, allowed, scaling, log_total, attended_grad):
    scores = masked_scores(queries, key_heads, allowed, scaling)
    probability = jnp.exp(scores - log_total)
    prob_grad = jnp.einsum(
        "gqhd,gkhd->ghqk", attended_grad, value_heads, preferred_element_type=jnp.float32
    )
    score_grad = probability * (prob_grad - jnp.sum(prob_grad * probability, axis=3, keepdims=True))
    score_low = score_grad.astype(jnp.bfloat16)
    query_grad = (
        jnp.einsum("ghqk,gkhd->gqhd", score_low, key_heads, preferred_element_type=jnp.float32)
        * scaling
    )
    return (query_grad, score_low, probability.astype(jnp.bfloat16))


def micro_batch(gathered, tokens, memory, lengths, memory_segments, out_grad):
    (
        self_query,
        self_key,
        self_value,
        self_out,
        cross_query,
        cross_key,
        cross_value,
        cross_out,
        expand_weight,
        shrink_weight,
        norm_gains,
        norm_biases,
    ) = gathered
    gains = norm_gains.astype(jnp.float32)
    biases = norm_biases.astype(jnp.float32)
    group_size, local_len, features = tokens.shape
    seq_count = lax.axis_size("seq")
    seq_index = lax.axis_index("seq")
    full_len = local_len * seq_count
    row_count = group_size * local_len
    scaling = HD ** (-0.5)
    sent_ends = jnp.cumsum(lengths, axis=1)[:, :-1]
    query_places = seq_index * local_len + jnp.arange(local_len, dtype=jnp.int32)
    key_places = jnp.arange(full_len, dtype=jnp.int32)
    query_ids = sentence_ids(sent_ends, query_places)
    key_ids = sentence_ids(sent_ends, key_places)
    self_allowed = (query_ids[:, :, None] == key_ids[:, None, :]) & (
        key_places[None, None, :] <= query_places[None, :, None]
    )
    cross_allowed = query_ids[:, :, None] == memory_segments[:, None, :]
    token_rows = tokens.reshape(row_count, features)
    queries = split_heads(
        project(token_rows, self_query)
        .astype(jnp.bfloat16)
        .reshape(group_size, local_len, features)
    )
    own_keys = (
        project(token_rows, self_key).astype(jnp.bfloat16).reshape(group_size, local_len, features)
    )
    own_values = (
        project(token_rows, self_value)
        .astype(jnp.bfloat16)
        .reshape(group_size, local_len, features)
    )
    all_keys, all_values = (
        lax.all_gather(own_keys, "seq", axis=1, tiled=True),
        lax.all_gather(own_values, "seq", axis=1, tiled=True),
    )
    key_heads = split_heads(all_keys)
    value_heads = split_heads(all_values)
    attended, self_log = attend_forward(queries, key_heads, value_heads, self_allowed, scaling)
    attended = attended.reshape(row_count, features).astype(jnp.bfloat16)
    first_pre = alpha_scale * token_rows.astype(jnp.float32) + project(attended, self_out)
    first, first_pull = jax.vjp(layer_norm, first_pre, gains[0], biases[0])
    first_low = first.astype(jnp.bfloat16)
    cross_queries = split_heads(
        project(first_low, cross_query)
        .astype(jnp.bfloat16)
        .reshape(group_size, local_len, features)
    )
    own_memory = memory.reshape(-1, features)
    memory_all = lax.all_gather(memory, "seq", axis=1, tiled=True)
    memory_rows = memory_all.reshape(-1, features)
    cross_keys = (
        project(memory_rows, cross_key).astype(jnp.bfloat16).reshape(group_size, -1, features)
    )
    cross_values = (
        project(memory_rows, cross_value).astype(jnp.bfloat16).reshape(group_size, -1, features)
    )
    cross_key_heads = split_heads(cross_keys)
    cross_value_heads = split_heads(cross_values)
    cross_attended, cross_log = attend_forward(
        cross_queries, cross_key_heads, cross_value_heads, cross_allowed, scaling
    )
    cross_attended = cross_attended.reshape(row_count, features).astype(jnp.bfloat16)
    second_pre = alpha_scale * first + project(cross_attended, cross_out)
    second, second_pull = jax.vjp(layer_norm, second_pre, gains[1], biases[1])
    second_low = second.astype(jnp.bfloat16)
    upward = project(second_low, expand_weight)
    active, gelu_pull = jax.vjp(jax.nn.gelu, upward)
    active_low = active.astype(jnp.bfloat16)
    third_pre = alpha_scale * second + project(active_low, shrink_weight)
    final, third_pull = jax.vjp(layer_norm, third_pre, gains[2], biases[2])
    third_grad, gain_third, bias_third = third_pull(
        out_grad.reshape(row_count, features).astype(jnp.float32)
    )
    branch_grad = third_grad.astype(jnp.bfloat16)
    shrink_grad = weight_term(active_low, branch_grad)
    (up_grad,) = gelu_pull(project_back(branch_grad, shrink_weight))
    up_low = up_grad.astype(jnp.bfloat16)
    expand_grad = weight_term(second_low, up_low)
    second_grad = alpha_scale * third_grad + project_back(up_low, expand_weight)
    second_pre_grad, gain_second, bias_second = second_pull(second_grad)
    cross_branch = second_pre_grad.astype(jnp.bfloat16)
    cross_out_grad = weight_term(cross_attended, cross_branch)
    cross_attended_grad = split_heads(
        project_back(cross_branch, cross_out)
        .astype(jnp.bfloat16)
        .reshape(group_size, local_len, features)
    )
    cross_q_grad, cross_scores, cross_probs = attend_backward(
        cross_queries,
        cross_key_heads,
        cross_value_heads,
        cross_allowed,
        scaling,
        cross_log,
        cross_attended_grad,
    )
    cross_q_low = cross_q_grad.reshape(row_count, features).astype(jnp.bfloat16)
    cross_query_grad = weight_term(first_low, cross_q_low)
    key_term = (
        jnp.einsum(
            "ghqk,gqhd->gkhd", cross_scores, cross_queries, preferred_element_type=jnp.float32
        )
        * scaling
    ).reshape(group_size, -1, features)
    value_term = jnp.einsum(
        "ghqk,gqhd->gkhd", cross_probs, cross_attended_grad, preferred_element_type=jnp.float32
    ).reshape(group_size, -1, features)
    key_summed, value_summed = (
        lax.psum_scatter(
            key_term.astype(jnp.bfloat16), "seq", scatter_dimension=1, tiled=True
        ).astype(jnp.float32),
        lax.psum_scatter(
            value_term.astype(jnp.bfloat16), "seq", scatter_dimension=1, tiled=True
        ).astype(jnp.float32),
    )
    key_low = key_summed.reshape(-1, features).astype(jnp.bfloat16)
    value_low = value_summed.reshape(-1, features).astype(jnp.bfloat16)
    cross_key_grad = weight_term(own_memory, key_low)
    cross_value_grad = weight_term(own_memory, value_low)
    memory_grad = (project_back(key_low, cross_key) + project_back(value_low, cross_value)).reshape(
        memory.shape
    )
    first_grad = alpha_scale * second_pre_grad + project_back(cross_q_low, cross_query)
    first_pre_grad, gain_first, bias_first = first_pull(first_grad)
    self_branch = first_pre_grad.astype(jnp.bfloat16)
    self_out_grad = weight_term(attended, self_branch)
    attended_grad = split_heads(
        project_back(self_branch, self_out)
        .astype(jnp.bfloat16)
        .reshape(group_size, local_len, features)
    )
    self_q_grad, self_scores, self_probs = attend_backward(
        queries, key_heads, value_heads, self_allowed, scaling, self_log, attended_grad
    )
    count = local_len * lax.axis_size("seq")
    key_part = (
        jnp.einsum("ghqk,gqhd->kghd", self_scores, queries, preferred_element_type=jnp.float32)
        * scaling
    )
    value_part = jnp.einsum(
        "ghqk,gqhd->kghd", self_probs, attended_grad, preferred_element_type=jnp.float32
    )
    pair_summed = lax.psum_scatter(
        jnp.concatenate(
            [
                key_part.reshape(count, group_size, features),
                value_part.reshape(count, group_size, features),
            ],
            axis=2,
        ).astype(jnp.bfloat16),
        "seq",
        scatter_dimension=0,
        tiled=True,
    ).astype(jnp.float32)
    key_grad = (
        pair_summed[:, :, :features]
        .astype(jnp.bfloat16)
        .transpose(1, 0, 2)
        .reshape(row_count, features)
    )
    value_grad = (
        pair_summed[:, :, features:]
        .astype(jnp.bfloat16)
        .transpose(1, 0, 2)
        .reshape(row_count, features)
    )
    query_low = self_q_grad.reshape(row_count, features).astype(jnp.bfloat16)
    self_query_grad = weight_term(token_rows, query_low)
    self_key_grad = weight_term(token_rows, key_grad)
    self_value_grad = weight_term(token_rows, value_grad)
    input_grad = (
        alpha_scale * first_pre_grad
        + project_back(query_low, self_query)
        + project_back(key_grad, self_key)
        + project_back(value_grad, self_value)
    )
    gains_grad = jnp.stack([gain_first, gain_second, gain_third])
    biases_grad = jnp.stack([bias_first, bias_second, bias_third])
    gradients = (
        self_query_grad,
        self_key_grad,
        self_value_grad,
        self_out_grad,
        cross_query_grad,
        cross_key_grad,
        cross_value_grad,
        cross_out_grad,
        expand_grad,
        shrink_grad,
        gains_grad,
        biases_grad,
    )
    result = final.astype(jnp.bfloat16).reshape(group_size, local_len, features)
    return (result, input_grad.reshape(group_size, local_len, features), memory_grad, gradients)


def shards(
    tokens,
    memory,
    lengths,
    memory_segments,
    out_grad,
    self_query,
    self_key,
    self_value,
    self_out,
    cross_query,
    cross_key,
    cross_value,
    cross_out,
    expand_weight,
    shrink_weight,
    norm_gains,
    norm_biases,
):
    group_size = tokens.shape[0] // MB
    outputs = []
    input_grads = []
    memory_grads = []
    totals = None
    for batch_index in range(MB):
        gathered = (
            lax.all_gather(self_query, ("dp", "seq"), axis=0, tiled=True),
            lax.all_gather(self_key, ("dp", "seq"), axis=0, tiled=True),
            lax.all_gather(self_value, ("dp", "seq"), axis=0, tiled=True),
            lax.all_gather(self_out, ("dp", "seq"), axis=0, tiled=True),
            lax.all_gather(cross_query, ("dp", "seq"), axis=0, tiled=True),
            lax.all_gather(cross_key, ("dp", "seq"), axis=0, tiled=True),
            lax.all_gather(cross_value, ("dp", "seq"), axis=0, tiled=True),
            lax.all_gather(cross_out, ("dp", "seq"), axis=0, tiled=True),
            lax.all_gather(expand_weight, ("dp", "seq"), axis=0, tiled=True),
            lax.all_gather(shrink_weight, ("dp", "seq"), axis=0, tiled=True),
            lax.all_gather(norm_gains, ("dp", "seq"), axis=1, tiled=True),
            lax.all_gather(norm_biases, ("dp", "seq"), axis=1, tiled=True),
        )
        start = batch_index * group_size
        stop = start + group_size
        result, input_grad, memory_grad, gradients = micro_batch(
            gathered,
            tokens[start:stop],
            memory[start:stop],
            lengths[start:stop],
            memory_segments[start:stop],
            out_grad[start:stop],
        )
        outputs.append(result)
        input_grads.append(input_grad)
        memory_grads.append(memory_grad)
        if totals is None:
            totals = gradients
        else:
            totals = tuple((running + gradient for running, gradient in zip(totals, gradients)))
    summed = (
        lax.psum_scatter(totals[0], ("dp", "seq"), scatter_dimension=0, tiled=True),
        lax.psum_scatter(totals[1], ("dp", "seq"), scatter_dimension=0, tiled=True),
        lax.psum_scatter(totals[2], ("dp", "seq"), scatter_dimension=0, tiled=True),
        lax.psum_scatter(totals[3], ("dp", "seq"), scatter_dimension=0, tiled=True),
        lax.psum_scatter(totals[4], ("dp", "seq"), scatter_dimension=0, tiled=True),
        lax.psum_scatter(totals[5], ("dp", "seq"), scatter_dimension=0, tiled=True),
        lax.psum_scatter(totals[6], ("dp", "seq"), scatter_dimension=0, tiled=True),
        lax.psum_scatter(totals[7], ("dp", "seq"), scatter_dimension=0, tiled=True),
        lax.psum_scatter(totals[8], ("dp", "seq"), scatter_dimension=0, tiled=True),
        lax.psum_scatter(totals[9], ("dp", "seq"), scatter_dimension=0, tiled=True),
        lax.psum_scatter(totals[10], ("dp", "seq"), scatter_dimension=1, tiled=True),
        lax.psum_scatter(totals[11], ("dp", "seq"), scatter_dimension=1, tiled=True),
    )
    return (
        jnp.concatenate(outputs, 0),
        jnp.concatenate(input_grads, 0),
        jnp.concatenate(memory_grads, 0),
        summed[0],
        summed[1],
        summed[2],
        summed[3],
        summed[4],
        summed[5],
        summed[6],
        summed[7],
        summed[8],
        summed[9],
        summed[10],
        summed[11],
    )


MESH = pl.DeviceIdType.MESH
BF = jnp.bfloat16
F32 = jnp.float32
ALL = slice(None)
D = 1024
LEN = 128
OWN = 2 * LEN
SPAN = 8 * LEN
MEM = 128
KEY, VALUE, QUERY, OUT, CROSS_QUERY, CROSS_KEY, CROSS_VALUE, CROSS_OUT = range(8)
EXPAND = 8
SQUARE = 12
UNITS = 16
GRID = (2, 2, 4, 2)
SQUARE_SHAPE = (SQUARE, *GRID, 32, D)
SHRINK_SHAPE = (UNITS - SQUARE, *GRID, LEN, OWN)
VMEM_BYTES = 60 << 20
GELU_SLOPE = (2.0 / 3.141592653589793) ** 0.5
GELU_CUBE = 0.044715


class Place:
    def __init__(self):
        dp, seq = lax.axis_index("dp"), lax.axis_index("seq")
        self.x, self.y, self.core, self.z, self.seq = dp % 2, dp // 2, seq % 2, seq // 2, seq
        self.number = dp * 8 + seq
        self.group = self.z // 2
        self.low = seq % 4
        self.mate_z = self.z + 1 - 2 * (self.z % 2)
        self.inner_z = 2 - self.group
        self.next_z = (self.z + 2) % 4
        self.inner = self.z % 3 != 0
        self.outer = self.z % 3 == 0

    def at(self, y=None, x=None, z=None, core=None):
        y = self.y if y is None else y
        x = self.x if x is None else x
        z = self.z if z is None else z
        core = self.core if core is None else core
        return (y * 2 + x, z * 2 + core)

    def across(self, axis):
        if axis == "x":
            return self.at(x=1 - self.x)
        if axis == "y":
            return self.at(y=1 - self.y)
        return self.at(core=1 - self.core)

    def along_z(self, step):
        return self.at(z=(self.z + step) % 4)

    def mate(self):
        return self.at(z=self.mate_z)

    def greet(self):
        barrier = pltpu.get_barrier_semaphore()
        peers = [self.across(axis) for axis in ("x", "y", "core")]
        peers += [self.along_z(step) for step in (1, 2, 3)]
        for peer in peers:
            pl.semaphore_signal(barrier, inc=1, device_id=peer, device_id_type=MESH)
        pl.semaphore_wait(barrier, len(peers))


def under(when, act):
    if when is None:
        act()
    else:
        pl.when(when)(act)


class Links:
    def __init__(self, place, send_sem, recv_sem):
        self.place, self.send_sem, self.recv_sem = place, send_sem, recv_sem
        self.sends, self.slots = 0, 0
        self.open = {}

    def slot(self, count=1):
        first = self.slots
        self.slots += count
        assert self.slots <= self.recv_sem.shape[0]
        return first

    def send(self, slot, source, target, device, when=None):
        assert self.sends < self.send_sem.shape[0]
        step = pltpu.make_async_remote_copy(
            src_ref=source,
            dst_ref=target,
            send_sem=self.send_sem.at[self.sends],
            recv_sem=self.recv_sem.at[slot],
            device_id=device,
            device_id_type=MESH,
        )
        under(when, step.start)
        self.sends += 1
        self.open[id(step)] = step, when
        return step

    def arrived(self, slot, target):
        pltpu.make_async_remote_copy(
            src_ref=target,
            dst_ref=target,
            send_sem=self.send_sem.at[0],
            recv_sem=self.recv_sem.at[slot],
            device_id=self.place.across("core"),
            device_id_type=MESH,
        ).wait_recv()

    def sent(self, step):
        step, when = self.open.pop(id(step))
        under(when, step.wait_send)

    def finish(self):
        for step, when in self.open.values():
            under(when, step.wait_send)
        self.open = {}


class Moves:
    def __init__(self, sem):
        self.sem, self.count, self.open = sem, 0, {}

    def start(self, source, target):
        assert self.count < self.sem.shape[0]
        step = pltpu.make_async_copy(source, target, self.sem.at[self.count])
        step.start()
        self.count += 1
        self.open[id(step)] = step
        return step

    def wait(self, step):
        self.open.pop(id(step)).wait()

    def finish(self):
        for step in self.open.values():
            step.wait()
        self.open = {}


def all_sum(links, part, total, work):
    place = links.place
    work[0] = part[...]
    for number, axis in enumerate(("core", "y", "x")):
        slot = links.slot()
        step = links.send(slot, work.at[0], work.at[1 + number], place.across(axis))
        yield
        links.arrived(slot, work.at[1 + number])
        links.sent(step)
        work[0] = work[0] + work[1 + number]
    slot = links.slot(4)
    for k in (1, 2, 3):
        links.send(slot + place.z, work.at[0], work.at[4 + place.z], place.along_z(k))
    yield
    result = work[0]
    for k in (1, 2, 3):
        source = (place.z + k) % 4
        links.arrived(slot + source, work.at[4 + source])
        result = result + work[4 + source]
    total[...] = result
    yield


def loop(count):
    return pl.loop(0, count)


def tile(index, size):
    return pl.ds(pl.multiple_of(index * size, size), size)


def rows_times(left, right, store, rows=OWN, width=256):
    for first in range(0, left.shape[0], rows):

        @loop(D // width)
        def _(index):
            columns = tile(index, width)
            store(pl.ds(first, rows), columns, jnp.dot(left[pl.ds(first, rows), :], right[:, columns], preferred_element_type=F32))


def rows_back(left, right, store, width=256):
    @loop(D // width)
    def _(index):
        columns = tile(index, width)
        store(columns, project_back(left[...], right[columns, :]))


def put(target, dtype=BF):
    def store(rows, columns, value):
        target[rows, columns] = value.astype(dtype)

    return store


def half_masks():
    lane = lax.broadcasted_iota(jnp.int32, (1, LEN), 1)
    return [(lane < HD).astype(F32), (lane >= HD).astype(F32)]


def attend_rows(queries, keys, values, bias, logs, out, segments, pairs=H // 2, first_pair=0):
    masks = half_masks()

    @loop(pairs)
    def _(step):
        pair = step + first_pair
        columns = tile(pair, LEN)
        for first, rows, count in segments:
            own = pl.ds(first, rows)
            key, value = keys[pl.ds(0, count), columns], values[pl.ds(0, count), columns]
            query = queries[own, columns]
            lane = lax.broadcasted_iota(jnp.int32, (rows, LEN), 1)
            parts = []
            for half in (0, 1):
                scores = project_back(query * (masks[half] * HD**-0.5).astype(BF), key) + bias[own, pl.ds(0, count)]
                top = jnp.max(scores, axis=1, keepdims=True)
                powers = jnp.exp(scores - top)
                total = jnp.sum(powers, axis=1, keepdims=True)
                parts.append(project((powers * (1.0 / total)).astype(BF), value))
                logs[own, :] = jnp.where(lane == 2 * pair + half, top + jnp.log(total), logs[own, :])
            out[own, columns] = jnp.where(lane < HD, parts[0], parts[1]).astype(BF)


def attend_rows_back(queries, keys, values, bias, logs, grads, query_grads, key_grads, value_grads, segments, pairs, first_pair=0):
    masks = half_masks()

    @loop(pairs)
    def _(step):
        pair = step + first_pair
        columns = tile(pair, LEN)
        for number, (first, rows, count) in enumerate(segments):
            own, met = pl.ds(first, rows), pl.ds(0, count)
            key, value = keys[met, columns], values[met, columns]
            lane = lax.broadcasted_iota(jnp.int32, (rows, LEN), 1)
            halves, score_lows, prob_lows, query_parts, grad_parts = [], [], [], [], []
            for half in (0, 1):
                query = queries[own, columns] * (masks[half] * HD**-0.5).astype(BF)
                grad = grads[own, columns] * masks[half].astype(BF)
                log_total = jnp.sum(jnp.where(lane == 2 * pair + half, logs[own, :], 0.0), axis=1, keepdims=True)
                probs = jnp.exp(project_back(query, key) + bias[own, met] - log_total)
                prob_grad = project_back(grad, value)
                score_grad = probs * (prob_grad - jnp.sum(prob_grad * probs, axis=1, keepdims=True))
                score_low = score_grad.astype(BF)
                halves.append(project(score_low, key) * HD**-0.5)
                score_lows.append(score_low)
                prob_lows.append(probs.astype(BF))
                query_parts.append(query)
                grad_parts.append(grad)
            query_grads[own, columns] = jnp.where(lane < HD, halves[0], halves[1]).astype(BF)
            key_term = weight_term(jnp.concatenate(score_lows), jnp.concatenate(query_parts))
            value_term = weight_term(jnp.concatenate(prob_lows), jnp.concatenate(grad_parts))
            if number == 0:
                key_grads[met, columns] = key_term.astype(BF)
                value_grads[met, columns] = value_term.astype(BF)
            else:
                key_grads[met, columns] = (key_grads[met, columns].astype(F32) + key_term).astype(BF)
                value_grads[met, columns] = (value_grads[met, columns].astype(F32) + value_term).astype(BF)


SELF_SEGMENTS = ((LEN, LEN, SPAN), (0, LEN, SPAN // 2))
CROSS_SEGMENTS = ((0, OWN, MEM),)
STEP = 32


def norm_rows(read, normal, inverse, emit):
    @loop(OWN // STEP)
    def _(index):
        rows = tile(index, STEP)
        value = read(rows)
        centred = value - jnp.mean(value, axis=1, keepdims=True)
        scale = lax.rsqrt(jnp.mean(centred * centred, axis=1, keepdims=True) + norm_eps)
        result = centred * scale
        if normal is not None:
            normal[rows, :] = result
            inverse[rows, :] = jnp.broadcast_to(scale, (STEP, LEN))
        emit(rows, result, scale)


def norm_rows_back(grad, normal, scale, gain, sums, number):
    sums[pl.ds(number, 1), :] += jnp.sum(grad * normal, axis=0, keepdims=True)
    sums[pl.ds(3 + number, 1), :] += jnp.sum(grad, axis=0, keepdims=True)
    scaled = grad * gain
    return scale * (
        scaled
        - jnp.mean(scaled, axis=1, keepdims=True)
        - normal * jnp.mean(scaled * normal, axis=1, keepdims=True)
    )


class Gather:
    WIDE = (6, 7, 8, 10, 11, 12, 13, 14, 15)
    EARLY = 3
    RELAY = 1
    ROUTES = {False: ("zxy", "zyx"), True: ("xzy", "yzx")}
    TIMES = {False: (-3, 0, 1, 2, 3), True: (-20, -3, 1, 2, 3)}
    SLOTS = 10

    def __init__(self, links, moves, own, square, shrink):
        self.links, self.moves, self.own, self.square, self.shrink = links, moves, own, square, shrink
        self.first_slot = links.slot(UNITS * 2 * self.SLOTS)
        self.local = {}
        for unit in range(UNITS):
            target = self.block(unit, links.place.y, links.place.x, links.place.z, links.place.core)
            self.local[unit] = moves.start(own(unit), target)
        self.now = -self.EARLY
        self.steps = {}
        for number, unit in enumerate(range(UNITS)):
            wide = number in self.WIDE
            for half in (0, 1):
                for phase, time in enumerate(self.TIMES[wide]):
                    step = (phase, number, unit, half, self.ROUTES[wide][half])
                    self.steps.setdefault(max(number + time, self.now), []).append(step)
                step = (-1, number, unit, half, self.ROUTES[wide][half])
                self.steps.setdefault(max(number - self.RELAY, self.now + 1), []).append(step)

    def block(self, unit, *index):
        if unit < SQUARE:
            return self.square.at[(unit,) + index]
        return self.shrink.at[(unit - SQUARE,) + index]

    def tick(self):
        for phase, _, unit, half, route in sorted(self.steps.pop(self.now, ())):
            self.move(phase, unit, half, route)
        self.now += 1

    def move(self, phase, unit, half, route):
        links, place = self.links, self.links.place
        here = {"y": place.y, "x": place.x, "z": place.z}
        slot = self.first_slot + (2 * unit + half) * self.SLOTS
        depth = 16 if unit < SQUARE else 64
        rows = pl.ds(depth * half, depth)
        turn = route.index("z")

        def part(where, core):
            return self.block(unit, where["y"], where["x"], where["z"], core, rows)

        def reached(count):
            return {**here, **{axis: ALL for axis in route[:count]}}

        def incoming(count):
            axis = route[count]
            if axis == "z":
                return reached(count + 1)
            return {**reached(count), axis: 1 - here[axis]}

        def line(source):
            return part({**reached(turn), "z": source}, place.core)

        if phase == -1:
            def hand_on():
                links.arrived(slot + place.next_z, line(place.next_z))

            under(place.inner, hand_on)
            links.send(slot + place.next_z, line(place.next_z), line(place.next_z), place.mate(), place.inner)
            return
        if phase == 1 and unit in self.local:
            self.moves.wait(self.local.pop(unit))
        if 1 <= phase <= 3:
            if phase - 1 == turn:
                links.arrived(slot + place.mate_z, line(place.mate_z))
                for source, when in ((place.next_z, place.outer), ((6 - place.z - place.mate_z - place.next_z), None)):
                    under(when, functools.partial(links.arrived, slot + source, line(source)))
            else:
                links.arrived(slot + 3 + phase, part(incoming(phase - 1), place.core))
        if phase < 3:
            source = self.own(unit).at[rows] if phase == 0 else part(reached(phase), place.core)
            target = part(reached(phase), place.core)
            if phase == turn:
                links.send(slot + place.z, source, target, place.mate())
                links.send(slot + place.z, source, target, place.at(z=place.inner_z))
                links.send(slot + place.z, source, target, place.at(z=place.next_z), place.inner)
            else:
                links.send(slot + 4 + phase, source, target, place.across(route[phase]))
        if 1 <= phase <= 3 and phase > turn:
            fresh = part(incoming(phase - 1), place.core)
            links.send(slot + 6 + phase, fresh, fresh, place.across("core"))
        if phase == 4:
            for number in range(turn, 3):
                links.arrived(slot + 7 + number, part(incoming(number), 1 - place.core))


def core_rows(core, count=OWN):
    return pl.ds(pl.multiple_of(core * count, count), count)


def block_rows(block):
    return pl.ds(pl.multiple_of(block * LEN, LEN), LEN)


FORWARD_SAVES = {
    "queries": ((OWN, D), BF),
    "keys": ((SPAN, D), BF),
    "values": ((SPAN, D), BF),
    "self_bias": ((OWN, SPAN), F32),
    "self_logs": ((OWN, LEN), F32),
    "normal_one": ((OWN, D), F32),
    "inverse_one": ((OWN, LEN), F32),
    "cross_queries": ((OWN, D), BF),
    "cross_keys": ((MEM, D), BF),
    "cross_values": ((MEM, D), BF),
    "cross_bias": ((OWN, MEM), F32),
    "cross_logs": ((OWN, LEN), F32),
    "normal_two": ((OWN, D), F32),
    "inverse_two": ((OWN, LEN), F32),
    "slopes": ((4, OWN, D), BF),
    "third_grad": ((OWN, D), F32),
    "norm_sums": ((8, D), F32),
    "gains": ((8, D), F32),
    "final_low": ((OWN, D), BF),
}
TURNED_SAVES = {
    "tokens_t": ((16, 32, 2 * OWN), BF),
    "attended_t": ((16, 32, 2 * OWN), BF),
    "first_t": ((16, 32, 2 * OWN), BF),
    "cross_t": ((16, 32, 2 * OWN), BF),
    "second_t": ((16, 32, 2 * OWN), BF),
    "active_t": ((4, 4, 4, 32, 2 * OWN), BF),
    "memory_t": ((16, 32, MEM), BF),
    "branch": ((2 * OWN, D), BF),
}
FORWARD_SCRATCH = {
    "stream": ((SPAN, D), BF),
    "mine": ((OWN, D), BF),
    "context": ((4, 2, 16, D), BF),
    "attended": ((OWN, D), BF),
    "first_low": ((OWN, D), BF),
    "cross_attended": ((OWN, D), BF),
    "second_low": ((OWN, D), BF),
    "active": ((4, OWN, D), BF),
    "sums": ((OWN, D), F32),
    "cotangent": ((OWN, D), BF),
    "branch_own": ((OWN, D), BF),
    "weights": ((4, D, D), BF),
    "shrink_in": ((2, 4, D, OWN), BF),
    "turned": ((3, 16, 2, 32, OWN), BF),
    "turned_active": ((2, 4, 2, 4, 32, OWN), BF),
    "turned_memory": ((16, 2, 32, MEM), BF),
    "work": ((8, 8, D), F32),
    "norms": ((8, D), F32),
}
FORWARD_SENDS, FORWARD_SLOTS, FORWARD_MOVES = 352, 384, 96


class Refs:
    def __init__(self, names, refs):
        for name, ref in zip(names, refs):
            setattr(self, name, ref)


def forward_kernel(lengths, segments, norm_gains, norm_biases, tokens, memory, out_grad, *refs):
    squares, expand_own, shrink_own = refs[:8], refs[8], refs[9]
    square, shrink = refs[10:12]
    rest = refs[12:]
    kept = Refs(FORWARD_SAVES, rest[: len(FORWARD_SAVES)])
    rest = rest[len(FORWARD_SAVES) :]
    turned = Refs(TURNED_SAVES, rest[: len(TURNED_SAVES)])
    rest = rest[len(TURNED_SAVES) :]
    held = Refs(FORWARD_SAVES, rest[: len(FORWARD_SAVES)])
    rest = rest[len(FORWARD_SAVES) :]
    held.__dict__.update(Refs(FORWARD_SCRATCH, rest[: len(FORWARD_SCRATCH)]).__dict__)
    send_sem, recv_sem, move_sem = rest[len(FORWARD_SCRATCH) :]

    place = Place()
    links, moves = Links(place, send_sem, recv_sem), Moves(move_sem)
    y, x, z, core, group, low, seq = place.y, place.x, place.z, place.core, place.group, place.low, place.seq
    partner = place.across("core")
    opposite = place.along_z(2)
    mate = place.mate()
    place.greet()

    def own(unit):
        if unit < EXPAND:
            return squares[unit]
        if unit < SQUARE:
            return expand_own.at[:, pl.ds(D * (unit - EXPAND), D)]
        return shrink_own.at[:, pl.ds(OWN * (unit - SQUARE), OWN)]

    stream = held.stream
    far, mate_seq = (seq + 4) % 8, (seq + 2) % 4 + 4 * group
    other_seq = 2 * z + 1 - core
    other_mate = (other_seq + 2) % 4 + 4 * group
    slot_far, slot_mate, slot_mate_far, slot_core = links.slot(), links.slot(), links.slot(), links.slot(4)
    home = moves.start(tokens.at[group], stream.at[block_rows(seq)])
    gather = Gather(links, moves, own, square, shrink)
    for _ in range(Gather.EARLY - 1):
        gather.tick()
    links.send(slot_far, tokens.at[1 - group], stream.at[block_rows(seq)], opposite)
    links.send(slot_mate, tokens.at[group], stream.at[block_rows(seq)], mate)
    links.send(slot_core, tokens.at[group], stream.at[block_rows(seq)], partner)
    gather.tick()
    slot_memory, slot_context = links.slot(4), links.slot()
    context_home = moves.start(memory.at[group], held.context.at[z, core])
    for k in (1, 2, 3):
        links.send(slot_memory + z, memory.at[((z + k) % 4) // 2], held.context.at[z, core], place.along_z(k))
    held.norms[...] = jnp.zeros_like(held.norms)
    held.norms[pl.ds(0, 3), pl.ds(0, 32)] = norm_gains[...].astype(F32)
    held.norms[pl.ds(3, 3), pl.ds(0, 32)] = norm_biases[...].astype(F32)
    held.norms[...] = pltpu.roll(held.norms[...], 32 * place.number, 1)
    norm_steps = all_sum(links, held.norms, held.gains, held.work)
    next(norm_steps)

    def sentence(places):
        result, end = jnp.zeros_like(places), 0
        for index in range(lengths.shape[1] - 1):
            end = end + lengths[group, index]
            result = result + (places >= end).astype(jnp.int32)
        return result

    held.norm_sums[...] = jnp.zeros_like(held.norm_sums)
    held.self_logs[...] = jnp.zeros_like(held.self_logs)
    held.cross_logs[...] = jnp.zeros_like(held.cross_logs)

    @loop(OWN // STEP)
    def _(index):
        row = index * STEP + lax.broadcasted_iota(jnp.int32, (STEP, 1), 0)
        row_place = LEN * low + row + jnp.where(row >= LEN, 3 * LEN, 0)
        row_sentence = sentence(row_place)
        key_place = lax.broadcasted_iota(jnp.int32, (1, SPAN), 1)
        allowed = (row_sentence == sentence(key_place)) & (key_place <= row_place)
        held.self_bias[tile(index, STEP), :] = jnp.where(allowed, 0.0, masked_score)
        met = row_sentence == segments[pl.ds(group, 1), :]
        held.cross_bias[tile(index, STEP), :] = jnp.where(met, 0.0, masked_score)

    def pass_on(number, block):
        links.send(slot_core + number, stream.at[block_rows(block)], stream.at[block_rows(block)], partner)

    gather.tick()
    next(norm_steps)
    gather.tick()
    next(norm_steps)
    gather.tick()
    links.arrived(slot_far, stream.at[block_rows(far)])
    links.send(slot_mate_far, stream.at[block_rows(far)], stream.at[block_rows(far)], mate)
    pass_on(1, far)
    gather.tick()
    links.arrived(slot_mate, stream.at[block_rows(mate_seq)])
    pass_on(2, mate_seq)
    moves.wait(context_home)
    for k in (1, 2, 3):
        links.arrived(slot_memory + (z + k) % 4, held.context.at[(z + k) % 4, core])
    links.send(slot_context, held.context.at[:, core], held.context.at[:, core], partner)
    next(norm_steps)
    gather.tick()
    links.arrived(slot_mate_far, stream.at[block_rows((mate_seq + 4) % 8)])
    pass_on(3, (mate_seq + 4) % 8)
    gather.tick()
    moves.wait(home)
    for number, block in enumerate((other_seq, (other_seq + 4) % 8, other_mate, (other_mate + 4) % 8)):
        links.arrived(slot_core + number, stream.at[block_rows(block)])
    links.arrived(slot_context, held.context.at[:, 1 - core])
    held.mine[pl.ds(0, LEN), :] = stream[block_rows(low), :]
    held.mine[pl.ds(LEN, LEN), :] = stream[block_rows(low + 4), :]

    loads = {}

    def fetch(unit, slot):
        if unit < SQUARE:
            target = held.weights.at[slot]
            loads[unit] = (moves.start(square.at[unit].reshape(D, D), target), target)
        else:
            target = held.shrink_in.at[slot]
            loads[unit] = (moves.start(shrink.at[unit - SQUARE].reshape(4, D, OWN), target), target)

    def weight(unit):
        step, target = loads.pop(unit)
        moves.wait(step)
        return target

    turning = {"count": 0, "open": {}}
    landing = []
    mine, theirs = core_rows(core), core_rows(1 - core)

    def turn(source, name):
        number = turning["count"] % 3
        for move, sent in turning["open"].pop(number, ()):
            moves.wait(move)
            links.sent(sent)
        turning["count"] += 1
        buffer, target = held.turned.at[number], getattr(turned, name)

        @loop(4)
        def _(index):
            buffer[pl.ds(4 * index, 4)] = source[:, tile(index, OWN)].T.reshape(4, 2, 32, OWN)

        slot = links.slot()
        move = moves.start(buffer.at[:, core], target.at[:, :, mine])
        sent = links.send(slot, buffer.at[:, 1 - core], target.at[:, :, mine], partner)
        landing.append((slot, target.at[:, :, theirs]))
        turning["open"][number] = [(move, sent)]

    def keep(*names):
        for name in names:
            moves.start(getattr(held, name), getattr(kept, name))

    def gain(number):
        return held.gains[pl.ds(number, 1), :]

    def bias(number):
        return held.gains[pl.ds(3 + number, 1), :]

    fetch(KEY, 0)
    turn(held.mine, "tokens_t")
    next(norm_steps)
    fetch(VALUE, 1)
    rows_times(stream, weight(KEY), put(held.keys))
    gather.tick()
    fetch(QUERY, 2)
    rows_times(stream, weight(VALUE), put(held.values))
    rows_times(held.mine, weight(QUERY), put(held.queries))

    def attend_part(first, pairs):
        attend_rows(
            held.queries, held.keys, held.values, held.self_bias, held.self_logs, held.attended, SELF_SEGMENTS, pairs, first
        )

    fetch(OUT, 3)
    attend_part(0, 3)
    gather.tick()
    fetch(CROSS_QUERY, 0)
    attend_part(3, 3)
    gather.tick()
    fetch(CROSS_KEY, 1)
    attend_part(6, 2)
    rows_times(held.attended, weight(OUT), put(held.sums, F32))
    keep("queries", "keys", "values", "self_bias", "self_logs", "cross_bias", "gains")

    def first_rows(rows, result, _):
        held.first_low[rows, :] = (result * gain(0) + bias(0)).astype(BF)

    def after(rows, previous):
        return held.sums[rows, :] + alpha_scale * previous

    norm_rows(lambda rows: after(rows, held.mine[rows, :].astype(F32)), held.normal_one, held.inverse_one, first_rows)
    turn(held.attended, "attended_t")
    rows_times(held.first_low, weight(CROSS_QUERY), put(held.cross_queries))
    context = held.context.reshape(MEM, D)
    rows_times(context, weight(CROSS_KEY), put(held.cross_keys), MEM)
    gather.tick()
    fetch(CROSS_VALUE, 2)
    turn(held.first_low, "first_t")

    @loop(4)
    def _(index):
        held.turned_memory[pl.ds(4 * index, 4)] = context[:, tile(index, OWN)].T.reshape(4, 2, 32, MEM)

    moves.start(held.turned_memory.at[:, core], turned.memory_t)
    rows_times(context, weight(CROSS_VALUE), put(held.cross_values), MEM)
    attend_rows(
        held.cross_queries, held.cross_keys, held.cross_values, held.cross_bias, held.cross_logs,
        held.cross_attended, CROSS_SEGMENTS,
    )
    gather.tick()
    cotangent_rows, cotangent_far = block_rows(group), block_rows(1 - group)
    slot_cotangent = links.slot()
    cotangent_home = moves.start(out_grad.at[group], held.cotangent.at[cotangent_rows])
    links.send(slot_cotangent, out_grad.at[1 - group], held.cotangent.at[cotangent_rows], opposite)
    fetch(CROSS_OUT, 3)
    keep("cross_queries", "cross_keys", "cross_values", "cross_logs", "normal_one", "inverse_one")
    rows_times(held.cross_attended, weight(CROSS_OUT), put(held.sums, F32))

    def second_rows(rows, result, _):
        held.second_low[rows, :] = (result * gain(1) + bias(1)).astype(BF)

    norm_rows(
        lambda rows: after(rows, held.normal_one[rows, :] * gain(0) + bias(0)),
        held.normal_two, held.inverse_two, second_rows,
    )
    keep("normal_two", "inverse_two")
    gather.tick()
    turn(held.cross_attended, "cross_t")
    turn(held.second_low, "second_t")
    turned_open = {}
    for part in range(4):
        if part > 0:
            gather.tick()
        fetch(EXPAND + part, part)
        active, slopes = held.active.at[part], held.slopes.at[part]

        def activate(rows, columns, value):
            inner = GELU_SLOPE * (value + GELU_CUBE * value * value * value)
            bend = jnp.tanh(inner)
            active[rows, columns] = (0.5 * value * (1.0 + bend)).astype(BF)
            slope = 0.5 * (1.0 + bend) + 0.5 * value * (1.0 - bend * bend) * (
                GELU_SLOPE * (1.0 + 3.0 * GELU_CUBE * value * value)
            )
            slopes[rows, columns] = slope.astype(BF)

        rows_times(held.second_low, weight(EXPAND + part), activate)
        number = part % 2
        for move, sent in turned_open.pop(number, ()):
            moves.wait(move)
            links.sent(sent)
        buffer = held.turned_active.at[number]

        @loop(4)
        def _(index):
            buffer[index] = active[:, tile(index, OWN)].T.reshape(2, 4, 32, OWN)

        slot = links.slot()
        move = moves.start(buffer.at[:, core], turned.active_t.at[part, :, :, :, mine])
        sent = links.send(slot, buffer.at[:, 1 - core], turned.active_t.at[part, :, :, :, mine], partner)
        landing.append((slot, turned.active_t.at[part, :, :, :, theirs]))
        turned_open[number] = [(move, sent)]
    keep("slopes")
    for part in range(4):
        gather.tick()
        fetch(SQUARE + part, part % 2)
        shrink_part = weight(SQUARE + part)
        for first in (0, LEN):
            rows = pl.ds(first, LEN)
            total = project(held.active[0, rows, :], shrink_part[0])
            for depth in (1, 2, 3):
                total = total + project(held.active[depth, rows, :], shrink_part[depth])
            held.sums[rows, pl.ds(OWN * part, OWN)] = total
    links.arrived(slot_cotangent, held.cotangent.at[cotangent_far])
    moves.wait(cotangent_home)

    def third_rows(rows, result, scale):
        held.final_low[rows, :] = (result * gain(2) + bias(2)).astype(BF)
        grad = norm_rows_back(held.cotangent[rows, :].astype(F32), result, scale, gain(2), held.norm_sums, 2)
        held.third_grad[rows, :] = grad
        held.branch_own[rows, :] = grad.astype(BF)

    norm_rows(lambda rows: after(rows, held.normal_two[rows, :] * gain(1) + bias(1)), None, None, third_rows)
    slot = links.slot()
    links.send(slot, held.branch_own, turned.branch.at[mine], partner)
    landing.append((slot, turned.branch.at[theirs]))
    moves.start(held.branch_own, turned.branch.at[mine])
    keep("third_grad", "norm_sums", "final_low")
    for arrival in landing:
        links.arrived(*arrival)
    moves.finish()
    links.finish()


IN_VMEM = pl.BlockSpec(memory_space=pltpu.VMEM)
IN_SMEM = pl.BlockSpec(memory_space=pltpu.SMEM)
IN_PLACE = pl.BlockSpec(memory_space=pl.ANY)


def shapes_of(table):
    return [jax.ShapeDtypeStruct(shape, dtype) for shape, dtype in table.values()]


def vmem_of(table):
    return [pltpu.VMEM(shape, dtype) for shape, dtype in table.values()]


def forward_call(lengths, segments, norm_gains, norm_biases, tokens, memory, out_grad, weights):
    results = [
        jax.ShapeDtypeStruct(SQUARE_SHAPE, BF),
        jax.ShapeDtypeStruct(SHRINK_SHAPE, BF),
        *shapes_of(FORWARD_SAVES),
        *shapes_of(TURNED_SAVES),
    ]
    values = pl.pallas_call(
        forward_kernel,
        in_specs=[IN_SMEM] + [IN_VMEM] * 3 + [IN_PLACE] * 13,
        out_specs=[IN_PLACE] * len(results),
        out_shape=results,
        scratch_shapes=[
            *vmem_of(FORWARD_SAVES),
            *vmem_of(FORWARD_SCRATCH),
            pltpu.SemaphoreType.DMA((FORWARD_SENDS,)),
            pltpu.SemaphoreType.DMA((FORWARD_SLOTS,)),
            pltpu.SemaphoreType.DMA((FORWARD_MOVES,)),
        ],
        compiler_params=pltpu.CompilerParams(collective_id=0, has_side_effects=True, vmem_limit_bytes=VMEM_BYTES),
    )(lengths, segments, norm_gains, norm_biases, tokens, memory, out_grad, *weights)
    saves = dict(zip([*FORWARD_SAVES, *TURNED_SAVES], values[2:]))
    return values[0], values[1], saves


class Scatter:
    WIDE = (0, 2, 4, 6, 8)

    def __init__(self, links, grads, from_first, from_second, from_z, from_line, from_last, result):
        self.links, self.grads, self.result = links, grads, result
        self.from_first, self.from_second, self.from_z = from_first, from_second, from_z
        self.from_line, self.from_last = from_line, from_last
        self.slots, self.pending, self.now = {}, {}, 0

    def home(self, unit):
        for step in self.pending.pop(unit - self.grads.shape[0], ()):
            self.links.sent(step)
        self.slots[unit] = self.links.slot(12)
        return self.grads.at[unit % self.grads.shape[0]]

    def add(self, total, part):
        for row in range(total.shape[0]):
            if len(total.shape) > 3:
                self.add(total.at[row], part.at[row])
            else:
                total[row] = (total[row].astype(F32) + part[row].astype(F32)).astype(BF)

    def phase(self, unit, half, number):
        links, place, wide = self.links, self.links.place, unit in self.WIDE
        y, x, z = place.y, place.x, place.z
        here = self.grads.at[unit % self.grads.shape[0]]
        depth = unit % self.from_first.shape[0]
        rows = pl.ds(16 * half, 16)
        slot = self.slots[unit] + 6 * half
        by_y = half == 0
        first, second = ("y", "x") if by_y else ("x", "y")
        away = (1 - y, ALL) if by_y else (ALL, 1 - x)
        kept = (y, ALL) if by_y else (ALL, x)
        corner, other, mine = ((y, 1 - x), 1 - x, x) if by_y else ((1 - y, x), 1 - y, y)
        home = here.at[y, x, :, rows]
        first_in = self.from_first.at[depth, :, :, rows]
        second_in = self.from_second.at[depth, :, rows]
        if wide:
            index = self.WIDE.index(unit)
            line_in = self.from_line.at[index, :, :, rows]
            last_in = self.from_last.at[index, rows]
        else:
            before = sum(wider < unit for wider in self.WIDE)
            line_in = self.from_z.at[(unit - before) % self.from_z.shape[0], :, :, rows]

        def owned(owner):
            return here.at[(*kept, owner, rows)] if wide else here.at[y, x, pl.ds(owner, 1), rows]

        def send(number, source, target, device, when=None):
            self.pending.setdefault(unit, []).append(links.send(slot + number, source, target, device, when))

        def along_line():
            send(2 + z, owned(place.mate_z), line_in.at[z], place.mate())
            send(2 + z, owned(place.inner_z), line_in.at[z], place.at(z=place.inner_z))
            send(2 + place.mate_z, owned(3 - z), line_in.at[place.mate_z], place.mate(), place.outer)

        def hand_on():
            def join():
                links.arrived(slot + 2 + z, line_in.at[z])
                self.add(owned(place.next_z), line_in.at[z])

            under(place.inner, join)
            send(2 + z, owned(place.next_z), line_in.at[z], place.at(z=place.next_z), place.inner)

        def line_sum():
            for source in (place.mate_z, place.next_z):
                links.arrived(slot + 2 + source, line_in.at[source])
                self.add(owned(z), line_in.at[source])

            def third():
                links.arrived(slot + 2 + 3 - z, line_in.at[3 - z])
                self.add(owned(z), line_in.at[3 - z])

            under(place.inner, third)

        if number == 0:
            send(0, here.at[(*away, ALL, rows)], first_in, place.across(first))
        if number == 1 and not wide:
            links.arrived(slot, first_in)
            corner_part = here.at[(*corner, ALL, rows)]
            self.add(corner_part, first_in.at[other])
            send(1, corner_part, second_in, place.across(second))
            self.add(home, first_in.at[mine])
        if number == 2 and not wide:
            links.arrived(slot + 1, second_in)
            self.add(home, second_in)
            along_line()
        if number == 3 and not wide:
            hand_on()
        if number == 4 and not wide:
            line_sum()
            self.result(unit, rows, home[z].astype(F32))
        if number == 1 and wide:
            links.arrived(slot, first_in)
            self.add(here.at[(*kept, ALL, rows)], first_in)
            along_line()
        if number == 2 and wide:
            hand_on()
        if number == 3 and wide:
            line_sum()
            send(1, owned(z).at[other], last_in, place.across(second))
        if number == 4 and wide:
            links.arrived(slot + 1, last_in)
            self.result(unit, rows, home[z].astype(F32) + last_in[...].astype(F32))

    def tick(self):
        for number in range(5):
            unit = self.now - number
            if 0 <= unit < UNITS:
                for half in (0, 1):
                    self.phase(unit, half, number)
        self.now += 1


DEPTH = 4
BACKWARD_SCRATCH = {
    "weights": ((3, D, D), BF),
    "shrink_in": ((4, D, OWN), BF),
    "grads": ((5, 2, 2, 4, 32, D), BF),
    "from_first": ((DEPTH, 2, 4, 32, D), BF),
    "from_second": ((DEPTH, 4, 32, D), BF),
    "from_z": ((6, 4, 1, 32, D), BF),
    "from_line": ((len(Scatter.WIDE), 4, 2, 32, D), BF),
    "from_last": ((len(Scatter.WIDE), 32, D), BF),
    "up": ((4, 2 * OWN, D), BF),
    "second_sum": ((OWN, D), F32),
    "cross_branch": ((2 * OWN, D), BF),
    "attended_grad": ((OWN, D), BF),
    "cross_query_grad": ((2 * OWN, D), BF),
    "cross_terms": ((2, 2, MEM, D), BF),
    "cross_sums": ((2, MEM, D), BF),
    "self_branch": ((2 * OWN, D), BF),
    "query_grad": ((2 * OWN, D), BF),
    "terms_core": ((2, 2, 2, LEN, D), BF),
    "terms_mate": ((2, 2, LEN, D), BF),
    "key_grad": ((2 * OWN, D), BF),
    "value_grad": ((2 * OWN, D), BF),
    "memory_own": ((4, 16, D), BF),
    "memory_in": ((4, 16, D), BF),
    "far_own": ((LEN, D), BF),
    "far_in": ((LEN, D), BF),
    "work": ((8, 8, D), F32),
}
BACKWARD_SENDS, BACKWARD_SLOTS, BACKWARD_MOVES = 256, 256, 64


def backward_kernel(square, shrink, *refs):
    saved = [*FORWARD_SAVES, *TURNED_SAVES]
    names = [name for name in saved if name != "final_low"]
    kept = Refs(saved, refs[: len(saved)])
    rest = refs[len(saved) :]
    output, input_grad, memory_grad, *unit_grads = rest[:11]
    expand_grad, shrink_grad, norm_grads = rest[11:14]
    rest = rest[14:]
    held = Refs(names, rest[: len(names)])
    rest = rest[len(names) :]
    held.__dict__.update(Refs(BACKWARD_SCRATCH, rest[: len(BACKWARD_SCRATCH)]).__dict__)
    send_sem, recv_sem, move_sem = rest[len(BACKWARD_SCRATCH) :]

    place = Place()
    links, moves = Links(place, send_sem, recv_sem), Moves(move_sem)
    z, core, group = place.z, place.core, place.group
    partner = place.across("core")
    mine, theirs = core_rows(core), core_rows(1 - core)
    loads = {}

    def bring(*wanted):
        for name in wanted:
            loads[name] = moves.start(getattr(kept, name), getattr(held, name))

    def have(*wanted):
        for name in wanted:
            moves.wait(loads.pop(name))

    def fetch(unit, slot):
        loads[unit] = moves.start(square.at[unit].reshape(D, D), held.weights.at[slot])

    def weight(unit, slot):
        moves.wait(loads.pop(unit))
        return held.weights.at[slot]

    bring("branch", "active_t")

    def fetch_shrink(part):
        loads[SQUARE] = moves.start(shrink.at[:, part], held.shrink_in)

    fetch_shrink(0)
    for part in range(3):
        fetch(EXPAND + part, part)
    bring("slopes", "third_grad", "second_t", "norm_sums", "gains", "normal_two", "inverse_two")
    bring("cross_queries", "cross_keys", "cross_values", "cross_bias", "cross_logs", "cross_t")
    bring("normal_one", "inverse_one", "first_t", "memory_t", "attended_t", "tokens_t")
    bring("queries", "keys", "values", "self_bias", "self_logs")
    place.greet()

    order = [12, 13, 14, 15, 8, 9, 10, 11, CROSS_OUT, CROSS_QUERY, CROSS_KEY, CROSS_VALUE, OUT, QUERY, KEY, VALUE]

    def result(number, rows, total):
        unit = order[number]
        if unit < EXPAND:
            unit_grads[unit][rows, :] = total
        elif unit < SQUARE:
            expand_grad[rows, pl.ds(D * (unit - EXPAND), D)] = total
        else:
            shrink_grad[pl.ds(32 * (unit - SQUARE) + rows.start, rows.size), :] = total

    buffers = (held.from_first, held.from_second, held.from_z, held.from_line, held.from_last)
    scatter = Scatter(links, held.grads, *buffers, result)
    made = {"count": 0}

    def produce(left, right, depth=2 * OWN):
        target = scatter.home(made["count"])
        made["count"] += 1

        @loop(4)
        def _(index):
            columns = tile(index, OWN)
            term = project(left().reshape(512, depth), right[:, columns])
            target[:, :, :, :, columns] = term.astype(BF).reshape(2, 2, 4, 32, OWN)

    def share(ref):
        slot = links.slot()
        links.send(slot, ref.at[mine], ref.at[mine], partner)
        return slot

    def shared(ref, slot):
        links.arrived(slot, ref.at[theirs])

    def gain(number):
        return held.gains[pl.ds(number, 1), :]

    have("branch", "active_t")

    def produce_shrink(part):
        produce(lambda: held.active_t[:, :, part], held.branch)

    def produce_expand(part):
        shared(held.up.at[part], up_slots[part])
        produce(lambda: held.second_t[...], held.up.at[part])

    produce_shrink(0)
    scatter.tick()
    slot_output = links.slot()
    moves.start(kept.final_low.at[block_rows(group)], output.at[group])
    links.send(slot_output, kept.final_low.at[block_rows(1 - group)], output.at[group], place.along_z(2))
    for part in (1, 2, 3):
        produce_shrink(part)
    scatter.tick()
    have("slopes")
    own_branch = held.branch.at[mine]
    up_slots, up_sends = [], []
    for part in range(4):
        if part == 2:
            scatter.tick()
        up = held.up.at[part, mine]
        slopes = held.slopes.at[part]

        moves.wait(loads.pop(SQUARE))

        @loop(4)
        def _(index):
            columns = tile(index, OWN)
            total = project_back(own_branch[:, pl.ds(0, OWN)], held.shrink_in[0, columns, :])
            for depth in (1, 2, 3):
                total = total + project_back(own_branch[:, pl.ds(OWN * depth, OWN)], held.shrink_in[depth, columns, :])
            up[:, columns] = (total * slopes[:, columns].astype(F32)).astype(BF)

        up_slots.append(links.slot())
        up_sends.append(links.send(up_slots[part], up, up, partner))
        if part < 3:
            fetch_shrink(part + 1)

        def add(columns, value):
            if part == 0:
                held.second_sum[:, columns] = value
            else:
                held.second_sum[:, columns] += value

        rows_back(up, weight(EXPAND + part, part % 3), add)
        fetch((EXPAND + 3, CROSS_OUT, CROSS_QUERY, CROSS_KEY)[part], part % 3)
    scatter.tick()
    have("third_grad", "norm_sums", "gains", "normal_two", "inverse_two", "second_t")

    def spread(inverse, rows):
        return inverse[rows, pl.ds(0, 1)]

    @loop(OWN // STEP)
    def _(index):
        rows = tile(index, STEP)
        grad = held.second_sum[rows, :] + alpha_scale * held.third_grad[rows, :]
        pre = norm_rows_back(grad, held.normal_two[rows, :], spread(held.inverse_two, rows), gain(1), held.norm_sums, 1)
        held.second_sum[rows, :] = pre
        held.cross_branch[pl.ds(pl.multiple_of(OWN * core + STEP * index, STEP), STEP), :] = pre.astype(BF)

    slot_cross_branch = share(held.cross_branch)
    produce_expand(0)
    scatter.tick()

    def low(target):
        def store(columns, value):
            target[:, columns] = value.astype(BF)

        return store

    rows_back(held.cross_branch.at[mine], weight(CROSS_OUT, 1), low(held.attended_grad))
    fetch(CROSS_VALUE, 1)
    have("cross_queries", "cross_keys", "cross_values", "cross_bias", "cross_logs", "cross_t")
    attend_rows_back(
        held.cross_queries, held.cross_keys, held.cross_values, held.cross_bias, held.cross_logs, held.attended_grad,
        held.cross_query_grad.at[mine], held.cross_terms.at[0, core], held.cross_terms.at[1, core], CROSS_SEGMENTS, H // 2,
    )
    slot_cross_query = share(held.cross_query_grad)
    slot_cross_terms = links.slot()
    links.send(slot_cross_terms, held.cross_terms.at[:, core], held.cross_terms.at[:, core], partner)
    produce_expand(1)
    scatter.tick()

    def add_first(columns, value):
        held.third_grad[:, columns] = value

    rows_back(held.cross_query_grad.at[mine], weight(CROSS_QUERY, 2), add_first)
    fetch(OUT, 2)
    have("normal_one", "inverse_one", "first_t", "memory_t", "attended_t", "tokens_t")

    @loop(OWN // STEP)
    def _(index):
        rows = tile(index, STEP)
        grad = held.third_grad[rows, :] + alpha_scale * held.second_sum[rows, :]
        pre = norm_rows_back(grad, held.normal_one[rows, :], spread(held.inverse_one, rows), gain(0), held.norm_sums, 0)
        held.second_sum[rows, :] = pre
        held.self_branch[pl.ds(pl.multiple_of(OWN * core + STEP * index, STEP), STEP), :] = pre.astype(BF)

    slot_self_branch = share(held.self_branch)
    norm_steps = all_sum(links, held.norm_sums, norm_grads, held.work)
    next(norm_steps)
    produce_expand(2)
    scatter.tick()
    produce_expand(3)
    rows_back(held.self_branch.at[mine], weight(OUT, 2), low(held.attended_grad))
    fetch(QUERY, 2)
    have("queries", "keys", "values", "self_bias", "self_logs")
    for step in up_sends:
        links.sent(step)
    terms = held.up.reshape(2, 2, 2, 2, LEN, D)
    key_terms, value_terms = (held.up.at[pl.ds(2 * which, 2)].reshape(SPAN, D) for which in (0, 1))

    def attend_part(first, pairs):
        attend_rows_back(
            held.queries, held.keys, held.values, held.self_bias, held.self_logs, held.attended_grad,
            held.query_grad.at[mine], key_terms, value_terms, SELF_SEGMENTS, pairs, first,
        )

    attend_part(0, 2)
    scatter.tick()
    next(norm_steps)
    attend_part(2, 2)
    shared(held.cross_branch, slot_cross_branch)
    produce(lambda: held.cross_t[...], held.cross_branch)
    scatter.tick()
    next(norm_steps)
    attend_part(4, 2)
    shared(held.cross_query_grad, slot_cross_query)
    produce(lambda: held.first_t[...], held.cross_query_grad)
    scatter.tick()
    next(norm_steps)
    attend_part(6, 2)
    slot_query = share(held.query_grad)
    slot_terms = links.slot()
    links.send(slot_terms, terms.at[:, :, :, 1 - core], held.terms_core, partner)

    links.arrived(slot_cross_terms, held.cross_terms.at[:, 1 - core])
    for which in (0, 1):
        held.cross_sums[which] = (held.cross_terms[which, 0].astype(F32) + held.cross_terms[which, 1].astype(F32)).astype(BF)
    produce(lambda: held.memory_t[...], held.cross_sums.at[0], MEM)
    scatter.tick()
    next(norm_steps)

    links.arrived(slot_terms, held.terms_core)
    near = z % 2

    def join(place_index):
        for which in (0, 1):
            for high in (0, 1):
                value = terms[which, high, place_index, core].astype(F32) + held.terms_core[which, high, place_index].astype(F32)
                terms[which, high, place_index, core] = value.astype(BF)

    join(1 - near)
    slot_mate = links.slot()
    links.send(slot_mate, terms.at[:, :, 1 - near, core], held.terms_mate, place.mate())
    join(near)

    produce(lambda: held.memory_t[...], held.cross_sums.at[1], MEM)
    scatter.tick()

    cross_key, cross_value = weight(CROSS_KEY, 0), weight(CROSS_VALUE, 1)
    sums = held.cross_sums.reshape(2, 4, 2, 16, D)

    @loop(4)
    def _(index):
        columns = tile(index, OWN)
        term = project_back(sums[0, :, core].reshape(64, D), cross_key[columns, :])
        term = term + project_back(sums[1, :, core].reshape(64, D), cross_value[columns, :])
        held.memory_own[:, :, columns] = term.astype(BF).reshape(4, 16, OWN)

    fetch(KEY, 0)
    fetch(VALUE, 1)
    slot_memory = links.slot(4)
    for k in (1, 2, 3):
        links.send(slot_memory + z, held.memory_own.at[(z + k) % 4], held.memory_in.at[z], place.along_z(k))
    held.memory_in[z] = held.memory_own[z]

    shared(held.self_branch, slot_self_branch)
    produce(lambda: held.attended_t[...], held.self_branch)
    scatter.tick()
    shared(held.query_grad, slot_query)
    produce(lambda: held.tokens_t[...], held.query_grad)
    scatter.tick()

    def add_input(columns, value):
        held.third_grad[:, columns] = alpha_scale * held.second_sum[:, columns] + value

    rows_back(held.query_grad.at[mine], weight(QUERY, 2), add_input)
    links.arrived(slot_mate, held.terms_mate)
    for which, target in enumerate((held.key_grad, held.value_grad)):
        for high in (0, 1):
            value = terms[which, high, near, core].astype(F32) + held.terms_mate[which, high].astype(F32)
            target[pl.ds(pl.multiple_of(OWN * core + LEN * high, LEN), LEN), :] = value.astype(BF)
    slot_key, slot_value = share(held.key_grad), share(held.value_grad)

    def add_more(columns, value):
        held.third_grad[:, columns] += value

    rows_back(held.key_grad.at[mine], weight(KEY, 0), add_more)
    rows_back(held.value_grad.at[mine], weight(VALUE, 1), add_more)
    held.far_own[...] = held.third_grad[block_rows(1 - group), :].astype(BF)
    slot_far = links.slot()
    links.send(slot_far, held.far_own, held.far_in, place.along_z(2))
    shared(held.key_grad, slot_key)
    produce(lambda: held.tokens_t[...], held.key_grad)
    scatter.tick()
    shared(held.value_grad, slot_value)
    produce(lambda: held.tokens_t[...], held.value_grad)
    scatter.tick()
    input_grad[group] = held.third_grad[block_rows(group), :]
    scatter.tick()
    for k in (1, 2, 3):
        links.arrived(slot_memory + (z + k) % 4, held.memory_in.at[(z + k) % 4])
    for which in (0, 1):
        memory_grad[which] = held.memory_in[2 * which].astype(F32) + held.memory_in[2 * which + 1].astype(F32)
    for _ in range(3):
        scatter.tick()
    links.arrived(slot_far, held.far_in)
    input_grad[1 - group] = held.far_in[...].astype(F32)
    links.arrived(slot_output, output.at[1 - group])
    moves.finish()
    links.finish()


def backward_call(square, shrink, saves, block_shape, memory_shape):
    results = [jax.ShapeDtypeStruct(block_shape, BF)]
    results += [jax.ShapeDtypeStruct(shape, F32) for shape in (block_shape, memory_shape)]
    results += [jax.ShapeDtypeStruct((32, D), F32)] * 8
    results += [jax.ShapeDtypeStruct(shape, F32) for shape in ((32, 4 * D), (LEN, D), (8, D))]
    saved = {**FORWARD_SAVES, **TURNED_SAVES}
    held = {name: saved[name] for name in saved if name != "final_low"}
    return pl.pallas_call(
        backward_kernel,
        in_specs=[IN_PLACE] * (2 + len(saved)),
        out_specs=[IN_PLACE] + [IN_VMEM] * (len(results) - 1),
        out_shape=results,
        scratch_shapes=[
            *vmem_of(held),
            *vmem_of(BACKWARD_SCRATCH),
            pltpu.SemaphoreType.DMA((BACKWARD_SENDS,)),
            pltpu.SemaphoreType.DMA((BACKWARD_SLOTS,)),
            pltpu.SemaphoreType.DMA((BACKWARD_MOVES,)),
        ],
        compiler_params=pltpu.CompilerParams(collective_id=1, has_side_effects=True, vmem_limit_bytes=63 << 20),
    )(square, shrink.reshape(4, 4, D, OWN), *(saves[name] for name in saved))


def hand_over_kernel(norms, *refs):
    count = (len(refs) - 3) // 3
    gains, biases, sem = refs[2 * count], refs[2 * count + 1], refs[-1]
    held = refs[2 * count + 2 : -1]
    loads = [pltpu.make_async_copy(refs[n], held[n], sem.at[0, n]) for n in range(count)]
    stores = [pltpu.make_async_copy(held[n], refs[count + n], sem.at[1, n]) for n in range(count)]
    for load in loads:
        load.start()
    for load, store in zip(loads, stores):
        load.wait()
        store.start()
    own = pltpu.roll(norms[...], (D - 32 * Place().number) % D, 1)
    gains[...] = own[:3, :32]
    biases[...] = own[3:6, :32]
    for store in stores:
        store.wait()


def hand_over(norms, values):
    shapes = [jax.ShapeDtypeStruct(value.shape, value.dtype) for value in values]
    return pl.pallas_call(
        hand_over_kernel,
        in_specs=[IN_VMEM] + [IN_PLACE] * len(values),
        out_specs=[IN_PLACE] * len(values) + [IN_VMEM] * 2,
        out_shape=shapes + [jax.ShapeDtypeStruct((3, 32), F32)] * 2,
        scratch_shapes=[
            *(pltpu.VMEM(shape.shape, shape.dtype) for shape in shapes),
            pltpu.SemaphoreType.DMA((2, len(values))),
        ],
        compiler_params=pltpu.CompilerParams(vmem_limit_bytes=VMEM_BYTES),
    )(norms, *values)


def fast_shards(
    tokens, memory, lengths, memory_segments, out_grad,
    self_query, self_key, self_value, self_out,
    cross_query, cross_key, cross_value, cross_out,
    expand_weight, shrink_weight, norm_gains, norm_biases,
):
    weights = (self_key, self_value, self_query, self_out, cross_query, cross_key, cross_value, cross_out)
    square, shrink, saves = forward_call(
        lengths, memory_segments, norm_gains, norm_biases, tokens, memory, out_grad, (*weights, expand_weight, shrink_weight)
    )
    *values, norm_grads = backward_call(square, shrink, saves, tokens.shape, memory.shape)
    output, input_grad, memory_grad, *units, expand_grad, shrink_grad, gains_grad, biases_grad = hand_over(norm_grads, values)
    return (
        output,
        input_grad,
        memory_grad,
        *(units[unit] for unit in (QUERY, KEY, VALUE, OUT, CROSS_QUERY, CROSS_KEY, CROSS_VALUE, CROSS_OUT)),
        expand_grad,
        shrink_grad,
        gains_grad,
        biases_grad,
    )


def solution(mesh):
    quick = dict(mesh.shape) == {"dp": 4, "seq": 8}
    return jax.shard_map(
        fast_shards if quick else shards,
        mesh=mesh,
        in_specs=(
            P("dp", "seq", None),
            P("dp", "seq", None),
            P("dp", None),
            P("dp", None),
            P("dp", "seq", None),
            P(("dp", "seq"), None),
            P(("dp", "seq"), None),
            P(("dp", "seq"), None),
            P(("dp", "seq"), None),
            P(("dp", "seq"), None),
            P(("dp", "seq"), None),
            P(("dp", "seq"), None),
            P(("dp", "seq"), None),
            P(("dp", "seq"), None),
            P(("dp", "seq"), None),
            P(None, ("dp", "seq")),
            P(None, ("dp", "seq")),
        ),
        out_specs=(
            P("dp", "seq", None),
            P("dp", "seq", None),
            P("dp", "seq", None),
            P(("dp", "seq"), None),
            P(("dp", "seq"), None),
            P(("dp", "seq"), None),
            P(("dp", "seq"), None),
            P(("dp", "seq"), None),
            P(("dp", "seq"), None),
            P(("dp", "seq"), None),
            P(("dp", "seq"), None),
            P(("dp", "seq"), None),
            P(("dp", "seq"), None),
            P(None, ("dp", "seq")),
            P(None, ("dp", "seq")),
        ),
        check_vma=False,
    )
```
